32 devices in a mesh: seq: 8 (over z, core), chan: 4 (over y, x).
Axes of the slice: x: 2, y: 2, z: 4, core: 2. Of those that a mesh axis runs over, the one named last changes fastest.
Arguments:
- tokens: bfloat16 [16384, 768], P(('seq', 'chan')), may hold values from -6 to 6
- norm_gain: float32 [768], replicated, may hold values from 0.5 to 1.5
- in_weight: bfloat16 [768, 3072], replicated, may hold values from -0.21875 to 0.21875
- conv_weight: float32 [4, 1536], P(None, 'chan'), may hold values from -3 to 3
- conv_bias: float32 [1536], P('chan'), may hold values from -3 to 3
- proj_weight: bfloat16 [1536, 80], P('chan'), may hold values from -0.15625 to 0.15625
- step_weight: bfloat16 [48, 1536], P(None, 'chan'), may hold values from -0.875 to 0.875
- step_bias: float32 [1536], P('chan'), may hold values from -6 to -1
- decay_log: float32 [16, 1536], P(None, 'chan'), may hold values from -3 to 2.5
- skip_gain: float32 [1536], P('chan'), may hold values from 0.5 to 1.5
- out_weight: bfloat16 [1536, 768], replicated, may hold values from -0.078125 to 0.078125
- cotangent: bfloat16 [16384, 768], P(('seq', 'chan')), may hold values from -6 to 6
- lengths: int32 [8, 4], P('seq'), may hold values from 64 to 1856, as said below
Outputs:
- block_out: bfloat16 [16384, 768], P(('seq', 'chan'))
- grad_tokens: float32 [16384, 768], P(('seq', 'chan'))
- grad_norm_gain: float32 [768], P('chan')
- grad_in_weight: float32 [768, 3072], P(None, 'chan')
- grad_conv_weight: float32 [4, 1536], P(None, 'chan')
- grad_conv_bias: float32 [1536], P('chan')
- grad_proj_weight: float32 [1536, 80], P('chan')
- grad_step_weight: float32 [48, 1536], P(None, 'chan')
- grad_step_bias: float32 [1536], P('chan')
- grad_decay_log: float32 [16, 1536], P(None, 'chan')
- grad_skip_gain: float32 [1536], P('chan')
- grad_out_weight: float32 [1536, 768], P('chan')
The draws below stay inside these ranges and needn't reach their ends.
Inputs may be any that keep to these rules, and one draw needn't show every extreme that they name: Each row lists the lengths of the 4 sequences of one group in packing order; they sum to 2048. One, the long one, begins within the group's first 512 rows and ends within its last 512 rows; the others are at most 128 long.
All inputs are finite; a program needn't handle non-finite values.
Results may differ from the reference program's by a relative error of at most 0.011.
Values may be sent and summed in bfloat16 or wider, within the bound.
A program may use at most 320 MiB of HBM per device.

```python
import jax
import jax.numpy as jnp
from jax import lax

D = 768
E = 1536
N = 16
R = 48
K = 4
SPAN = 256
TOK_DEV = 512
COUNT = 4
GROUPS = 8
GROUP_TOK = 2048
TOKENS = 16384


def draw_lengths(key, part):
    key = jax.random.fold_in(key, 7)
    short_key, order_key = jax.random.split(key)
    random_shorts = jax.random.randint(short_key, (GROUPS, COUNT - 2), TOK_DEV // 8, TOK_DEV // 4 + 1, dtype=jnp.int32)
    first_group = jnp.arange(GROUPS, dtype=jnp.int32)[:, None] == 0
    random_shorts = jnp.where(first_group, jnp.int32(TOK_DEV // 8), random_shorts).astype(jnp.int32)
    fixed_short = jnp.full((GROUPS, 1), TOK_DEV // 8, jnp.int32)
    shorts = jnp.concatenate([fixed_short, random_shorts], axis=1)
    leading = jax.random.randint(order_key, (GROUPS, 1), 0, COUNT, dtype=jnp.int32)
    longest = GROUP_TOK - jnp.sum(shorts, axis=1, keepdims=True).astype(jnp.int32)
    places = jnp.arange(COUNT, dtype=jnp.int32)[None, :]
    column = jnp.zeros((GROUPS, 1), jnp.int32)
    early = jnp.concatenate([shorts, column], axis=1)
    later = jnp.concatenate([column, shorts], axis=1)
    return jnp.where(places < leading, early, jnp.where(places == leading, longest, later)).astype(jnp.int32)


def levels(key, shape, shards, low, top_value):
    loudness, own = 1.0, jax.random.fold_in(key, 6)
    for dim, parts in shards:
        heights = jnp.exp(jax.random.uniform(jax.random.fold_in(own, dim), (parts,), jnp.float32, low / len(shards), top_value / len(shards)))
        loudness = loudness * jnp.repeat(heights, shape[dim] // parts).reshape([-1 if axis == dim else 1 for axis in range(len(shape))])
    return loudness


def gaussian(key, dims, scale, bound, cuts=(), held_as=jnp.bfloat16):
    values = jax.random.normal(key, dims, jnp.float32) * scale
    if len(cuts) > 0:
        values = levels(key, dims, cuts, -0.22, 0.18) * values
    return jnp.clip(values, min=-bound, max=bound).astype(held_as)


def setup_inputs(seed: int = 0) -> dict:
    seeds = jax.random.split(jax.random.key(seed), 14)
    return {
        "tokens": gaussian(seeds[0], (TOKENS, D), 1.0, 6.0, ((0, 32),)),
        "norm_gain": jnp.clip(1.0 + 0.1 * jax.random.normal(seeds[1], (D,), jnp.float32), 0.5, 1.5),
        "in_weight": gaussian(seeds[2], (D, 2 * E), D ** -0.5, 0.21875),
        "conv_weight": gaussian(seeds[3], (K, E), K ** -0.5, 3.0, ((1, 4),), jnp.float32),
        "conv_bias": gaussian(seeds[4], (E,), 0.5, 3.0, ((0, 4),), jnp.float32),
        "proj_weight": gaussian(seeds[5], (E, R + 2 * N), E ** -0.5, 0.15625, ((0, 4),)),
        "step_weight": gaussian(seeds[6], (R, E), R ** -0.5, 0.875, ((1, 4),)),
        "step_bias": jnp.clip(-6.0 + 5.0 * jax.random.uniform(seeds[7], (E,), jnp.float32) ** levels(seeds[7], (E,), ((0, 4),), -0.2, 0.2), -6.0, -1.0),
        "decay_log": jnp.clip(-3.0 + 5.5 * jax.random.uniform(seeds[8], (N, E), jnp.float32) ** levels(seeds[8], (N, E), ((1, 4),), -0.2, 0.2), -3.0, 2.5),
        "skip_gain": jnp.clip(0.5 + 1.0 * jax.random.uniform(seeds[9], (E,), jnp.float32) ** levels(seeds[9], (E,), ((0, 4),), -0.2, 0.2), 0.5, 1.5),
        "out_weight": gaussian(seeds[10], (E, D), (4 * E) ** -0.5, 0.078125),
        "cotangent": gaussian(seeds[11], (TOKENS, D), 1.0, 6.0, ((0, 32),)),
        "lengths": draw_lengths(jax.random.fold_in(seeds[13], 71), 0),
    }


epsilon = 1e-05

@jax.custom_vjp
def low(v):
    return lax.optimization_barrier(v.astype(jnp.bfloat16)).astype(jnp.float32)

@jax.custom_vjp
def low_back(v):
    return v

def low_keep(v):
    return (low(v), None)

def low_pass(kept, grad):
    return (grad,)

def back_keep(v):
    return (v, None)

def back_low(kept, grad):
    return (low(grad),)
low.defvjp(low_keep, low_pass)
low_back.defvjp(back_keep, back_low)

def product(left, right):
    return jnp.dot(left, right, precision=lax.Precision.HIGHEST, preferred_element_type=jnp.float32)

def group_marks(lengths_row, row_count):
    starts = (jnp.cumsum(lengths_row) - lengths_row).astype(jnp.int32)
    places = jnp.arange(row_count, dtype=jnp.int32)
    segment = lax.optimization_barrier(jnp.sum((places[:, None] >= starts[None, :]).astype(jnp.int32), axis=1)).astype(jnp.int32)
    starts_here = jnp.any(places[:, None] == starts[None, :], axis=1)
    return (segment, starts_here)

def delayed(values, offset):
    return jnp.concatenate([jnp.zeros((offset,) + values.shape[1:], values.dtype), values[:-offset]], axis=0)

def usable_taps(segment, offset):
    same = segment[offset:] == segment[:-offset]
    return jnp.concatenate([jnp.zeros((offset,), jnp.bool_), same])

def selective_scan(activation, step_size, b_proj, c_proj, keep_mask, decay_rate):
    row_count = activation.shape[0]
    spans = row_count // SPAN

    def shaped(values):
        return values.reshape((spans, SPAN) + values.shape[1:])

    def span_step(carried, pieces):

        def position(inner_state, entries):
            input_now, step_now, b_now, c_now, keep_now = entries
            factor = jnp.exp(step_now[None, :] * decay_rate) * keep_now
            inner_state = factor * inner_state + b_now[:, None] * (step_now * input_now)[None, :]
            return (inner_state, lax.optimization_barrier(jnp.sum(c_now[:, None] * inner_state, axis=0)))
        return lax.scan(position, carried, pieces)
    start_state = jnp.zeros(decay_rate.shape, jnp.float32)
    pieces = (shaped(activation), shaped(step_size), shaped(b_proj), shaped(c_proj), shaped(keep_mask))
    unused, results = lax.scan(jax.checkpoint(span_step), start_state, pieces)
    return results.reshape(row_count, activation.shape[1])

def forward_group(weights, tokens_f, lengths_row):
    norm_gain, in_weight, conv_weight, conv_bias, proj_weight, step_weight, step_bias, decay_log, skip_gain, out_weight = weights
    row_count = tokens_f.shape[0]
    segment, starts_here = group_marks(lengths_row, row_count)
    keep_mask = 1.0 - starts_here.astype(jnp.float32)
    inv_rms = lax.rsqrt(lax.optimization_barrier(jnp.mean(tokens_f * tokens_f, axis=1, keepdims=True)) + epsilon)
    normed = low(tokens_f * inv_rms * norm_gain)
    mixed_in = low_back(product(normed, in_weight))
    inner_chan = low(mixed_in[:, :E])
    gate_in = mixed_in[:, E:]
    conv_sum = conv_bias + conv_weight[K - 1] * inner_chan
    for offset in range(1, K):
        usable = usable_taps(segment, offset)
        conv_sum = conv_sum + conv_weight[K - 1 - offset] * jnp.where(usable[:, None], delayed(inner_chan, offset), 0.0)
    activation = jax.nn.silu(conv_sum)
    projected = low_back(product(low(activation), proj_weight))
    step_low = low(projected[:, :R])
    b_proj = projected[:, R:R + N]
    c_proj = projected[:, R + N:]
    step_pre = low_back(product(step_low, step_weight))
    step_size = jax.nn.softplus(step_pre + step_bias)
    decay_rate = -jnp.exp(decay_log)
    scanned = selective_scan(activation, step_size, b_proj, c_proj, keep_mask, decay_rate)
    mixer_out = low_back(low(scanned + skip_gain * activation))
    gated_out = mixer_out * jax.nn.silu(gate_in)
    return tokens_f + product(low(gated_out), out_weight)

def reference(tokens, norm_gain, in_weight, conv_weight, conv_bias, proj_weight, step_weight, step_bias, decay_log, skip_gain, out_weight, cotangent, lengths):
    weights = tuple((values.astype(jnp.float32) for values in (norm_gain, in_weight, conv_weight, conv_bias, proj_weight, step_weight, step_bias, decay_log, skip_gain, out_weight)))
    token_groups = tokens.astype(jnp.float32).reshape(GROUPS, GROUP_TOK, D)
    grad_groups = cotangent.astype(jnp.float32).reshape(GROUPS, GROUP_TOK, D)

    def one_group(totals, pieces):
        group_tokens, group_grad, lengths_row = pieces

        def forward(weight_list, inputs):
            return forward_group(weight_list, inputs, lengths_row)
        result, pullback = jax.vjp(forward, weights, group_tokens)
        grad_weights, grad_inputs = pullback(group_grad)
        totals = jax.tree.map(jnp.add, totals, grad_weights)
        return (totals, (result.astype(jnp.bfloat16), grad_inputs))
    zero_grads = tuple((jnp.zeros_like(values) for values in weights))
    totals, (results, grad_inputs) = lax.scan(one_group, zero_grads, (token_groups, grad_groups, lengths))
    return (results.reshape(TOKENS, D), grad_inputs.reshape(TOKENS, D), totals[0], totals[1], totals[2], totals[3], totals[4], totals[5], totals[6], totals[7], totals[8], totals[9])
```

```python
import functools
import math

import jax
import jax.numpy as jnp
from jax import lax
from jax.experimental import pallas as pl
from jax.experimental.pallas import tpu as pltpu
from jax.sharding import PartitionSpec as P

epsilon = 1e-05
LOG2E = math.log2(math.e)
CUT = 1e30
TC = 16
EB = 512
f32 = jnp.float32
bf16 = jnp.bfloat16


def pre_kernel(dtk_ref, u_ref, g_ref, b_ref, c_ref, rate_ref, hend_ref, head_ref, thru_ref):
    rate = rate_ref[...]
    chunks = b_ref.shape[0]

    def chunk(c, carry):
        h, through, head = carry
        base = pl.multiple_of(c * TC, TC)
        b_cols, c_cols = b_ref[c], c_ref[c]
        for j in range(TC):
            d = dtk_ref[pl.ds(base + j, 1), :]
            u = u_ref[pl.ds(base + j, 1), :]
            g = g_ref[pl.ds(base + j, 1), :]
            factor = jnp.exp2(d * rate)
            h = factor * h + b_cols[:, j : j + 1] * u
            through = factor * through
            head = head + through * (c_cols[:, j : j + 1] * g)
        return h, through, head

    zero = jnp.zeros(rate.shape, f32)
    h, through, head = lax.fori_loop(0, chunks, chunk, (zero, zero + 1.0, zero))
    hend_ref[...] = h
    head_ref[...] = head
    thru_ref[...] = through


def fwd_kernel(dtk_ref, u_ref, b_ref, cd_ref, g_ref, rate_ref, hin_ref, y_ref, h_ref, gc_ref):
    rate = rate_ref[...]
    chunks, states = b_ref.shape[0], b_ref.shape[1]
    width = TC * states
    diag = same_step(states)

    @pl.when(pl.program_id(0) == 0)
    def _():
        gc_ref[...] = jnp.zeros_like(gc_ref)

    h_ref[0:states, :] = hin_ref[...].astype(bf16)

    def chunk(c, h):
        base = pl.multiple_of(c * TC, TC)
        row = pl.multiple_of(c * width, width)
        b_cols = b_ref[c]
        for j in range(TC):
            d = dtk_ref[pl.ds(base + j, 1), :]
            u = u_ref[pl.ds(base + j, 1), :]
            h = jnp.exp2(d * rate) * h + b_cols[:, j : j + 1] * u
            h_ref[pl.ds(row + (j + 1) * states, states), :] = h.astype(bf16)
        held = h_ref[pl.ds(row + states, width), :]
        y_ref[pl.ds(base, TC), :] = jnp.dot(cd_ref[c], held, preferred_element_type=f32)
        g_low = g_ref[pl.ds(base, TC), :].astype(bf16)
        part = lax.dot_general(g_low, held, (((1,), (1,)), ((), ())), preferred_element_type=f32)
        gc_ref[pl.ds(c, 1), :] += jnp.sum(jnp.where(diag, part, 0.0), axis=0, keepdims=True)
        return h

    lax.fori_loop(0, chunks, chunk, hin_ref[...])


def bwd_kernel(
    dtk_ref, u_ref, g_ref, c_ref, bd_ref, rate_ref, fin_ref, h_ref,
    bsum_ref, wsum_ref, gb_ref, acc_ref, adj_ref, wr_ref,
):
    rate = rate_ref[...]
    chunks, states = c_ref.shape[0], c_ref.shape[1]
    width = TC * states
    diag = same_step(states)
    ones = diag.astype(f32).astype(bf16)

    @pl.when(pl.program_id(0) == 0)
    def _():
        gb_ref[...] = jnp.zeros_like(gb_ref)

    def chunk(i, carry):
        flow, acc = carry
        c = chunks - 1 - i
        base = pl.multiple_of(c * TC, TC)
        row = pl.multiple_of(c * width, width)
        c_cols = c_ref[c]
        for j in reversed(range(TC)):
            d = dtk_ref[pl.ds(base + j, 1), :]
            g = g_ref[pl.ds(base + j, 1), :]
            adj = c_cols[:, j : j + 1] * g + flow
            flow = jnp.exp2(d * rate) * adj
            before = h_ref[pl.ds(row + j * states, states), :].astype(f32)
            wr = flow * before * rate
            acc = acc + wr * d
            adj_ref[j * states : (j + 1) * states, :] = adj.astype(bf16)
            wr_ref[j * states : (j + 1) * states, :] = wr.astype(bf16)
        held = adj_ref[...]
        bsum_ref[pl.ds(base, TC), :] = jnp.dot(bd_ref[c], held, preferred_element_type=f32)
        wsum_ref[pl.ds(base, TC), :] = jnp.dot(ones, wr_ref[...], preferred_element_type=f32)
        u_low = u_ref[pl.ds(base, TC), :].astype(bf16)
        part = lax.dot_general(u_low, held, (((1,), (1,)), ((), ())), preferred_element_type=f32)
        gb_ref[pl.ds(c, 1), :] += jnp.sum(jnp.where(diag, part, 0.0), axis=0, keepdims=True)
        return flow, acc

    unused, acc = lax.fori_loop(0, chunks, chunk, (fin_ref[...], jnp.zeros(rate.shape, f32)))
    acc_ref[...] = acc


def same_step(states):
    shape = (TC, TC * states)
    here = lax.broadcasted_iota(jnp.int32, shape, 0) * states
    place = lax.broadcasted_iota(jnp.int32, shape, 1)
    return (place >= here) & (place < here + states)


def params():
    return pltpu.CompilerParams(
        dimension_semantics=("arbitrary",), vmem_limit_bytes=56 * 1024 * 1024
    )


def cols(rows):
    return pl.BlockSpec((rows, EB), lambda i: (0, i))


def whole(shape):
    return pl.BlockSpec(shape, lambda i: (0,) * len(shape))


def pre_scan(dtk, u, g, b_cols, c_cols, rate):
    T, E = dtk.shape
    N = rate.shape[0]
    state = jax.ShapeDtypeStruct((N, E), f32)
    return pl.pallas_call(
        pre_kernel,
        grid=(E // EB,),
        in_specs=[cols(T), cols(T), cols(T), whole(b_cols.shape), whole(c_cols.shape), cols(N)],
        out_specs=[cols(N)] * 3,
        out_shape=[state] * 3,
        compiler_params=params(),
        name="pre_scan",
    )(dtk, u, g, b_cols, c_cols, rate)


def fwd_scan(dtk, u, b_cols, c_diag, g, rate, entering):
    T, E = dtk.shape
    N = rate.shape[0]
    rows = (T + 1) * N
    return pl.pallas_call(
        fwd_kernel,
        grid=(E // EB,),
        in_specs=[cols(T), cols(T), whole(b_cols.shape), whole(c_diag.shape), cols(T), cols(N), cols(N)],
        out_specs=[cols(T), cols(rows), whole((T // TC, TC * N))],
        out_shape=[
            jax.ShapeDtypeStruct((T, E), f32),
            jax.ShapeDtypeStruct((rows, E), bf16),
            jax.ShapeDtypeStruct((T // TC, TC * N), f32),
        ],
        compiler_params=params(),
        name="fwd_scan",
    )(dtk, u, b_cols, c_diag, g, rate, entering)


def bwd_scan(dtk, u, g, c_cols, b_diag, rate, arriving, held):
    T, E = dtk.shape
    N = rate.shape[0]
    return pl.pallas_call(
        bwd_kernel,
        grid=(E // EB,),
        in_specs=[cols(T), cols(T), cols(T), whole(c_cols.shape), whole(b_diag.shape), cols(N), cols(N), cols(held.shape[0])],
        out_specs=[cols(T), cols(T), whole((T // TC, TC * N)), cols(N)],
        out_shape=[
            jax.ShapeDtypeStruct((T, E), f32),
            jax.ShapeDtypeStruct((T, E), f32),
            jax.ShapeDtypeStruct((T // TC, TC * N), f32),
            jax.ShapeDtypeStruct((N, E), f32),
        ],
        scratch_shapes=[pltpu.VMEM((TC * N, EB), bf16), pltpu.VMEM((TC * N, EB), bf16)],
        compiler_params=params(),
        name="bwd_scan",
    )(dtk, u, g, c_cols, b_diag, rate, arriving, held)


def chunk_cols(values):
    T, N = values.shape
    return jnp.swapaxes(values.reshape(T // TC, TC, N), 1, 2)


def chunk_diag(values):
    T, N = values.shape
    eye = jnp.eye(TC, dtype=f32)
    spread = values.reshape(T // TC, 1, TC, N) * eye[None, :, :, None]
    return spread.reshape(T // TC, TC, TC * N).astype(bf16)


def shifted(values, offset, count):
    pairs = [(i, i + offset) for i in range(count) if 0 <= i + offset < count]
    return lax.ppermute(values, "chan", pairs)


def free_of_starts(starts, places, offset):
    inside = (starts[None, :] > places[:, None] - offset) & (starts[None, :] <= places[:, None])
    return jnp.logical_not(jnp.any(inside, axis=1))


def local(
    tokens, norm_gain, in_weight, conv_weight, conv_bias, proj_weight, step_weight,
    step_bias, decay_log, skip_gain, out_weight, cotangent, lengths,
):
    T, D = tokens.shape
    E = in_weight.shape[1] // 2
    R = step_weight.shape[0]
    N = decay_log.shape[0]
    K = conv_weight.shape[0]
    ci = lax.axis_index("chan")
    cc = lax.axis_size("chan")
    packed = jnp.concatenate(
        [
            conv_weight, conv_bias[None], step_bias[None], decay_log, skip_gain[None],
            proj_weight.T.astype(f32), step_weight.astype(f32),
        ],
        axis=0,
    )
    packed = lax.all_gather(packed, "chan", axis=1, tiled=True)
    sizes = [K, 1, 1, N, 1, R + 2 * N, R]
    ends = [sum(sizes[: i + 1]) for i in range(len(sizes))]
    conv_w, conv_b, step_b, decay_log, skip, proj_t, step_w = [
        packed[e - s : e] for s, e in zip(sizes, ends)
    ]
    proj_t, step_w = proj_t.astype(bf16), step_w.astype(bf16)

    tokens_f = tokens.astype(f32)
    inv_rms = lax.rsqrt(jnp.mean(tokens_f * tokens_f, axis=1, keepdims=True) + epsilon)
    normed = (tokens_f * inv_rms * norm_gain).astype(bf16)
    mixed_in = jnp.dot(normed, in_weight, preferred_element_type=f32)
    inner_low = mixed_in[:, :E].astype(bf16)
    gate_in = mixed_in[:, E:]
    before = shifted(inner_low[T - (K - 1) :], 1, cc)
    inner_ext = jnp.concatenate([before, inner_low], axis=0).astype(f32)

    grad_gated = lax.dot_general(
        cotangent, out_weight, (((1,), (1,)), ((), ())), preferred_element_type=f32
    )
    sig_gate = jax.nn.sigmoid(gate_in)
    gate_act = gate_in * sig_gate
    grad_mixer = (grad_gated * gate_act).astype(bf16).astype(f32)

    starts = jnp.cumsum(lengths[0]) - lengths[0]
    places = ci * T + jnp.arange(T + K - 1, dtype=jnp.int32)
    usable = [None] + [free_of_starts(starts, places, j) for j in range(1, K)]
    cut = jnp.any(places[:T, None] == starts[None, :], axis=1)

    conv_sum = conv_b + conv_w[K - 1] * inner_ext[K - 1 :]
    for j in range(1, K):
        delayed = inner_ext[K - 1 - j : K - 1 - j + T]
        conv_sum = conv_sum + conv_w[K - 1 - j] * jnp.where(usable[j][:T, None], delayed, 0.0)
    sig_conv = jax.nn.sigmoid(conv_sum)
    act = conv_sum * sig_conv
    act_low = act.astype(bf16)
    nt = (((1,), (1,)), ((), ()))
    tn = (((0,), (0,)), ((), ()))
    projected = lax.dot_general(act_low, proj_t, nt, preferred_element_type=f32)
    step_low = projected[:, :R].astype(bf16)
    b_proj = projected[:, R : R + N]
    c_proj = projected[:, R + N :]
    step_pre = jnp.dot(step_low, step_w, preferred_element_type=f32) + step_b
    step = jax.nn.softplus(step_pre)
    u = step * act
    dtk = step + jnp.where(cut, CUT, 0.0)[:, None]
    decay_rate = -jnp.exp(decay_log)
    rate = decay_rate * LOG2E

    b_cols, c_cols = chunk_cols(b_proj), chunk_cols(c_proj)
    b_diag, c_diag = chunk_diag(b_proj), chunk_diag(c_proj)
    h_end, head, through = pre_scan(dtk, u, grad_mixer, b_cols, c_cols, rate)
    ahead = jnp.stack([h_end, through])
    behind = jnp.stack([head, through])
    entering = jnp.zeros_like(h_end)
    arriving = jnp.zeros_like(h_end)
    for offset in range(cc - 1, 0, -1):
        got = shifted(ahead, offset, cc)
        entering = got[0] + got[1] * entering
        got = shifted(behind, -offset, cc)
        arriving = got[0] + got[1] * arriving
    y, held, grad_c = fwd_scan(dtk, u, b_cols, c_diag, grad_mixer, rate, entering)

    mixer = (y + skip * act).astype(bf16).astype(f32)
    gated_low = (mixer * gate_act).astype(bf16)
    branch = jnp.dot(gated_low, out_weight, preferred_element_type=f32)
    block_out = (tokens_f + branch).astype(bf16)
    grad_out_part = lax.dot_general(gated_low, cotangent, tn, preferred_element_type=f32)
    grad_gate = (grad_gated * mixer * sig_gate * (1.0 + gate_in * (1.0 - sig_gate))).astype(bf16)

    bsum, wsum, grad_b, acc = bwd_scan(dtk, u, grad_mixer, c_cols, b_diag, rate, arriving, held)
    grad_skip = jnp.sum(grad_mixer * act, axis=0)
    grad_step = wsum * (1.0 / LOG2E) + act * bsum
    grad_decay = acc * (1.0 / LOG2E)
    grad_pre_f = grad_step * jax.nn.sigmoid(step_pre)
    grad_step_bias = jnp.sum(grad_pre_f, axis=0)
    grad_pre = grad_pre_f.astype(bf16)
    grad_step_w = lax.dot_general(step_low, grad_pre, tn, preferred_element_type=f32)
    grad_rank = lax.dot_general(grad_pre, step_w, nt, preferred_element_type=f32)
    grad_proj = jnp.concatenate(
        [grad_rank, grad_b.reshape(T, N), grad_c.reshape(T, N)], axis=1
    ).astype(bf16)
    grad_proj_t = lax.dot_general(grad_proj, act_low, tn, preferred_element_type=f32)
    grad_act = (
        grad_mixer * skip + step * bsum + jnp.dot(grad_proj, proj_t, preferred_element_type=f32)
    )
    grad_conv = grad_act * sig_conv * (1.0 + conv_sum * (1.0 - sig_conv))
    grad_conv_b = jnp.sum(grad_conv, axis=0)
    after = shifted(grad_conv[: K - 1], -1, cc)
    conv_ext = jnp.concatenate([grad_conv, after], axis=0)
    conv_rows = [None] * K
    conv_rows[K - 1] = jnp.sum(grad_conv * inner_ext[K - 1 :], axis=0)
    grad_inner = conv_w[K - 1] * grad_conv
    for j in range(1, K):
        masked = jnp.where(usable[j][:, None], conv_ext, 0.0)
        delayed = inner_ext[K - 1 - j : K - 1 - j + T]
        conv_rows[K - 1 - j] = jnp.sum(masked[:T] * delayed, axis=0)
        grad_inner = grad_inner + conv_w[K - 1 - j] * masked[j : j + T]
    grad_mixed = jnp.concatenate([grad_inner.astype(bf16), grad_gate], axis=1)
    grad_in_part = lax.dot_general(normed, grad_mixed, tn, preferred_element_type=f32)
    grad_normed = lax.dot_general(grad_mixed, in_weight, nt, preferred_element_type=f32)
    grad_gain = jnp.sum(grad_normed * tokens_f * inv_rms, axis=0)
    scaled = grad_normed * norm_gain
    mean = jnp.mean(tokens_f * scaled, axis=1, keepdims=True)
    grad_tokens = (
        cotangent.astype(f32) + inv_rms * scaled - tokens_f * inv_rms * inv_rms * inv_rms * mean
    )

    channel = jnp.concatenate(
        [
            jnp.stack(conv_rows), grad_conv_b[None], grad_step_bias[None], grad_decay,
            grad_skip[None], grad_proj_t, grad_step_w,
        ],
        axis=0,
    ).astype(bf16)
    rows = channel.shape[0]
    in_share, out_share, gain_share, e_share = 2 * E // cc, E // cc, D // cc, E // cc
    flat = jnp.concatenate(
        [
            jnp.swapaxes(grad_in_part.astype(bf16).reshape(D, cc, in_share), 0, 1).reshape(cc, -1),
            grad_out_part.astype(bf16).reshape(cc, -1),
            jnp.swapaxes(channel.reshape(rows, cc, e_share), 0, 1).reshape(cc, -1),
            grad_gain.astype(bf16).reshape(cc, gain_share),
        ],
        axis=1,
    )
    mine = lax.psum_scatter(flat, "chan", scatter_dimension=0, tiled=True)
    mine = lax.psum(mine, "seq").astype(f32)[0]
    cuts = [D * in_share, out_share * D, rows * e_share, gain_share]
    stops = [sum(cuts[: i + 1]) for i in range(4)]
    g_in, g_out, g_chan, g_gain = [mine[e - s : e] for s, e in zip(cuts, stops)]
    g_chan = g_chan.reshape(rows, e_share)
    g_conv_w, g_conv_b, g_step_b, g_decay, g_skip, g_proj_t, g_step_w = [
        g_chan[e - s : e] for s, e in zip(sizes, ends)
    ]
    return (
        block_out,
        grad_tokens,
        g_gain,
        g_in.reshape(D, in_share),
        g_conv_w,
        g_conv_b[0],
        g_proj_t.T,
        g_step_w,
        g_step_b[0],
        g_decay,
        g_skip[0],
        g_out.reshape(out_share, D),
    )


def solution(mesh):
    tok, row, vec = P(("seq", "chan"), None), P(None, "chan"), P("chan")
    in_specs = (
        tok, P(), P(), row, vec, P("chan", None), row, vec, row, vec, P(), tok, P("seq", None),
    )
    out_specs = (
        tok, tok, vec, row, row, vec, P("chan", None), row, vec, row, vec, P("chan", None),
    )
    return jax.shard_map(local, mesh=mesh, in_specs=in_specs, out_specs=out_specs, check_vma=False)
```

```python
import functools
import math

import jax
import jax.numpy as jnp
from jax import lax
from jax.experimental import pallas as pl
from jax.experimental.pallas import tpu as pltpu
from jax.sharding import PartitionSpec as P

epsilon = 1e-05
LOG2E = math.log2(math.e)
CUT = 1e30
TC = 16
EB = 512
f32 = jnp.float32
bf16 = jnp.bfloat16


def pre_kernel(dtk_ref, u_ref, g_ref, b_ref, c_ref, rate_ref, hend_ref, head_ref, thru_ref):
    rate = rate_ref[...]
    chunks = b_ref.shape[0]

    def chunk(c, carry):
        h, through, head = carry
        base = pl.multiple_of(c * TC, TC)
        b_cols, c_cols = b_ref[c], c_ref[c]
        for j in range(TC):
            d = dtk_ref[pl.ds(base + j, 1), :]
            u = u_ref[pl.ds(base + j, 1), :]
            g = g_ref[pl.ds(base + j, 1), :]
            factor = jnp.exp2(d * rate)
            h = factor * h + b_cols[:, j : j + 1] * u
            through = factor * through
            head = head + through * (c_cols[:, j : j + 1] * g)
        return h, through, head

    zero = jnp.zeros(rate.shape, f32)
    h, through, head = lax.fori_loop(0, chunks, chunk, (zero, zero + 1.0, zero))
    hend_ref[...] = h
    head_ref[...] = head
    thru_ref[...] = through


def fwd_kernel(dtk_ref, u_ref, b_ref, cd_ref, g_ref, rate_ref, hin_ref, y_ref, h_ref, gc_ref):
    rate = rate_ref[...]
    chunks, states = b_ref.shape[0], b_ref.shape[1]
    width = TC * states
    diag = same_step(states)

    @pl.when(pl.program_id(0) == 0)
    def _():
        gc_ref[...] = jnp.zeros_like(gc_ref)

    h_ref[0:states, :] = hin_ref[...].astype(bf16)

    def chunk(c, h):
        base = pl.multiple_of(c * TC, TC)
        row = pl.multiple_of(c * width, width)
        b_cols = b_ref[c]
        for j in range(TC):
            d = dtk_ref[pl.ds(base + j, 1), :]
            u = u_ref[pl.ds(base + j, 1), :]
            h = jnp.exp2(d * rate) * h + b_cols[:, j : j + 1] * u
            h_ref[pl.ds(row + (j + 1) * states, states), :] = h.astype(bf16)
        held = h_ref[pl.ds(row + states, width), :]
        y_ref[pl.ds(base, TC), :] = jnp.dot(cd_ref[c], held, preferred_element_type=f32)
        g_low = g_ref[pl.ds(base, TC), :].astype(bf16)
        part = lax.dot_general(g_low, held, (((1,), (1,)), ((), ())), preferred_element_type=f32)
        gc_ref[pl.ds(c, 1), :] += jnp.sum(jnp.where(diag, part, 0.0), axis=0, keepdims=True)
        return h

    lax.fori_loop(0, chunks, chunk, hin_ref[...])


def bwd_kernel(
    dtk_ref, u_ref, g_ref, c_ref, bd_ref, rate_ref, fin_ref, h_ref,
    bsum_ref, wsum_ref, gb_ref, acc_ref, adj_ref, wr_ref,
):
    rate = rate_ref[...]
    chunks, states = c_ref.shape[0], c_ref.shape[1]
    width = TC * states
    diag = same_step(states)
    ones = diag.astype(f32).astype(bf16)

    @pl.when(pl.program_id(0) == 0)
    def _():
        gb_ref[...] = jnp.zeros_like(gb_ref)

    def chunk(i, carry):
        flow, acc = carry
        c = chunks - 1 - i
        base = pl.multiple_of(c * TC, TC)
        row = pl.multiple_of(c * width, width)
        c_cols = c_ref[c]
        for j in reversed(range(TC)):
            d = dtk_ref[pl.ds(base + j, 1), :]
            g = g_ref[pl.ds(base + j, 1), :]
            adj = c_cols[:, j : j + 1] * g + flow
            flow = jnp.exp2(d * rate) * adj
            before = h_ref[pl.ds(row + j * states, states), :].astype(f32)
            wr = flow * before * rate
            acc = acc + wr * d
            adj_ref[j * states : (j + 1) * states, :] = adj.astype(bf16)
            wr_ref[j * states : (j + 1) * states, :] = wr.astype(bf16)
        held = adj_ref[...]
        bsum_ref[pl.ds(base, TC), :] = jnp.dot(bd_ref[c], held, preferred_element_type=f32)
        wsum_ref[pl.ds(base, TC), :] = jnp.dot(ones, wr_ref[...], preferred_element_type=f32)
        u_low = u_ref[pl.ds(base, TC), :].astype(bf16)
        part = lax.dot_general(u_low, held, (((1,), (1,)), ((), ())), preferred_element_type=f32)
        gb_ref[pl.ds(c, 1), :] += jnp.sum(jnp.where(diag, part, 0.0), axis=0, keepdims=True)
        return flow, acc

    unused, acc = lax.fori_loop(0, chunks, chunk, (fin_ref[...], jnp.zeros(rate.shape, f32)))
    acc_ref[...] = acc


def same_step(states):
    shape = (TC, TC * states)
    here = lax.broadcasted_iota(jnp.int32, shape, 0) * states
    place = lax.broadcasted_iota(jnp.int32, shape, 1)
    return (place >= here) & (place < here + states)


def params():
    return pltpu.CompilerParams(
        dimension_semantics=("arbitrary",), vmem_limit_bytes=56 * 1024 * 1024
    )


def cols(rows):
    return pl.BlockSpec((rows, EB), lambda i: (0, i))


def whole(shape):
    return pl.BlockSpec(shape, lambda i: (0,) * len(shape))


def pre_scan(dtk, u, g, b_cols, c_cols, rate):
    T, E = dtk.shape
    N = rate.shape[0]
    state = jax.ShapeDtypeStruct((N, E), f32)
    return pl.pallas_call(
        pre_kernel,
        grid=(E // EB,),
        in_specs=[cols(T), cols(T), cols(T), whole(b_cols.shape), whole(c_cols.shape), cols(N)],
        out_specs=[cols(N)] * 3,
        out_shape=[state] * 3,
        compiler_params=params(),
        name="pre_scan",
    )(dtk, u, g, b_cols, c_cols, rate)


def fwd_scan(dtk, u, b_cols, c_diag, g, rate, entering):
    T, E = dtk.shape
    N = rate.shape[0]
    rows = (T + 1) * N
    return pl.pallas_call(
        fwd_kernel,
        grid=(E // EB,),
        in_specs=[cols(T), cols(T), whole(b_cols.shape), whole(c_diag.shape), cols(T), cols(N), cols(N)],
        out_specs=[cols(T), cols(rows), whole((T // TC, TC * N))],
        out_shape=[
            jax.ShapeDtypeStruct((T, E), f32),
            jax.ShapeDtypeStruct((rows, E), bf16),
            jax.ShapeDtypeStruct((T // TC, TC * N), f32),
        ],
        compiler_params=params(),
        name="fwd_scan",
    )(dtk, u, b_cols, c_diag, g, rate, entering)


def bwd_scan(dtk, u, g, c_cols, b_diag, rate, arriving, held):
    T, E = dtk.shape
    N = rate.shape[0]
    return pl.pallas_call(
        bwd_kernel,
        grid=(E // EB,),
        in_specs=[cols(T), cols(T), cols(T), whole(c_cols.shape), whole(b_diag.shape), cols(N), cols(N), cols(held.shape[0])],
        out_specs=[cols(T), cols(T), whole((T // TC, TC * N)), cols(N)],
        out_shape=[
            jax.ShapeDtypeStruct((T, E), f32),
            jax.ShapeDtypeStruct((T, E), f32),
            jax.ShapeDtypeStruct((T // TC, TC * N), f32),
            jax.ShapeDtypeStruct((N, E), f32),
        ],
        scratch_shapes=[pltpu.VMEM((TC * N, EB), bf16), pltpu.VMEM((TC * N, EB), bf16)],
        compiler_params=params(),
        name="bwd_scan",
    )(dtk, u, g, c_cols, b_diag, rate, arriving, held)


def chunk_cols(values):
    T, N = values.shape
    return jnp.swapaxes(values.reshape(T // TC, TC, N), 1, 2)


def chunk_diag(values):
    T, N = values.shape
    eye = jnp.eye(TC, dtype=f32)
    spread = values.reshape(T // TC, 1, TC, N) * eye[None, :, :, None]
    return spread.reshape(T // TC, TC, TC * N).astype(bf16)


PIECE = 256
WIDE = 768


def sum_plan(chan_count, seq_count):
    chan_bits = [("chan", 1 << i) for i in range(chan_count.bit_length() - 1)]
    seq_bits = [("seq", 1 << i) for i in range(seq_count.bit_length() - 1)]
    return chan_bits, seq_bits


def sum_kernel(chan_count, seq_count, pieces, x_ref, o_ref, *scratch):
    chan_bits, seq_bits = sum_plan(chan_count, seq_count)
    nc, ns = len(chan_bits), len(seq_bits)
    stages = nc + ns
    held, send_sem, recv_sem = scratch[:stages], scratch[stages], scratch[stages + 1]
    mine = {"seq": lax.axis_index("seq"), "chan": lax.axis_index("chan")}

    def bit_of(name, bit):
        return (mine[name] // bit) % 2

    def partner(name, bit):
        other = dict(mine)
        other[name] = mine[name] + bit - 2 * bit * bit_of(name, bit)
        return (other["seq"], other["chan"])

    def order(p):
        inner = chan_bits if p % 2 == 0 else chan_bits[::-1]
        return seq_bits[:1] + inner + seq_bits[1:]

    barrier = pltpu.get_barrier_semaphore()
    for name, bit in chan_bits + seq_bits:
        pl.semaphore_signal(
            barrier, inc=1, device_id=partner(name, bit), device_id_type=pl.DeviceIdType.MESH
        )
    pl.semaphore_wait(barrier, stages)

    def view(p, s):
        if s == 0:
            return x_ref, p * PIECE
        return held[s - 1].at[p], 0

    def half(p, s, keep):
        name, bit = order(p)[s]
        side = bit_of(name, bit) if keep else 1 - bit_of(name, bit)
        ref, start = view(p, s)
        if name == "seq":
            size = PIECE >> sum(1 for n, b in order(p)[:s] if n == "seq")
            rows = pl.ds(pl.multiple_of(start + side * (size // 2), 16), size // 2)
            return ref.at[:, rows, :]
        left = [b for n, b in chan_bits if b not in [d for m, d in order(p)[:s] if m == "chan"]]
        size = PIECE >> sum(1 for n, b in order(p)[:s] if n == "seq")
        place = sorted(left).index(bit)
        low = 1 << place
        count = 1 << len(left)
        return [
            ref.at[pl.ds((i // low) * 2 * low + side * low + i % low, 1), pl.ds(start, size), :]
            for i in range(count // 2)
        ]

    def parts(p, s, keep):
        found = half(p, s, keep)
        return found if isinstance(found, list) else [found]

    def landing(p, s):
        name, bit = order(p)[s]
        dst = held[s].at[p]
        if name == "seq":
            return [dst]
        return [dst.at[pl.ds(i, 1)] for i in range(dst.shape[0])]

    def copies(p, s):
        name, bit = order(p)[s]
        out = []
        for i, (src, dst) in enumerate(zip(parts(p, s, False), landing(p, s))):
            out.append(
                pltpu.make_async_remote_copy(
                    src_ref=src,
                    dst_ref=dst,
                    send_sem=send_sem.at[p, s, i],
                    recv_sem=recv_sem.at[p, s, i],
                    device_id=partner(name, bit),
                    device_id_type=pl.DeviceIdType.MESH,
                )
            )
        return out

    def my_rows(done):
        start, size = 0, PIECE
        for name, bit in seq_bits[:done]:
            size //= 2
            start = start + bit_of(name, bit) * size
        return start, size

    def gather_copy(p, k):
        start, size = my_rows(ns - k)
        rows = pl.ds(pl.multiple_of(p * PIECE + start, 16), size)
        name, bit = seq_bits[ns - 1 - k]
        return pltpu.make_async_remote_copy(
            src_ref=o_ref.at[rows, :],
            dst_ref=o_ref.at[rows, :],
            send_sem=send_sem.at[p, stages + k, 0],
            recv_sem=recv_sem.at[p, stages + k, 0],
            device_id=partner(name, bit),
            device_id_type=pl.DeviceIdType.MESH,
        )

    total = stages + ns
    for tick in range(pieces + total):
        for p in range(pieces):
            s = tick - p
            if not 0 <= s <= total:
                continue
            if 1 <= s <= stages:
                for copy in copies(p, s - 1):
                    copy.wait_recv()
                for src, dst in zip(parts(p, s - 1, True), landing(p, s - 1)):
                    dst[...] = (dst[...].astype(f32) + src[...].astype(f32)).astype(bf16)
                if s == stages:
                    start, size = my_rows(ns)
                    rows = pl.ds(pl.multiple_of(p * PIECE + start, 16), size)
                    o_ref[rows, :] = held[stages - 1][p, 0]
            elif s > stages:
                gather_copy(p, s - 1 - stages).wait_recv()
            if s < stages:
                for copy in copies(p, s):
                    copy.start()
            elif s < total:
                gather_copy(p, s - stages).start()
    for p in range(pieces):
        for s in range(stages):
            for copy in copies(p, s):
                copy.wait_send()
        for k in range(ns):
            gather_copy(p, k).wait_send()


def sum_owned(parts, seq_count):
    chan_count, rows, wide = parts.shape
    chan_bits, seq_bits = sum_plan(chan_count, seq_count)
    pieces = rows // PIECE
    ordered = seq_bits[:1] + chan_bits + seq_bits[1:]
    scratch, owners, size = [], chan_count, PIECE
    for name, bit in ordered:
        if name == "chan":
            owners //= 2
        else:
            size //= 2
        scratch.append(pltpu.VMEM((pieces, owners, size, wide), bf16))
    total = len(ordered) + len(seq_bits)
    most = max(1, chan_count // 2)
    sems = pltpu.SemaphoreType.DMA((pieces, total, most))
    return pl.pallas_call(
        functools.partial(sum_kernel, chan_count, seq_count, pieces),
        in_specs=[pl.BlockSpec(memory_space=pltpu.VMEM)],
        out_specs=pl.BlockSpec(memory_space=pltpu.VMEM),
        out_shape=jax.ShapeDtypeStruct((rows, wide), bf16),
        scratch_shapes=scratch + [sems, sems],
        compiler_params=pltpu.CompilerParams(
            collective_id=0, has_side_effects=True, vmem_limit_bytes=56 * 1024 * 1024
        ),
        name="sum_owned",
    )(parts)


def shifted(values, offset, count):
    pairs = [(i, i + offset) for i in range(count) if 0 <= i + offset < count]
    return lax.ppermute(values, "chan", pairs)


def free_of_starts(starts, places, offset):
    inside = (starts[None, :] > places[:, None] - offset) & (starts[None, :] <= places[:, None])
    return jnp.logical_not(jnp.any(inside, axis=1))


def local(
    tokens, norm_gain, in_weight, conv_weight, conv_bias, proj_weight, step_weight,
    step_bias, decay_log, skip_gain, out_weight, cotangent, lengths,
):
    T, D = tokens.shape
    E = in_weight.shape[1] // 2
    R = step_weight.shape[0]
    N = decay_log.shape[0]
    K = conv_weight.shape[0]
    ci = lax.axis_index("chan")
    cc = lax.axis_size("chan")
    packed = jnp.concatenate(
        [
            conv_weight, conv_bias[None], step_bias[None], decay_log, skip_gain[None],
            proj_weight.T.astype(f32), step_weight.astype(f32),
        ],
        axis=0,
    )
    packed = lax.all_gather(packed, "chan", axis=1, tiled=True)
    sizes = [K, 1, 1, N, 1, R + 2 * N, R]
    ends = [sum(sizes[: i + 1]) for i in range(len(sizes))]
    conv_w, conv_b, step_b, decay_log, skip, proj_t, step_w = [
        packed[e - s : e] for s, e in zip(sizes, ends)
    ]
    proj_t, step_w = proj_t.astype(bf16), step_w.astype(bf16)

    tokens_f = tokens.astype(f32)
    inv_rms = lax.rsqrt(jnp.mean(tokens_f * tokens_f, axis=1, keepdims=True) + epsilon)
    normed = (tokens_f * inv_rms * norm_gain).astype(bf16)
    mixed_in = jnp.dot(normed, in_weight, preferred_element_type=f32)
    inner_low = mixed_in[:, :E].astype(bf16)
    gate_in = mixed_in[:, E:]
    before = shifted(inner_low[T - (K - 1) :], 1, cc)
    inner_ext = jnp.concatenate([before, inner_low], axis=0).astype(f32)

    grad_gated = lax.dot_general(
        cotangent, out_weight, (((1,), (1,)), ((), ())), preferred_element_type=f32
    )
    sig_gate = jax.nn.sigmoid(gate_in)
    gate_act = gate_in * sig_gate
    grad_mixer = (grad_gated * gate_act).astype(bf16).astype(f32)

    starts = jnp.cumsum(lengths[0]) - lengths[0]
    places = ci * T + jnp.arange(T + K - 1, dtype=jnp.int32)
    usable = [None] + [free_of_starts(starts, places, j) for j in range(1, K)]
    cut = jnp.any(places[:T, None] == starts[None, :], axis=1)

    conv_sum = conv_b + conv_w[K - 1] * inner_ext[K - 1 :]
    for j in range(1, K):
        delayed = inner_ext[K - 1 - j : K - 1 - j + T]
        conv_sum = conv_sum + conv_w[K - 1 - j] * jnp.where(usable[j][:T, None], delayed, 0.0)
    sig_conv = jax.nn.sigmoid(conv_sum)
    act = conv_sum * sig_conv
    act_low = act.astype(bf16)
    nt = (((1,), (1,)), ((), ()))
    tn = (((0,), (0,)), ((), ()))
    projected = lax.dot_general(act_low, proj_t, nt, preferred_element_type=f32)
    step_low = projected[:, :R].astype(bf16)
    b_proj = projected[:, R : R + N]
    c_proj = projected[:, R + N :]
    step_pre = jnp.dot(step_low, step_w, preferred_element_type=f32) + step_b
    step = jax.nn.softplus(step_pre)
    u = step * act
    dtk = step + jnp.where(cut, CUT, 0.0)[:, None]
    decay_rate = -jnp.exp(decay_log)
    rate = decay_rate * LOG2E

    b_cols, c_cols = chunk_cols(b_proj), chunk_cols(c_proj)
    b_diag, c_diag = chunk_diag(b_proj), chunk_diag(c_proj)
    h_end, head, through = pre_scan(dtk, u, grad_mixer, b_cols, c_cols, rate)
    ahead = jnp.stack([h_end, through])
    behind = jnp.stack([head, through])
    entering = jnp.zeros_like(h_end)
    arriving = jnp.zeros_like(h_end)
    for offset in range(cc - 1, 0, -1):
        got = shifted(ahead, offset, cc)
        entering = got[0] + got[1] * entering
        got = shifted(behind, -offset, cc)
        arriving = got[0] + got[1] * arriving
    y, held, grad_c = fwd_scan(dtk, u, b_cols, c_diag, grad_mixer, rate, entering)

    mixer = (y + skip * act).astype(bf16).astype(f32)
    gated_low = (mixer * gate_act).astype(bf16)
    branch = jnp.dot(gated_low, out_weight, preferred_element_type=f32)
    block_out = (tokens_f + branch).astype(bf16)
    grad_out_part = lax.dot_general(gated_low, cotangent, tn, preferred_element_type=f32)
    grad_gate = (grad_gated * mixer * sig_gate * (1.0 + gate_in * (1.0 - sig_gate))).astype(bf16)

    bsum, wsum, grad_b, acc = bwd_scan(dtk, u, grad_mixer, c_cols, b_diag, rate, arriving, held)
    grad_skip = jnp.sum(grad_mixer * act, axis=0)
    grad_step = wsum * (1.0 / LOG2E) + act * bsum
    grad_decay = acc * (1.0 / LOG2E)
    grad_pre_f = grad_step * jax.nn.sigmoid(step_pre)
    grad_step_bias = jnp.sum(grad_pre_f, axis=0)
    grad_pre = grad_pre_f.astype(bf16)
    grad_step_w = lax.dot_general(step_low, grad_pre, tn, preferred_element_type=f32)
    grad_rank = lax.dot_general(grad_pre, step_w, nt, preferred_element_type=f32)
    grad_proj = jnp.concatenate(
        [grad_rank, grad_b.reshape(T, N), grad_c.reshape(T, N)], axis=1
    ).astype(bf16)
    grad_proj_t = lax.dot_general(grad_proj, act_low, tn, preferred_element_type=f32)
    grad_act = (
        grad_mixer * skip + step * bsum + jnp.dot(grad_proj, proj_t, preferred_element_type=f32)
    )
    grad_conv = grad_act * sig_conv * (1.0 + conv_sum * (1.0 - sig_conv))
    grad_conv_b = jnp.sum(grad_conv, axis=0)
    after = shifted(grad_conv[: K - 1], -1, cc)
    conv_ext = jnp.concatenate([grad_conv, after], axis=0)
    conv_rows = [None] * K
    conv_rows[K - 1] = jnp.sum(grad_conv * inner_ext[K - 1 :], axis=0)
    grad_inner = conv_w[K - 1] * grad_conv
    for j in range(1, K):
        masked = jnp.where(usable[j][:, None], conv_ext, 0.0)
        delayed = inner_ext[K - 1 - j : K - 1 - j + T]
        conv_rows[K - 1 - j] = jnp.sum(masked[:T] * delayed, axis=0)
        grad_inner = grad_inner + conv_w[K - 1 - j] * masked[j : j + T]
    grad_mixed = jnp.concatenate([grad_inner.astype(bf16), grad_gate], axis=1)
    grad_in_part = lax.dot_general(normed, grad_mixed, tn, preferred_element_type=f32)
    grad_normed = lax.dot_general(grad_mixed, in_weight, nt, preferred_element_type=f32)
    grad_gain = jnp.sum(grad_normed * tokens_f * inv_rms, axis=0)
    scaled = grad_normed * norm_gain
    mean = jnp.mean(tokens_f * scaled, axis=1, keepdims=True)
    grad_tokens = (
        cotangent.astype(f32) + inv_rms * scaled - tokens_f * inv_rms * inv_rms * inv_rms * mean
    )

    channel = jnp.concatenate(
        [
            jnp.stack(conv_rows), grad_conv_b[None], grad_step_bias[None], grad_decay,
            grad_skip[None], grad_proj_t, grad_step_w,
        ],
        axis=0,
    )
    rows = channel.shape[0]
    in_share, out_share, gain_share, e_share = 2 * E // cc, E // cc, D // cc, E // cc
    small = jnp.concatenate(
        [
            jnp.swapaxes(channel.reshape(rows, cc, e_share), 0, 1).reshape(cc, -1),
            grad_gain.reshape(cc, gain_share),
        ],
        axis=1,
    ).astype(bf16)
    in_rows, out_rows = D * in_share // WIDE, out_share * D // WIDE
    used = in_rows + out_rows
    total_rows = -(-(used * WIDE + small.shape[1]) // (WIDE * PIECE)) * PIECE
    small = jnp.pad(small, ((0, 0), (0, (total_rows - used) * WIDE - small.shape[1])))
    owned = jnp.concatenate(
        [
            jnp.swapaxes(grad_in_part.astype(bf16).reshape(D, cc, in_share), 0, 1).reshape(cc, in_rows, WIDE),
            grad_out_part.astype(bf16).reshape(cc, out_rows, WIDE),
            small.reshape(cc, total_rows - used, WIDE),
        ],
        axis=1,
    )
    mine = sum_owned(owned, lax.axis_size("seq")).astype(f32)
    g_in = mine[:in_rows]
    g_out = mine[in_rows:used]
    tail = mine[used:].reshape(-1)
    g_chan = tail[: rows * e_share].reshape(rows, e_share)
    g_gain = tail[rows * e_share : rows * e_share + gain_share]
    g_conv_w, g_conv_b, g_step_b, g_decay, g_skip, g_proj_t, g_step_w = [
        g_chan[e - s : e] for s, e in zip(sizes, ends)
    ]
    return (
        block_out,
        grad_tokens,
        g_gain,
        g_in.reshape(D, in_share),
        g_conv_w,
        g_conv_b[0],
        g_proj_t.T,
        g_step_w,
        g_step_b[0],
        g_decay,
        g_skip[0],
        g_out.reshape(out_share, D),
    )


def solution(mesh):
    tok, row, vec = P(("seq", "chan"), None), P(None, "chan"), P("chan")
    in_specs = (
        tok, P(), P(), row, vec, P("chan", None), row, vec, row, vec, P(), tok, P("seq", None),
    )
    out_specs = (
        tok, tok, vec, row, row, vec, P("chan", None), row, vec, row, vec, P("chan", None),
    )
    return jax.shard_map(local, mesh=mesh, in_specs=in_specs, out_specs=out_specs, check_vma=False)
```

```python
import functools
import math

import jax
import jax.numpy as jnp
from jax import lax
from jax.experimental import pallas as pl
from jax.experimental.pallas import tpu as pltpu
from jax.sharding import PartitionSpec as P

epsilon = 1e-05
LOG2E = math.log2(math.e)
CUT = 1e30
TC = 16
EB = 512
UNROLL = 4
f32 = jnp.float32
bf16 = jnp.bfloat16


def pre_kernel(dtk_ref, u_ref, g_ref, b_ref, c_ref, rate_ref, hend_ref, head_ref, thru_ref):
    rate = rate_ref[...]
    chunks = b_ref.shape[0]

    def chunk(c, carry):
        h, through, head = carry
        base = pl.multiple_of(c * TC, TC)
        b_cols, c_cols = b_ref[c], c_ref[c]
        for j in range(TC):
            d = dtk_ref[pl.ds(base + j, 1), :]
            u = u_ref[pl.ds(base + j, 1), :]
            g = g_ref[pl.ds(base + j, 1), :]
            factor = jnp.exp2(d * rate)
            h = factor * h + b_cols[:, j : j + 1] * u
            through = factor * through
            head = head + through * (c_cols[:, j : j + 1] * g)
        return h, through, head

    zero = jnp.zeros(rate.shape, f32)
    h, through, head = lax.fori_loop(0, chunks, chunk, (zero, zero + 1.0, zero))
    hend_ref[...] = h
    head_ref[...] = head
    thru_ref[...] = through


def fwd_kernel(dtk_ref, u_ref, b_ref, cd_ref, g_ref, rate_ref, hin_ref, y_ref, h_ref, gc_ref):
    rate = rate_ref[...]
    chunks, states = b_ref.shape[0], b_ref.shape[1]
    width = TC * states
    diag = same_step(states)

    @pl.when(pl.program_id(0) == 0)
    def _():
        gc_ref[...] = jnp.zeros_like(gc_ref)

    h_ref[0:states, :] = hin_ref[...].astype(bf16)

    def chunk(c, h):
        base = pl.multiple_of(c * TC, TC)
        row = pl.multiple_of(c * width, width)
        b_cols = b_ref[c]
        for j in range(TC):
            d = dtk_ref[pl.ds(base + j, 1), :]
            u = u_ref[pl.ds(base + j, 1), :]
            h = jnp.exp2(d * rate) * h + b_cols[:, j : j + 1] * u
            h_ref[pl.ds(row + (j + 1) * states, states), :] = h.astype(bf16)
        return h

    lax.fori_loop(0, chunks, chunk, hin_ref[...])

    def contract(i, unused):
        for k in range(UNROLL):
            c = i * UNROLL + k
            base = pl.multiple_of(c * TC, TC)
            row = pl.multiple_of(c * width, width)
            held = h_ref[pl.ds(row + states, width), :]
            y_ref[pl.ds(base, TC), :] = jnp.dot(cd_ref[c], held, preferred_element_type=f32)
            g_low = g_ref[pl.ds(base, TC), :].astype(bf16)
            part = lax.dot_general(g_low, held, (((1,), (1,)), ((), ())), preferred_element_type=f32)
            gc_ref[pl.ds(c, 1), :] += jnp.sum(jnp.where(diag, part, 0.0), axis=0, keepdims=True)
        return unused

    lax.fori_loop(0, chunks // UNROLL, contract, 0)


def bwd_kernel(
    dtk_ref, u_ref, g_ref, c_ref, bd_ref, rate_ref, fin_ref, h_ref,
    bsum_ref, wsum_ref, gb_ref, acc_ref, adj_ref, wr_ref,
):
    rate = rate_ref[...]
    chunks, states = c_ref.shape[0], c_ref.shape[1]
    width = TC * states
    diag = same_step(states)
    ones = diag.astype(f32).astype(bf16)

    @pl.when(pl.program_id(0) == 0)
    def _():
        gb_ref[...] = jnp.zeros_like(gb_ref)

    def chunk(i, carry):
        flow, acc = carry
        c = chunks - 1 - i
        base = pl.multiple_of(c * TC, TC)
        row = pl.multiple_of(c * width, width)
        c_cols = c_ref[c]
        for j in reversed(range(TC)):
            d = dtk_ref[pl.ds(base + j, 1), :]
            g = g_ref[pl.ds(base + j, 1), :]
            adj = c_cols[:, j : j + 1] * g + flow
            flow = jnp.exp2(d * rate) * adj
            before = h_ref[pl.ds(row + j * states, states), :].astype(f32)
            wr = flow * before * rate
            acc = acc + wr * d
            adj_ref[pl.ds(row + j * states, states), :] = adj.astype(bf16)
            wr_ref[pl.ds(row + j * states, states), :] = wr.astype(bf16)
        return flow, acc

    unused, acc = lax.fori_loop(0, chunks, chunk, (fin_ref[...], jnp.zeros(rate.shape, f32)))
    acc_ref[...] = acc

    def contract(i, unused):
        for k in range(UNROLL):
            c = i * UNROLL + k
            base = pl.multiple_of(c * TC, TC)
            rows = pl.ds(pl.multiple_of(c * width, width), width)
            held = adj_ref[rows, :]
            bsum_ref[pl.ds(base, TC), :] = jnp.dot(bd_ref[c], held, preferred_element_type=f32)
            wsum_ref[pl.ds(base, TC), :] = jnp.dot(ones, wr_ref[rows, :], preferred_element_type=f32)
            u_low = u_ref[pl.ds(base, TC), :].astype(bf16)
            part = lax.dot_general(u_low, held, (((1,), (1,)), ((), ())), preferred_element_type=f32)
            gb_ref[pl.ds(c, 1), :] += jnp.sum(jnp.where(diag, part, 0.0), axis=0, keepdims=True)
        return unused

    lax.fori_loop(0, chunks // UNROLL, contract, 0)


def same_step(states):
    shape = (TC, TC * states)
    here = lax.broadcasted_iota(jnp.int32, shape, 0) * states
    place = lax.broadcasted_iota(jnp.int32, shape, 1)
    return (place >= here) & (place < here + states)


def params():
    return pltpu.CompilerParams(
        dimension_semantics=("arbitrary",), vmem_limit_bytes=56 * 1024 * 1024
    )


def cols(rows):
    return pl.BlockSpec((rows, EB), lambda i: (0, i))


def whole(shape):
    return pl.BlockSpec(shape, lambda i: (0,) * len(shape))


def pre_scan(dtk, u, g, b_cols, c_cols, rate):
    T, E = dtk.shape
    N = rate.shape[0]
    state = jax.ShapeDtypeStruct((N, E), f32)
    return pl.pallas_call(
        pre_kernel,
        grid=(E // EB,),
        in_specs=[cols(T), cols(T), cols(T), whole(b_cols.shape), whole(c_cols.shape), cols(N)],
        out_specs=[cols(N)] * 3,
        out_shape=[state] * 3,
        compiler_params=params(),
        name="pre_scan",
    )(dtk, u, g, b_cols, c_cols, rate)


def fwd_scan(dtk, u, b_cols, c_diag, g, rate, entering):
    T, E = dtk.shape
    N = rate.shape[0]
    rows = (T + 1) * N
    return pl.pallas_call(
        fwd_kernel,
        grid=(E // EB,),
        in_specs=[cols(T), cols(T), whole(b_cols.shape), whole(c_diag.shape), cols(T), cols(N), cols(N)],
        out_specs=[cols(T), cols(rows), whole((T // TC, TC * N))],
        out_shape=[
            jax.ShapeDtypeStruct((T, E), f32),
            jax.ShapeDtypeStruct((rows, E), bf16),
            jax.ShapeDtypeStruct((T // TC, TC * N), f32),
        ],
        compiler_params=params(),
        name="fwd_scan",
    )(dtk, u, b_cols, c_diag, g, rate, entering)


def bwd_scan(dtk, u, g, c_cols, b_diag, rate, arriving, held):
    T, E = dtk.shape
    N = rate.shape[0]
    return pl.pallas_call(
        bwd_kernel,
        grid=(E // EB,),
        in_specs=[cols(T), cols(T), cols(T), whole(c_cols.shape), whole(b_diag.shape), cols(N), cols(N), cols(held.shape[0])],
        out_specs=[cols(T), cols(T), whole((T // TC, TC * N)), cols(N)],
        out_shape=[
            jax.ShapeDtypeStruct((T, E), f32),
            jax.ShapeDtypeStruct((T, E), f32),
            jax.ShapeDtypeStruct((T // TC, TC * N), f32),
            jax.ShapeDtypeStruct((N, E), f32),
        ],
        scratch_shapes=[pltpu.VMEM((T * N, EB), bf16), pltpu.VMEM((T * N, EB), bf16)],
        compiler_params=params(),
        name="bwd_scan",
    )(dtk, u, g, c_cols, b_diag, rate, arriving, held)


def chunk_cols(values):
    T, N = values.shape
    return jnp.swapaxes(values.reshape(T // TC, TC, N), 1, 2)


def chunk_diag(values):
    T, N = values.shape
    eye = jnp.eye(TC, dtype=f32)
    spread = values.reshape(T // TC, 1, TC, N) * eye[None, :, :, None]
    return spread.reshape(T // TC, TC, TC * N).astype(bf16)


WIDE = 768


def sum_plan(chan_count, seq_count):
    chan_bits = [("chan", 1 << i) for i in range(chan_count.bit_length() - 1)]
    seq_bits = [("seq", 1 << i) for i in range(seq_count.bit_length() - 1)]
    return chan_bits, seq_bits


def sum_kernel(chan_count, seq_count, pieces, x_ref, o_ref, *scratch):
    PIECE = 16 * seq_count
    chan_bits, seq_bits = sum_plan(chan_count, seq_count)
    nc, ns = len(chan_bits), len(seq_bits)
    stages = nc + ns
    held, send_sem, recv_sem = scratch[:stages], scratch[stages], scratch[stages + 1]
    mine = {"seq": lax.axis_index("seq"), "chan": lax.axis_index("chan")}

    def bit_of(name, bit):
        return (mine[name] // bit) % 2

    def partner(name, bit):
        other = dict(mine)
        other[name] = mine[name] + bit - 2 * bit * bit_of(name, bit)
        return (other["seq"], other["chan"])

    def order(p):
        inner = chan_bits if p % 2 == 0 else chan_bits[::-1]
        return seq_bits[:1] + inner + seq_bits[1:]

    barrier = pltpu.get_barrier_semaphore()
    for name, bit in chan_bits + seq_bits:
        pl.semaphore_signal(
            barrier, inc=1, device_id=partner(name, bit), device_id_type=pl.DeviceIdType.MESH
        )
    pl.semaphore_wait(barrier, stages)

    def view(p, s):
        if s == 0:
            return x_ref, p * PIECE
        return held[s - 1].at[p], 0

    def half(p, s, keep):
        name, bit = order(p)[s]
        side = bit_of(name, bit) if keep else 1 - bit_of(name, bit)
        ref, start = view(p, s)
        if name == "seq":
            size = PIECE >> sum(1 for n, b in order(p)[:s] if n == "seq")
            rows = pl.ds(pl.multiple_of(start + side * (size // 2), 16), size // 2)
            return ref.at[:, rows, :]
        left = [b for n, b in chan_bits if b not in [d for m, d in order(p)[:s] if m == "chan"]]
        size = PIECE >> sum(1 for n, b in order(p)[:s] if n == "seq")
        place = sorted(left).index(bit)
        low = 1 << place
        count = 1 << len(left)
        return [
            ref.at[pl.ds((i // low) * 2 * low + side * low + i % low, 1), pl.ds(start, size), :]
            for i in range(count // 2)
        ]

    def parts(p, s, keep):
        found = half(p, s, keep)
        return found if isinstance(found, list) else [found]

    def landing(p, s):
        name, bit = order(p)[s]
        dst = held[s].at[p]
        if name == "seq":
            return [dst]
        return [dst.at[pl.ds(i, 1)] for i in range(dst.shape[0])]

    def copies(p, s):
        name, bit = order(p)[s]
        out = []
        for i, (src, dst) in enumerate(zip(parts(p, s, False), landing(p, s))):
            out.append(
                pltpu.make_async_remote_copy(
                    src_ref=src,
                    dst_ref=dst,
                    send_sem=send_sem.at[p, s, i],
                    recv_sem=recv_sem.at[p, s, i],
                    device_id=partner(name, bit),
                    device_id_type=pl.DeviceIdType.MESH,
                )
            )
        return out

    def my_rows(done):
        start, size = 0, PIECE
        for name, bit in seq_bits[:done]:
            size //= 2
            start = start + bit_of(name, bit) * size
        return start, size

    def gather_copy(p, k):
        start, size = my_rows(ns - k)
        rows = pl.ds(pl.multiple_of(p * PIECE + start, 16), size)
        name, bit = seq_bits[ns - 1 - k]
        return pltpu.make_async_remote_copy(
            src_ref=o_ref.at[rows, :],
            dst_ref=o_ref.at[rows, :],
            send_sem=send_sem.at[p, stages + k, 0],
            recv_sem=recv_sem.at[p, stages + k, 0],
            device_id=partner(name, bit),
            device_id_type=pl.DeviceIdType.MESH,
        )

    total = stages + ns
    for tick in range((pieces + 1) // 2 + total):
        for p in range(pieces):
            s = tick - p // 2
            if not 0 <= s <= total:
                continue
            if 1 <= s <= stages:
                for copy in copies(p, s - 1):
                    copy.wait_recv()
                for src, dst in zip(parts(p, s - 1, True), landing(p, s - 1)):
                    dst[...] = (dst[...].astype(f32) + src[...].astype(f32)).astype(bf16)
                if s == stages:
                    start, size = my_rows(ns)
                    rows = pl.ds(pl.multiple_of(p * PIECE + start, 16), size)
                    o_ref[rows, :] = held[stages - 1][p, 0]
            elif s > stages:
                gather_copy(p, s - 1 - stages).wait_recv()
            if s < stages:
                for copy in copies(p, s):
                    copy.start()
            elif s < total:
                gather_copy(p, s - stages).start()
    for p in range(pieces):
        for s in range(stages):
            for copy in copies(p, s):
                copy.wait_send()
        for k in range(ns):
            gather_copy(p, k).wait_send()


def sum_owned(parts, seq_count):
    chan_count, rows, wide = parts.shape
    chan_bits, seq_bits = sum_plan(chan_count, seq_count)
    PIECE = 16 * seq_count
    pieces = rows // PIECE
    ordered = seq_bits[:1] + chan_bits + seq_bits[1:]
    scratch, owners, size = [], chan_count, PIECE
    for name, bit in ordered:
        if name == "chan":
            owners //= 2
        else:
            size //= 2
        scratch.append(pltpu.VMEM((pieces, owners, size, wide), bf16))
    total = len(ordered) + len(seq_bits)
    most = max(1, chan_count // 2)
    sems = pltpu.SemaphoreType.DMA((pieces, total, most))
    return pl.pallas_call(
        functools.partial(sum_kernel, chan_count, seq_count, pieces),
        in_specs=[pl.BlockSpec(memory_space=pltpu.VMEM)],
        out_specs=pl.BlockSpec(memory_space=pltpu.VMEM),
        out_shape=jax.ShapeDtypeStruct((rows, wide), bf16),
        scratch_shapes=scratch + [sems, sems],
        compiler_params=pltpu.CompilerParams(
            collective_id=0, has_side_effects=True, vmem_limit_bytes=56 * 1024 * 1024
        ),
        name="sum_owned",
    )(parts)


def shifted(values, offset, count):
    pairs = [(i, i + offset) for i in range(count) if 0 <= i + offset < count]
    return lax.ppermute(values, "chan", pairs)


def free_of_starts(starts, places, offset):
    inside = (starts[None, :] > places[:, None] - offset) & (starts[None, :] <= places[:, None])
    return jnp.logical_not(jnp.any(inside, axis=1))


def local(
    tokens, norm_gain, in_weight, conv_weight, conv_bias, proj_weight, step_weight,
    step_bias, decay_log, skip_gain, out_weight, cotangent, lengths,
):
    T, D = tokens.shape
    E = in_weight.shape[1] // 2
    R = step_weight.shape[0]
    N = decay_log.shape[0]
    K = conv_weight.shape[0]
    ci = lax.axis_index("chan")
    cc = lax.axis_size("chan")
    packed = jnp.concatenate(
        [
            conv_weight, conv_bias[None], step_bias[None], decay_log, skip_gain[None],
            proj_weight.T.astype(f32), step_weight.astype(f32),
        ],
        axis=0,
    )
    packed = lax.all_gather(packed, "chan", axis=1, tiled=True)
    sizes = [K, 1, 1, N, 1, R + 2 * N, R]
    ends = [sum(sizes[: i + 1]) for i in range(len(sizes))]
    conv_w, conv_b, step_b, decay_log, skip, proj_t, step_w = [
        packed[e - s : e] for s, e in zip(sizes, ends)
    ]
    proj_t, step_w = proj_t.astype(bf16), step_w.astype(bf16)

    tokens_f = tokens.astype(f32)
    inv_rms = lax.rsqrt(jnp.mean(tokens_f * tokens_f, axis=1, keepdims=True) + epsilon)
    normed = (tokens_f * inv_rms * norm_gain).astype(bf16)
    mixed_in = jnp.dot(normed, in_weight, preferred_element_type=f32)
    inner_low = mixed_in[:, :E].astype(bf16)
    gate_in = mixed_in[:, E:]
    before = shifted(inner_low[T - (K - 1) :], 1, cc)
    inner_ext = jnp.concatenate([before, inner_low], axis=0).astype(f32)

    grad_gated = lax.dot_general(
        cotangent, out_weight, (((1,), (1,)), ((), ())), preferred_element_type=f32
    )
    sig_gate = jax.nn.sigmoid(gate_in)
    gate_act = gate_in * sig_gate
    grad_mixer = (grad_gated * gate_act).astype(bf16).astype(f32)

    starts = jnp.cumsum(lengths[0]) - lengths[0]
    places = ci * T + jnp.arange(T + K - 1, dtype=jnp.int32)
    usable = [None] + [free_of_starts(starts, places, j) for j in range(1, K)]
    cut = jnp.any(places[:T, None] == starts[None, :], axis=1)

    conv_sum = conv_b + conv_w[K - 1] * inner_ext[K - 1 :]
    for j in range(1, K):
        delayed = inner_ext[K - 1 - j : K - 1 - j + T]
        conv_sum = conv_sum + conv_w[K - 1 - j] * jnp.where(usable[j][:T, None], delayed, 0.0)
    sig_conv = jax.nn.sigmoid(conv_sum)
    act = conv_sum * sig_conv
    act_low = act.astype(bf16)
    nt = (((1,), (1,)), ((), ()))
    tn = (((0,), (0,)), ((), ()))
    projected = lax.dot_general(act_low, proj_t, nt, preferred_element_type=f32)
    step_low = projected[:, :R].astype(bf16)
    b_proj = projected[:, R : R + N]
    c_proj = projected[:, R + N :]
    step_pre = jnp.dot(step_low, step_w, preferred_element_type=f32) + step_b
    step = jax.nn.softplus(step_pre)
    u = step * act
    dtk = step + jnp.where(cut, CUT, 0.0)[:, None]
    decay_rate = -jnp.exp(decay_log)
    rate = decay_rate * LOG2E

    b_cols, c_cols = chunk_cols(b_proj), chunk_cols(c_proj)
    b_diag, c_diag = chunk_diag(b_proj), chunk_diag(c_proj)
    h_end, head, through = pre_scan(dtk, u, grad_mixer, b_cols, c_cols, rate)
    ahead = jnp.stack([h_end, through])
    behind = jnp.stack([head, through])
    entering = jnp.zeros_like(h_end)
    arriving = jnp.zeros_like(h_end)
    for offset in range(cc - 1, 0, -1):
        got = shifted(ahead, offset, cc)
        entering = got[0] + got[1] * entering
        got = shifted(behind, -offset, cc)
        arriving = got[0] + got[1] * arriving
    y, held, grad_c = fwd_scan(dtk, u, b_cols, c_diag, grad_mixer, rate, entering)

    mixer = (y + skip * act).astype(bf16).astype(f32)
    gated_low = (mixer * gate_act).astype(bf16)
    branch = jnp.dot(gated_low, out_weight, preferred_element_type=f32)
    block_out = (tokens_f + branch).astype(bf16)
    grad_out_part = lax.dot_general(gated_low, cotangent, tn, preferred_element_type=f32)
    grad_gate = (grad_gated * mixer * sig_gate * (1.0 + gate_in * (1.0 - sig_gate))).astype(bf16)

    bsum, wsum, grad_b, acc = bwd_scan(dtk, u, grad_mixer, c_cols, b_diag, rate, arriving, held)
    grad_skip = jnp.sum(grad_mixer * act, axis=0)
    grad_step = wsum * (1.0 / LOG2E) + act * bsum
    grad_decay = acc * (1.0 / LOG2E)
    grad_pre_f = grad_step * jax.nn.sigmoid(step_pre)
    grad_step_bias = jnp.sum(grad_pre_f, axis=0)
    grad_pre = grad_pre_f.astype(bf16)
    grad_step_w = lax.dot_general(step_low, grad_pre, tn, preferred_element_type=f32)
    grad_rank = lax.dot_general(grad_pre, step_w, nt, preferred_element_type=f32)
    grad_proj = jnp.concatenate(
        [grad_rank, grad_b.reshape(T, N), grad_c.reshape(T, N)], axis=1
    ).astype(bf16)
    grad_proj_t = lax.dot_general(grad_proj, act_low, tn, preferred_element_type=f32)
    grad_act = (
        grad_mixer * skip + step * bsum + jnp.dot(grad_proj, proj_t, preferred_element_type=f32)
    )
    grad_conv = grad_act * sig_conv * (1.0 + conv_sum * (1.0 - sig_conv))
    grad_conv_b = jnp.sum(grad_conv, axis=0)
    after = shifted(grad_conv[: K - 1], -1, cc)
    conv_ext = jnp.concatenate([grad_conv, after], axis=0)
    conv_rows = [None] * K
    conv_rows[K - 1] = jnp.sum(grad_conv * inner_ext[K - 1 :], axis=0)
    grad_inner = conv_w[K - 1] * grad_conv
    for j in range(1, K):
        masked = jnp.where(usable[j][:, None], conv_ext, 0.0)
        delayed = inner_ext[K - 1 - j : K - 1 - j + T]
        conv_rows[K - 1 - j] = jnp.sum(masked[:T] * delayed, axis=0)
        grad_inner = grad_inner + conv_w[K - 1 - j] * masked[j : j + T]
    grad_mixed = jnp.concatenate([grad_inner.astype(bf16), grad_gate], axis=1)
    grad_in_part = lax.dot_general(normed, grad_mixed, tn, preferred_element_type=f32)
    grad_normed = lax.dot_general(grad_mixed, in_weight, nt, preferred_element_type=f32)
    grad_gain = jnp.sum(grad_normed * tokens_f * inv_rms, axis=0)
    scaled = grad_normed * norm_gain
    mean = jnp.mean(tokens_f * scaled, axis=1, keepdims=True)
    grad_tokens = (
        cotangent.astype(f32) + inv_rms * scaled - tokens_f * inv_rms * inv_rms * inv_rms * mean
    )

    channel = jnp.concatenate(
        [
            jnp.stack(conv_rows), grad_conv_b[None], grad_step_bias[None], grad_decay,
            grad_skip[None], grad_proj_t, grad_step_w,
        ],
        axis=0,
    )
    rows = channel.shape[0]
    in_share, out_share, gain_share, e_share = 2 * E // cc, E // cc, D // cc, E // cc
    small = jnp.concatenate(
        [
            jnp.swapaxes(channel.reshape(rows, cc, e_share), 0, 1).reshape(cc, -1),
            grad_gain.reshape(cc, gain_share),
        ],
        axis=1,
    ).astype(bf16)
    in_rows, out_rows = D * in_share // WIDE, out_share * D // WIDE
    used = in_rows + out_rows
    PIECE = 32 * lax.axis_size("seq")
    total_rows = -(-(used * WIDE + small.shape[1]) // (WIDE * PIECE)) * PIECE
    small = jnp.pad(small, ((0, 0), (0, (total_rows - used) * WIDE - small.shape[1])))
    owned = jnp.concatenate(
        [
            jnp.swapaxes(grad_in_part.astype(bf16).reshape(D, cc, in_share), 0, 1).reshape(cc, in_rows, WIDE),
            grad_out_part.astype(bf16).reshape(cc, out_rows, WIDE),
            small.reshape(cc, total_rows - used, WIDE),
        ],
        axis=1,
    )
    mine = sum_owned(owned, lax.axis_size("seq")).astype(f32)
    g_in = mine[:in_rows]
    g_out = mine[in_rows:used]
    tail = mine[used:].reshape(-1)
    g_chan = tail[: rows * e_share].reshape(rows, e_share)
    g_gain = tail[rows * e_share : rows * e_share + gain_share]
    g_conv_w, g_conv_b, g_step_b, g_decay, g_skip, g_proj_t, g_step_w = [
        g_chan[e - s : e] for s, e in zip(sizes, ends)
    ]
    return (
        block_out,
        grad_tokens,
        g_gain,
        g_in.reshape(D, in_share),
        g_conv_w,
        g_conv_b[0],
        g_proj_t.T,
        g_step_w,
        g_step_b[0],
        g_decay,
        g_skip[0],
        g_out.reshape(out_share, D),
    )


def solution(mesh):
    tok, row, vec = P(("seq", "chan"), None), P(None, "chan"), P("chan")
    in_specs = (
        tok, P(), P(), row, vec, P("chan", None), row, vec, row, vec, P(), tok, P("seq", None),
    )
    out_specs = (
        tok, tok, vec, row, row, vec, P("chan", None), row, vec, row, vec, P("chan", None),
    )
    return jax.shard_map(local, mesh=mesh, in_specs=in_specs, out_specs=out_specs, check_vma=False)
```

```python
import functools
import math

import jax
import jax.numpy as jnp
from jax import lax
from jax.experimental import pallas as pl
from jax.experimental.pallas import tpu as pltpu
from jax.sharding import PartitionSpec as P

epsilon = 1e-05
LOG2E = math.log2(math.e)
CUT = 1e30
TC = 16
EB = 384
RT = 32
HALO = 16
UNROLL = 4
PAR = 160
f32 = jnp.float32
bf16 = jnp.bfloat16
NT = (((1,), (1,)), ((), ()))
TN = (((0,), (0,)), ((), ()))


def params(**more):
    return pltpu.CompilerParams(vmem_limit_bytes=60 * 1024 * 1024, **more)


def cols(rows, width=EB, shift=0):
    return pl.BlockSpec((rows, width), lambda i: (0, i + shift))


def tall(rows, width, shift=0):
    return pl.BlockSpec((rows, width), lambda i: (i + shift, 0))


def lead(rows, width, count=1):
    return pl.BlockSpec((count, rows, width), lambda i: (i, 0, 0))


def whole(*shape):
    return pl.BlockSpec(shape, lambda i: (0,) * len(shape))


def shape(dtype, *dims):
    return jax.ShapeDtypeStruct(dims, dtype)


def row_tiles(count, body):
    def step(i, unused):
        body(pl.multiple_of(i * RT, RT))
        return unused

    lax.fori_loop(0, count // RT, step, 0)


def same_step(states, rows):
    dims = (rows, TC * states)
    here = lax.rem(lax.broadcasted_iota(jnp.int32, dims, 0), TC) * states
    place = lax.broadcasted_iota(jnp.int32, dims, 1)
    return (place >= here) & (place < here + states)


class Layout:
    def __init__(self, R, N, K):
        self.R, self.N, self.K = R, N, K
        self.proj = 0
        self.step = R + 2 * N
        self.decay = self.step + R
        self.conv = self.decay + N
        self.conv_b = self.conv + K
        self.step_b = self.conv_b + 1
        self.skip = self.step_b + 1
        self.end = self.skip + 1


def gather_kernel(
    L, count, cw_ref, cb_ref, pw_ref, sw_ref, sb_ref, dl_ref, sk_ref, tok_ref,
    par_ref, halo_ref, send_sem, recv_sem, halo_sems,
):
    si, ci = lax.axis_index("seq"), lax.axis_index("chan")
    T = tok_ref.shape[0]
    barrier = pltpu.get_barrier_semaphore()
    for k in range(1, count):
        pl.semaphore_signal(
            barrier, inc=1, device_id=(si, lax.rem(ci + k, count)),
            device_id_type=pl.DeviceIdType.MESH,
        )
    own = par_ref.at[ci]
    own[L.end :, :] = jnp.zeros((PAR - L.end, par_ref.shape[2]), f32)
    own[L.proj : L.proj + L.R + 2 * L.N, :] = pw_ref[...].astype(f32).T
    own[L.step : L.step + L.R, :] = sw_ref[...].astype(f32)
    own[L.decay : L.decay + L.N, :] = dl_ref[...]
    own[L.conv : L.conv + L.K, :] = cw_ref[...]
    own[L.conv_b : L.conv_b + 1, :] = cb_ref[...]
    own[L.step_b : L.step_b + 1, :] = sb_ref[...]
    own[L.skip : L.skip + 1, :] = sk_ref[...]
    pl.semaphore_wait(barrier, count - 1)

    def share(k):
        return pltpu.make_async_remote_copy(
            src_ref=own, dst_ref=own, send_sem=send_sem.at[k], recv_sem=recv_sem.at[k],
            device_id=(si, lax.rem(ci + k, count)), device_id_type=pl.DeviceIdType.MESH,
        )

    edge = pltpu.make_async_remote_copy(
        src_ref=tok_ref.at[pl.ds(T - HALO, HALO)], dst_ref=halo_ref,
        send_sem=halo_sems.at[0], recv_sem=halo_sems.at[1],
        device_id=(si, lax.rem(ci + 1, count)), device_id_type=pl.DeviceIdType.MESH,
    )
    edge.start()
    for k in range(1, count):
        share(k).start()
    edge.wait()
    for k in range(1, count):
        share(k).wait()


def gather_params(L, count, parts, tokens):
    width = parts[0].shape[1]
    T, D = tokens.shape
    vmem = pl.BlockSpec(memory_space=pltpu.VMEM)
    return pl.pallas_call(
        functools.partial(gather_kernel, L, count),
        in_specs=[vmem] * 8,
        out_specs=[vmem, vmem],
        out_shape=[shape(f32, count, PAR, width), shape(bf16, HALO, D)],
        scratch_shapes=[
            pltpu.SemaphoreType.DMA((count,)),
            pltpu.SemaphoreType.DMA((count,)),
            pltpu.SemaphoreType.DMA((2,)),
        ],
        compiler_params=params(collective_id=1, has_side_effects=True),
        name="gather_params",
    )(*parts, tokens)


def front_kernel(
    L, tok_ref, halo_ref, gain_ref, wi_ref, wg_ref, wo_ref, cot_ref, par_ref, marks_ref,
    normed_ref, inner_ref, gate_ref, gg_ref, g_ref, cs_ref, act_ref, proj_ref,
    bch_ref, cch_ref, bd_ref, cd_ref, hn_ref, xs_ref, low_ref,
):
    T = tok_ref.shape[0]
    N, K = L.N, L.K
    i = pl.program_id(0)

    def norm(x):
        x = x.astype(f32)
        inv = lax.rsqrt(jnp.mean(x * x, axis=1, keepdims=True) + epsilon)
        return (x * inv * gain_ref[...]).astype(bf16)

    @pl.when(i == 0)
    def _():
        first = lax.axis_index("chan") == 0
        halo = jnp.where(first, jnp.zeros(halo_ref.shape, f32), halo_ref[...].astype(f32))
        hn_ref[...] = norm(halo)

        def tile(r):
            normed_ref[pl.ds(r, RT), :] = norm(tok_ref[pl.ds(r, RT), :])

        row_tiles(T, tile)
        proj_ref[...] = jnp.zeros_like(proj_ref)

    low = jnp.dot(hn_ref[...], wi_ref[...], preferred_element_type=f32).astype(bf16)
    inner_ref[0:HALO, :] = low
    xs_ref[0:HALO, :] = low.astype(f32)
    low = jnp.dot(normed_ref[...], wi_ref[...], preferred_element_type=f32).astype(bf16)
    inner_ref[HALO:, :] = low
    xs_ref[HALO:, :] = low.astype(f32)
    gate_ref[...] = jnp.dot(normed_ref[...], wg_ref[...], preferred_element_type=f32)
    gg_ref[...] = lax.dot_general(cot_ref[...], wo_ref[...], NT, preferred_element_type=f32)

    for k in range(par_ref.shape[0]):
        c = slice(k * EB, (k + 1) * EB)
        taps = [par_ref[k, L.conv + j : L.conv + j + 1, :] for j in range(K)]
        bias = par_ref[k, L.conv_b : L.conv_b + 1, :]

        def tile(r, c=c, taps=taps, bias=bias):
            rows = pl.ds(r, RT)
            block = xs_ref[pl.ds(pl.multiple_of(r + HALO - 8, 8), RT + 8), c]
            total = bias + taps[K - 1] * block[8:]
            for j in range(1, K):
                usable = marks_ref[rows, j - 1 : j]
                total = total + taps[K - 1 - j] * (block[8 - j : RT + 8 - j] * usable)
            act = total * jax.nn.sigmoid(total)
            cs_ref[rows, c] = total
            act_ref[rows, c] = act
            low_ref[rows, c] = act.astype(bf16)
            gate = gate_ref[rows, c]
            passed = gg_ref[rows, c] * (gate * jax.nn.sigmoid(gate))
            g_ref[rows, c] = passed.astype(bf16).astype(f32)

        row_tiles(T, tile)
        weights = par_ref[k, 0:128, :].astype(bf16)
        proj_ref[...] += lax.dot_general(low_ref[:, c], weights, NT, preferred_element_type=f32)

    @pl.when(i == pl.num_programs(0) - 1)
    def _():
        turned = proj_ref[...].T
        for ref, start in ((bch_ref, L.R), (cch_ref, L.R + N)):
            for j in range(T // TC):
                ref[j] = turned[start : start + N, j * TC : (j + 1) * TC]
        dims = (128, TC * N)
        source = lax.broadcasted_iota(jnp.int32, dims, 0)
        state = lax.rem(lax.broadcasted_iota(jnp.int32, dims, 1), N)
        diag = same_step(N, T)
        small = proj_ref[...].astype(bf16)
        for ref, start in ((bd_ref, L.R), (cd_ref, L.R + N)):
            spread = (source == state + start).astype(f32).astype(bf16)
            wide = jnp.dot(small, spread, preferred_element_type=f32)
            ref[...] = jnp.where(diag, wide, 0.0).astype(bf16)


def front(L, tokens, halo, gain, in_weight, out_weight, cot, par, marks):
    T, D = tokens.shape
    E = out_weight.shape[0]
    sub = 2
    wide = EB * sub
    steps = E // wide
    N = L.N
    arrays = [shape(f32, T, E)] * 5
    return pl.pallas_call(
        functools.partial(front_kernel, L),
        grid=(steps,),
        in_specs=[
            whole(T, D), whole(HALO, D), whole(1, D), cols(D, wide), cols(D, wide, steps),
            tall(wide, D), whole(T, D), lead(PAR, EB, sub), whole(*marks.shape),
        ],
        out_specs=[whole(T, D), cols(T + HALO, wide)] + [cols(T, wide)] * 5 + [
            whole(T, 128), whole(T // TC, N, TC), whole(T // TC, N, TC),
            whole(T, TC * N), whole(T, TC * N),
        ],
        out_shape=[shape(bf16, T, D), shape(bf16, T + HALO, E)] + arrays + [
            shape(f32, T, 128), shape(f32, T // TC, N, TC), shape(f32, T // TC, N, TC),
            shape(bf16, T, TC * N), shape(bf16, T, TC * N),
        ],
        scratch_shapes=[
            pltpu.VMEM((HALO, D), bf16),
            pltpu.VMEM((T + HALO, wide), f32),
            pltpu.VMEM((T, wide), bf16),
        ],
        compiler_params=params(),
        name="front",
    )(tokens, halo, gain, in_weight, in_weight, out_weight, cot, par, marks)


def rates(L, par_ref):
    return -jnp.exp(par_ref[0, L.decay : L.decay + L.N, :]) * LOG2E


def softplus(x):
    return jnp.maximum(x, 0.0) + jnp.log1p(jnp.exp(-jnp.abs(x)))


def pre_kernel(
    L, count, proj_ref, par_ref, act_ref, g_ref, marks_ref, b_ref, c_ref,
    spre_ref, dtk_ref, u_ref, enter_ref, arrive_ref, ahead_ref, behind_ref, got_ref,
    send_sem, recv_sem,
):
    T, E = act_ref.shape[0], enter_ref.shape[1]
    N = L.N
    i = pl.program_id(0)
    blocks = E // EB
    si, ci = lax.axis_index("seq"), lax.axis_index("chan")

    @pl.when(i == 0)
    def _():
        barrier = pltpu.get_barrier_semaphore()
        for k in range(1, count):
            pl.semaphore_signal(
                barrier, inc=1, device_id=(si, lax.rem(ci + k, count)),
                device_id_type=pl.DeviceIdType.MESH,
            )
        pl.semaphore_wait(barrier, count - 1)

    low = proj_ref[:, 0 : L.R].astype(bf16)
    weights = par_ref[0, L.step : L.step + L.R, :].astype(bf16)
    bias = par_ref[0, L.step_b : L.step_b + 1, :]
    spre_ref[...] = jnp.dot(low, weights, preferred_element_type=f32) + bias

    def tile(r):
        rows = pl.ds(r, RT)
        step = softplus(spre_ref[rows, :])
        u_ref[rows, :] = step * act_ref[rows, :]
        dtk_ref[rows, :] = step + marks_ref[rows, 3:4]

    row_tiles(T, tile)
    rate = rates(L, par_ref)

    def chunk(c, carry):
        h, through, head = carry
        base = pl.multiple_of(c * TC, TC)
        b_cols, c_cols = b_ref[c], c_ref[c]
        for j in range(TC):
            d = dtk_ref[pl.ds(base + j, 1), :]
            u = u_ref[pl.ds(base + j, 1), :]
            g = g_ref[pl.ds(base + j, 1), :]
            factor = jnp.exp2(d * rate)
            h = factor * h + b_cols[:, j : j + 1] * u
            through = factor * through
            head = head + through * (c_cols[:, j : j + 1] * g)
        return h, through, head

    zero = jnp.zeros(rate.shape, f32)
    h, through, head = lax.fori_loop(0, T // TC, chunk, (zero, zero + 1.0, zero))
    ahead_ref[i, 0:N, :] = h
    ahead_ref[i, N:, :] = through
    behind_ref[i, 0:N, :] = head
    behind_ref[i, N:, :] = through

    def send(b, k, forward):
        return pltpu.make_async_remote_copy(
            src_ref=(ahead_ref if forward else behind_ref).at[b], dst_ref=got_ref.at[count - k, b],
            send_sem=send_sem.at[k, b], recv_sem=recv_sem.at[count - k, b],
            device_id=(si, lax.rem(ci + k, count)), device_id_type=pl.DeviceIdType.MESH,
        )

    for k in range(1, count):
        @pl.when(ci + k < count)
        def _(k=k):
            send(i, k, True).start()

        @pl.when(ci + k >= count)
        def _(k=k):
            send(i, k, False).start()

    @pl.when(i == blocks - 1)
    def _():
        for b in range(blocks):
            for k in range(1, count):
                send(b, k, True).wait()
        for b in range(blocks):
            span = slice(b * EB, (b + 1) * EB)
            entering, arriving = zero, zero
            for k in range(1, count):
                before = ci + k >= count
                got = got_ref[k, b]
                entering = jnp.where(before, got[0:N] + got[N:] * entering, entering)
            for k in range(count - 1, 0, -1):
                behind = ci + k < count
                got = got_ref[k, b]
                arriving = jnp.where(behind, got[0:N] + got[N:] * arriving, arriving)
            enter_ref[:, span] = entering
            arrive_ref[:, span] = arriving


def pre_scan(L, count, proj, par, act, g, marks, b_cols, c_cols):
    T, E = act.shape
    N = L.N
    blocks = E // EB
    state = shape(f32, N, E)
    return pl.pallas_call(
        functools.partial(pre_kernel, L, count),
        grid=(blocks,),
        in_specs=[
            whole(T, 128), lead(PAR, EB), cols(T), cols(T), whole(*marks.shape),
            whole(*b_cols.shape), whole(*c_cols.shape),
        ],
        out_specs=[cols(T)] * 3 + [whole(N, E)] * 2,
        out_shape=[shape(f32, T, E)] * 3 + [state] * 2,
        scratch_shapes=[
            pltpu.VMEM((blocks, 2 * N, EB), f32),
            pltpu.VMEM((blocks, 2 * N, EB), f32),
            pltpu.VMEM((count, blocks, 2 * N, EB), f32),
            pltpu.SemaphoreType.DMA((count, blocks)),
            pltpu.SemaphoreType.DMA((count, blocks)),
        ],
        compiler_params=params(collective_id=2, has_side_effects=True),
        name="pre_scan",
    )(proj, par, act, g, marks, b_cols, c_cols)


def fwd_kernel(
    L, dtk_ref, u_ref, b_ref, cd_ref, g_ref, par_ref, hin_ref, act_ref, gate_ref, gg_ref,
    wo_ref, cot_ref, tok_ref, normed_ref, wg_ref,
    h_ref, gc_ref, block_ref, gout_ref, gin_ref, gn_ref, y_ref, gated_ref, ggate_ref, branch_ref,
):
    rate = rates(L, par_ref)
    chunks, states = b_ref.shape[0], b_ref.shape[1]
    T = chunks * TC
    width = TC * states
    i = pl.program_id(0)

    @pl.when(i == 0)
    def _():
        gc_ref[...] = jnp.zeros_like(gc_ref)
        gn_ref[...] = jnp.zeros_like(gn_ref)
        branch_ref[...] = jnp.zeros_like(branch_ref)

    h_ref[0:states, :] = hin_ref[...].astype(bf16)

    def chunk(c, h):
        base = pl.multiple_of(c * TC, TC)
        row = pl.multiple_of(c * width, width)
        b_cols = b_ref[c]
        for j in range(TC):
            d = dtk_ref[pl.ds(base + j, 1), :]
            u = u_ref[pl.ds(base + j, 1), :]
            h = jnp.exp2(d * rate) * h + b_cols[:, j : j + 1] * u
            h_ref[pl.ds(row + (j + 1) * states, states), :] = h.astype(bf16)
        return h

    lax.fori_loop(0, chunks, chunk, hin_ref[...])

    def contract(i, unused):
        for k in range(UNROLL):
            c = i * UNROLL + k
            rows = pl.ds(pl.multiple_of(c * TC, TC), TC)
            held = h_ref[pl.ds(pl.multiple_of(c * width, width) + states, width), :]
            y_ref[rows, :] = jnp.dot(cd_ref[rows, :], held, preferred_element_type=f32)
            g_low = g_ref[rows, :].astype(bf16)
            gc_ref[rows, :] += lax.dot_general(g_low, held, NT, preferred_element_type=f32)
        return unused

    lax.fori_loop(0, chunks // UNROLL, contract, 0)
    skip = par_ref[0, L.skip : L.skip + 1, :]

    def tile(r):
        rows = pl.ds(r, RT)
        mixer = (y_ref[rows, :] + skip * act_ref[rows, :]).astype(bf16).astype(f32)
        gate = gate_ref[rows, :]
        sig = jax.nn.sigmoid(gate)
        gated_ref[rows, :] = (mixer * (gate * sig)).astype(bf16)
        ggate_ref[rows, :] = (gg_ref[rows, :] * mixer * sig * (1.0 + gate * (1.0 - sig))).astype(bf16)

    row_tiles(T, tile)
    branch_ref[...] += jnp.dot(gated_ref[...], wo_ref[...], preferred_element_type=f32)
    gout_ref[...] = lax.dot_general(
        gated_ref[...], cot_ref[...], TN, preferred_element_type=f32
    ).astype(bf16)
    gin_ref[...] = lax.dot_general(
        ggate_ref[...], normed_ref[...], TN, preferred_element_type=f32
    ).astype(bf16)
    gn_ref[...] += lax.dot_general(ggate_ref[...], wg_ref[...], NT, preferred_element_type=f32)

    @pl.when(i == pl.num_programs(0) - 1)
    def _():
        block_ref[...] = (tok_ref[...].astype(f32) + branch_ref[...]).astype(bf16)


def fwd_scan(L, dtk, u, b_cols, c_diag, g, par, entering, act, gate, gg, out_weight, cot, tokens, normed, in_weight):
    T, E = dtk.shape
    D = tokens.shape[1]
    N = L.N
    rows = (T + 1) * N
    blocks = E // EB
    return pl.pallas_call(
        functools.partial(fwd_kernel, L),
        grid=(blocks,),
        in_specs=[
            cols(T), cols(T), whole(*b_cols.shape), whole(T, TC * N), cols(T), lead(PAR, EB), cols(N),
            cols(T), cols(T), cols(T), tall(EB, D), whole(T, D), whole(T, D), whole(T, D),
            cols(D, EB, blocks),
        ],
        out_specs=[
            cols(rows), whole(T, TC * N), whole(T, D), tall(EB, D), tall(EB, D, blocks), whole(T, D),
        ],
        out_shape=[
            shape(bf16, rows, E), shape(f32, T, TC * N), shape(bf16, T, D), shape(bf16, E, D),
            shape(bf16, 2 * E, D), shape(f32, T, D),
        ],
        scratch_shapes=[
            pltpu.VMEM((T, EB), f32), pltpu.VMEM((T, EB), bf16), pltpu.VMEM((T, EB), bf16),
            pltpu.VMEM((T, D), f32),
        ],
        compiler_params=params(),
        name="fwd_scan",
    )(dtk, u, b_cols, c_diag, g, par, entering, act, gate, gg, out_weight, cot, tokens, normed, in_weight)


def bwd_kernel(
    L, dtk_ref, u_ref, g_ref, c_ref, bd_ref, par_ref, fin_ref, h_ref, spre_ref, act_ref, proj_ref,
    gc_ref, gap_ref, chan_ref, gproj_ref, adj_ref, wr_ref, bsum_ref, wsum_ref, gb_ref, rank_ref, pre_ref,
):
    rate = rates(L, par_ref)
    chunks, states = c_ref.shape[0], c_ref.shape[1]
    T = chunks * TC
    width = TC * states
    i = pl.program_id(0)

    @pl.when(i == 0)
    def _():
        gb_ref[...] = jnp.zeros_like(gb_ref)
        rank_ref[...] = jnp.zeros_like(rank_ref)

    def chunk(i, carry):
        flow, acc = carry
        c = chunks - 1 - i
        base = pl.multiple_of(c * TC, TC)
        row = pl.multiple_of(c * width, width)
        c_cols = c_ref[c]
        for j in reversed(range(TC)):
            d = dtk_ref[pl.ds(base + j, 1), :]
            g = g_ref[pl.ds(base + j, 1), :]
            adj = c_cols[:, j : j + 1] * g + flow
            flow = jnp.exp2(d * rate) * adj
            before = h_ref[pl.ds(row + j * states, states), :].astype(f32)
            wr = flow * before * rate
            acc = acc + wr * d
            adj_ref[pl.ds(row + j * states, states), :] = adj.astype(bf16)
            wr_ref[pl.ds(row + j * states, states), :] = wr.astype(bf16)
        return flow, acc

    unused, acc = lax.fori_loop(0, chunks, chunk, (fin_ref[...], jnp.zeros(rate.shape, f32)))
    ones = same_step(states, TC).astype(f32).astype(bf16)

    def contract(i, unused):
        for k in range(UNROLL):
            c = i * UNROLL + k
            rows = pl.ds(pl.multiple_of(c * TC, TC), TC)
            span = pl.ds(pl.multiple_of(c * width, width), width)
            held = adj_ref[span, :]
            bsum_ref[rows, :] = jnp.dot(bd_ref[rows, :], held, preferred_element_type=f32)
            wsum_ref[rows, :] = jnp.dot(ones, wr_ref[span, :], preferred_element_type=f32)
            u_low = u_ref[rows, :].astype(bf16)
            gb_ref[rows, :] += lax.dot_general(u_low, held, NT, preferred_element_type=f32)
        return unused

    lax.fori_loop(0, chunks // UNROLL, contract, 0)
    skip = par_ref[0, L.skip : L.skip + 1, :]

    def tile(k, carry):
        bias_sum, skip_sum = carry
        rows = pl.ds(pl.multiple_of(k * RT, RT), RT)
        spre, act, g, bsum = spre_ref[rows, :], act_ref[rows, :], g_ref[rows, :], bsum_ref[rows, :]
        grad = (wsum_ref[rows, :] * (1.0 / LOG2E) + act * bsum) * jax.nn.sigmoid(spre)
        gap_ref[rows, :] = g * skip + softplus(spre) * bsum
        pre_ref[rows, :] = grad.astype(bf16)
        bias_sum = bias_sum + jnp.sum(grad.reshape(RT // 8, 8, EB), axis=0)
        skip_sum = skip_sum + jnp.sum((g * act).reshape(RT // 8, 8, EB), axis=0)
        return bias_sum, skip_sum

    none = jnp.zeros((8, EB), f32)
    bias_sum, skip_sum = lax.fori_loop(0, T // RT, tile, (none, none))
    R = L.R
    pre = pre_ref[...]
    step_low = proj_ref[...].astype(bf16)
    grad_step_w = lax.dot_general(step_low, pre, TN, preferred_element_type=f32)
    chan_ref[0] = jnp.concatenate(
        [
            grad_step_w[0:R],
            acc * (1.0 / LOG2E),
            jnp.sum(bias_sum, axis=0, keepdims=True),
            jnp.sum(skip_sum, axis=0, keepdims=True),
            jnp.zeros((128 - R - states - 2, EB), f32),
        ],
        axis=0,
    ).astype(bf16)
    weights = par_ref[0, L.step : L.step + R, :]
    weights = jnp.concatenate([weights, jnp.zeros((128 - R, EB), f32)], axis=0).astype(bf16)
    rank_ref[...] += lax.dot_general(pre, weights, NT, preferred_element_type=f32)

    @pl.when(i == pl.num_programs(0) - 1)
    def _():
        dims = (width, 128)
        state = lax.rem(lax.broadcasted_iota(jnp.int32, dims, 0), states)
        target = lax.broadcasted_iota(jnp.int32, dims, 1)
        diag = same_step(states, T)
        total = rank_ref[...]
        for ref, start in ((gb_ref, R), (gc_ref, R + states)):
            fold = (target == state + start).astype(f32)
            kept = jnp.where(diag, ref[...], 0.0)
            total = total + jnp.dot(
                kept, fold, precision=lax.Precision.HIGHEST, preferred_element_type=f32
            )
        gproj_ref[...] = total.astype(bf16)


def bwd_scan(L, dtk, u, g, c_cols, b_diag, par, arriving, held, spre, act, proj, grad_c):
    T, E = dtk.shape
    N = L.N
    blocks = E // EB
    return pl.pallas_call(
        functools.partial(bwd_kernel, L),
        grid=(blocks,),
        in_specs=[
            cols(T), cols(T), cols(T), whole(*c_cols.shape), whole(T, TC * N), lead(PAR, EB), cols(N),
            cols(held.shape[0]), cols(T), cols(T), whole(T, 128), whole(T, TC * N),
        ],
        out_specs=[cols(T), lead(128, EB), whole(T, 128)],
        out_shape=[shape(f32, T, E), shape(bf16, blocks, 128, EB), shape(bf16, T, 128)],
        scratch_shapes=[
            pltpu.VMEM((T * N, EB), bf16), pltpu.VMEM((T * N, EB), bf16),
            pltpu.VMEM((T, EB), f32), pltpu.VMEM((T, EB), f32),
            pltpu.VMEM((T, TC * N), f32), pltpu.VMEM((T, 128), f32), pltpu.VMEM((T, EB), bf16),
        ],
        compiler_params=params(),
        name="bwd_scan",
    )(dtk, u, g, c_cols, b_diag, par, arriving, held, spre, act, proj, grad_c)


def conv_kernel(L, gap_ref, gproj_ref, par_ref, act_ref, cs_ref, inner_ref, marks_ref, gc_ref, chan_ref, xs_ref):
    T = gap_ref.shape[0]
    K, wide = L.K, L.R + 2 * L.N
    weights = par_ref[0, 0:128, :]
    row = lax.broadcasted_iota(jnp.int32, weights.shape, 0)
    weights = jnp.where(row < wide, weights, 0.0).astype(bf16)
    gc_ref[...] = jnp.dot(gproj_ref[...], weights, preferred_element_type=f32)
    act_low = act_ref[...].astype(bf16)
    grad_proj = lax.dot_general(gproj_ref[...], act_low, TN, preferred_element_type=f32)
    xs_ref[...] = inner_ref[...].astype(f32)

    def tile(k, carry):
        r = pl.multiple_of(k * RT, RT)
        rows = pl.ds(r, RT)
        total = cs_ref[rows, :]
        sig = jax.nn.sigmoid(total)
        grad = (gc_ref[rows, :] + gap_ref[rows, :]) * sig * (1.0 + total * (1.0 - sig))
        gc_ref[rows, :] = grad
        block = xs_ref[pl.ds(pl.multiple_of(r + HALO - 8, 8), RT + 8), :]
        out = [carry[K] + jnp.sum(grad.reshape(RT // 8, 8, EB), axis=0)]
        for j in range(K):
            part = grad * block[8 - j : RT + 8 - j]
            if j > 0:
                part = part * marks_ref[rows, j - 1 : j]
            out.insert(0, carry[K - 1 - j] + jnp.sum(part.reshape(RT // 8, 8, EB), axis=0))
        return tuple(out)

    none = jnp.zeros((8, EB), f32)
    sums = lax.fori_loop(0, T // RT, tile, (none,) * (K + 1))
    chan_ref[0] = jnp.concatenate(
        [grad_proj[0:wide]]
        + [jnp.sum(s, axis=0, keepdims=True) for s in sums]
        + [jnp.zeros((128 - wide - K - 1, EB), f32)],
        axis=0,
    ).astype(bf16)


def conv_back(L, gap, gproj, par, act, cs, inner, marks):
    T, E = gap.shape
    blocks = E // EB
    return pl.pallas_call(
        functools.partial(conv_kernel, L),
        grid=(blocks,),
        in_specs=[
            cols(T), whole(T, 128), lead(PAR, EB), cols(T), cols(T), cols(T + HALO), whole(*marks.shape),
        ],
        out_specs=[cols(T), lead(128, EB)],
        out_shape=[shape(f32, T, E), shape(bf16, blocks, 128, EB)],
        scratch_shapes=[pltpu.VMEM((T + HALO, EB), f32)],
        compiler_params=params(),
        name="conv_back",
    )(gap, gproj, par, act, cs, inner, marks)


def tail_kernel(
    L, gc_ref, after_ref, par_ref, marks_ref, normed_ref, wi_ref, gn_ref, tok_ref, cot_ref, gain_ref,
    held_ref, gin_ref, gtok_ref, ggain_ref, ext_ref, low_ref, sum_ref,
):
    T, D = tok_ref.shape
    K = L.K
    i = pl.program_id(0)
    ext_ref[0:T, :] = gc_ref[...]
    ext_ref[T : T + 8, :] = after_ref[...]
    taps = [par_ref[0, L.conv + j : L.conv + j + 1, :] for j in range(K)]

    def tile(r):
        block = ext_ref[pl.ds(r, RT + 8), :]
        marks = marks_ref[pl.ds(r, RT + 8), :]
        total = taps[K - 1] * block[0:RT]
        for j in range(1, K):
            masked = block * marks[:, j - 1 : j]
            total = total + taps[K - 1 - j] * masked[j : RT + j]
        low_ref[pl.ds(r, RT), :] = total.astype(bf16)

    row_tiles(T, tile)
    gin_ref[...] = lax.dot_general(
        low_ref[...], normed_ref[...], TN, preferred_element_type=f32
    ).astype(bf16)
    part = lax.dot_general(low_ref[...], wi_ref[...], NT, preferred_element_type=f32)

    @pl.when(i == 0)
    def _():
        sum_ref[...] = gn_ref[...] + part

    @pl.when(i > 0)
    def _():
        sum_ref[...] += part

    @pl.when(i == pl.num_programs(0) - 1)
    def _():
        gain = gain_ref[...]

        def last(k, total):
            rows = pl.ds(pl.multiple_of(k * 16, 16), 16)
            x = tok_ref[rows, :].astype(f32)
            grad = sum_ref[rows, :]
            inv = lax.rsqrt(jnp.mean(x * x, axis=1, keepdims=True) + epsilon)
            scaled = grad * gain
            mean = jnp.mean(x * scaled, axis=1, keepdims=True)
            gtok_ref[rows, :] = (
                cot_ref[rows, :].astype(f32) + inv * scaled - x * (inv * inv * inv * mean)
            )
            return total + jnp.sum((grad * x * inv).reshape(2, 8, D), axis=0)

        total = lax.fori_loop(0, T // 16, last, jnp.zeros((8, D), f32))
        ggain_ref[...] = jnp.sum(total, axis=0, keepdims=True)


def tail(L, gc, after, par, marks, normed, in_weight, gn, tokens, cot, gain, held):
    T, E = gc.shape
    D = tokens.shape[1]
    blocks = E // EB
    return pl.pallas_call(
        functools.partial(tail_kernel, L),
        grid=(blocks,),
        in_specs=[
            cols(T), cols(8), lead(PAR, EB), whole(*marks.shape), whole(T, D), cols(D), whole(T, D),
            whole(T, D), whole(T, D), whole(1, D), pl.BlockSpec(memory_space=pl.ANY),
        ],
        out_specs=[tall(EB, D), whole(T, D), whole(1, D)],
        out_shape=[shape(bf16, 2 * E, D), shape(f32, T, D), shape(f32, 1, D)],
        scratch_shapes=[
            pltpu.VMEM((T + 8, EB), f32), pltpu.VMEM((T, EB), bf16), pltpu.VMEM((T, D), f32),
        ],
        input_output_aliases={10: 0},
        compiler_params=params(),
        name="tail",
    )(gc, after, par, marks, normed, in_weight, gn, tokens, cot, gain, held)


def sum_plan(chan_count, seq_count):
    chan_bits = [("chan", 1 << i) for i in range(chan_count.bit_length() - 1)]
    seq_bits = [("seq", 1 << i) for i in range(seq_count.bit_length() - 1)]
    return chan_bits, seq_bits


def sum_kernel(chan_count, seq_count, pieces, arrays, *refs):
    piece_rows = 16 * seq_count
    x_refs, o_refs = refs[:arrays], refs[arrays : 2 * arrays]
    chan_bits, seq_bits = sum_plan(chan_count, seq_count)
    nc, ns = len(chan_bits), len(seq_bits)
    stages = nc + ns
    count = len(pieces)
    scratch = refs[2 * arrays :]
    held = [scratch[p * stages : (p + 1) * stages] for p in range(count)]
    send_sem, recv_sem = scratch[count * stages :]
    mine = {"seq": lax.axis_index("seq"), "chan": lax.axis_index("chan")}

    def bit_of(name, bit):
        return (mine[name] // bit) % 2

    def partner(name, bit):
        other = dict(mine)
        other[name] = mine[name] + bit - 2 * bit * bit_of(name, bit)
        return (other["seq"], other["chan"])

    def order(p):
        inner = chan_bits if p % 2 == 0 else chan_bits[::-1]
        return seq_bits[:1] + inner + seq_bits[1:]

    barrier = pltpu.get_barrier_semaphore()
    for name, bit in chan_bits + seq_bits:
        pl.semaphore_signal(
            barrier, inc=1, device_id=partner(name, bit), device_id_type=pl.DeviceIdType.MESH
        )
    pl.semaphore_wait(barrier, stages)

    def parts(p, s, keep):
        name, bit = order(p)[s]
        side = bit_of(name, bit) if keep else 1 - bit_of(name, bit)
        done = order(p)[:s]
        size = piece_rows >> sum(1 for n, b in done if n == "seq")
        ref, start = (x_refs[pieces[p][0]], pieces[p][1]) if s == 0 else (held[p][s - 1], 0)
        if name == "seq":
            rows = pl.ds(pl.multiple_of(start + side * (size // 2), 16), size // 2)
            return [ref.at[:, rows, :]]
        left = [b for n, b in chan_bits if ("chan", b) not in done]
        low = 1 << left.index(bit)
        return [
            ref.at[pl.ds((i // low) * 2 * low + side * low + i % low, 1), pl.ds(start, size), :]
            for i in range((1 << len(left)) // 2)
        ]

    def landing(p, s):
        dst = held[p][s]
        if order(p)[s][0] == "seq":
            return [dst]
        return [dst.at[pl.ds(i, 1)] for i in range(dst.shape[0])]

    def copies(p, s):
        return [
            pltpu.make_async_remote_copy(
                src_ref=src, dst_ref=dst, send_sem=send_sem.at[p, s, i], recv_sem=recv_sem.at[p, s, i],
                device_id=partner(*order(p)[s]), device_id_type=pl.DeviceIdType.MESH,
            )
            for i, (src, dst) in enumerate(zip(parts(p, s, False), landing(p, s)))
        ]

    def my_rows(p, done):
        start, size = pieces[p][1], piece_rows
        for name, bit in seq_bits[:done]:
            size //= 2
            start = start + bit_of(name, bit) * size
        return pl.ds(pl.multiple_of(start, 16), size)

    def gather_copy(p, k):
        place = o_refs[pieces[p][0]].at[my_rows(p, ns - k), :]
        return pltpu.make_async_remote_copy(
            src_ref=place, dst_ref=place,
            send_sem=send_sem.at[p, stages + k, 0], recv_sem=recv_sem.at[p, stages + k, 0],
            device_id=partner(*seq_bits[ns - 1 - k]), device_id_type=pl.DeviceIdType.MESH,
        )

    total = stages + ns
    for tick in range((count + 1) // 2 + total):
        for p in range(count):
            s = tick - p // 2
            if not 0 <= s <= total:
                continue
            if 1 <= s <= stages:
                for copy in copies(p, s - 1):
                    copy.wait_recv()
                for src, dst in zip(parts(p, s - 1, True), landing(p, s - 1)):
                    dst[...] = (dst[...].astype(f32) + src[...].astype(f32)).astype(bf16)
                if s == stages:
                    o_refs[pieces[p][0]][my_rows(p, ns), :] = held[p][stages - 1][0]
            elif s > stages:
                gather_copy(p, s - 1 - stages).wait_recv()
            if s < stages:
                for copy in copies(p, s):
                    copy.start()
            elif s < total:
                gather_copy(p, s - stages).start()
    for p in range(count):
        for s in range(stages):
            for copy in copies(p, s):
                copy.wait_send()
        for k in range(ns):
            gather_copy(p, k).wait_send()


def sum_owned(arrays, seq_count):
    chan_count = arrays[0].shape[0]
    chan_bits, seq_bits = sum_plan(chan_count, seq_count)
    piece_rows = 16 * seq_count
    pieces = [(a, r) for a, v in enumerate(arrays) for r in range(0, v.shape[1], piece_rows)]
    ordered = seq_bits[:1] + chan_bits + seq_bits[1:]
    scratch = []
    for a, r in pieces:
        owners, size = chan_count, piece_rows
        for name, bit in ordered:
            if name == "chan":
                owners //= 2
            else:
                size //= 2
            scratch.append(pltpu.VMEM((owners, size, arrays[a].shape[2]), bf16))
    total = len(ordered) + len(seq_bits)
    sems = pltpu.SemaphoreType.DMA((len(pieces), total, max(1, chan_count // 2)))
    vmem = pl.BlockSpec(memory_space=pltpu.VMEM)
    return pl.pallas_call(
        functools.partial(sum_kernel, chan_count, seq_count, pieces, len(arrays)),
        in_specs=[vmem] * len(arrays),
        out_specs=[vmem] * len(arrays),
        out_shape=[shape(bf16, *v.shape[1:]) for v in arrays],
        scratch_shapes=scratch + [sems, sems],
        compiler_params=params(collective_id=0, has_side_effects=True),
        name="sum_owned",
    )(*arrays)


def unpack_kernel(L, in_ref, out_ref, d_ref, e_ref, gin_ref, gout_ref, *refs):
    gin_ref[...] = in_ref[...].astype(f32).T
    gout_ref[...] = out_ref[...].astype(f32)
    d, e = d_ref[...].astype(f32), e_ref[...].astype(f32)
    R, N, K = L.R, L.N, L.K
    wide = R + 2 * N
    conv_w, conv_b, proj, step_w, step_b, decay, skip, gain = refs
    step_w[...] = d[0:R]
    decay[...] = d[R : R + N]
    step_b[...] = d[R + N : R + N + 1]
    skip[...] = d[R + N + 1 : R + N + 2]
    proj[...] = e.T[:, 0:wide]
    conv_w[...] = e[wide : wide + K]
    conv_b[...] = e[wide + K : wide + K + 1]
    gain[...] = e[wide + K + 1 : wide + K + 2]


def unpack(L, sums):
    width = sums[2].shape[1]
    rows, D = sums[0].shape
    R, N, K = L.R, L.N, L.K
    return pl.pallas_call(
        functools.partial(unpack_kernel, L),
        out_shape=[
            shape(f32, D, rows), shape(f32, *sums[1].shape), shape(f32, K, width), shape(f32, 1, width),
            shape(f32, width, R + 2 * N), shape(f32, R, width), shape(f32, 1, width),
            shape(f32, N, width), shape(f32, 1, width), shape(f32, 1, width),
        ],
        compiler_params=params(),
        name="unpack",
    )(*sums)


def free_of_starts(starts, places, offset):
    inside = (starts[None, :] > places[:, None] - offset) & (starts[None, :] <= places[:, None])
    return jnp.logical_not(jnp.any(inside, axis=1))


def local(
    tokens, norm_gain, in_weight, conv_weight, conv_bias, proj_weight, step_weight,
    step_bias, decay_log, skip_gain, out_weight, cotangent, lengths,
):
    T, D = tokens.shape
    E = in_weight.shape[1] // 2
    L = Layout(step_weight.shape[0], decay_log.shape[0], conv_weight.shape[0])
    ci = lax.axis_index("chan")
    cc = lax.axis_size("chan")
    sc = lax.axis_size("seq")
    blocks, share = E // EB, E // cc

    parts = (
        conv_weight, conv_bias[None], proj_weight, step_weight, step_bias[None], decay_log, skip_gain[None],
    )
    par, halo = gather_params(L, cc, parts, tokens)
    if share != EB:
        par = jnp.moveaxis(par, 0, 1).reshape(PAR, blocks, EB)
        par = jnp.moveaxis(par, 1, 0)
    gain = norm_gain[None]

    starts = jnp.cumsum(lengths[0]) - lengths[0]
    places = ci * T + jnp.arange(T + 8, dtype=jnp.int32)
    marks = [free_of_starts(starts, places, j).astype(f32) for j in range(1, L.K)]
    marks.append(jnp.where(jnp.any(places[:, None] == starts[None, :], axis=1), CUT, 0.0))
    marks = jnp.stack(marks + [jnp.zeros_like(marks[0])] * (8 - len(marks)), axis=1)

    normed, inner, gate, gg, g, cs, act, proj, b_cols, c_cols, b_diag, c_diag = front(
        L, tokens, halo, gain, in_weight, out_weight, cotangent, par, marks
    )
    spre, dtk, u, entering, arriving = pre_scan(L, cc, proj, par, act, g, marks, b_cols, c_cols)
    held, grad_c, block_out, grad_out, grad_in, gn = fwd_scan(
        L, dtk, u, b_cols, c_diag, g, par, entering, act, gate, gg, out_weight, cotangent, tokens,
        normed, in_weight,
    )
    gap, chan_d, gproj = bwd_scan(
        L, dtk, u, g, c_cols, b_diag, par, arriving, held, spre, act, proj, grad_c
    )
    gc, chan_e = conv_back(L, gap, gproj, par, act, cs, inner, marks)
    after = lax.ppermute(gc[0:8], "chan", [(k, k - 1) for k in range(1, cc)])
    grad_in, grad_tokens, grad_gain = tail(
        L, gc, after, par, marks, normed, in_weight, gn, tokens, cotangent, gain, grad_in
    )

    def by_owner(values):
        if share == EB:
            return values
        values = jnp.moveaxis(values, 0, 1).reshape(128, cc, share)
        return jnp.moveaxis(values, 1, 0)

    chan_d, chan_e = by_owner(chan_d), by_owner(chan_e)
    row = L.R + 2 * L.N + L.K + 1
    owned_gain = jnp.pad(grad_gain.reshape(cc, 1, D // cc), ((0, 0), (0, 0), (0, share - D // cc)))
    chan_e = lax.dynamic_update_slice(chan_e, owned_gain.astype(bf16), (0, row, 0))
    arrays = [grad_in.reshape(cc, 2 * E // cc, D), grad_out.reshape(cc, share, D), chan_d, chan_e]
    piece = 16 * sc
    rows = [v.shape[1] for v in arrays]
    arrays = [jnp.pad(v, ((0, 0), (0, -v.shape[1] % piece), (0, 0))) for v in arrays]
    sums = sum_owned(arrays, sc)
    sums = [v[:r] for v, r in zip(sums, rows)]
    g_in, g_out, conv_w, conv_b, proj_w, step_w, step_b, decay, skip, g_gain = unpack(L, sums)
    return (
        block_out, grad_tokens, g_gain[0, : D // cc], g_in, conv_w, conv_b[0], proj_w, step_w,
        step_b[0], decay, skip[0], g_out,
    )


def solution(mesh):
    tok, row, vec = P(("seq", "chan"), None), P(None, "chan"), P("chan")
    in_specs = (
        tok, P(), P(), row, vec, P("chan", None), row, vec, row, vec, P(), tok, P("seq", None),
    )
    out_specs = (
        tok, tok, vec, row, row, vec, P("chan", None), row, vec, row, vec, P("chan", None),
    )
    return jax.shard_map(local, mesh=mesh, in_specs=in_specs, out_specs=out_specs, check_vma=False)
```

```python
import functools
import math

import jax
import jax.numpy as jnp
from jax import lax
from jax.experimental import pallas as pl
from jax.experimental.pallas import tpu as pltpu
from jax.sharding import PartitionSpec as P

epsilon = 1e-05
LOG2E = math.log2(math.e)
CUT = 1e30
TC = 16
EB = 384
RT = 32
HALO = 16
PAR = 24
WTS = 128
f32 = jnp.float32
bf16 = jnp.bfloat16
NT = (((1,), (1,)), ((), ()))
TN = (((0,), (0,)), ((), ()))


def params(**more):
    return pltpu.CompilerParams(vmem_limit_bytes=60 * 1024 * 1024, **more)


def cols(rows, width=EB, shift=0):
    return pl.BlockSpec((rows, width), lambda i: (0, i + shift))


def tall(rows, width, shift=0):
    return pl.BlockSpec((rows, width), lambda i: (i + shift, 0))


def lead(rows, width, count=1):
    return pl.BlockSpec((count, rows, width), lambda i: (i, 0, 0))


def whole(*shape):
    return pl.BlockSpec(shape, lambda i: (0,) * len(shape))


def shape(dtype, *dims):
    return jax.ShapeDtypeStruct(dims, dtype)


def row_tiles(count, body):
    def step(i, unused):
        body(pl.multiple_of(i * RT, RT))
        return unused

    lax.fori_loop(0, count // RT, step, 0)


def same_step(states, rows):
    dims = (rows, TC * states)
    here = lax.rem(lax.broadcasted_iota(jnp.int32, dims, 0), TC) * states
    place = lax.broadcasted_iota(jnp.int32, dims, 1)
    return (place >= here) & (place < here + states)


class Layout:
    def __init__(self, R, N, K):
        self.R, self.N, self.K = R, N, K
        self.step = R + 2 * N
        self.decay = 0
        self.conv = self.decay + N
        self.conv_b = self.conv + K
        self.step_b = self.conv_b + 1
        self.skip = self.step_b + 1
        self.end = self.skip + 1


def gather_kernel(
    L, count, cw_ref, cb_ref, pw_ref, sw_ref, sb_ref, dl_ref, sk_ref, tok_ref,
    wts_ref, par_ref, halo_ref, send_sem, recv_sem, halo_sems,
):
    si, ci = lax.axis_index("seq"), lax.axis_index("chan")
    T = tok_ref.shape[0]
    width = par_ref.shape[2]
    barrier = pltpu.get_barrier_semaphore()
    for k in range(1, count):
        pl.semaphore_signal(
            barrier, inc=1, device_id=(si, lax.rem(ci + k, count)),
            device_id_type=pl.DeviceIdType.MESH,
        )
    own, weights = par_ref.at[ci], wts_ref.at[ci]
    weights[...] = jnp.concatenate(
        [pw_ref[...].astype(f32), sw_ref[...].astype(f32)], axis=0
    ).astype(bf16)
    own[...] = jnp.concatenate(
        [
            dl_ref[...], cw_ref[...], cb_ref[...].reshape(1, width), sb_ref[...].reshape(1, width),
            sk_ref[...].reshape(1, width), jnp.zeros((PAR - L.end, width), f32),
        ],
        axis=0,
    )
    pl.semaphore_wait(barrier, count - 1)

    def share(ref, j, k):
        return pltpu.make_async_remote_copy(
            src_ref=ref, dst_ref=ref, send_sem=send_sem.at[j, k], recv_sem=recv_sem.at[j, k],
            device_id=(si, lax.rem(ci + k, count)), device_id_type=pl.DeviceIdType.MESH,
        )

    edge = pltpu.make_async_remote_copy(
        src_ref=tok_ref.at[pl.ds(T - HALO, HALO)], dst_ref=halo_ref,
        send_sem=halo_sems.at[0], recv_sem=halo_sems.at[1],
        device_id=(si, lax.rem(ci + 1, count)), device_id_type=pl.DeviceIdType.MESH,
    )
    edge.start()
    for j, ref in enumerate((own, weights)):
        for k in range(1, count):
            share(ref, j, k).start()
    edge.wait()
    for j, ref in enumerate((own, weights)):
        for k in range(1, count):
            share(ref, j, k).wait()


def gather_params(L, count, parts, tokens):
    width = parts[0].shape[1]
    T, D = tokens.shape
    vmem = pl.BlockSpec(memory_space=pltpu.VMEM)
    return pl.pallas_call(
        functools.partial(gather_kernel, L, count),
        in_specs=[vmem] * 8,
        out_specs=[vmem] * 3,
        out_shape=[shape(bf16, count, WTS, width), shape(f32, count, PAR, width), shape(bf16, HALO, D)],
        scratch_shapes=[
            pltpu.SemaphoreType.DMA((2, count)),
            pltpu.SemaphoreType.DMA((2, count)),
            pltpu.SemaphoreType.DMA((2,)),
        ],
        compiler_params=params(collective_id=1, has_side_effects=True),
        name="gather_params",
    )(*parts, tokens)


def front_kernel(
    L, len_ref, tok_ref, halo_ref, gain_ref, wi_ref, wg_ref, wo_ref, cot_ref, par_ref, wts_ref,
    marks_ref, normed_ref, inner_ref, gate_ref, gg_ref, g_ref, cs_ref, act_ref, proj_ref,
    bch_ref, cch_ref, hn_ref, xs_ref, low_ref,
):
    T = tok_ref.shape[0]
    N, K = L.N, L.K
    i = pl.program_id(0)

    def norm(x):
        x = x.astype(f32)
        inv = lax.rsqrt(jnp.mean(x * x, axis=1, keepdims=True) + epsilon)
        return (x * inv * gain_ref[...].reshape(1, x.shape[1])).astype(bf16)

    @pl.when(i == 0)
    def _():
        first = lax.axis_index("chan") == 0
        halo = jnp.where(first, jnp.zeros(halo_ref.shape, f32), halo_ref[...].astype(f32))
        hn_ref[...] = norm(halo)

        def tile(r):
            normed_ref[pl.ds(r, RT), :] = norm(tok_ref[pl.ds(r, RT), :])

        row_tiles(T, tile)
        proj_ref[...] = jnp.zeros_like(proj_ref)
        dims = marks_ref.shape
        place = lax.broadcasted_iota(jnp.int32, dims, 0) + lax.axis_index("chan") * T
        lane = lax.broadcasted_iota(jnp.int32, dims, 1)
        reach = jnp.where(lane < K - 1, lane + 1, 1)
        inside = jnp.zeros(dims, f32)
        start = jnp.int32(0)
        for k in range(len_ref.shape[1]):
            inside = jnp.where((start > place - reach) & (start <= place), 1.0, inside)
            start = start + len_ref[0, k]
        marks_ref[...] = jnp.where(lane < K - 1, 1.0 - inside, inside * CUT)

    low = jnp.dot(hn_ref[...], wi_ref[...], preferred_element_type=f32).astype(bf16)
    inner_ref[0:HALO, :] = low
    xs_ref[0:HALO, :] = low.astype(f32)
    low = jnp.dot(normed_ref[...], wi_ref[...], preferred_element_type=f32).astype(bf16)
    inner_ref[HALO:, :] = low
    xs_ref[HALO:, :] = low.astype(f32)
    gate_ref[...] = jnp.dot(normed_ref[...], wg_ref[...], preferred_element_type=f32)
    gg_ref[...] = lax.dot_general(cot_ref[...], wo_ref[...], NT, preferred_element_type=f32)

    for k in range(par_ref.shape[0]):
        c = slice(k * EB, (k + 1) * EB)
        taps = [par_ref[k, L.conv + j : L.conv + j + 1, :] for j in range(K)]
        bias = par_ref[k, L.conv_b : L.conv_b + 1, :]

        def tile(r, c=c, taps=taps, bias=bias):
            rows = pl.ds(r, RT)
            block = xs_ref[pl.ds(pl.multiple_of(r + HALO - 8, 8), RT + 8), c]
            total = bias + taps[K - 1] * block[8:]
            for j in range(1, K):
                usable = marks_ref[rows, j - 1 : j]
                total = total + taps[K - 1 - j] * (block[8 - j : RT + 8 - j] * usable)
            act = total * jax.nn.sigmoid(total)
            cs_ref[rows, c] = total
            act_ref[rows, c] = act
            low_ref[rows, c] = act.astype(bf16)
            gate = gate_ref[rows, c]
            passed = gg_ref[rows, c] * (gate * jax.nn.sigmoid(gate))
            g_ref[rows, c] = passed.astype(bf16).astype(f32)

        row_tiles(T, tile)
        proj_ref[...] += lax.dot_general(low_ref[:, c], wts_ref[k], NT, preferred_element_type=f32)

    @pl.when(i == pl.num_programs(0) - 1)
    def _():
        turned = proj_ref[...].T
        for ref, start in ((bch_ref, L.R), (cch_ref, L.R + N)):
            for j in range(T // TC):
                ref[j] = turned[start : start + N, j * TC : (j + 1) * TC]


def front(L, lengths, tokens, halo, gain, in_weight, out_weight, cot, par, wts):
    T, D = tokens.shape
    E = out_weight.shape[0]
    sub = 2
    wide = EB * sub
    steps = E // wide
    N = L.N
    arrays = [shape(f32, T, E)] * 5
    return pl.pallas_call(
        functools.partial(front_kernel, L),
        grid=(steps,),
        in_specs=[
            pl.BlockSpec(memory_space=pltpu.SMEM),
            whole(T, D), whole(HALO, D), whole(D), cols(D, wide), cols(D, wide, steps),
            tall(wide, D), whole(T, D), lead(PAR, EB, sub), lead(WTS, EB, sub),
        ],
        out_specs=[whole(T + 8, 8), whole(T, D), cols(T + HALO, wide)] + [cols(T, wide)] * 5 + [
            whole(T, 128), whole(T // TC, N, TC), whole(T // TC, N, TC),
        ],
        out_shape=[shape(f32, T + 8, 8), shape(bf16, T, D), shape(bf16, T + HALO, E)] + arrays + [
            shape(f32, T, 128), shape(f32, T // TC, N, TC), shape(f32, T // TC, N, TC),
        ],
        scratch_shapes=[
            pltpu.VMEM((HALO, D), bf16),
            pltpu.VMEM((T + HALO, wide), f32),
            pltpu.VMEM((T, wide), bf16),
        ],
        compiler_params=params(),
        name="front",
    )(lengths, tokens, halo, gain, in_weight, in_weight, out_weight, cot, par, wts)


def rates(L, par_ref):
    return -jnp.exp(par_ref[0, L.decay : L.decay + L.N, :]) * LOG2E


def softplus(x):
    return jnp.maximum(x, 0.0) + jnp.log1p(jnp.exp(-jnp.abs(x)))


def pre_kernel(
    L, count, proj_ref, par_ref, wts_ref, act_ref, g_ref, marks_ref, b_ref, c_ref,
    spre_ref, dtk_ref, u_ref, enter_ref, arrive_ref, ahead_ref, behind_ref, got_ref,
    send_sem, recv_sem,
):
    T, E = act_ref.shape[0], enter_ref.shape[1]
    N = L.N
    i = pl.program_id(0)
    blocks = E // EB
    si, ci = lax.axis_index("seq"), lax.axis_index("chan")

    @pl.when(i == 0)
    def _():
        barrier = pltpu.get_barrier_semaphore()
        for k in range(1, count):
            pl.semaphore_signal(
                barrier, inc=1, device_id=(si, lax.rem(ci + k, count)),
                device_id_type=pl.DeviceIdType.MESH,
            )
        pl.semaphore_wait(barrier, count - 1)

    low = proj_ref[:, 0 : L.R].astype(bf16)
    weights = wts_ref[0, L.step : L.step + L.R, :]
    bias = par_ref[0, L.step_b : L.step_b + 1, :]
    spre_ref[...] = jnp.dot(low, weights, preferred_element_type=f32) + bias

    def tile(r):
        rows = pl.ds(r, RT)
        step = softplus(spre_ref[rows, :])
        u_ref[rows, :] = step * act_ref[rows, :]
        dtk_ref[rows, :] = step + marks_ref[rows, 3:4]

    row_tiles(T, tile)
    rate = rates(L, par_ref)

    def chunk(c, carry):
        h, through, head = carry
        base = pl.multiple_of(c * TC, TC)
        b_cols, c_cols = b_ref[c], c_ref[c]
        for j in range(TC):
            d = dtk_ref[pl.ds(base + j, 1), :]
            u = u_ref[pl.ds(base + j, 1), :]
            g = g_ref[pl.ds(base + j, 1), :]
            factor = jnp.exp2(d * rate)
            h = factor * h + b_cols[:, j : j + 1] * u
            through = factor * through
            head = head + through * (c_cols[:, j : j + 1] * g)
        return h, through, head

    zero = jnp.zeros(rate.shape, f32)
    h, through, head = lax.fori_loop(0, T // TC, chunk, (zero, zero + 1.0, zero))
    ahead_ref[i, 0:N, :] = h
    ahead_ref[i, N:, :] = through
    behind_ref[i, 0:N, :] = head
    behind_ref[i, N:, :] = through

    def send(b, k, forward):
        return pltpu.make_async_remote_copy(
            src_ref=(ahead_ref if forward else behind_ref).at[b], dst_ref=got_ref.at[count - k, b],
            send_sem=send_sem.at[k, b], recv_sem=recv_sem.at[count - k, b],
            device_id=(si, lax.rem(ci + k, count)), device_id_type=pl.DeviceIdType.MESH,
        )

    for k in range(1, count):
        @pl.when(ci + k < count)
        def _(k=k):
            send(i, k, True).start()

        @pl.when(ci + k >= count)
        def _(k=k):
            send(i, k, False).start()

    @pl.when(i == blocks - 1)
    def _():
        for b in range(blocks):
            for k in range(1, count):
                send(b, k, True).wait()
        for b in range(blocks):
            span = slice(b * EB, (b + 1) * EB)
            entering, arriving = zero, zero
            for k in range(1, count):
                before = ci + k >= count
                got = got_ref[k, b]
                entering = jnp.where(before, got[0:N] + got[N:] * entering, entering)
            for k in range(count - 1, 0, -1):
                behind = ci + k < count
                got = got_ref[k, b]
                arriving = jnp.where(behind, got[0:N] + got[N:] * arriving, arriving)
            enter_ref[:, span] = entering
            arrive_ref[:, span] = arriving


def pre_scan(L, count, proj, par, wts, act, g, marks, b_cols, c_cols):
    T, E = act.shape
    N = L.N
    blocks = E // EB
    state = shape(f32, N, E)
    return pl.pallas_call(
        functools.partial(pre_kernel, L, count),
        grid=(blocks,),
        in_specs=[
            whole(T, 128), lead(PAR, EB), lead(WTS, EB), cols(T), cols(T), whole(*marks.shape),
            whole(*b_cols.shape), whole(*c_cols.shape),
        ],
        out_specs=[cols(T)] * 3 + [whole(N, E)] * 2,
        out_shape=[shape(f32, T, E)] * 3 + [state] * 2,
        scratch_shapes=[
            pltpu.VMEM((blocks, 2 * N, EB), f32),
            pltpu.VMEM((blocks, 2 * N, EB), f32),
            pltpu.VMEM((count, blocks, 2 * N, EB), f32),
            pltpu.SemaphoreType.DMA((count, blocks)),
            pltpu.SemaphoreType.DMA((count, blocks)),
        ],
        compiler_params=params(collective_id=2, has_side_effects=True),
        name="pre_scan",
    )(proj, par, wts, act, g, marks, b_cols, c_cols)


def lane_tiles(values):
    return [values[:, k * 128 : (k + 1) * 128] for k in range(EB // 128)]


def row_at(ref, t):
    return lane_tiles(ref[pl.ds(t, 1), :])


def fold_rows(refs, r):
    sums = []
    for ref in refs:
        parts = [ref[pl.ds(r * 8 + k, 8, stride=8), :] for k in range(8)]
        while len(parts) > 1:
            parts = [x + y for x, y in zip(parts[::2], parts[1::2])]
        sums.append(parts[0])
    return jnp.concatenate(sums, axis=1)


def halves(values):
    return values[0:8] + values[8:16]


def lane_sums(states, acc_ref, out_ref, chunks):
    width = TC * states
    ones = jnp.ones((TC, 128), bf16)

    def step(c, unused):
        rows = pl.ds(pl.multiple_of(c * width, width), width)
        out_ref[pl.ds(pl.multiple_of(c * TC, TC), TC), :] = lax.dot_general(
            ones, acc_ref[rows, :].astype(bf16), NT, preferred_element_type=f32
        )
        return unused

    lax.fori_loop(0, chunks, step, 0)


def fwd_kernel(
    L, dtk_ref, u_ref, b_ref, c_ref, g_ref, par_ref, hin_ref, act_ref, gate_ref, gg_ref,
    wo_ref, cot_ref, tok_ref, normed_ref, wg_ref,
    h_ref, gc_ref, block_ref, gout_ref, gin_ref, gn_ref,
    acc_ref, gated_ref, ggate_ref, branch_ref, *y_refs,
):
    rate = lane_tiles(rates(L, par_ref))
    chunks, states = b_ref.shape[0], b_ref.shape[1]
    T = chunks * TC
    width = TC * states
    i = pl.program_id(0)

    @pl.when(i == 0)
    def _():
        acc_ref[...] = jnp.zeros_like(acc_ref)
        gn_ref[...] = jnp.zeros_like(gn_ref)
        branch_ref[...] = jnp.zeros_like(branch_ref)

    h_ref[0:states, :] = hin_ref[...].astype(bf16)

    def chunk(c, carry):
        h = list(carry)
        base = pl.multiple_of(c * TC, TC)
        row = pl.multiple_of(c * width, width)
        b_cols, c_cols = b_ref[c], c_ref[c]
        for j in range(TC):
            d, u, g = (row_at(ref, base + j) for ref in (dtk_ref, u_ref, g_ref))
            b_now = jnp.broadcast_to(b_cols[:, j : j + 1], (states, 128))
            c_now = jnp.broadcast_to(c_cols[:, j : j + 1], (states, 128))
            at = pl.ds(row + j * states, states)
            acc = acc_ref[at, :]
            for k in range(len(h)):
                h[k] = jnp.exp2(d[k] * rate[k]) * h[k] + b_now * u[k]
                h_ref[pl.ds(row + (j + 1) * states, states), k * 128 : (k + 1) * 128] = h[k].astype(bf16)
                y_refs[k][pl.ds((base + j) * 8, 8), :] = halves(c_now * h[k])
                acc = acc + h[k] * g[k]
            acc_ref[at, :] = acc
        return tuple(h)

    lax.fori_loop(0, chunks, chunk, tuple(lane_tiles(hin_ref[...])))
    skip = par_ref[0, L.skip : L.skip + 1, :]

    def tile(k, unused):
        rows = pl.ds(pl.multiple_of(k * 16, 16), 16)
        y = jnp.concatenate([fold_rows(y_refs, k * 16), fold_rows(y_refs, k * 16 + 8)], axis=0)
        mixer = (y + skip * act_ref[rows, :]).astype(bf16).astype(f32)
        gate = gate_ref[rows, :]
        sig = jax.nn.sigmoid(gate)
        gated_ref[rows, :] = (mixer * (gate * sig)).astype(bf16)
        ggate_ref[rows, :] = (gg_ref[rows, :] * mixer * sig * (1.0 + gate * (1.0 - sig))).astype(bf16)
        return unused

    lax.fori_loop(0, T // 16, tile, 0)
    branch_ref[...] += jnp.dot(gated_ref[...], wo_ref[...], preferred_element_type=f32)
    gout_ref[...] = lax.dot_general(
        gated_ref[...], cot_ref[...], TN, preferred_element_type=f32
    ).astype(bf16)
    gin_ref[...] = lax.dot_general(
        ggate_ref[...], normed_ref[...], TN, preferred_element_type=f32
    ).astype(bf16)
    gn_ref[...] += lax.dot_general(ggate_ref[...], wg_ref[...], NT, preferred_element_type=f32)

    @pl.when(i == pl.num_programs(0) - 1)
    def _():
        block_ref[...] = (tok_ref[...].astype(f32) + branch_ref[...]).astype(bf16)
        lane_sums(states, acc_ref, gc_ref, chunks)


def fwd_scan(L, dtk, u, b_cols, c_cols, g, par, entering, act, gate, gg, out_weight, cot, tokens, normed, in_weight):
    T, E = dtk.shape
    D = tokens.shape[1]
    N = L.N
    rows = (T + 1) * N
    blocks = E // EB
    return pl.pallas_call(
        functools.partial(fwd_kernel, L),
        grid=(blocks,),
        in_specs=[
            cols(T), cols(T), whole(*b_cols.shape), whole(*c_cols.shape), cols(T), lead(PAR, EB), cols(N),
            cols(T), cols(T), cols(T), tall(EB, D), whole(T, D), whole(T, D), whole(T, D),
            cols(D, EB, blocks),
        ],
        out_specs=[
            cols(rows), whole(T, TC * N), whole(T, D), tall(EB, D), tall(EB, D, blocks), whole(T, D),
        ],
        out_shape=[
            shape(bf16, rows, E), shape(f32, T, TC * N), shape(bf16, T, D), shape(bf16, E, D),
            shape(bf16, 2 * E, D), shape(f32, T, D),
        ],
        scratch_shapes=[
            pltpu.VMEM((T * N, 128), f32), pltpu.VMEM((T, EB), bf16), pltpu.VMEM((T, EB), bf16),
            pltpu.VMEM((T, D), f32),
        ] + [pltpu.VMEM((T * 8, 128), f32)] * (EB // 128),
        compiler_params=params(),
        name="fwd_scan",
    )(dtk, u, b_cols, c_cols, g, par, entering, act, gate, gg, out_weight, cot, tokens, normed, in_weight)


def bwd_kernel(
    L, dtk_ref, u_ref, g_ref, b_ref, c_ref, par_ref, wts_ref, fin_ref, h_ref, spre_ref, act_ref, proj_ref,
    gc_ref, gap_ref, chan_ref, gproj_ref, acc_ref, gb_ref, rank_ref, pre_ref, *part_refs,
):
    rate = lane_tiles(rates(L, par_ref))
    tiles = len(rate)
    bsum_refs, wsum_refs = part_refs[:tiles], part_refs[tiles:]
    chunks, states = c_ref.shape[0], c_ref.shape[1]
    T = chunks * TC
    width = TC * states
    i = pl.program_id(0)

    @pl.when(i == 0)
    def _():
        acc_ref[...] = jnp.zeros_like(acc_ref)
        rank_ref[...] = jnp.zeros_like(rank_ref)

    def chunk(i, carry):
        flow, total = list(carry[:tiles]), list(carry[tiles:])
        c = chunks - 1 - i
        base = pl.multiple_of(c * TC, TC)
        row = pl.multiple_of(c * width, width)
        b_cols, c_cols = b_ref[c], c_ref[c]
        for j in reversed(range(TC)):
            d, u, g = (row_at(ref, base + j) for ref in (dtk_ref, u_ref, g_ref))
            b_now = jnp.broadcast_to(b_cols[:, j : j + 1], (states, 128))
            c_now = jnp.broadcast_to(c_cols[:, j : j + 1], (states, 128))
            at = pl.ds(row + j * states, states)
            part = pl.ds((base + j) * 8, 8)
            acc = acc_ref[at, :]
            for k in range(tiles):
                adj = c_now * g[k] + flow[k]
                flow[k] = jnp.exp2(d[k] * rate[k]) * adj
                wr = flow[k] * h_ref[at, k * 128 : (k + 1) * 128].astype(f32) * rate[k]
                total[k] = total[k] + wr * d[k]
                wsum_refs[k][part, :] = halves(wr)
                bsum_refs[k][part, :] = halves(adj * b_now)
                acc = acc + adj * u[k]
            acc_ref[at, :] = acc
        return tuple(flow) + tuple(total)

    none = jnp.zeros((states, 128), f32)
    out = lax.fori_loop(0, chunks, chunk, tuple(lane_tiles(fin_ref[...])) + (none,) * tiles)
    total = jnp.concatenate(out[tiles:], axis=1)
    skip = par_ref[0, L.skip : L.skip + 1, :]

    def tile(k, carry):
        bias_sum, skip_sum = carry
        rows = pl.ds(pl.multiple_of(k * 16, 16), 16)
        bsum, wsum = (
            jnp.concatenate([fold_rows(refs, k * 16), fold_rows(refs, k * 16 + 8)], axis=0)
            for refs in (bsum_refs, wsum_refs)
        )
        spre, act, g = spre_ref[rows, :], act_ref[rows, :], g_ref[rows, :]
        grad = (wsum * (1.0 / LOG2E) + act * bsum) * jax.nn.sigmoid(spre)
        gap_ref[rows, :] = g * skip + softplus(spre) * bsum
        pre_ref[rows, :] = grad.astype(bf16)
        bias_sum = bias_sum + halves(grad)
        skip_sum = skip_sum + halves(g * act)
        return bias_sum, skip_sum

    none = jnp.zeros((8, EB), f32)
    bias_sum, skip_sum = lax.fori_loop(0, T // 16, tile, (none, none))
    R = L.R
    pre = pre_ref[...]
    step_low = proj_ref[...].astype(bf16)
    grad_step_w = lax.dot_general(step_low, pre, TN, preferred_element_type=f32)
    chan_ref[0] = jnp.concatenate(
        [
            grad_step_w[0:R],
            total * (1.0 / LOG2E),
            jnp.sum(bias_sum, axis=0, keepdims=True),
            jnp.sum(skip_sum, axis=0, keepdims=True),
            jnp.zeros((128 - R - states - 2, EB), f32),
        ],
        axis=0,
    ).astype(bf16)
    weights = wts_ref[0, L.step : L.step + R, :].astype(f32)
    weights = jnp.concatenate([weights, jnp.zeros((128 - R, EB), f32)], axis=0).astype(bf16)
    rank_ref[...] += lax.dot_general(pre, weights, NT, preferred_element_type=f32)

    @pl.when(i == pl.num_programs(0) - 1)
    def _():
        lane_sums(states, acc_ref, gb_ref, chunks)
        dims = (width, 128)
        state = lax.rem(lax.broadcasted_iota(jnp.int32, dims, 0), states)
        target = lax.broadcasted_iota(jnp.int32, dims, 1)
        diag = same_step(states, T)
        sums = rank_ref[...]
        for ref, start in ((gb_ref, R), (gc_ref, R + states)):
            fold = (target == state + start).astype(f32)
            kept = jnp.where(diag, ref[...], 0.0)
            sums = sums + jnp.dot(
                kept, fold, precision=lax.Precision.HIGHEST, preferred_element_type=f32
            )
        gproj_ref[...] = sums.astype(bf16)


def bwd_scan(L, dtk, u, g, b_cols, c_cols, par, wts, arriving, held, spre, act, proj, grad_c):
    T, E = dtk.shape
    N = L.N
    blocks = E // EB
    return pl.pallas_call(
        functools.partial(bwd_kernel, L),
        grid=(blocks,),
        in_specs=[
            cols(T), cols(T), cols(T), whole(*b_cols.shape), whole(*c_cols.shape), lead(PAR, EB),
            lead(WTS, EB), cols(N), cols(held.shape[0]), cols(T), cols(T), whole(T, 128), whole(T, TC * N),
        ],
        out_specs=[cols(T), lead(128, EB), whole(T, 128)],
        out_shape=[shape(f32, T, E), shape(bf16, blocks, 128, EB), shape(bf16, T, 128)],
        scratch_shapes=[
            pltpu.VMEM((T * N, 128), f32),
            pltpu.VMEM((T, TC * N), f32), pltpu.VMEM((T, 128), f32), pltpu.VMEM((T, EB), bf16),
        ] + [pltpu.VMEM((T * 8, 128), f32)] * (2 * EB // 128),
        compiler_params=params(),
        name="bwd_scan",
    )(dtk, u, g, b_cols, c_cols, par, wts, arriving, held, spre, act, proj, grad_c)


def conv_kernel(L, gap_ref, gproj_ref, wts_ref, act_ref, cs_ref, inner_ref, marks_ref, gc_ref, chan_ref, xs_ref):
    T = gap_ref.shape[0]
    K, wide = L.K, L.R + 2 * L.N
    weights = wts_ref[0].astype(f32)
    row = lax.broadcasted_iota(jnp.int32, weights.shape, 0)
    weights = jnp.where(row < wide, weights, 0.0).astype(bf16)
    gc_ref[...] = jnp.dot(gproj_ref[...], weights, preferred_element_type=f32)
    act_low = act_ref[...].astype(bf16)
    grad_proj = lax.dot_general(gproj_ref[...], act_low, TN, preferred_element_type=f32)
    xs_ref[...] = inner_ref[...].astype(f32)

    def tile(k, carry):
        r = pl.multiple_of(k * RT, RT)
        rows = pl.ds(r, RT)
        total = cs_ref[rows, :]
        sig = jax.nn.sigmoid(total)
        grad = (gc_ref[rows, :] + gap_ref[rows, :]) * sig * (1.0 + total * (1.0 - sig))
        gc_ref[rows, :] = grad
        block = xs_ref[pl.ds(pl.multiple_of(r + HALO - 8, 8), RT + 8), :]
        out = [carry[K] + jnp.sum(grad.reshape(RT // 8, 8, EB), axis=0)]
        for j in range(K):
            part = grad * block[8 - j : RT + 8 - j]
            if j > 0:
                part = part * marks_ref[rows, j - 1 : j]
            out.insert(0, carry[K - 1 - j] + jnp.sum(part.reshape(RT // 8, 8, EB), axis=0))
        return tuple(out)

    none = jnp.zeros((8, EB), f32)
    sums = lax.fori_loop(0, T // RT, tile, (none,) * (K + 1))
    chan_ref[0] = jnp.concatenate(
        [grad_proj[0:wide]]
        + [jnp.sum(s, axis=0, keepdims=True) for s in sums]
        + [jnp.zeros((128 - wide - K - 1, EB), f32)],
        axis=0,
    ).astype(bf16)


def conv_back(L, gap, gproj, wts, act, cs, inner, marks):
    T, E = gap.shape
    blocks = E // EB
    return pl.pallas_call(
        functools.partial(conv_kernel, L),
        grid=(blocks,),
        in_specs=[
            cols(T), whole(T, 128), lead(WTS, EB), cols(T), cols(T), cols(T + HALO), whole(*marks.shape),
        ],
        out_specs=[cols(T), lead(128, EB)],
        out_shape=[shape(f32, T, E), shape(bf16, blocks, 128, EB)],
        scratch_shapes=[pltpu.VMEM((T + HALO, EB), f32)],
        compiler_params=params(),
        name="conv_back",
    )(gap, gproj, wts, act, cs, inner, marks)


def tail_kernel(
    L, gc_ref, after_ref, par_ref, marks_ref, normed_ref, wi_ref, gn_ref, tok_ref, cot_ref, gain_ref,
    held_ref, gin_ref, gtok_ref, ggain_ref, ext_ref, low_ref, sum_ref,
):
    T, D = tok_ref.shape
    K = L.K
    i = pl.program_id(0)
    ext_ref[0:T, :] = gc_ref[...]
    ext_ref[T : T + 8, :] = after_ref[...]
    taps = [par_ref[0, L.conv + j : L.conv + j + 1, :] for j in range(K)]

    def tile(r):
        block = ext_ref[pl.ds(r, RT + 8), :]
        marks = marks_ref[pl.ds(r, RT + 8), :]
        total = taps[K - 1] * block[0:RT]
        for j in range(1, K):
            masked = block * marks[:, j - 1 : j]
            total = total + taps[K - 1 - j] * masked[j : RT + j]
        low_ref[pl.ds(r, RT), :] = total.astype(bf16)

    row_tiles(T, tile)
    gin_ref[...] = lax.dot_general(
        low_ref[...], normed_ref[...], TN, preferred_element_type=f32
    ).astype(bf16)
    part = lax.dot_general(low_ref[...], wi_ref[...], NT, preferred_element_type=f32)

    @pl.when(i == 0)
    def _():
        sum_ref[...] = gn_ref[...] + part

    @pl.when(i > 0)
    def _():
        sum_ref[...] += part

    @pl.when(i == pl.num_programs(0) - 1)
    def _():
        gain = gain_ref[...].reshape(1, D)

        def last(k, total):
            rows = pl.ds(pl.multiple_of(k * 16, 16), 16)
            x = tok_ref[rows, :].astype(f32)
            grad = sum_ref[rows, :]
            inv = lax.rsqrt(jnp.mean(x * x, axis=1, keepdims=True) + epsilon)
            scaled = grad * gain
            mean = jnp.mean(x * scaled, axis=1, keepdims=True)
            gtok_ref[rows, :] = (
                cot_ref[rows, :].astype(f32) + inv * scaled - x * (inv * inv * inv * mean)
            )
            return total + jnp.sum((grad * x * inv).reshape(2, 8, D), axis=0)

        total = lax.fori_loop(0, T // 16, last, jnp.zeros((8, D), f32))
        ggain_ref[...] = jnp.sum(total, axis=0, keepdims=True)


def tail(L, gc, after, par, marks, normed, in_weight, gn, tokens, cot, gain, held):
    T, E = gc.shape
    D = tokens.shape[1]
    blocks = E // EB
    return pl.pallas_call(
        functools.partial(tail_kernel, L),
        grid=(blocks,),
        in_specs=[
            cols(T), cols(8), lead(PAR, EB), whole(*marks.shape), whole(T, D), cols(D), whole(T, D),
            whole(T, D), whole(T, D), whole(D), pl.BlockSpec(memory_space=pl.ANY),
        ],
        out_specs=[tall(EB, D), whole(T, D), whole(1, D)],
        out_shape=[shape(bf16, 2 * E, D), shape(f32, T, D), shape(f32, 1, D)],
        scratch_shapes=[
            pltpu.VMEM((T + 8, EB), f32), pltpu.VMEM((T, EB), bf16), pltpu.VMEM((T, D), f32),
        ],
        input_output_aliases={10: 0},
        compiler_params=params(),
        name="tail",
    )(gc, after, par, marks, normed, in_weight, gn, tokens, cot, gain, held)


def sum_plan(chan_count, seq_count):
    chan_bits = [("chan", 1 << i) for i in range(chan_count.bit_length() - 1)]
    seq_bits = [("seq", 1 << i) for i in range(seq_count.bit_length() - 1)]
    return chan_bits, seq_bits


def sum_kernel(chan_count, seq_count, pieces, arrays, *refs):
    piece_rows = 16 * seq_count
    x_refs, o_refs = refs[:arrays], refs[arrays : 2 * arrays]
    chan_bits, seq_bits = sum_plan(chan_count, seq_count)
    nc, ns = len(chan_bits), len(seq_bits)
    stages = nc + ns
    count = len(pieces)
    scratch = refs[2 * arrays :]
    held = [scratch[p * stages : (p + 1) * stages] for p in range(count)]
    send_sem, recv_sem = scratch[count * stages :]
    mine = {"seq": lax.axis_index("seq"), "chan": lax.axis_index("chan")}

    def bit_of(name, bit):
        return (mine[name] // bit) % 2

    def partner(name, bit):
        other = dict(mine)
        other[name] = mine[name] + bit - 2 * bit * bit_of(name, bit)
        return (other["seq"], other["chan"])

    def order(p):
        inner = chan_bits if p % 2 == 0 else chan_bits[::-1]
        return seq_bits[:1] + inner + seq_bits[1:]

    barrier = pltpu.get_barrier_semaphore()
    for name, bit in chan_bits + seq_bits:
        pl.semaphore_signal(
            barrier, inc=1, device_id=partner(name, bit), device_id_type=pl.DeviceIdType.MESH
        )
    pl.semaphore_wait(barrier, stages)

    def parts(p, s, keep):
        name, bit = order(p)[s]
        side = bit_of(name, bit) if keep else 1 - bit_of(name, bit)
        done = order(p)[:s]
        size = piece_rows >> sum(1 for n, b in done if n == "seq")
        ref, start = (x_refs[pieces[p][0]], pieces[p][1]) if s == 0 else (held[p][s - 1], 0)
        if name == "seq":
            rows = pl.ds(pl.multiple_of(start + side * (size // 2), 16), size // 2)
            return [ref.at[:, rows, :]]
        left = [b for n, b in chan_bits if ("chan", b) not in done]
        low = 1 << left.index(bit)
        return [
            ref.at[pl.ds((i // low) * 2 * low + side * low + i % low, 1), pl.ds(start, size), :]
            for i in range((1 << len(left)) // 2)
        ]

    def landing(p, s):
        dst = held[p][s]
        if order(p)[s][0] == "seq":
            return [dst]
        return [dst.at[pl.ds(i, 1)] for i in range(dst.shape[0])]

    def copies(p, s):
        return [
            pltpu.make_async_remote_copy(
                src_ref=src, dst_ref=dst, send_sem=send_sem.at[p, s, i], recv_sem=recv_sem.at[p, s, i],
                device_id=partner(*order(p)[s]), device_id_type=pl.DeviceIdType.MESH,
            )
            for i, (src, dst) in enumerate(zip(parts(p, s, False), landing(p, s)))
        ]

    def my_rows(p, done):
        start, size = pieces[p][1], piece_rows
        for name, bit in seq_bits[:done]:
            size //= 2
            start = start + bit_of(name, bit) * size
        return pl.ds(pl.multiple_of(start, 16), size)

    def gather_copy(p, k):
        place = o_refs[pieces[p][0]].at[my_rows(p, ns - k), :]
        return pltpu.make_async_remote_copy(
            src_ref=place, dst_ref=place,
            send_sem=send_sem.at[p, stages + k, 0], recv_sem=recv_sem.at[p, stages + k, 0],
            device_id=partner(*seq_bits[ns - 1 - k]), device_id_type=pl.DeviceIdType.MESH,
        )

    total = stages + ns
    for tick in range((count + 1) // 2 + total):
        for p in range(count):
            s = tick - p // 2
            if not 0 <= s <= total:
                continue
            if 1 <= s <= stages:
                for copy in copies(p, s - 1):
                    copy.wait_recv()
                for src, dst in zip(parts(p, s - 1, True), landing(p, s - 1)):
                    dst[...] = (dst[...].astype(f32) + src[...].astype(f32)).astype(bf16)
                if s == stages:
                    o_refs[pieces[p][0]][my_rows(p, ns), :] = held[p][stages - 1][0]
            elif s > stages:
                gather_copy(p, s - 1 - stages).wait_recv()
            if s < stages:
                for copy in copies(p, s):
                    copy.start()
            elif s < total:
                gather_copy(p, s - stages).start()
    for p in range(count):
        for s in range(stages):
            for copy in copies(p, s):
                copy.wait_send()
        for k in range(ns):
            gather_copy(p, k).wait_send()


def sum_owned(arrays, seq_count):
    chan_count = arrays[0].shape[0]
    chan_bits, seq_bits = sum_plan(chan_count, seq_count)
    piece_rows = 16 * seq_count
    pieces = [(a, r) for a, v in enumerate(arrays) for r in range(0, v.shape[1], piece_rows)]
    ordered = seq_bits[:1] + chan_bits + seq_bits[1:]
    scratch = []
    for a, r in pieces:
        owners, size = chan_count, piece_rows
        for name, bit in ordered:
            if name == "chan":
                owners //= 2
            else:
                size //= 2
            scratch.append(pltpu.VMEM((owners, size, arrays[a].shape[2]), bf16))
    total = len(ordered) + len(seq_bits)
    sems = pltpu.SemaphoreType.DMA((len(pieces), total, max(1, chan_count // 2)))
    vmem = pl.BlockSpec(memory_space=pltpu.VMEM)
    return pl.pallas_call(
        functools.partial(sum_kernel, chan_count, seq_count, pieces, len(arrays)),
        in_specs=[vmem] * len(arrays),
        out_specs=[vmem] * len(arrays),
        out_shape=[shape(bf16, *v.shape[1:]) for v in arrays],
        scratch_shapes=scratch + [sems, sems],
        compiler_params=params(collective_id=0, has_side_effects=True),
        name="sum_owned",
    )(*arrays)


def unpack_kernel(L, in_ref, out_ref, d_ref, e_ref, gin_ref, gout_ref, *refs):
    gin_ref[...] = in_ref[...].astype(f32).T
    gout_ref[...] = out_ref[...].astype(f32)
    d, e = d_ref[...].astype(f32), e_ref[...].astype(f32)
    R, N, K = L.R, L.N, L.K
    wide = R + 2 * N
    conv_w, conv_b, proj, step_w, step_b, decay, skip, gain = refs
    width = d.shape[1]
    step_w[...] = d[0:R]
    decay[...] = d[R : R + N]
    step_b[...] = d[R + N].reshape(width)
    skip[...] = d[R + N + 1].reshape(width)
    proj[...] = e[0:wide]
    conv_w[...] = e[wide : wide + K]
    conv_b[...] = e[wide + K].reshape(width)
    gain[...] = e[wide + K + 1].reshape(width)


def unpack(L, sums):
    width = sums[2].shape[1]
    rows, D = sums[0].shape
    R, N, K = L.R, L.N, L.K
    return pl.pallas_call(
        functools.partial(unpack_kernel, L),
        out_shape=[
            shape(f32, D, rows), shape(f32, *sums[1].shape), shape(f32, K, width), shape(f32, width),
            shape(f32, R + 2 * N, width), shape(f32, R, width), shape(f32, width),
            shape(f32, N, width), shape(f32, width), shape(f32, width),
        ],
        compiler_params=params(),
        name="unpack",
    )(*sums)


def local(
    tokens, norm_gain, in_weight, conv_weight, conv_bias, proj_weight, step_weight,
    step_bias, decay_log, skip_gain, out_weight, cotangent, lengths,
):
    T, D = tokens.shape
    E = in_weight.shape[1] // 2
    L = Layout(step_weight.shape[0], decay_log.shape[0], conv_weight.shape[0])
    ci = lax.axis_index("chan")
    cc = lax.axis_size("chan")
    sc = lax.axis_size("seq")
    blocks, share = E // EB, E // cc

    parts = (conv_weight, conv_bias, proj_weight.T, step_weight, step_bias, decay_log, skip_gain)
    wts, par, halo = gather_params(L, cc, parts, tokens)

    def by_block(values):
        if share == EB:
            return values
        values = jnp.moveaxis(values, 0, 1).reshape(-1, blocks, EB)
        return jnp.moveaxis(values, 1, 0)

    wts, par = by_block(wts), by_block(par)
    marks, normed, inner, gate, gg, g, cs, act, proj, b_cols, c_cols = front(
        L, lengths, tokens, halo, norm_gain, in_weight, out_weight, cotangent, par, wts
    )
    spre, dtk, u, entering, arriving = pre_scan(L, cc, proj, par, wts, act, g, marks, b_cols, c_cols)
    held, grad_c, block_out, grad_out, grad_in, gn = fwd_scan(
        L, dtk, u, b_cols, c_cols, g, par, entering, act, gate, gg, out_weight, cotangent, tokens,
        normed, in_weight,
    )
    gap, chan_d, gproj = bwd_scan(
        L, dtk, u, g, b_cols, c_cols, par, wts, arriving, held, spre, act, proj, grad_c
    )
    gc, chan_e = conv_back(L, gap, gproj, wts, act, cs, inner, marks)
    after = lax.ppermute(gc[0:8], "chan", [(k, k - 1) for k in range(1, cc)])
    grad_in, grad_tokens, grad_gain = tail(
        L, gc, after, par, marks, normed, in_weight, gn, tokens, cotangent, norm_gain, grad_in
    )

    def by_owner(values):
        if share == EB:
            return values
        values = jnp.moveaxis(values, 0, 1).reshape(128, cc, share)
        return jnp.moveaxis(values, 1, 0)

    chan_d, chan_e = by_owner(chan_d), by_owner(chan_e)
    row = L.R + 2 * L.N + L.K + 1
    owned_gain = jnp.pad(grad_gain.reshape(cc, 1, D // cc), ((0, 0), (0, 0), (0, share - D // cc)))
    chan_e = lax.dynamic_update_slice(chan_e, owned_gain.astype(bf16), (0, row, 0))
    arrays = [grad_in.reshape(cc, 2 * E // cc, D), grad_out.reshape(cc, share, D), chan_d, chan_e]
    piece = 16 * sc
    rows = [v.shape[1] for v in arrays]
    arrays = [jnp.pad(v, ((0, 0), (0, -v.shape[1] % piece), (0, 0))) for v in arrays]
    sums = sum_owned(arrays, sc)
    sums = [v[:r] for v, r in zip(sums, rows)]
    g_in, g_out, conv_w, conv_b, proj_w, step_w, step_b, decay, skip, g_gain = unpack(L, sums)
    return (
        block_out, grad_tokens, g_gain[: D // cc], g_in, conv_w, conv_b, proj_w.T, step_w,
        step_b, decay, skip, g_out,
    )


def solution(mesh):
    tok, row, vec = P(("seq", "chan"), None), P(None, "chan"), P("chan")
    in_specs = (
        tok, P(), P(), row, vec, P("chan", None), row, vec, row, vec, P(), tok, P("seq", None),
    )
    out_specs = (
        tok, tok, vec, row, row, vec, P("chan", None), row, vec, row, vec, P("chan", None),
    )
    return jax.shard_map(local, mesh=mesh, in_specs=in_specs, out_specs=out_specs, check_vma=False)
```

```python
import functools
import math

import jax
import jax.numpy as jnp
from jax import lax
from jax.experimental import pallas as pl
from jax.experimental.pallas import tpu as pltpu
from jax.sharding import PartitionSpec as P

epsilon = 1e-05
LOG2E = math.log2(math.e)
CUT = 1e30
TC = 16
EB = 384
RT = 32
BLOCK_SLOTS = 4
HALO = 16
PAR = 24
WTS = 128
f32 = jnp.float32
bf16 = jnp.bfloat16
NT = (((1,), (1,)), ((), ()))
TN = (((0,), (0,)), ((), ()))


def params(**more):
    return pltpu.CompilerParams(vmem_limit_bytes=60 * 1024 * 1024, **more)


def cols(rows, width=EB, shift=0):
    return pl.BlockSpec((rows, width), lambda i: (0, i + shift))


def tall(rows, width, shift=0):
    return pl.BlockSpec((rows, width), lambda i: (i + shift, 0))


def lead(rows, width, count=1):
    return pl.BlockSpec((count, rows, width), lambda i: (i, 0, 0))


def whole(*shape):
    return pl.BlockSpec(shape, lambda i: (0,) * len(shape))


def once(*shape):
    return pl.BlockSpec(shape, lambda i: (0,) * len(shape), pipeline_mode=pl.Buffered(1))


def shape(dtype, *dims):
    return jax.ShapeDtypeStruct(dims, dtype)


def row_tiles(count, body):
    def step(i, unused):
        body(pl.multiple_of(i * RT, RT))
        return unused

    lax.fori_loop(0, count // RT, step, 0)


def same_step(states, rows):
    dims = (rows, TC * states)
    here = lax.rem(lax.broadcasted_iota(jnp.int32, dims, 0), TC) * states
    place = lax.broadcasted_iota(jnp.int32, dims, 1)
    return (place >= here) & (place < here + states)


class Layout:
    def __init__(self, R, N, K):
        self.R, self.N, self.K = R, N, K
        self.step = R + 2 * N
        self.decay = 0
        self.conv = self.decay + N
        self.conv_b = self.conv + K
        self.step_b = self.conv_b + 1
        self.skip = self.step_b + 1
        self.end = self.skip + 1


def gather_kernel(
    L, count, cw_ref, cb_ref, pw_ref, sw_ref, sb_ref, dl_ref, sk_ref, tok_ref,
    wts_ref, par_ref, halo_ref, send_sem, recv_sem, halo_sems,
):
    si, ci = lax.axis_index("seq"), lax.axis_index("chan")
    T = tok_ref.shape[0]
    width = par_ref.shape[2]
    barrier = pltpu.get_barrier_semaphore()
    for k in range(1, count):
        pl.semaphore_signal(
            barrier, inc=1, device_id=(si, lax.rem(ci + k, count)),
            device_id_type=pl.DeviceIdType.MESH,
        )
    own, weights = par_ref.at[ci], wts_ref.at[ci]
    weights[...] = jnp.concatenate(
        [pw_ref[...].astype(f32), sw_ref[...].astype(f32)], axis=0
    ).astype(bf16)
    own[...] = jnp.concatenate(
        [
            dl_ref[...], cw_ref[...], cb_ref[...].reshape(1, width), sb_ref[...].reshape(1, width),
            sk_ref[...].reshape(1, width), jnp.zeros((PAR - L.end, width), f32),
        ],
        axis=0,
    )
    pl.semaphore_wait(barrier, count - 1)

    def share(ref, j, k):
        return pltpu.make_async_remote_copy(
            src_ref=ref, dst_ref=ref, send_sem=send_sem.at[j, k], recv_sem=recv_sem.at[j, k],
            device_id=(si, lax.rem(ci + k, count)), device_id_type=pl.DeviceIdType.MESH,
        )

    edge = pltpu.make_async_remote_copy(
        src_ref=tok_ref.at[pl.ds(T - HALO, HALO)], dst_ref=halo_ref,
        send_sem=halo_sems.at[0], recv_sem=halo_sems.at[1],
        device_id=(si, lax.rem(ci + 1, count)), device_id_type=pl.DeviceIdType.MESH,
    )
    edge.start()
    for j, ref in enumerate((own, weights)):
        for k in range(1, count):
            share(ref, j, k).start()
    edge.wait()
    for j, ref in enumerate((own, weights)):
        for k in range(1, count):
            share(ref, j, k).wait()


def gather_params(L, count, parts, tokens):
    width = parts[0].shape[1]
    T, D = tokens.shape
    vmem = pl.BlockSpec(memory_space=pltpu.VMEM)
    return pl.pallas_call(
        functools.partial(gather_kernel, L, count),
        in_specs=[vmem] * 8,
        out_specs=[vmem] * 3,
        out_shape=[shape(bf16, count, WTS, width), shape(f32, count, PAR, width), shape(bf16, HALO, D)],
        scratch_shapes=[
            pltpu.SemaphoreType.DMA((2, count)),
            pltpu.SemaphoreType.DMA((2, count)),
            pltpu.SemaphoreType.DMA((2,)),
        ],
        compiler_params=params(collective_id=1, has_side_effects=True),
        name="gather_params",
    )(*parts, tokens)


def front_kernel(
    L, len_ref, tok_ref, halo_ref, gain_ref, wi_ref, wg_ref, wo_ref, cot_ref, par_ref, wts_ref,
    marks_ref, normed_ref, inner_ref, gate_ref, gg_ref, g_ref, cs_ref, act_ref, proj_ref,
    bch_ref, cch_ref, hn_ref, xs_ref, low_ref,
):
    T = tok_ref.shape[0]
    N, K = L.N, L.K
    i = pl.program_id(0)

    def norm(x):
        x = x.astype(f32)
        inv = lax.rsqrt(jnp.mean(x * x, axis=1, keepdims=True) + epsilon)
        return (x * inv * gain_ref[...].reshape(1, x.shape[1])).astype(bf16)

    @pl.when(i == 0)
    def _():
        first = lax.axis_index("chan") == 0
        halo = jnp.where(first, jnp.zeros(halo_ref.shape, f32), halo_ref[...].astype(f32))
        hn_ref[...] = norm(halo)

        def tile(r):
            normed_ref[pl.ds(r, RT), :] = norm(tok_ref[pl.ds(r, RT), :])

        row_tiles(T, tile)
        proj_ref[...] = jnp.zeros_like(proj_ref)
        dims = marks_ref.shape
        place = lax.broadcasted_iota(jnp.int32, dims, 0) + lax.axis_index("chan") * T
        lane = lax.broadcasted_iota(jnp.int32, dims, 1)
        reach = jnp.where(lane < K - 1, lane + 1, 1)
        inside = jnp.zeros(dims, f32)
        start = jnp.int32(0)
        for k in range(len_ref.shape[1]):
            inside = jnp.where((start > place - reach) & (start <= place), 1.0, inside)
            start = start + len_ref[0, k]
        marks_ref[...] = jnp.where(lane < K - 1, 1.0 - inside, inside * CUT)

    low = jnp.dot(hn_ref[...], wi_ref[...], preferred_element_type=f32).astype(bf16)
    inner_ref[0:HALO, :] = low
    xs_ref[0:HALO, :] = low.astype(f32)
    low = jnp.dot(normed_ref[...], wi_ref[...], preferred_element_type=f32).astype(bf16)
    inner_ref[HALO:, :] = low
    xs_ref[HALO:, :] = low.astype(f32)
    gate_ref[...] = jnp.dot(normed_ref[...], wg_ref[...], preferred_element_type=f32)
    gg_ref[...] = lax.dot_general(cot_ref[...], wo_ref[...], NT, preferred_element_type=f32)

    for k in range(par_ref.shape[0]):
        c = slice(k * EB, (k + 1) * EB)
        taps = [par_ref[k, L.conv + j : L.conv + j + 1, :] for j in range(K)]
        bias = par_ref[k, L.conv_b : L.conv_b + 1, :]

        def tile(r, c=c, taps=taps, bias=bias):
            rows = pl.ds(r, RT)
            block = xs_ref[pl.ds(pl.multiple_of(r + HALO - 8, 8), RT + 8), c]
            total = bias + taps[K - 1] * block[8:]
            for j in range(1, K):
                usable = marks_ref[rows, j - 1 : j]
                total = total + taps[K - 1 - j] * (block[8 - j : RT + 8 - j] * usable)
            act = total * jax.nn.sigmoid(total)
            cs_ref[rows, c] = total
            act_ref[rows, c] = act
            low_ref[rows, c] = act.astype(bf16)
            gate = gate_ref[rows, c]
            passed = gg_ref[rows, c] * (gate * jax.nn.sigmoid(gate))
            g_ref[rows, c] = passed.astype(bf16).astype(f32)

        row_tiles(T, tile)
        proj_ref[...] += lax.dot_general(low_ref[:, c], wts_ref[k], NT, preferred_element_type=f32)

    @pl.when(i == pl.num_programs(0) - 1)
    def _():
        turned = proj_ref[...].T
        for ref, start in ((bch_ref, L.R), (cch_ref, L.R + N)):
            for j in range(T // TC):
                ref[j] = turned[start : start + N, j * TC : (j + 1) * TC]


def front(L, lengths, tokens, halo, gain, in_weight, out_weight, cot, par, wts):
    T, D = tokens.shape
    E = out_weight.shape[0]
    sub = 2
    wide = EB * sub
    steps = E // wide
    N = L.N
    arrays = [shape(f32, T, E)] * 5
    return pl.pallas_call(
        functools.partial(front_kernel, L),
        grid=(steps,),
        in_specs=[
            pl.BlockSpec(memory_space=pltpu.SMEM),
            whole(T, D), whole(HALO, D), whole(D), cols(D, wide), cols(D, wide, steps),
            tall(wide, D), whole(T, D), lead(PAR, EB, sub), lead(WTS, EB, sub),
        ],
        out_specs=[whole(T + 8, 8), whole(T, D), cols(T + HALO, wide)] + [cols(T, wide)] * 5 + [
            whole(T, 128), whole(T // TC, N, TC), whole(T // TC, N, TC),
        ],
        out_shape=[shape(f32, T + 8, 8), shape(bf16, T, D), shape(bf16, T + HALO, E)] + arrays + [
            shape(f32, T, 128), shape(f32, T // TC, N, TC), shape(f32, T // TC, N, TC),
        ],
        scratch_shapes=[
            pltpu.VMEM((HALO, D), bf16),
            pltpu.VMEM((T + HALO, wide), f32),
            pltpu.VMEM((T, wide), bf16),
        ],
        compiler_params=params(),
        name="front",
    )(lengths, tokens, halo, gain, in_weight, in_weight, out_weight, cot, par, wts)


def rates(L, par_ref):
    return -jnp.exp(par_ref[0, L.decay : L.decay + L.N, :]) * LOG2E


def softplus(x):
    return jnp.maximum(x, 0.0) + jnp.log1p(jnp.exp(-jnp.abs(x)))


def pre_kernel(
    L, count, proj_ref, par_ref, wts_ref, act_ref, g_ref, marks_ref, b_ref, c_ref,
    spre_ref, dtk_ref, u_ref, enter_ref, arrive_ref, ahead_ref, behind_ref, got_ref,
    send_sem, recv_sem,
):
    T, E = act_ref.shape[0], enter_ref.shape[1]
    N = L.N
    i = pl.program_id(0)
    blocks = E // EB
    si, ci = lax.axis_index("seq"), lax.axis_index("chan")

    @pl.when(i == 0)
    def _():
        barrier = pltpu.get_barrier_semaphore()
        for k in range(1, count):
            pl.semaphore_signal(
                barrier, inc=1, device_id=(si, lax.rem(ci + k, count)),
                device_id_type=pl.DeviceIdType.MESH,
            )
        pl.semaphore_wait(barrier, count - 1)

    low = proj_ref[:, 0 : L.R].astype(bf16)
    weights = wts_ref[0, L.step : L.step + L.R, :]
    bias = par_ref[0, L.step_b : L.step_b + 1, :]
    spre_ref[...] = jnp.dot(low, weights, preferred_element_type=f32) + bias

    def tile(r):
        rows = pl.ds(r, RT)
        step = softplus(spre_ref[rows, :])
        u_ref[rows, :] = step * act_ref[rows, :]
        dtk_ref[rows, :] = step + marks_ref[rows, 3:4]

    row_tiles(T, tile)
    rate = rates(L, par_ref)

    def chunk(c, carry):
        h, through, head = carry
        base = pl.multiple_of(c * TC, TC)
        b_cols, c_cols = b_ref[c], c_ref[c]
        for j in range(TC):
            d = dtk_ref[pl.ds(base + j, 1), :]
            u = u_ref[pl.ds(base + j, 1), :]
            g = g_ref[pl.ds(base + j, 1), :]
            factor = jnp.exp2(d * rate)
            h = factor * h + b_cols[:, j : j + 1] * u
            through = factor * through
            head = head + through * (c_cols[:, j : j + 1] * g)
        return h, through, head

    zero = jnp.zeros(rate.shape, f32)
    h, through, head = lax.fori_loop(0, T // TC, chunk, (zero, zero + 1.0, zero))
    ahead_ref[i, 0:N, :] = h
    ahead_ref[i, N:, :] = through
    behind_ref[i, 0:N, :] = head
    behind_ref[i, N:, :] = through

    def send(b, k, forward):
        return pltpu.make_async_remote_copy(
            src_ref=(ahead_ref if forward else behind_ref).at[b], dst_ref=got_ref.at[count - k, b],
            send_sem=send_sem.at[k, b], recv_sem=recv_sem.at[count - k, b],
            device_id=(si, lax.rem(ci + k, count)), device_id_type=pl.DeviceIdType.MESH,
        )

    for k in range(1, count):
        @pl.when(ci + k < count)
        def _(k=k):
            send(i, k, True).start()

        @pl.when(ci + k >= count)
        def _(k=k):
            send(i, k, False).start()

    @pl.when(i == blocks - 1)
    def _():
        for b in range(blocks):
            for k in range(1, count):
                send(b, k, True).wait()
        for b in range(blocks):
            span = slice(b * EB, (b + 1) * EB)
            entering, arriving = zero, zero
            for k in range(1, count):
                before = ci + k >= count
                got = got_ref[k, b]
                entering = jnp.where(before, got[0:N] + got[N:] * entering, entering)
            for k in range(count - 1, 0, -1):
                behind = ci + k < count
                got = got_ref[k, b]
                arriving = jnp.where(behind, got[0:N] + got[N:] * arriving, arriving)
            enter_ref[:, span] = entering
            arrive_ref[:, span] = arriving


def pre_scan(L, count, proj, par, wts, act, g, marks, b_cols, c_cols):
    T, E = act.shape
    N = L.N
    blocks = E // EB
    state = shape(f32, N, E)
    return pl.pallas_call(
        functools.partial(pre_kernel, L, count),
        grid=(blocks,),
        in_specs=[
            whole(T, 128), lead(PAR, EB), lead(WTS, EB), cols(T), cols(T), whole(*marks.shape),
            whole(*b_cols.shape), whole(*c_cols.shape),
        ],
        out_specs=[cols(T)] * 3 + [whole(N, E)] * 2,
        out_shape=[shape(f32, T, E)] * 3 + [state] * 2,
        scratch_shapes=[
            pltpu.VMEM((blocks, 2 * N, EB), f32),
            pltpu.VMEM((blocks, 2 * N, EB), f32),
            pltpu.VMEM((count, blocks, 2 * N, EB), f32),
            pltpu.SemaphoreType.DMA((count, blocks)),
            pltpu.SemaphoreType.DMA((count, blocks)),
        ],
        compiler_params=params(collective_id=2, has_side_effects=True),
        name="pre_scan",
    )(proj, par, wts, act, g, marks, b_cols, c_cols)


def lane_tiles(values):
    return [values[:, k * 128 : (k + 1) * 128] for k in range(EB // 128)]


def row_at(ref, t):
    return lane_tiles(ref[pl.ds(t, 1), :])


def fold_rows(refs, r):
    sums = []
    for ref in refs:
        parts = [ref[pl.ds(r * 8 + k, 8, stride=8), :] for k in range(8)]
        while len(parts) > 1:
            parts = [x + y for x, y in zip(parts[::2], parts[1::2])]
        sums.append(parts[0])
    return jnp.concatenate(sums, axis=1)


def halves(values):
    return values[0:8] + values[8:16]


def lane_sums(states, acc_ref, out_ref, chunks):
    width = TC * states
    ones = jnp.ones((TC, 128), bf16)

    def step(c, unused):
        rows = pl.ds(pl.multiple_of(c * width, width), width)
        out_ref[pl.ds(pl.multiple_of(c * TC, TC), TC), :] = lax.dot_general(
            ones, acc_ref[rows, :].astype(bf16), NT, preferred_element_type=f32
        )
        return unused

    lax.fori_loop(0, chunks, step, 0)


def fwd_kernel(
    L, dtk_ref, u_ref, b_ref, c_ref, g_ref, par_ref, hin_ref, act_ref, gate_ref, gg_ref,
    wo_ref, cot_ref, tok_ref, normed_ref, wg_ref,
    h_ref, gc_ref, block_ref, gout_ref, gin_ref, gn_ref,
    acc_ref, gated_ref, ggate_ref, branch_ref, *y_refs,
):
    rate = lane_tiles(rates(L, par_ref))
    chunks, states = b_ref.shape[0], b_ref.shape[1]
    T = chunks * TC
    width = TC * states
    i = pl.program_id(0)

    @pl.when(i == 0)
    def _():
        acc_ref[...] = jnp.zeros_like(acc_ref)
        gn_ref[...] = jnp.zeros_like(gn_ref)
        branch_ref[...] = jnp.zeros_like(branch_ref)

    h_ref[0:states, :] = hin_ref[...].astype(bf16)

    def chunk(c, carry):
        h = list(carry)
        base = pl.multiple_of(c * TC, TC)
        row = pl.multiple_of(c * width, width)
        b_cols, c_cols = b_ref[c], c_ref[c]
        for j in range(TC):
            d, u, g = (row_at(ref, base + j) for ref in (dtk_ref, u_ref, g_ref))
            b_now = jnp.broadcast_to(b_cols[:, j : j + 1], (states, 128))
            c_now = jnp.broadcast_to(c_cols[:, j : j + 1], (states, 128))
            at = pl.ds(row + j * states, states)
            acc = acc_ref[at, :]
            for k in range(len(h)):
                h[k] = jnp.exp2(d[k] * rate[k]) * h[k] + b_now * u[k]
                h_ref[pl.ds(row + (j + 1) * states, states), k * 128 : (k + 1) * 128] = h[k].astype(bf16)
                y_refs[k][pl.ds((base + j) * 8, 8), :] = halves(c_now * h[k])
                acc = acc + h[k] * g[k]
            acc_ref[at, :] = acc
        return tuple(h)

    lax.fori_loop(0, chunks, chunk, tuple(lane_tiles(hin_ref[...])))
    skip = par_ref[0, L.skip : L.skip + 1, :]

    def tile(k, unused):
        rows = pl.ds(pl.multiple_of(k * 16, 16), 16)
        y = jnp.concatenate([fold_rows(y_refs, k * 16), fold_rows(y_refs, k * 16 + 8)], axis=0)
        mixer = (y + skip * act_ref[rows, :]).astype(bf16).astype(f32)
        gate = gate_ref[rows, :]
        sig = jax.nn.sigmoid(gate)
        gated_ref[rows, :] = (mixer * (gate * sig)).astype(bf16)
        ggate_ref[rows, :] = (gg_ref[rows, :] * mixer * sig * (1.0 + gate * (1.0 - sig))).astype(bf16)
        return unused

    lax.fori_loop(0, T // 16, tile, 0)
    branch_ref[...] += jnp.dot(gated_ref[...], wo_ref[...], preferred_element_type=f32)
    gout_ref[...] = lax.dot_general(
        gated_ref[...], cot_ref[...], TN, preferred_element_type=f32
    ).astype(bf16)
    gin_ref[...] = lax.dot_general(
        ggate_ref[...], normed_ref[...], TN, preferred_element_type=f32
    ).astype(bf16)
    gn_ref[...] += lax.dot_general(ggate_ref[...], wg_ref[...], NT, preferred_element_type=f32)

    @pl.when(i == pl.num_programs(0) - 1)
    def _():
        block_ref[...] = (tok_ref[...].astype(f32) + branch_ref[...]).astype(bf16)
        lane_sums(states, acc_ref, gc_ref, chunks)


def fwd_scan(L, dtk, u, b_cols, c_cols, g, par, entering, act, gate, gg, out_weight, cot, tokens, normed, in_weight):
    T, E = dtk.shape
    D = tokens.shape[1]
    N = L.N
    rows = (T + 1) * N
    blocks = E // EB
    return pl.pallas_call(
        functools.partial(fwd_kernel, L),
        grid=(blocks,),
        in_specs=[
            cols(T), cols(T), whole(*b_cols.shape), whole(*c_cols.shape), cols(T), lead(PAR, EB), cols(N),
            cols(T), cols(T), cols(T), tall(EB, D), whole(T, D), whole(T, D), whole(T, D),
            cols(D, EB, blocks),
        ],
        out_specs=[
            cols(rows), whole(T, TC * N), whole(T, D), tall(EB, D), tall(EB, D), whole(T, D),
        ],
        out_shape=[
            shape(bf16, rows, E), shape(f32, T, TC * N), shape(bf16, T, D), shape(bf16, E, D),
            shape(bf16, E, D), shape(f32, T, D),
        ],
        scratch_shapes=[
            pltpu.VMEM((T * N, 128), f32), pltpu.VMEM((T, EB), bf16), pltpu.VMEM((T, EB), bf16),
            pltpu.VMEM((T, D), f32),
        ] + [pltpu.VMEM((T * 8, 128), f32)] * (EB // 128),
        compiler_params=params(),
        name="fwd_scan",
    )(dtk, u, b_cols, c_cols, g, par, entering, act, gate, gg, out_weight, cot, tokens, normed, in_weight)


def bwd_kernel(
    L, sums, dtk_ref, u_ref, g_ref, b_ref, c_ref, par_ref, wts_ref, fin_ref, h_ref, spre_ref, act_ref, proj_ref,
    gc_ref, *refs,
):
    arrays = len(sums.kinds)
    x_refs, refs = refs[:arrays], refs[arrays:]
    gap_ref, chan_ref, gproj_ref = refs[:3]
    o_refs, refs = refs[3 : 3 + arrays], refs[3 + arrays :]
    held_refs, refs = refs[:arrays], refs[arrays:]
    acc_ref, gb_ref, rank_ref, pre_ref = refs[:4]
    rate = lane_tiles(rates(L, par_ref))
    tiles = len(rate)
    bsum_refs, wsum_refs = refs[4 : 4 + tiles], refs[4 + tiles : 4 + 2 * tiles]
    sums.bind(x_refs, held_refs, refs[4 + 2 * tiles :])
    chunks, states = c_ref.shape[0], c_ref.shape[1]
    T = chunks * TC
    width = TC * states
    i = pl.program_id(0)

    @pl.when(i == 0)
    def _():
        acc_ref[...] = jnp.zeros_like(acc_ref)
        rank_ref[...] = jnp.zeros_like(rank_ref)
        sums.barrier()

    def chunk(i, carry):
        flow, total = list(carry[:tiles]), list(carry[tiles:])
        c = chunks - 1 - i
        base = pl.multiple_of(c * TC, TC)
        row = pl.multiple_of(c * width, width)
        b_cols, c_cols = b_ref[c], c_ref[c]
        for j in reversed(range(TC)):
            d, u, g = (row_at(ref, base + j) for ref in (dtk_ref, u_ref, g_ref))
            b_now = jnp.broadcast_to(b_cols[:, j : j + 1], (states, 128))
            c_now = jnp.broadcast_to(c_cols[:, j : j + 1], (states, 128))
            at = pl.ds(row + j * states, states)
            part = pl.ds((base + j) * 8, 8)
            acc = acc_ref[at, :]
            for k in range(tiles):
                adj = c_now * g[k] + flow[k]
                flow[k] = jnp.exp2(d[k] * rate[k]) * adj
                wr = flow[k] * h_ref[at, k * 128 : (k + 1) * 128].astype(f32) * rate[k]
                total[k] = total[k] + wr * d[k]
                wsum_refs[k][part, :] = halves(wr)
                bsum_refs[k][part, :] = halves(adj * b_now)
                acc = acc + adj * u[k]
            acc_ref[at, :] = acc
        return tuple(flow) + tuple(total)

    none = jnp.zeros((states, 128), f32)
    out = tuple(lane_tiles(fin_ref[...])) + (none,) * tiles
    for q in range(BLOCK_SLOTS):
        for n in range(sums.ticks()):
            block, quarter = divmod(n * 3 // 2, BLOCK_SLOTS)
            if quarter == q:
                pl.when(i == block)(functools.partial(sums.tick, n))
        out = lax.fori_loop(q * chunks // BLOCK_SLOTS, (q + 1) * chunks // BLOCK_SLOTS, chunk, out)
    total = jnp.concatenate(out[tiles:], axis=1)
    skip = par_ref[0, L.skip : L.skip + 1, :]

    def tile(k, carry):
        bias_sum, skip_sum = carry
        rows = pl.ds(pl.multiple_of(k * 16, 16), 16)
        bsum, wsum = (
            jnp.concatenate([fold_rows(refs, k * 16), fold_rows(refs, k * 16 + 8)], axis=0)
            for refs in (bsum_refs, wsum_refs)
        )
        spre, act, g = spre_ref[rows, :], act_ref[rows, :], g_ref[rows, :]
        grad = (wsum * (1.0 / LOG2E) + act * bsum) * jax.nn.sigmoid(spre)
        gap_ref[rows, :] = g * skip + softplus(spre) * bsum
        pre_ref[rows, :] = grad.astype(bf16)
        bias_sum = bias_sum + halves(grad)
        skip_sum = skip_sum + halves(g * act)
        return bias_sum, skip_sum

    none = jnp.zeros((8, EB), f32)
    bias_sum, skip_sum = lax.fori_loop(0, T // 16, tile, (none, none))
    R = L.R
    pre = pre_ref[...]
    step_low = proj_ref[...].astype(bf16)
    grad_step_w = lax.dot_general(step_low, pre, TN, preferred_element_type=f32)
    chan_ref[0] = jnp.concatenate(
        [
            grad_step_w[0:R],
            total * (1.0 / LOG2E),
            jnp.sum(bias_sum, axis=0, keepdims=True),
            jnp.sum(skip_sum, axis=0, keepdims=True),
            jnp.zeros((128 - R - states - 2, EB), f32),
        ],
        axis=0,
    ).astype(bf16)
    weights = wts_ref[0, L.step : L.step + R, :].astype(f32)
    weights = jnp.concatenate([weights, jnp.zeros((128 - R, EB), f32)], axis=0).astype(bf16)
    rank_ref[...] += lax.dot_general(pre, weights, NT, preferred_element_type=f32)

    @pl.when(i == pl.num_programs(0) - 1)
    def _():
        lane_sums(states, acc_ref, gb_ref, chunks)
        dims = (width, 128)
        state = lax.rem(lax.broadcasted_iota(jnp.int32, dims, 0), states)
        target = lax.broadcasted_iota(jnp.int32, dims, 1)
        diag = same_step(states, T)
        total = rank_ref[...]
        for ref, start in ((gb_ref, R), (gc_ref, R + states)):
            fold = (target == state + start).astype(f32)
            kept = jnp.where(diag, ref[...], 0.0)
            total = total + jnp.dot(
                kept, fold, precision=lax.Precision.HIGHEST, preferred_element_type=f32
            )
        gproj_ref[...] = total.astype(bf16)
        sums.drain()
        sums.hand_over(o_refs)


def bwd_scan(L, dtk, u, g, b_cols, c_cols, par, wts, arriving, held, spre, act, proj, grad_c, arrays, kinds, counts):
    T, E = dtk.shape
    N = L.N
    blocks = E // EB
    sums = Sums(*counts, kinds, [v.shape for v in arrays])
    assert sums.ticks() * 3 // 2 <= BLOCK_SLOTS * blocks
    return pl.pallas_call(
        functools.partial(bwd_kernel, L, sums),
        grid=(blocks,),
        in_specs=[
            cols(T), cols(T), cols(T), whole(*b_cols.shape), whole(*c_cols.shape), lead(PAR, EB),
            lead(WTS, EB), cols(N), cols(held.shape[0]), cols(T), cols(T), whole(T, 128), whole(T, TC * N),
        ] + [once(*v.shape) for v in arrays],
        out_specs=[cols(T), lead(128, EB), whole(T, 128)] + [whole(*o.shape) for o in sums.outs()],
        out_shape=[shape(f32, T, E), shape(bf16, blocks, 128, EB), shape(bf16, T, 128)] + sums.outs(),
        scratch_shapes=[pltpu.VMEM(o.shape, o.dtype) for o in sums.outs()] + [
            pltpu.VMEM((T * N, 128), f32),
            pltpu.VMEM((T, TC * N), f32), pltpu.VMEM((T, 128), f32), pltpu.VMEM((T, EB), bf16),
        ] + [pltpu.VMEM((T * 8, 128), f32)] * (2 * EB // 128) + sums.scratch(),
        compiler_params=params(collective_id=3, has_side_effects=True),
        name="bwd_scan",
    )(dtk, u, g, b_cols, c_cols, par, wts, arriving, held, spre, act, proj, grad_c, *arrays)


def conv_kernel(L, gap_ref, gproj_ref, wts_ref, act_ref, cs_ref, inner_ref, marks_ref, gc_ref, chan_ref, xs_ref):
    T = gap_ref.shape[0]
    K, wide = L.K, L.R + 2 * L.N
    weights = wts_ref[0].astype(f32)
    row = lax.broadcasted_iota(jnp.int32, weights.shape, 0)
    weights = jnp.where(row < wide, weights, 0.0).astype(bf16)
    gc_ref[...] = jnp.dot(gproj_ref[...], weights, preferred_element_type=f32)
    act_low = act_ref[...].astype(bf16)
    grad_proj = lax.dot_general(gproj_ref[...], act_low, TN, preferred_element_type=f32)
    xs_ref[...] = inner_ref[...].astype(f32)

    def tile(k, carry):
        r = pl.multiple_of(k * RT, RT)
        rows = pl.ds(r, RT)
        total = cs_ref[rows, :]
        sig = jax.nn.sigmoid(total)
        grad = (gc_ref[rows, :] + gap_ref[rows, :]) * sig * (1.0 + total * (1.0 - sig))
        gc_ref[rows, :] = grad
        block = xs_ref[pl.ds(pl.multiple_of(r + HALO - 8, 8), RT + 8), :]
        out = [carry[K] + jnp.sum(grad.reshape(RT // 8, 8, EB), axis=0)]
        for j in range(K):
            part = grad * block[8 - j : RT + 8 - j]
            if j > 0:
                part = part * marks_ref[rows, j - 1 : j]
            out.insert(0, carry[K - 1 - j] + jnp.sum(part.reshape(RT // 8, 8, EB), axis=0))
        return tuple(out)

    none = jnp.zeros((8, EB), f32)
    sums = lax.fori_loop(0, T // RT, tile, (none,) * (K + 1))
    chan_ref[0] = jnp.concatenate(
        [grad_proj[0:wide]]
        + [jnp.sum(s, axis=0, keepdims=True) for s in sums]
        + [jnp.zeros((128 - wide - K - 1, EB), f32)],
        axis=0,
    ).astype(bf16)


def conv_back(L, gap, gproj, wts, act, cs, inner, marks):
    T, E = gap.shape
    blocks = E // EB
    return pl.pallas_call(
        functools.partial(conv_kernel, L),
        grid=(blocks,),
        in_specs=[
            cols(T), whole(T, 128), lead(WTS, EB), cols(T), cols(T), cols(T + HALO), whole(*marks.shape),
        ],
        out_specs=[cols(T), lead(128, EB)],
        out_shape=[shape(f32, T, E), shape(bf16, blocks, 128, EB)],
        scratch_shapes=[pltpu.VMEM((T + HALO, EB), f32)],
        compiler_params=params(),
        name="conv_back",
    )(gap, gproj, wts, act, cs, inner, marks)


def tail_kernel(
    L, gc_ref, after_ref, par_ref, marks_ref, normed_ref, wi_ref, gn_ref, tok_ref, cot_ref, gain_ref,
    gin_ref, gtok_ref, ggain_ref, ext_ref, low_ref, sum_ref,
):
    T, D = tok_ref.shape
    K = L.K
    i = pl.program_id(0)
    ext_ref[0:T, :] = gc_ref[...]
    ext_ref[T : T + 8, :] = after_ref[...]
    taps = [par_ref[0, L.conv + j : L.conv + j + 1, :] for j in range(K)]

    def tile(r):
        block = ext_ref[pl.ds(r, RT + 8), :]
        marks = marks_ref[pl.ds(r, RT + 8), :]
        total = taps[K - 1] * block[0:RT]
        for j in range(1, K):
            masked = block * marks[:, j - 1 : j]
            total = total + taps[K - 1 - j] * masked[j : RT + j]
        low_ref[pl.ds(r, RT), :] = total.astype(bf16)

    row_tiles(T, tile)
    gin_ref[...] = lax.dot_general(
        low_ref[...], normed_ref[...], TN, preferred_element_type=f32
    ).astype(bf16)
    part = lax.dot_general(low_ref[...], wi_ref[...], NT, preferred_element_type=f32)

    @pl.when(i == 0)
    def _():
        sum_ref[...] = gn_ref[...] + part

    @pl.when(i > 0)
    def _():
        sum_ref[...] += part

    @pl.when(i == pl.num_programs(0) - 1)
    def _():
        gain = gain_ref[...].reshape(1, D)

        def last(k, total):
            rows = pl.ds(pl.multiple_of(k * 16, 16), 16)
            x = tok_ref[rows, :].astype(f32)
            grad = sum_ref[rows, :]
            inv = lax.rsqrt(jnp.mean(x * x, axis=1, keepdims=True) + epsilon)
            scaled = grad * gain
            mean = jnp.mean(x * scaled, axis=1, keepdims=True)
            gtok_ref[rows, :] = (
                cot_ref[rows, :].astype(f32) + inv * scaled - x * (inv * inv * inv * mean)
            )
            return total + jnp.sum((grad * x * inv).reshape(2, 8, D), axis=0)

        total = lax.fori_loop(0, T // 16, last, jnp.zeros((8, D), f32))
        ggain_ref[...] = jnp.sum(total, axis=0, keepdims=True)


def tail(L, gc, after, par, marks, normed, in_weight, gn, tokens, cot, gain):
    T, E = gc.shape
    D = tokens.shape[1]
    blocks = E // EB
    return pl.pallas_call(
        functools.partial(tail_kernel, L),
        grid=(blocks,),
        in_specs=[
            cols(T), cols(8), lead(PAR, EB), whole(*marks.shape), whole(T, D), cols(D), whole(T, D),
            whole(T, D), whole(T, D), whole(D),
        ],
        out_specs=[tall(EB, D), whole(T, D), whole(1, D)],
        out_shape=[shape(bf16, E, D), shape(f32, T, D), shape(f32, 1, D)],
        scratch_shapes=[
            pltpu.VMEM((T + 8, EB), f32), pltpu.VMEM((T, EB), bf16), pltpu.VMEM((T, D), f32),
        ],
        compiler_params=params(),
        name="tail",
    )(gc, after, par, marks, normed, in_weight, gn, tokens, cot, gain)


class Sums:
    def __init__(self, chan_count, seq_count, kinds, shapes):
        self.cc, self.sc, self.zc = chan_count, seq_count, seq_count // 2
        self.kinds = kinds
        self.piece_rows = 16 * seq_count
        self.bits = [1 << i for i in range(chan_count.bit_length() - 1)]
        self.pieces = [
            (a, r, dims[2]) for a, dims in enumerate(shapes) for r in range(0, dims[1], self.piece_rows)
        ]
        self.shapes = shapes
        self.slots = max(2 * self.zc, chan_count // 2, 1)

    def stages(self, p):
        bits = self.bits if p % 2 == 0 else self.bits[::-1]
        half = self.kinds[self.pieces[p][0]] is not None
        return (
            [("core", 1)] + [("chan", b) for b in bits] + [("z", 0)] + ([("move", 0)] if half else [])
            + [("zgather", 0), ("cgather", 0)]
        )

    def ticks(self):
        return max(len(self.stages(p)) + p // 2 for p in range(len(self.pieces))) + 1

    def outs(self):
        return [
            shape(bf16, *(dims[1:] if kind is None else (2,) + tuple(dims[1:])))
            for kind, dims in zip(self.kinds, self.shapes)
        ]

    def scratch(self):
        found = []
        for a, r, width in self.pieces:
            for k in range(len(self.bits) + 1):
                found.append(pltpu.VMEM((self.cc >> k, self.piece_rows // 2, width), bf16))
            found.append(pltpu.VMEM((self.zc, 16, width), bf16))
            found.append(pltpu.VMEM((16, width), bf16))
        dims = (len(self.pieces), len(self.bits) + 5, self.slots)
        return found + [pltpu.SemaphoreType.DMA(dims), pltpu.SemaphoreType.DMA(dims)]

    def bind(self, x_refs, o_refs, scratch):
        self.x, self.o = x_refs, o_refs
        each = len(self.bits) + 3
        self.held = [scratch[p * each : (p + 1) * each] for p in range(len(self.pieces))]
        self.send_sem, self.recv_sem = scratch[-2:]
        self.si, self.ci = lax.axis_index("seq"), lax.axis_index("chan")
        self.core, self.z = lax.rem(self.si, 2), self.si // 2

    def barrier(self):
        barrier = pltpu.get_barrier_semaphore()
        for k in range(1, self.cc):
            pl.semaphore_signal(
                barrier, inc=1, device_id=(self.si, lax.rem(self.ci + k, self.cc)),
                device_id_type=pl.DeviceIdType.MESH,
            )
        for k in range(1, self.zc):
            pl.semaphore_signal(
                barrier, inc=1, device_id=(lax.rem(self.si + 2 * k, self.sc), self.ci),
                device_id_type=pl.DeviceIdType.MESH,
            )
        pl.semaphore_signal(
            barrier, inc=1, device_id=(self.si + 1 - 2 * self.core, self.ci),
            device_id_type=pl.DeviceIdType.MESH,
        )
        pl.semaphore_wait(barrier, self.cc + self.zc - 1)

    def copy(self, p, s, slot, src, dst, seq, chan):
        return pltpu.make_async_remote_copy(
            src_ref=src, dst_ref=dst, send_sem=self.send_sem.at[p, s, slot],
            recv_sem=self.recv_sem.at[p, s, slot], device_id=(seq, chan),
            device_id_type=pl.DeviceIdType.MESH,
        )

    def kept(self, p, s, keep):
        name, bit = self.stages(p)[s]
        size = self.piece_rows // 2
        if name == "core":
            a, start, width = self.pieces[p]
            side = self.core if keep else 1 - self.core
            return [self.x[a].at[:, pl.ds(pl.multiple_of(start + side * size, 16), size), :]]
        mine = lax.rem(self.ci // bit, 2)
        side = mine if keep else 1 - mine
        left = sorted(b for n, b in self.stages(p)[s : 1 + len(self.bits)])
        low = 1 << left.index(bit)
        ref = self.held[p][s - 1]
        return [
            ref.at[pl.ds((i // low) * 2 * low + side * low + i % low, 1)]
            for i in range((1 << len(left)) // 2)
        ]

    def landing(self, p, s):
        dst = self.held[p][s]
        return [dst] if s == 0 else [dst.at[pl.ds(i, 1)] for i in range(dst.shape[0])]

    def places(self, p, start, size):
        a, first, width = self.pieces[p]
        rows = pl.ds(pl.multiple_of(first + start, 16), size)
        if self.kinds[a] is None:
            return [self.o[a].at[rows, :]]
        return [self.o[a].at[b, rows, :] for b in range(2)]

    def move(self, p, s, v):
        a = self.pieces[p][0]
        goal = self.kinds[a] + v // 2
        rows = self.core * (self.piece_rows // 2) + self.z * 16
        place = self.places(p, rows, 16)[v % 2]
        return goal, place, self.copy(p, s, v % 2, self.held[p][-1], place, self.si, goal)

    def copies(self, p, s):
        name, bit = self.stages(p)[s]
        size = self.piece_rows // 2
        sibling = self.si + 1 - 2 * self.core
        if name in ("core", "chan"):
            seq, chan = sibling, self.ci
            if name == "chan":
                seq, chan = self.si, self.ci + bit - 2 * bit * lax.rem(self.ci // bit, 2)
            pairs = zip(self.kept(p, s, False), self.landing(p, s))
            return [self.copy(p, s, i, src, dst, seq, chan) for i, (src, dst) in enumerate(pairs)]
        if name == "z":
            src = self.held[p][len(self.bits)]
            found = []
            for k in range(1, self.zc):
                goal = lax.rem(self.z + k, self.zc)
                rows = pl.ds(pl.multiple_of(goal * 16, 16), 16)
                found.append(
                    self.copy(p, s, k, src.at[0, rows, :], self.held[p][-2].at[k], goal * 2 + self.core, self.ci)
                )
            return found
        if name == "zgather":
            found = []
            for b, place in enumerate(self.places(p, self.core * size + self.z * 16, 16)):
                for k in range(1, self.zc):
                    seq = lax.rem(self.z + k, self.zc) * 2 + self.core
                    found.append(self.copy(p, s, b * self.zc + k, place, place, seq, self.ci))
            return found
        return [
            self.copy(p, s, b, place, place, sibling, self.ci)
            for b, place in enumerate(self.places(p, self.core * size, size))
        ]

    def gathering(self, p, s, work):
        kind = self.kinds[self.pieces[p][0]]
        if kind is None or self.stages(p)[s][0] not in ("zgather", "cgather"):
            work()
        else:
            pl.when((self.ci >= kind) & (self.ci < kind + self.cc // 2))(work)

    def start(self, p, s):
        if self.stages(p)[s][0] == "move":
            for v in range(self.cc):
                @pl.when(self.ci == v)
                def _(v=v):
                    goal, place, copy = self.move(p, s, v)
                    if goal == v:
                        place[...] = self.held[p][-1][...]
                    else:
                        copy.start()
            return

        def work():
            for copy in self.copies(p, s):
                copy.start()

        self.gathering(p, s, work)

    def finish(self, p, s):
        name, bit = self.stages(p)[s]
        if name == "move":
            for v in range(self.cc):
                goal, place, copy = self.move(p, s, v)
                if goal != v:
                    pl.when(self.ci == goal)(copy.wait_recv)
            return

        def work():
            for copy in self.copies(p, s):
                copy.wait_recv()

        self.gathering(p, s, work)
        if name in ("core", "chan"):
            for src, dst in zip(self.kept(p, s, True), self.landing(p, s)):
                dst[...] = (dst[...].astype(f32) + src[...].astype(f32)).astype(bf16)
        if name == "z":
            rows = pl.ds(pl.multiple_of(self.z * 16, 16), 16)
            total = self.held[p][len(self.bits)][0, rows, :].astype(f32)
            for k in range(1, self.zc):
                total = total + self.held[p][-2][k].astype(f32)
            if self.kinds[self.pieces[p][0]] is None:
                place = self.places(p, self.core * (self.piece_rows // 2) + self.z * 16, 16)[0]
                place[...] = total.astype(bf16)
            else:
                self.held[p][-1][...] = total.astype(bf16)

    def tick(self, n):
        for p in range(len(self.pieces)):
            s = n - p // 2
            if 1 <= s <= len(self.stages(p)):
                self.finish(p, s - 1)
            if 0 <= s < len(self.stages(p)):
                self.start(p, s)

    def hand_over(self, refs):
        for kind, src, dst in zip(self.kinds, self.o, refs):
            def work(src=src, dst=dst):
                dst[...] = src[...]

            if kind is None:
                work()
            else:
                pl.when((self.ci >= kind) & (self.ci < kind + self.cc // 2))(work)

    def drain(self):
        for p in range(len(self.pieces)):
            for s, (name, bit) in enumerate(self.stages(p)):
                if name == "move":
                    for v in range(self.cc):
                        goal, place, copy = self.move(p, s, v)
                        if goal != v:
                            pl.when(self.ci == v)(copy.wait_send)
                    continue

                def work(p=p, s=s):
                    for copy in self.copies(p, s):
                        copy.wait_send()

                self.gathering(p, s, work)


def sum_kernel(sums, *refs):
    arrays = len(sums.kinds)
    sums.bind(refs[:arrays], refs[arrays : 2 * arrays], refs[2 * arrays :])
    sums.barrier()
    for n in range(sums.ticks()):
        sums.tick(n)
    sums.drain()


def sum_owned(arrays, kinds, chan_count, seq_count):
    sums = Sums(chan_count, seq_count, kinds, [v.shape for v in arrays])
    vmem = pl.BlockSpec(memory_space=pltpu.VMEM)
    return pl.pallas_call(
        functools.partial(sum_kernel, sums),
        in_specs=[vmem] * len(arrays),
        out_specs=[vmem] * len(arrays),
        out_shape=sums.outs(),
        scratch_shapes=sums.scratch(),
        compiler_params=params(collective_id=0, has_side_effects=True),
        name="sum_owned",
    )(*arrays)


def unpack_kernel(L, inner_ref, gate_ref, out_ref, d_ref, e_ref, gin_ref, gout_ref, *refs):
    first = lax.axis_index("chan") < lax.axis_size("chan") // 2

    @pl.when(first)
    def _():
        gin_ref[...] = inner_ref[...].astype(f32).T

    @pl.when(jnp.logical_not(first))
    def _():
        gin_ref[...] = gate_ref[...].astype(f32).T

    gout_ref[...] = out_ref[...].astype(f32)
    d, e = d_ref[...].astype(f32), e_ref[...].astype(f32)
    R, N, K = L.R, L.N, L.K
    wide = R + 2 * N
    conv_w, conv_b, proj, step_w, step_b, decay, skip, gain = refs
    width = d.shape[1]
    step_w[...] = d[0:R]
    decay[...] = d[R : R + N]
    step_b[...] = d[R + N].reshape(width)
    skip[...] = d[R + N + 1].reshape(width)
    proj[...] = e[0:wide]
    conv_w[...] = e[wide : wide + K]
    conv_b[...] = e[wide + K].reshape(width)
    gain[...] = e[wide + K + 1].reshape(width)


def unpack(L, sums):
    width = sums[3].shape[1]
    rows, D = sums[0].shape
    R, N, K = L.R, L.N, L.K
    return pl.pallas_call(
        functools.partial(unpack_kernel, L),
        out_shape=[
            shape(f32, D, rows), shape(f32, *sums[2].shape), shape(f32, K, width), shape(f32, width),
            shape(f32, R + 2 * N, width), shape(f32, R, width), shape(f32, width),
            shape(f32, N, width), shape(f32, width), shape(f32, width),
        ],
        compiler_params=params(),
        name="unpack",
    )(*sums)


def local(
    tokens, norm_gain, in_weight, conv_weight, conv_bias, proj_weight, step_weight,
    step_bias, decay_log, skip_gain, out_weight, cotangent, lengths,
):
    T, D = tokens.shape
    E = in_weight.shape[1] // 2
    L = Layout(step_weight.shape[0], decay_log.shape[0], conv_weight.shape[0])
    ci = lax.axis_index("chan")
    cc = lax.axis_size("chan")
    sc = lax.axis_size("seq")
    blocks, share = E // EB, E // cc

    parts = (conv_weight, conv_bias, proj_weight.T, step_weight, step_bias, decay_log, skip_gain)
    wts, par, halo = gather_params(L, cc, parts, tokens)

    def by_block(values):
        if share == EB:
            return values
        values = jnp.moveaxis(values, 0, 1).reshape(-1, blocks, EB)
        return jnp.moveaxis(values, 1, 0)

    wts, par = by_block(wts), by_block(par)
    marks, normed, inner, gate, gg, g, cs, act, proj, b_cols, c_cols = front(
        L, lengths, tokens, halo, norm_gain, in_weight, out_weight, cotangent, par, wts
    )
    spre, dtk, u, entering, arriving = pre_scan(L, cc, proj, par, wts, act, g, marks, b_cols, c_cols)
    held, grad_c, block_out, grad_out, grad_in_gate, gn = fwd_scan(
        L, dtk, u, b_cols, c_cols, g, par, entering, act, gate, gg, out_weight, cotangent, tokens,
        normed, in_weight,
    )

    piece = 16 * sc
    fold = 2 if 2 * share <= piece else 1

    def owned(values):
        values = values.reshape(cc, -1, values.shape[-1] // fold)
        return jnp.pad(values, ((0, 0), (0, -values.shape[1] % piece), (0, 0)))

    def unfolded(values):
        if values.ndim == 2:
            return values[: share * fold].reshape(share, D)
        return values[:, : share * fold].reshape(2 * share, D)

    def by_owner(values):
        if share != EB:
            values = jnp.moveaxis(values, 0, 1).reshape(values.shape[1], cc, share)
            values = jnp.moveaxis(values, 1, 0)
        return jnp.pad(values, ((0, 0), (0, -values.shape[1] % piece), (0, 0)))

    gap, chan_d, gproj, sum_out, sum_gate = bwd_scan(
        L, dtk, u, g, b_cols, c_cols, par, wts, arriving, held, spre, act, proj, grad_c,
        [owned(grad_out), owned(grad_in_gate)], [None, cc // 2], (cc, sc),
    )
    gc, chan_e = conv_back(L, gap, gproj, wts, act, cs, inner, marks)
    after = lax.ppermute(gc[0:8], "chan", [(k, k - 1) for k in range(1, cc)])
    grad_in_inner, grad_tokens, grad_gain = tail(
        L, gc, after, par, marks, normed, in_weight, gn, tokens, cotangent, norm_gain
    )
    row = L.R + 2 * L.N + L.K + 1
    gain_part = jnp.pad(grad_gain.reshape(cc, 1, D // cc), ((0, 0), (0, 0), (0, share - D // cc)))
    chan_e = lax.dynamic_update_slice(by_owner(chan_e), gain_part.astype(bf16), (0, row, 0))
    sum_inner, sum_d, sum_e = sum_owned(
        [owned(grad_in_inner), by_owner(chan_d), chan_e], [0, None, None], cc, sc
    )
    sums = [unfolded(v) for v in (sum_inner, sum_gate, sum_out)] + [sum_d, sum_e]
    g_in, g_out, conv_w, conv_b, proj_w, step_w, step_b, decay, skip, g_gain = unpack(L, sums)
    return (
        block_out, grad_tokens, g_gain[: D // cc], g_in, conv_w, conv_b, proj_w.T, step_w,
        step_b, decay, skip, g_out,
    )


def solution(mesh):
    tok, row, vec = P(("seq", "chan"), None), P(None, "chan"), P("chan")
    in_specs = (
        tok, P(), P(), row, vec, P("chan", None), row, vec, row, vec, P(), tok, P("seq", None),
    )
    out_specs = (
        tok, tok, vec, row, row, vec, P("chan", None), row, vec, row, vec, P("chan", None),
    )
    return jax.shard_map(local, mesh=mesh, in_specs=in_specs, out_specs=out_specs, check_vma=False)
```

```python
import functools
import math

import jax
import jax.numpy as jnp
from jax import lax
from jax.experimental import pallas as pl
from jax.experimental.pallas import tpu as pltpu
from jax.sharding import PartitionSpec as P

epsilon = 1e-05
LOG2E = math.log2(math.e)
CUT = 1e30
TC = 16
EB = 384
RT = 32
BLOCK_SLOTS = 4
HALO = 16
PAR = 24
WTS = 128
f32 = jnp.float32
bf16 = jnp.bfloat16
NT = (((1,), (1,)), ((), ()))
TN = (((0,), (0,)), ((), ()))


def params(**more):
    return pltpu.CompilerParams(vmem_limit_bytes=60 * 1024 * 1024, **more)


def cols(rows, width=EB, shift=0):
    return pl.BlockSpec((rows, width), lambda i: (0, i + shift))


def tall(rows, width, shift=0):
    return pl.BlockSpec((rows, width), lambda i: (i + shift, 0))


def lead(rows, width, count=1):
    return pl.BlockSpec((count, rows, width), lambda i: (i, 0, 0))


def whole(*shape):
    return pl.BlockSpec(shape, lambda i: (0,) * len(shape))


def once(*shape):
    return pl.BlockSpec(shape, lambda i: (0,) * len(shape), pipeline_mode=pl.Buffered(1))


def shape(dtype, *dims):
    return jax.ShapeDtypeStruct(dims, dtype)


def row_tiles(count, body):
    def step(i, unused):
        body(pl.multiple_of(i * RT, RT))
        return unused

    lax.fori_loop(0, count // RT, step, 0)


def same_step(states, rows):
    dims = (rows, TC * states)
    here = lax.rem(lax.broadcasted_iota(jnp.int32, dims, 0), TC) * states
    place = lax.broadcasted_iota(jnp.int32, dims, 1)
    return (place >= here) & (place < here + states)


class Layout:
    def __init__(self, R, N, K):
        self.R, self.N, self.K = R, N, K
        self.step = R + 2 * N
        self.decay = 0
        self.conv = self.decay + N
        self.conv_b = self.conv + K
        self.step_b = self.conv_b + 1
        self.skip = self.step_b + 1
        self.end = self.skip + 1


def gather_kernel(
    L, count, cw_ref, cb_ref, pw_ref, sw_ref, sb_ref, dl_ref, sk_ref, tok_ref,
    wts_ref, par_ref, halo_ref, send_sem, recv_sem, halo_sems,
):
    si, ci = lax.axis_index("seq"), lax.axis_index("chan")
    T = tok_ref.shape[0]
    width = par_ref.shape[2]
    barrier = pltpu.get_barrier_semaphore()
    for k in range(1, count):
        pl.semaphore_signal(
            barrier, inc=1, device_id=(si, lax.rem(ci + k, count)),
            device_id_type=pl.DeviceIdType.MESH,
        )
    own, weights = par_ref.at[ci], wts_ref.at[ci]
    weights[...] = jnp.concatenate(
        [pw_ref[...].astype(f32), sw_ref[...].astype(f32)], axis=0
    ).astype(bf16)
    own[...] = jnp.concatenate(
        [
            dl_ref[...], cw_ref[...], cb_ref[...].reshape(1, width), sb_ref[...].reshape(1, width),
            sk_ref[...].reshape(1, width), jnp.zeros((PAR - L.end, width), f32),
        ],
        axis=0,
    )
    pl.semaphore_wait(barrier, count - 1)

    def share(ref, j, k):
        return pltpu.make_async_remote_copy(
            src_ref=ref, dst_ref=ref, send_sem=send_sem.at[j, k], recv_sem=recv_sem.at[j, k],
            device_id=(si, lax.rem(ci + k, count)), device_id_type=pl.DeviceIdType.MESH,
        )

    edge = pltpu.make_async_remote_copy(
        src_ref=tok_ref.at[pl.ds(T - HALO, HALO)], dst_ref=halo_ref,
        send_sem=halo_sems.at[0], recv_sem=halo_sems.at[1],
        device_id=(si, lax.rem(ci + 1, count)), device_id_type=pl.DeviceIdType.MESH,
    )
    edge.start()
    for j, ref in enumerate((own, weights)):
        for k in range(1, count):
            share(ref, j, k).start()
    edge.wait()
    for j, ref in enumerate((own, weights)):
        for k in range(1, count):
            share(ref, j, k).wait()


def gather_params(L, count, parts, tokens):
    width = parts[0].shape[1]
    T, D = tokens.shape
    vmem = pl.BlockSpec(memory_space=pltpu.VMEM)
    return pl.pallas_call(
        functools.partial(gather_kernel, L, count),
        in_specs=[vmem] * 8,
        out_specs=[vmem] * 3,
        out_shape=[shape(bf16, count, WTS, width), shape(f32, count, PAR, width), shape(bf16, HALO, D)],
        scratch_shapes=[
            pltpu.SemaphoreType.DMA((2, count)),
            pltpu.SemaphoreType.DMA((2, count)),
            pltpu.SemaphoreType.DMA((2,)),
        ],
        compiler_params=params(collective_id=1, has_side_effects=True),
        name="gather_params",
    )(*parts, tokens)


def front_kernel(
    L, len_ref, tok_ref, halo_ref, gain_ref, wi_ref, wg_ref, wo_ref, cot_ref, par_ref, wts_ref,
    marks_ref, normed_ref, inner_ref, gate_ref, gg_ref, g_ref, cs_ref, act_ref, proj_ref,
    bch_ref, cch_ref, hn_ref, xs_ref, low_ref,
):
    T = tok_ref.shape[0]
    N, K = L.N, L.K
    i = pl.program_id(0)

    def norm(x):
        x = x.astype(f32)
        inv = lax.rsqrt(jnp.mean(x * x, axis=1, keepdims=True) + epsilon)
        return (x * inv * gain_ref[...].reshape(1, x.shape[1])).astype(bf16)

    @pl.when(i == 0)
    def _():
        first = lax.axis_index("chan") == 0
        halo = jnp.where(first, jnp.zeros(halo_ref.shape, f32), halo_ref[...].astype(f32))
        hn_ref[...] = norm(halo)

        def tile(r):
            normed_ref[pl.ds(r, RT), :] = norm(tok_ref[pl.ds(r, RT), :])

        row_tiles(T, tile)
        proj_ref[...] = jnp.zeros_like(proj_ref)
        dims = marks_ref.shape
        place = lax.broadcasted_iota(jnp.int32, dims, 0) + lax.axis_index("chan") * T
        lane = lax.broadcasted_iota(jnp.int32, dims, 1)
        reach = jnp.where(lane < K - 1, lane + 1, 1)
        inside = jnp.zeros(dims, f32)
        start = jnp.int32(0)
        for k in range(len_ref.shape[1]):
            inside = jnp.where((start > place - reach) & (start <= place), 1.0, inside)
            start = start + len_ref[0, k]
        marks_ref[...] = jnp.where(lane < K - 1, 1.0 - inside, inside * CUT)

    low = jnp.dot(hn_ref[...], wi_ref[...], preferred_element_type=f32).astype(bf16)
    inner_ref[0:HALO, :] = low
    xs_ref[0:HALO, :] = low.astype(f32)
    low = jnp.dot(normed_ref[...], wi_ref[...], preferred_element_type=f32).astype(bf16)
    inner_ref[HALO:, :] = low
    xs_ref[HALO:, :] = low.astype(f32)
    gate_ref[...] = jnp.dot(normed_ref[...], wg_ref[...], preferred_element_type=f32)
    gg_ref[...] = lax.dot_general(cot_ref[...], wo_ref[...], NT, preferred_element_type=f32)

    for k in range(par_ref.shape[0]):
        c = slice(k * EB, (k + 1) * EB)
        taps = [par_ref[k, L.conv + j : L.conv + j + 1, :] for j in range(K)]
        bias = par_ref[k, L.conv_b : L.conv_b + 1, :]

        def tile(r, c=c, taps=taps, bias=bias):
            rows = pl.ds(r, RT)
            block = xs_ref[pl.ds(pl.multiple_of(r + HALO - 8, 8), RT + 8), c]
            total = bias + taps[K - 1] * block[8:]
            for j in range(1, K):
                usable = marks_ref[rows, j - 1 : j]
                total = total + taps[K - 1 - j] * (block[8 - j : RT + 8 - j] * usable)
            act = total * jax.nn.sigmoid(total)
            cs_ref[rows, c] = total
            act_ref[rows, c] = act
            low_ref[rows, c] = act.astype(bf16)
            gate = gate_ref[rows, c]
            passed = gg_ref[rows, c] * (gate * jax.nn.sigmoid(gate))
            g_ref[rows, c] = passed.astype(bf16).astype(f32)

        row_tiles(T, tile)
        proj_ref[...] += lax.dot_general(low_ref[:, c], wts_ref[k], NT, preferred_element_type=f32)

    @pl.when(i == pl.num_programs(0) - 1)
    def _():
        turned = proj_ref[...].T
        for ref, start in ((bch_ref, L.R), (cch_ref, L.R + N)):
            for j in range(T // TC):
                ref[j] = turned[start : start + N, j * TC : (j + 1) * TC]


def front(L, lengths, tokens, halo, gain, in_weight, out_weight, cot, par, wts):
    T, D = tokens.shape
    E = out_weight.shape[0]
    sub = 2
    wide = EB * sub
    steps = E // wide
    N = L.N
    arrays = [shape(f32, T, E)] * 5
    return pl.pallas_call(
        functools.partial(front_kernel, L),
        grid=(steps,),
        in_specs=[
            pl.BlockSpec(memory_space=pltpu.SMEM),
            whole(T, D), whole(HALO, D), whole(D), cols(D, wide), cols(D, wide, steps),
            tall(wide, D), whole(T, D), lead(PAR, EB, sub), lead(WTS, EB, sub),
        ],
        out_specs=[whole(T + 8, 8), whole(T, D), cols(T + HALO, wide)] + [cols(T, wide)] * 5 + [
            whole(T, 128), whole(T // TC, N, TC), whole(T // TC, N, TC),
        ],
        out_shape=[shape(f32, T + 8, 8), shape(bf16, T, D), shape(bf16, T + HALO, E)] + arrays + [
            shape(f32, T, 128), shape(f32, T // TC, N, TC), shape(f32, T // TC, N, TC),
        ],
        scratch_shapes=[
            pltpu.VMEM((HALO, D), bf16),
            pltpu.VMEM((T + HALO, wide), f32),
            pltpu.VMEM((T, wide), bf16),
        ],
        compiler_params=params(),
        name="front",
    )(lengths, tokens, halo, gain, in_weight, in_weight, out_weight, cot, par, wts)


def rates(L, par_ref):
    return -jnp.exp(par_ref[0, L.decay : L.decay + L.N, :]) * LOG2E


def softplus(x):
    return jnp.maximum(x, 0.0) + jnp.log1p(jnp.exp(-jnp.abs(x)))


def pre_kernel(
    L, count, proj_ref, par_ref, wts_ref, act_ref, g_ref, marks_ref, b_ref, c_ref,
    spre_ref, dtk_ref, u_ref, enter_ref, arrive_ref, ahead_ref, behind_ref, got_ref,
    send_sem, recv_sem,
):
    T, E = act_ref.shape[0], enter_ref.shape[1]
    N = L.N
    i = pl.program_id(0)
    blocks = E // EB
    si, ci = lax.axis_index("seq"), lax.axis_index("chan")

    @pl.when(i == 0)
    def _():
        barrier = pltpu.get_barrier_semaphore()
        for k in range(1, count):
            pl.semaphore_signal(
                barrier, inc=1, device_id=(si, lax.rem(ci + k, count)),
                device_id_type=pl.DeviceIdType.MESH,
            )
        pl.semaphore_wait(barrier, count - 1)

    low = proj_ref[:, 0 : L.R].astype(bf16)
    weights = wts_ref[0, L.step : L.step + L.R, :]
    bias = par_ref[0, L.step_b : L.step_b + 1, :]
    spre_ref[...] = jnp.dot(low, weights, preferred_element_type=f32) + bias

    def tile(r):
        rows = pl.ds(r, RT)
        step = softplus(spre_ref[rows, :])
        u_ref[rows, :] = step * act_ref[rows, :]
        dtk_ref[rows, :] = step + marks_ref[rows, 3:4]

    row_tiles(T, tile)
    rate = rates(L, par_ref)

    def chunk(c, carry):
        h, through, head = carry
        base = pl.multiple_of(c * TC, TC)
        b_cols, c_cols = b_ref[c], c_ref[c]
        for j in range(TC):
            d = dtk_ref[pl.ds(base + j, 1), :]
            u = u_ref[pl.ds(base + j, 1), :]
            g = g_ref[pl.ds(base + j, 1), :]
            factor = jnp.exp2(d * rate)
            h = factor * h + b_cols[:, j : j + 1] * u
            through = factor * through
            head = head + through * (c_cols[:, j : j + 1] * g)
        return h, through, head

    zero = jnp.zeros(rate.shape, f32)
    h, through, head = lax.fori_loop(0, T // TC, chunk, (zero, zero + 1.0, zero))
    ahead_ref[i, 0:N, :] = h
    ahead_ref[i, N:, :] = through
    behind_ref[i, 0:N, :] = head
    behind_ref[i, N:, :] = through

    def send(b, k, forward):
        return pltpu.make_async_remote_copy(
            src_ref=(ahead_ref if forward else behind_ref).at[b], dst_ref=got_ref.at[count - k, b],
            send_sem=send_sem.at[k, b], recv_sem=recv_sem.at[count - k, b],
            device_id=(si, lax.rem(ci + k, count)), device_id_type=pl.DeviceIdType.MESH,
        )

    for k in range(1, count):
        @pl.when(ci + k < count)
        def _(k=k):
            send(i, k, True).start()

        @pl.when(ci + k >= count)
        def _(k=k):
            send(i, k, False).start()

    @pl.when(i == blocks - 1)
    def _():
        for b in range(blocks):
            for k in range(1, count):
                send(b, k, True).wait()
        for b in range(blocks):
            span = slice(b * EB, (b + 1) * EB)
            entering, arriving = zero, zero
            for k in range(1, count):
                before = ci + k >= count
                got = got_ref[k, b]
                entering = jnp.where(before, got[0:N] + got[N:] * entering, entering)
            for k in range(count - 1, 0, -1):
                behind = ci + k < count
                got = got_ref[k, b]
                arriving = jnp.where(behind, got[0:N] + got[N:] * arriving, arriving)
            enter_ref[:, span] = entering
            arrive_ref[:, span] = arriving


def pre_scan(L, count, proj, par, wts, act, g, marks, b_cols, c_cols):
    T, E = act.shape
    N = L.N
    blocks = E // EB
    state = shape(f32, N, E)
    return pl.pallas_call(
        functools.partial(pre_kernel, L, count),
        grid=(blocks,),
        in_specs=[
            whole(T, 128), lead(PAR, EB), lead(WTS, EB), cols(T), cols(T), whole(*marks.shape),
            whole(*b_cols.shape), whole(*c_cols.shape),
        ],
        out_specs=[cols(T)] * 3 + [whole(N, E)] * 2,
        out_shape=[shape(f32, T, E)] * 3 + [state] * 2,
        scratch_shapes=[
            pltpu.VMEM((blocks, 2 * N, EB), f32),
            pltpu.VMEM((blocks, 2 * N, EB), f32),
            pltpu.VMEM((count, blocks, 2 * N, EB), f32),
            pltpu.SemaphoreType.DMA((count, blocks)),
            pltpu.SemaphoreType.DMA((count, blocks)),
        ],
        compiler_params=params(collective_id=2, has_side_effects=True),
        name="pre_scan",
    )(proj, par, wts, act, g, marks, b_cols, c_cols)


def lane_tiles(values):
    return [values[:, k * 128 : (k + 1) * 128] for k in range(EB // 128)]


def row_at(ref, t):
    return lane_tiles(ref[pl.ds(t, 1), :])


def fold_rows(refs, r):
    sums = []
    for ref in refs:
        parts = [ref[pl.ds(r * 8 + k, 8, stride=8), :] for k in range(8)]
        while len(parts) > 1:
            parts = [x + y for x, y in zip(parts[::2], parts[1::2])]
        sums.append(parts[0])
    return jnp.concatenate(sums, axis=1)


def halves(values):
    return values[0:8] + values[8:16]


def lane_sums(states, acc_ref, out_ref, chunks):
    width = TC * states
    ones = jnp.ones((TC, 128), bf16)

    def step(c, unused):
        rows = pl.ds(pl.multiple_of(c * width, width), width)
        out_ref[pl.ds(pl.multiple_of(c * TC, TC), TC), :] = lax.dot_general(
            ones, acc_ref[rows, :].astype(bf16), NT, preferred_element_type=f32
        )
        return unused

    lax.fori_loop(0, chunks, step, 0)


def fwd_kernel(
    L, dtk_ref, u_ref, b_ref, c_ref, g_ref, par_ref, hin_ref, act_ref, gate_ref, gg_ref,
    wo_ref, cot_ref, tok_ref, normed_ref, wg_ref,
    h_ref, gc_ref, block_ref, gout_ref, gin_ref, gn_ref,
    acc_ref, gated_ref, ggate_ref, branch_ref, *y_refs,
):
    rate = lane_tiles(rates(L, par_ref))
    chunks, states = b_ref.shape[0], b_ref.shape[1]
    T = chunks * TC
    width = TC * states
    i = pl.program_id(0)

    @pl.when(i == 0)
    def _():
        acc_ref[...] = jnp.zeros_like(acc_ref)
        gn_ref[...] = jnp.zeros_like(gn_ref)
        branch_ref[...] = jnp.zeros_like(branch_ref)

    h_ref[0:states, :] = hin_ref[...].astype(bf16)

    def chunk(c, carry):
        h = list(carry)
        base = pl.multiple_of(c * TC, TC)
        row = pl.multiple_of(c * width, width)
        b_cols, c_cols = b_ref[c], c_ref[c]
        for j in range(TC):
            d, u, g = (row_at(ref, base + j) for ref in (dtk_ref, u_ref, g_ref))
            b_now = jnp.broadcast_to(b_cols[:, j : j + 1], (states, 128))
            c_now = jnp.broadcast_to(c_cols[:, j : j + 1], (states, 128))
            at = pl.ds(row + j * states, states)
            acc = acc_ref[at, :]
            for k in range(len(h)):
                h[k] = jnp.exp2(d[k] * rate[k]) * h[k] + b_now * u[k]
                h_ref[pl.ds(row + (j + 1) * states, states), k * 128 : (k + 1) * 128] = h[k].astype(bf16)
                y_refs[k][pl.ds((base + j) * 8, 8), :] = halves(c_now * h[k])
                acc = acc + h[k] * g[k]
            acc_ref[at, :] = acc
        return tuple(h)

    lax.fori_loop(0, chunks, chunk, tuple(lane_tiles(hin_ref[...])))
    skip = par_ref[0, L.skip : L.skip + 1, :]

    def tile(k, unused):
        rows = pl.ds(pl.multiple_of(k * 16, 16), 16)
        y = jnp.concatenate([fold_rows(y_refs, k * 16), fold_rows(y_refs, k * 16 + 8)], axis=0)
        mixer = (y + skip * act_ref[rows, :]).astype(bf16).astype(f32)
        gate = gate_ref[rows, :]
        sig = jax.nn.sigmoid(gate)
        gated_ref[rows, :] = (mixer * (gate * sig)).astype(bf16)
        ggate_ref[rows, :] = (gg_ref[rows, :] * mixer * sig * (1.0 + gate * (1.0 - sig))).astype(bf16)
        return unused

    lax.fori_loop(0, T // 16, tile, 0)
    branch_ref[...] += jnp.dot(gated_ref[...], wo_ref[...], preferred_element_type=f32)
    gout_ref[...] = lax.dot_general(
        gated_ref[...], cot_ref[...], TN, preferred_element_type=f32
    ).astype(bf16)
    gin_ref[...] = lax.dot_general(
        ggate_ref[...], normed_ref[...], TN, preferred_element_type=f32
    ).astype(bf16)
    gn_ref[...] += lax.dot_general(ggate_ref[...], wg_ref[...], NT, preferred_element_type=f32)

    @pl.when(i == pl.num_programs(0) - 1)
    def _():
        block_ref[...] = (tok_ref[...].astype(f32) + branch_ref[...]).astype(bf16)
        lane_sums(states, acc_ref, gc_ref, chunks)


def fwd_scan(L, dtk, u, b_cols, c_cols, g, par, entering, act, gate, gg, out_weight, cot, tokens, normed, in_weight):
    T, E = dtk.shape
    D = tokens.shape[1]
    N = L.N
    rows = (T + 1) * N
    blocks = E // EB
    return pl.pallas_call(
        functools.partial(fwd_kernel, L),
        grid=(blocks,),
        in_specs=[
            cols(T), cols(T), whole(*b_cols.shape), whole(*c_cols.shape), cols(T), lead(PAR, EB), cols(N),
            cols(T), cols(T), cols(T), tall(EB, D), whole(T, D), whole(T, D), whole(T, D),
            cols(D, EB, blocks),
        ],
        out_specs=[
            cols(rows), whole(T, TC * N), whole(T, D), tall(EB, D), tall(EB, D), whole(T, D),
        ],
        out_shape=[
            shape(bf16, rows, E), shape(f32, T, TC * N), shape(bf16, T, D), shape(bf16, E, D),
            shape(bf16, E, D), shape(f32, T, D),
        ],
        scratch_shapes=[
            pltpu.VMEM((T * N, 128), f32), pltpu.VMEM((T, EB), bf16), pltpu.VMEM((T, EB), bf16),
            pltpu.VMEM((T, D), f32),
        ] + [pltpu.VMEM((T * 8, 128), f32)] * (EB // 128),
        compiler_params=params(),
        name="fwd_scan",
    )(dtk, u, b_cols, c_cols, g, par, entering, act, gate, gg, out_weight, cot, tokens, normed, in_weight)


def bwd_kernel(
    L, sums, dtk_ref, u_ref, g_ref, b_ref, c_ref, par_ref, wts_ref, fin_ref, h_ref, spre_ref, act_ref, proj_ref,
    gc_ref, *refs,
):
    arrays = len(sums.kinds)
    x_refs, refs = refs[:arrays], refs[arrays:]
    gap_ref, chan_ref, gproj_ref = refs[:3]
    o_refs, refs = refs[3 : 3 + arrays], refs[3 + arrays :]
    held_refs, refs = refs[:arrays], refs[arrays:]
    acc_ref, gb_ref, rank_ref, pre_ref = refs[:4]
    rate = lane_tiles(rates(L, par_ref))
    tiles = len(rate)
    bsum_refs, wsum_refs = refs[4 : 4 + tiles], refs[4 + tiles : 4 + 2 * tiles]
    sums.bind(x_refs, held_refs, refs[4 + 2 * tiles :])
    chunks, states = c_ref.shape[0], c_ref.shape[1]
    T = chunks * TC
    width = TC * states
    i = pl.program_id(0)

    @pl.when(i == 0)
    def _():
        acc_ref[...] = jnp.zeros_like(acc_ref)
        rank_ref[...] = jnp.zeros_like(rank_ref)
        sums.barrier()

    def chunk(i, carry):
        flow, total = list(carry[:tiles]), list(carry[tiles:])
        c = chunks - 1 - i
        base = pl.multiple_of(c * TC, TC)
        row = pl.multiple_of(c * width, width)
        b_cols, c_cols = b_ref[c], c_ref[c]
        for j in reversed(range(TC)):
            d, u, g = (row_at(ref, base + j) for ref in (dtk_ref, u_ref, g_ref))
            b_now = jnp.broadcast_to(b_cols[:, j : j + 1], (states, 128))
            c_now = jnp.broadcast_to(c_cols[:, j : j + 1], (states, 128))
            at = pl.ds(row + j * states, states)
            part = pl.ds((base + j) * 8, 8)
            acc = acc_ref[at, :]
            for k in range(tiles):
                adj = c_now * g[k] + flow[k]
                flow[k] = jnp.exp2(d[k] * rate[k]) * adj
                wr = flow[k] * h_ref[at, k * 128 : (k + 1) * 128].astype(f32) * rate[k]
                total[k] = total[k] + wr * d[k]
                wsum_refs[k][part, :] = halves(wr)
                bsum_refs[k][part, :] = halves(adj * b_now)
                acc = acc + adj * u[k]
            acc_ref[at, :] = acc
        return tuple(flow) + tuple(total)

    none = jnp.zeros((states, 128), f32)
    out = tuple(lane_tiles(fin_ref[...])) + (none,) * tiles
    for q in range(BLOCK_SLOTS):
        for n in range(sums.ticks()):
            block, quarter = divmod(n, BLOCK_SLOTS)
            if quarter == q:
                pl.when(i == block)(functools.partial(sums.tick, n))
        out = lax.fori_loop(q * chunks // BLOCK_SLOTS, (q + 1) * chunks // BLOCK_SLOTS, chunk, out)
    total = jnp.concatenate(out[tiles:], axis=1)
    skip = par_ref[0, L.skip : L.skip + 1, :]

    def tile(k, carry):
        bias_sum, skip_sum = carry
        rows = pl.ds(pl.multiple_of(k * 16, 16), 16)
        bsum, wsum = (
            jnp.concatenate([fold_rows(refs, k * 16), fold_rows(refs, k * 16 + 8)], axis=0)
            for refs in (bsum_refs, wsum_refs)
        )
        spre, act, g = spre_ref[rows, :], act_ref[rows, :], g_ref[rows, :]
        grad = (wsum * (1.0 / LOG2E) + act * bsum) * jax.nn.sigmoid(spre)
        gap_ref[rows, :] = g * skip + softplus(spre) * bsum
        pre_ref[rows, :] = grad.astype(bf16)
        bias_sum = bias_sum + halves(grad)
        skip_sum = skip_sum + halves(g * act)
        return bias_sum, skip_sum

    none = jnp.zeros((8, EB), f32)
    bias_sum, skip_sum = lax.fori_loop(0, T // 16, tile, (none, none))
    R = L.R
    pre = pre_ref[...]
    step_low = proj_ref[...].astype(bf16)
    grad_step_w = lax.dot_general(step_low, pre, TN, preferred_element_type=f32)
    chan_ref[0] = jnp.concatenate(
        [
            grad_step_w[0:R],
            total * (1.0 / LOG2E),
            jnp.sum(bias_sum, axis=0, keepdims=True),
            jnp.sum(skip_sum, axis=0, keepdims=True),
            jnp.zeros((128 - R - states - 2, EB), f32),
        ],
        axis=0,
    ).astype(bf16)
    weights = wts_ref[0, L.step : L.step + R, :].astype(f32)
    weights = jnp.concatenate([weights, jnp.zeros((128 - R, EB), f32)], axis=0).astype(bf16)
    rank_ref[...] += lax.dot_general(pre, weights, NT, preferred_element_type=f32)

    @pl.when(i == pl.num_programs(0) - 1)
    def _():
        lane_sums(states, acc_ref, gb_ref, chunks)
        dims = (width, 128)
        state = lax.rem(lax.broadcasted_iota(jnp.int32, dims, 0), states)
        target = lax.broadcasted_iota(jnp.int32, dims, 1)
        diag = same_step(states, T)
        total = rank_ref[...]
        for ref, start in ((gb_ref, R), (gc_ref, R + states)):
            fold = (target == state + start).astype(f32)
            kept = jnp.where(diag, ref[...], 0.0)
            total = total + jnp.dot(
                kept, fold, precision=lax.Precision.HIGHEST, preferred_element_type=f32
            )
        gproj_ref[...] = total.astype(bf16)
        sums.drain()
        sums.hand_over(o_refs)


def bwd_scan(L, dtk, u, g, b_cols, c_cols, par, wts, arriving, held, spre, act, proj, grad_c, arrays, kinds, counts):
    T, E = dtk.shape
    N = L.N
    blocks = E // EB
    sums = Sums(*counts, kinds, [v.shape for v in arrays], skew=2)
    assert sums.ticks() <= BLOCK_SLOTS * blocks
    return pl.pallas_call(
        functools.partial(bwd_kernel, L, sums),
        grid=(blocks,),
        in_specs=[
            cols(T), cols(T), cols(T), whole(*b_cols.shape), whole(*c_cols.shape), lead(PAR, EB),
            lead(WTS, EB), cols(N), cols(held.shape[0]), cols(T), cols(T), whole(T, 128), whole(T, TC * N),
        ] + [once(*v.shape) for v in arrays],
        out_specs=[cols(T), lead(128, EB), whole(T, 128)] + [whole(*o.shape) for o in sums.outs()],
        out_shape=[shape(f32, T, E), shape(bf16, blocks, 128, EB), shape(bf16, T, 128)] + sums.outs(),
        scratch_shapes=[pltpu.VMEM(o.shape, o.dtype) for o in sums.outs()] + [
            pltpu.VMEM((T * N, 128), f32),
            pltpu.VMEM((T, TC * N), f32), pltpu.VMEM((T, 128), f32), pltpu.VMEM((T, EB), bf16),
        ] + [pltpu.VMEM((T * 8, 128), f32)] * (2 * EB // 128) + sums.scratch(),
        compiler_params=params(collective_id=3, has_side_effects=True),
        name="bwd_scan",
    )(dtk, u, g, b_cols, c_cols, par, wts, arriving, held, spre, act, proj, grad_c, *arrays)


def conv_kernel(L, gap_ref, gproj_ref, wts_ref, act_ref, cs_ref, inner_ref, marks_ref, gc_ref, chan_ref, xs_ref):
    T = gap_ref.shape[0]
    K, wide = L.K, L.R + 2 * L.N
    weights = wts_ref[0].astype(f32)
    row = lax.broadcasted_iota(jnp.int32, weights.shape, 0)
    weights = jnp.where(row < wide, weights, 0.0).astype(bf16)
    gc_ref[...] = jnp.dot(gproj_ref[...], weights, preferred_element_type=f32)
    act_low = act_ref[...].astype(bf16)
    grad_proj = lax.dot_general(gproj_ref[...], act_low, TN, preferred_element_type=f32)
    xs_ref[...] = inner_ref[...].astype(f32)

    def tile(k, carry):
        r = pl.multiple_of(k * RT, RT)
        rows = pl.ds(r, RT)
        total = cs_ref[rows, :]
        sig = jax.nn.sigmoid(total)
        grad = (gc_ref[rows, :] + gap_ref[rows, :]) * sig * (1.0 + total * (1.0 - sig))
        gc_ref[rows, :] = grad
        block = xs_ref[pl.ds(pl.multiple_of(r + HALO - 8, 8), RT + 8), :]
        out = [carry[K] + jnp.sum(grad.reshape(RT // 8, 8, EB), axis=0)]
        for j in range(K):
            part = grad * block[8 - j : RT + 8 - j]
            if j > 0:
                part = part * marks_ref[rows, j - 1 : j]
            out.insert(0, carry[K - 1 - j] + jnp.sum(part.reshape(RT // 8, 8, EB), axis=0))
        return tuple(out)

    none = jnp.zeros((8, EB), f32)
    sums = lax.fori_loop(0, T // RT, tile, (none,) * (K + 1))
    chan_ref[0] = jnp.concatenate(
        [grad_proj[0:wide]]
        + [jnp.sum(s, axis=0, keepdims=True) for s in sums]
        + [jnp.zeros((128 - wide - K - 1, EB), f32)],
        axis=0,
    ).astype(bf16)


def conv_back(L, gap, gproj, wts, act, cs, inner, marks):
    T, E = gap.shape
    blocks = E // EB
    return pl.pallas_call(
        functools.partial(conv_kernel, L),
        grid=(blocks,),
        in_specs=[
            cols(T), whole(T, 128), lead(WTS, EB), cols(T), cols(T), cols(T + HALO), whole(*marks.shape),
        ],
        out_specs=[cols(T), lead(128, EB)],
        out_shape=[shape(f32, T, E), shape(bf16, blocks, 128, EB)],
        scratch_shapes=[pltpu.VMEM((T + HALO, EB), f32)],
        compiler_params=params(),
        name="conv_back",
    )(gap, gproj, wts, act, cs, inner, marks)


def tail_kernel(
    L, gc_ref, after_ref, par_ref, marks_ref, normed_ref, wi_ref, gn_ref, tok_ref, cot_ref, gain_ref,
    gin_ref, gtok_ref, ggain_ref, ext_ref, low_ref, sum_ref,
):
    T, D = tok_ref.shape
    K = L.K
    i = pl.program_id(0)
    ext_ref[0:T, :] = gc_ref[...]
    ext_ref[T : T + 8, :] = after_ref[...]
    taps = [par_ref[0, L.conv + j : L.conv + j + 1, :] for j in range(K)]

    def tile(r):
        block = ext_ref[pl.ds(r, RT + 8), :]
        marks = marks_ref[pl.ds(r, RT + 8), :]
        total = taps[K - 1] * block[0:RT]
        for j in range(1, K):
            masked = block * marks[:, j - 1 : j]
            total = total + taps[K - 1 - j] * masked[j : RT + j]
        low_ref[pl.ds(r, RT), :] = total.astype(bf16)

    row_tiles(T, tile)
    gin_ref[...] = lax.dot_general(
        low_ref[...], normed_ref[...], TN, preferred_element_type=f32
    ).astype(bf16)
    part = lax.dot_general(low_ref[...], wi_ref[...], NT, preferred_element_type=f32)

    @pl.when(i == 0)
    def _():
        sum_ref[...] = gn_ref[...] + part

    @pl.when(i > 0)
    def _():
        sum_ref[...] += part

    @pl.when(i == pl.num_programs(0) - 1)
    def _():
        gain = gain_ref[...].reshape(1, D)

        def last(k, total):
            rows = pl.ds(pl.multiple_of(k * 16, 16), 16)
            x = tok_ref[rows, :].astype(f32)
            grad = sum_ref[rows, :]
            inv = lax.rsqrt(jnp.mean(x * x, axis=1, keepdims=True) + epsilon)
            scaled = grad * gain
            mean = jnp.mean(x * scaled, axis=1, keepdims=True)
            gtok_ref[rows, :] = (
                cot_ref[rows, :].astype(f32) + inv * scaled - x * (inv * inv * inv * mean)
            )
            return total + jnp.sum((grad * x * inv).reshape(2, 8, D), axis=0)

        total = lax.fori_loop(0, T // 16, last, jnp.zeros((8, D), f32))
        ggain_ref[...] = jnp.sum(total, axis=0, keepdims=True)


def tail(L, gc, after, par, marks, normed, in_weight, gn, tokens, cot, gain):
    T, E = gc.shape
    D = tokens.shape[1]
    blocks = E // EB
    return pl.pallas_call(
        functools.partial(tail_kernel, L),
        grid=(blocks,),
        in_specs=[
            cols(T), cols(8), lead(PAR, EB), whole(*marks.shape), whole(T, D), cols(D), whole(T, D),
            whole(T, D), whole(T, D), whole(D),
        ],
        out_specs=[tall(EB, D), whole(T, D), whole(1, D)],
        out_shape=[shape(bf16, E, D), shape(f32, T, D), shape(f32, 1, D)],
        scratch_shapes=[
            pltpu.VMEM((T + 8, EB), f32), pltpu.VMEM((T, EB), bf16), pltpu.VMEM((T, D), f32),
        ],
        compiler_params=params(),
        name="tail",
    )(gc, after, par, marks, normed, in_weight, gn, tokens, cot, gain)


class Sums:
    def __init__(self, chan_count, seq_count, kinds, shapes, skew=1):
        self.cc, self.sc = chan_count, seq_count
        self.kinds = kinds
        self.skew = skew
        self.size = 8 * seq_count
        self.bits = [1 << i for i in range(chan_count.bit_length() - 1)]
        self.z_bits = [2 << i for i in range(seq_count.bit_length() - 2)]
        self.pieces = [
            (a, r, dims[2]) for a, dims in enumerate(shapes) for r in range(0, dims[1], 2 * self.size)
        ]
        self.shapes = shapes

    def half(self, p):
        return self.kinds[self.pieces[p][0]] is not None

    def stages(self, p):
        bits = self.bits if p % 2 == 0 else self.bits[::-1]
        return (
            [("core", 1)] + [("chan", b) for b in bits] + [("z", b) for b in self.z_bits]
            + [("zgather", b) for b in self.z_bits[::-1]] + ([("move", 0)] if self.half(p) else [])
            + [("cgather", 1)]
        )

    def ticks(self):
        return max(len(self.stages(p)) + self.skew * (p // 2) for p in range(len(self.pieces))) + 1

    def outs(self):
        return [
            shape(bf16, *(dims[1:] if kind is None else (2,) + tuple(dims[1:])))
            for kind, dims in zip(self.kinds, self.shapes)
        ]

    def scratch(self):
        found = []
        for a, r, width in self.pieces:
            for k in range(len(self.bits) + 1):
                found.append(pltpu.VMEM((self.cc >> k, self.size, width), bf16))
            for k in range(len(self.z_bits)):
                found.append(pltpu.VMEM((self.size >> (k + 1), width), bf16))
            found.append(pltpu.VMEM((self.size, width), bf16))
        dims = (len(self.pieces), len(self.bits) + 2 * len(self.z_bits) + 3, max(2, self.cc // 2))
        return found + [pltpu.SemaphoreType.DMA(dims), pltpu.SemaphoreType.DMA(dims)]

    def bind(self, x_refs, o_refs, scratch):
        self.x, self.o = x_refs, o_refs
        each = len(self.bits) + len(self.z_bits) + 2
        self.held = [scratch[p * each : (p + 1) * each] for p in range(len(self.pieces))]
        self.send_sem, self.recv_sem = scratch[-2:]
        self.si, self.ci = lax.axis_index("seq"), lax.axis_index("chan")
        self.core = lax.rem(self.si, 2)

    def side(self, bit):
        return lax.rem(self.si // bit, 2)

    def across(self, bit):
        return (self.si + bit - 2 * bit * self.side(bit), self.ci)

    def barrier(self):
        barrier = pltpu.get_barrier_semaphore()
        others = [(self.si, lax.rem(self.ci + k, self.cc)) for k in range(1, self.cc)]
        others += [self.across(bit) for bit in [1] + self.z_bits]
        for other in others:
            pl.semaphore_signal(barrier, inc=1, device_id=other, device_id_type=pl.DeviceIdType.MESH)
        pl.semaphore_wait(barrier, len(others))

    def copy(self, p, s, slot, src, dst, device):
        return pltpu.make_async_remote_copy(
            src_ref=src, dst_ref=dst, send_sem=self.send_sem.at[p, s, slot],
            recv_sem=self.recv_sem.at[p, s, slot], device_id=device, device_id_type=pl.DeviceIdType.MESH,
        )

    def kept(self, p, s, keep):
        name, bit = self.stages(p)[s]
        if name == "core":
            a, start, width = self.pieces[p]
            side = self.core if keep else 1 - self.core
            return [self.x[a].at[:, pl.ds(pl.multiple_of(start + side * self.size, 16), self.size), :]]
        ref = self.held[p][s - 1]
        if name == "z":
            side = self.side(bit) if keep else 1 - self.side(bit)
            k = self.z_bits.index(bit)
            rows = self.size >> (k + 1)
            rows = pl.ds(pl.multiple_of(side * rows, 16), rows)
            return [ref.at[0, rows, :] if k == 0 else ref.at[rows, :]]
        mine = lax.rem(self.ci // bit, 2)
        side = mine if keep else 1 - mine
        left = sorted(b for n, b in self.stages(p)[s : 1 + len(self.bits)])
        low = 1 << left.index(bit)
        return [
            ref.at[pl.ds((i // low) * 2 * low + side * low + i % low, 1)]
            for i in range((1 << len(left)) // 2)
        ]

    def landing(self, p, s):
        dst = self.held[p][s]
        return [dst.at[pl.ds(i, 1)] for i in range(dst.shape[0])] if self.stages(p)[s][0] == "chan" else [dst]

    def gathered(self, p, done):
        start, rows = 0, self.size
        for bit in self.z_bits[:done]:
            rows //= 2
            start = start + self.side(bit) * rows
        if self.half(p):
            return self.held[p][-1].at[pl.ds(pl.multiple_of(start, 16), rows), :]
        start = start + self.pieces[p][1] + self.core * self.size
        return self.o[self.pieces[p][0]].at[pl.ds(pl.multiple_of(start, 16), rows), :]

    def places(self, p):
        a, first, width = self.pieces[p]
        rows = pl.ds(pl.multiple_of(first + self.core * self.size, 16), self.size)
        return [self.o[a].at[b, rows, :] for b in range(2)] if self.half(p) else [self.o[a].at[rows, :]]

    def move(self, p, s, v):
        goal = self.kinds[self.pieces[p][0]] + v // 2
        place = self.places(p)[v % 2]
        return goal, place, self.copy(p, s, v % 2, self.held[p][-1], place, (self.si, goal))

    def copies(self, p, s):
        name, bit = self.stages(p)[s]
        if name in ("core", "chan", "z"):
            device = (self.si, self.ci + bit - 2 * bit * lax.rem(self.ci // bit, 2))
            device = device if name == "chan" else self.across(bit)
            pairs = zip(self.kept(p, s, False), self.landing(p, s))
            return [self.copy(p, s, i, src, dst, device) for i, (src, dst) in enumerate(pairs)]
        places = self.places(p)
        if name == "zgather":
            places = [self.gathered(p, self.z_bits.index(bit) + 1)]
        return [self.copy(p, s, b, place, place, self.across(bit)) for b, place in enumerate(places)]

    def taking_part(self, p, s, work):
        if self.half(p) and self.stages(p)[s][0] == "cgather":
            base = self.kinds[self.pieces[p][0]]
            pl.when((self.ci >= base) & (self.ci < base + self.cc // 2))(work)
        else:
            work()

    def start(self, p, s):
        if self.stages(p)[s][0] == "move":
            for v in range(self.cc):
                @pl.when(self.ci == v)
                def _(v=v):
                    goal, place, copy = self.move(p, s, v)
                    if goal == v:
                        place[...] = self.held[p][-1][...]
                    else:
                        copy.start()
            return

        def work():
            for copy in self.copies(p, s):
                copy.start()

        self.taking_part(p, s, work)

    def finish(self, p, s):
        name, bit = self.stages(p)[s]
        if name == "move":
            for v in range(self.cc):
                goal, place, copy = self.move(p, s, v)
                if goal != v:
                    pl.when(self.ci == goal)(copy.wait_recv)
            return

        def work():
            for copy in self.copies(p, s):
                copy.wait_recv()

        self.taking_part(p, s, work)
        if name in ("core", "chan", "z"):
            last = s == len(self.bits) + len(self.z_bits)
            for src, dst in zip(self.kept(p, s, True), self.landing(p, s)):
                total = (dst[...].astype(f32) + src[...].astype(f32)).astype(bf16)
                if last:
                    dst = self.gathered(p, len(self.z_bits))
                dst[...] = total

    def tick(self, n):
        for p in range(len(self.pieces)):
            s = n - self.skew * (p // 2)
            if 1 <= s <= len(self.stages(p)):
                self.finish(p, s - 1)
            if 0 <= s < len(self.stages(p)):
                self.start(p, s)

    def drain(self):
        for p in range(len(self.pieces)):
            for s, (name, bit) in enumerate(self.stages(p)):
                if name == "move":
                    for v in range(self.cc):
                        goal, place, copy = self.move(p, s, v)
                        if goal != v:
                            pl.when(self.ci == v)(copy.wait_send)
                    continue

                def work(p=p, s=s):
                    for copy in self.copies(p, s):
                        copy.wait_send()

                self.taking_part(p, s, work)

    def hand_over(self, refs):
        for kind, src, dst in zip(self.kinds, self.o, refs):
            def work(src=src, dst=dst):
                dst[...] = src[...]

            if kind is None:
                work()
            else:
                pl.when((self.ci >= kind) & (self.ci < kind + self.cc // 2))(work)


def sum_kernel(sums, *refs):
    arrays = len(sums.kinds)
    sums.bind(refs[:arrays], refs[arrays : 2 * arrays], refs[2 * arrays :])
    sums.barrier()
    for n in range(sums.ticks()):
        sums.tick(n)
    sums.drain()


def sum_owned(arrays, kinds, chan_count, seq_count):
    sums = Sums(chan_count, seq_count, kinds, [v.shape for v in arrays])
    vmem = pl.BlockSpec(memory_space=pltpu.VMEM)
    return pl.pallas_call(
        functools.partial(sum_kernel, sums),
        in_specs=[vmem] * len(arrays),
        out_specs=[vmem] * len(arrays),
        out_shape=sums.outs(),
        scratch_shapes=sums.scratch(),
        compiler_params=params(collective_id=0, has_side_effects=True),
        name="sum_owned",
    )(*arrays)


def unpack_kernel(L, inner_ref, gate_ref, out_ref, d_ref, e_ref, gin_ref, gout_ref, *refs):
    first = lax.axis_index("chan") < lax.axis_size("chan") // 2

    @pl.when(first)
    def _():
        gin_ref[...] = inner_ref[...].astype(f32).T

    @pl.when(jnp.logical_not(first))
    def _():
        gin_ref[...] = gate_ref[...].astype(f32).T

    gout_ref[...] = out_ref[...].astype(f32)
    d, e = d_ref[...].astype(f32), e_ref[...].astype(f32)
    R, N, K = L.R, L.N, L.K
    wide = R + 2 * N
    conv_w, conv_b, proj, step_w, step_b, decay, skip, gain = refs
    width = d.shape[1]
    step_w[...] = d[0:R]
    decay[...] = d[R : R + N]
    step_b[...] = d[R + N].reshape(width)
    skip[...] = d[R + N + 1].reshape(width)
    proj[...] = e[0:wide]
    conv_w[...] = e[wide : wide + K]
    conv_b[...] = e[wide + K].reshape(width)
    gain[...] = e[wide + K + 1].reshape(width)


def unpack(L, sums):
    width = sums[3].shape[1]
    rows, D = sums[0].shape
    R, N, K = L.R, L.N, L.K
    return pl.pallas_call(
        functools.partial(unpack_kernel, L),
        out_shape=[
            shape(f32, D, rows), shape(f32, *sums[2].shape), shape(f32, K, width), shape(f32, width),
            shape(f32, R + 2 * N, width), shape(f32, R, width), shape(f32, width),
            shape(f32, N, width), shape(f32, width), shape(f32, width),
        ],
        compiler_params=params(),
        name="unpack",
    )(*sums)


def local(
    tokens, norm_gain, in_weight, conv_weight, conv_bias, proj_weight, step_weight,
    step_bias, decay_log, skip_gain, out_weight, cotangent, lengths,
):
    T, D = tokens.shape
    E = in_weight.shape[1] // 2
    L = Layout(step_weight.shape[0], decay_log.shape[0], conv_weight.shape[0])
    ci = lax.axis_index("chan")
    cc = lax.axis_size("chan")
    sc = lax.axis_size("seq")
    blocks, share = E // EB, E // cc

    parts = (conv_weight, conv_bias, proj_weight.T, step_weight, step_bias, decay_log, skip_gain)
    wts, par, halo = gather_params(L, cc, parts, tokens)

    def by_block(values):
        if share == EB:
            return values
        values = jnp.moveaxis(values, 0, 1).reshape(-1, blocks, EB)
        return jnp.moveaxis(values, 1, 0)

    wts, par = by_block(wts), by_block(par)
    marks, normed, inner, gate, gg, g, cs, act, proj, b_cols, c_cols = front(
        L, lengths, tokens, halo, norm_gain, in_weight, out_weight, cotangent, par, wts
    )
    spre, dtk, u, entering, arriving = pre_scan(L, cc, proj, par, wts, act, g, marks, b_cols, c_cols)
    held, grad_c, block_out, grad_out, grad_in_gate, gn = fwd_scan(
        L, dtk, u, b_cols, c_cols, g, par, entering, act, gate, gg, out_weight, cotangent, tokens,
        normed, in_weight,
    )

    piece = 16 * sc
    fold = 2 if 2 * share <= piece else 1

    def owned(values):
        values = values.reshape(cc, -1, values.shape[-1] // fold)
        return jnp.pad(values, ((0, 0), (0, -values.shape[1] % piece), (0, 0)))

    def unfolded(values):
        if values.ndim == 2:
            return values[: share * fold].reshape(share, D)
        return values[:, : share * fold].reshape(2 * share, D)

    def by_owner(values):
        if share != EB:
            values = jnp.moveaxis(values, 0, 1).reshape(values.shape[1], cc, share)
            values = jnp.moveaxis(values, 1, 0)
        return jnp.pad(values, ((0, 0), (0, -values.shape[1] % piece), (0, 0)))

    gap, chan_d, gproj, sum_out, sum_gate = bwd_scan(
        L, dtk, u, g, b_cols, c_cols, par, wts, arriving, held, spre, act, proj, grad_c,
        [owned(grad_out), owned(grad_in_gate)], [None, cc // 2], (cc, sc),
    )
    gc, chan_e = conv_back(L, gap, gproj, wts, act, cs, inner, marks)
    after = lax.ppermute(gc[0:8], "chan", [(k, k - 1) for k in range(1, cc)])
    grad_in_inner, grad_tokens, grad_gain = tail(
        L, gc, after, par, marks, normed, in_weight, gn, tokens, cotangent, norm_gain
    )
    row = L.R + 2 * L.N + L.K + 1
    gain_part = jnp.pad(grad_gain.reshape(cc, 1, D // cc), ((0, 0), (0, 0), (0, share - D // cc)))
    chan_e = lax.dynamic_update_slice(by_owner(chan_e), gain_part.astype(bf16), (0, row, 0))
    sum_inner, sum_d, sum_e = sum_owned(
        [owned(grad_in_inner), by_owner(chan_d), chan_e], [0, None, None], cc, sc
    )
    sums = [unfolded(v) for v in (sum_inner, sum_gate, sum_out)] + [sum_d, sum_e]
    g_in, g_out, conv_w, conv_b, proj_w, step_w, step_b, decay, skip, g_gain = unpack(L, sums)
    return (
        block_out, grad_tokens, g_gain[: D // cc], g_in, conv_w, conv_b, proj_w.T, step_w,
        step_b, decay, skip, g_out,
    )


def solution(mesh):
    tok, row, vec = P(("seq", "chan"), None), P(None, "chan"), P("chan")
    in_specs = (
        tok, P(), P(), row, vec, P("chan", None), row, vec, row, vec, P(), tok, P("seq", None),
    )
    out_specs = (
        tok, tok, vec, row, row, vec, P("chan", None), row, vec, row, vec, P("chan", None),
    )
    return jax.shard_map(local, mesh=mesh, in_specs=in_specs, out_specs=out_specs, check_vma=False)
```

```python
import functools
import math

import jax
import jax.numpy as jnp
from jax import lax
from jax.experimental import pallas as pl
from jax.experimental.pallas import tpu as pltpu
from jax.sharding import PartitionSpec as P

epsilon = 1e-05
LOG2E = math.log2(math.e)
CUT = 1e30
TC = 16
EB = 384
RT = 32
HALO = 16
PAR = 24
WTS = 128
f32 = jnp.float32
bf16 = jnp.bfloat16
NT = (((1,), (1,)), ((), ()))
TN = (((0,), (0,)), ((), ()))


def params(**more):
    return pltpu.CompilerParams(vmem_limit_bytes=60 * 1024 * 1024, **more)


def cols(rows, width=EB, shift=0):
    return pl.BlockSpec((rows, width), lambda i: (0, i + shift))


def tall(rows, width, shift=0):
    return pl.BlockSpec((rows, width), lambda i: (i + shift, 0))


def lead(rows, width, count=1):
    return pl.BlockSpec((count, rows, width), lambda i: (i, 0, 0))


def whole(*shape):
    return pl.BlockSpec(shape, lambda i: (0,) * len(shape))


def shape(dtype, *dims):
    return jax.ShapeDtypeStruct(dims, dtype)


def row_tiles(count, body):
    def step(i, unused):
        body(pl.multiple_of(i * RT, RT))
        return unused

    lax.fori_loop(0, count // RT, step, 0)


def same_step(states, rows):
    dims = (rows, TC * states)
    here = lax.rem(lax.broadcasted_iota(jnp.int32, dims, 0), TC) * states
    place = lax.broadcasted_iota(jnp.int32, dims, 1)
    return (place >= here) & (place < here + states)


class Layout:
    def __init__(self, R, N, K):
        self.R, self.N, self.K = R, N, K
        self.step = R + 2 * N
        self.decay = 0
        self.conv = self.decay + N
        self.conv_b = self.conv + K
        self.step_b = self.conv_b + 1
        self.skip = self.step_b + 1
        self.end = self.skip + 1


def gather_kernel(
    L, count, cw_ref, cb_ref, pw_ref, sw_ref, sb_ref, dl_ref, sk_ref, tok_ref,
    wts_ref, par_ref, halo_ref, send_sem, recv_sem, halo_sems,
):
    si, ci = lax.axis_index("seq"), lax.axis_index("chan")
    T = tok_ref.shape[0]
    width = par_ref.shape[2]
    barrier = pltpu.get_barrier_semaphore()
    for k in range(1, count):
        pl.semaphore_signal(
            barrier, inc=1, device_id=(si, lax.rem(ci + k, count)),
            device_id_type=pl.DeviceIdType.MESH,
        )
    own, weights = par_ref.at[ci], wts_ref.at[ci]
    weights[...] = jnp.concatenate(
        [pw_ref[...].astype(f32), sw_ref[...].astype(f32)], axis=0
    ).astype(bf16)
    own[...] = jnp.concatenate(
        [
            dl_ref[...], cw_ref[...], cb_ref[...].reshape(1, width), sb_ref[...].reshape(1, width),
            sk_ref[...].reshape(1, width), jnp.zeros((PAR - L.end, width), f32),
        ],
        axis=0,
    )
    pl.semaphore_wait(barrier, count - 1)

    def share(ref, j, k):
        return pltpu.make_async_remote_copy(
            src_ref=ref, dst_ref=ref, send_sem=send_sem.at[j, k], recv_sem=recv_sem.at[j, k],
            device_id=(si, lax.rem(ci + k, count)), device_id_type=pl.DeviceIdType.MESH,
        )

    edge = pltpu.make_async_remote_copy(
        src_ref=tok_ref.at[pl.ds(T - HALO, HALO)], dst_ref=halo_ref,
        send_sem=halo_sems.at[0], recv_sem=halo_sems.at[1],
        device_id=(si, lax.rem(ci + 1, count)), device_id_type=pl.DeviceIdType.MESH,
    )
    edge.start()
    for j, ref in enumerate((own, weights)):
        for k in range(1, count):
            share(ref, j, k).start()
    edge.wait()
    for j, ref in enumerate((own, weights)):
        for k in range(1, count):
            share(ref, j, k).wait()


def gather_params(L, count, parts, tokens):
    width = parts[0].shape[1]
    T, D = tokens.shape
    vmem = pl.BlockSpec(memory_space=pltpu.VMEM)
    return pl.pallas_call(
        functools.partial(gather_kernel, L, count),
        in_specs=[vmem] * 8,
        out_specs=[vmem] * 3,
        out_shape=[shape(bf16, count, WTS, width), shape(f32, count, PAR, width), shape(bf16, HALO, D)],
        scratch_shapes=[
            pltpu.SemaphoreType.DMA((2, count)),
            pltpu.SemaphoreType.DMA((2, count)),
            pltpu.SemaphoreType.DMA((2,)),
        ],
        compiler_params=params(collective_id=1, has_side_effects=True),
        name="gather_params",
    )(*parts, tokens)


def front_kernel(
    L, len_ref, tok_ref, halo_ref, gain_ref, wi_ref, wg_ref, wo_ref, cot_ref, par_ref, wts_ref,
    marks_ref, normed_ref, inner_ref, gate_ref, gg_ref, g_ref, cs_ref, act_ref, proj_ref,
    bch_ref, cch_ref, bd_ref, cd_ref, hn_ref, xs_ref, low_ref,
):
    T = tok_ref.shape[0]
    N, K = L.N, L.K
    i = pl.program_id(0)

    def norm(x):
        x = x.astype(f32)
        inv = lax.rsqrt(jnp.mean(x * x, axis=1, keepdims=True) + epsilon)
        return (x * inv * gain_ref[...].reshape(1, x.shape[1])).astype(bf16)

    @pl.when(i == 0)
    def _():
        first = lax.axis_index("chan") == 0
        halo = jnp.where(first, jnp.zeros(halo_ref.shape, f32), halo_ref[...].astype(f32))
        hn_ref[...] = norm(halo)

        def tile(r):
            normed_ref[pl.ds(r, RT), :] = norm(tok_ref[pl.ds(r, RT), :])

        row_tiles(T, tile)
        proj_ref[...] = jnp.zeros_like(proj_ref)
        dims = marks_ref.shape
        place = lax.broadcasted_iota(jnp.int32, dims, 0) + lax.axis_index("chan") * T
        lane = lax.broadcasted_iota(jnp.int32, dims, 1)
        reach = jnp.where(lane < K - 1, lane + 1, 1)
        inside = jnp.zeros(dims, f32)
        start = jnp.int32(0)
        for k in range(len_ref.shape[1]):
            inside = jnp.where((start > place - reach) & (start <= place), 1.0, inside)
            start = start + len_ref[0, k]
        marks_ref[...] = jnp.where(lane < K - 1, 1.0 - inside, inside * CUT)

    low = jnp.dot(hn_ref[...], wi_ref[...], preferred_element_type=f32).astype(bf16)
    inner_ref[0:HALO, :] = low
    xs_ref[0:HALO, :] = low.astype(f32)
    low = jnp.dot(normed_ref[...], wi_ref[...], preferred_element_type=f32).astype(bf16)
    inner_ref[HALO:, :] = low
    xs_ref[HALO:, :] = low.astype(f32)
    gate_ref[...] = jnp.dot(normed_ref[...], wg_ref[...], preferred_element_type=f32)
    gg_ref[...] = lax.dot_general(cot_ref[...], wo_ref[...], NT, preferred_element_type=f32)

    for k in range(par_ref.shape[0]):
        c = slice(k * EB, (k + 1) * EB)
        taps = [par_ref[k, L.conv + j : L.conv + j + 1, :] for j in range(K)]
        bias = par_ref[k, L.conv_b : L.conv_b + 1, :]

        def tile(r, c=c, taps=taps, bias=bias):
            rows = pl.ds(r, RT)
            block = xs_ref[pl.ds(pl.multiple_of(r + HALO - 8, 8), RT + 8), c]
            total = bias + taps[K - 1] * block[8:]
            for j in range(1, K):
                usable = marks_ref[rows, j - 1 : j]
                total = total + taps[K - 1 - j] * (block[8 - j : RT + 8 - j] * usable)
            act = total * jax.nn.sigmoid(total)
            cs_ref[rows, c] = total
            act_ref[rows, c] = act
            low_ref[rows, c] = act.astype(bf16)
            gate = gate_ref[rows, c]
            passed = gg_ref[rows, c] * (gate * jax.nn.sigmoid(gate))
            g_ref[rows, c] = passed.astype(bf16).astype(f32)

        row_tiles(T, tile)
        proj_ref[...] += lax.dot_general(low_ref[:, c], wts_ref[k], NT, preferred_element_type=f32)

    @pl.when(i == pl.num_programs(0) - 1)
    def _():
        turned = proj_ref[...].T
        for ref, start in ((bch_ref, L.R), (cch_ref, L.R + N)):
            for j in range(T // TC):
                ref[j] = turned[start : start + N, j * TC : (j + 1) * TC]
        dims = (128, TC * N)
        source = lax.broadcasted_iota(jnp.int32, dims, 0)
        state = lax.rem(lax.broadcasted_iota(jnp.int32, dims, 1), N)
        diag = same_step(N, T)
        small = proj_ref[...].astype(bf16)
        for ref, start in ((bd_ref, L.R), (cd_ref, L.R + N)):
            spread = (source == state + start).astype(f32).astype(bf16)
            wide = jnp.dot(small, spread, preferred_element_type=f32)
            ref[...] = jnp.where(diag, wide, 0.0).astype(bf16)


def front(L, lengths, tokens, halo, gain, in_weight, out_weight, cot, par, wts):
    T, D = tokens.shape
    E = out_weight.shape[0]
    sub = 2
    wide = EB * sub
    steps = E // wide
    N = L.N
    arrays = [shape(f32, T, E)] * 5
    return pl.pallas_call(
        functools.partial(front_kernel, L),
        grid=(steps,),
        in_specs=[
            pl.BlockSpec(memory_space=pltpu.SMEM),
            whole(T, D), whole(HALO, D), whole(D), cols(D, wide), cols(D, wide, steps),
            tall(wide, D), whole(T, D), lead(PAR, EB, sub), lead(WTS, EB, sub),
        ],
        out_specs=[whole(T + 8, 8), whole(T, D), cols(T + HALO, wide)] + [cols(T, wide)] * 5 + [
            whole(T, 128), whole(T // TC, N, TC), whole(T // TC, N, TC),
            whole(T, TC * N), whole(T, TC * N),
        ],
        out_shape=[shape(f32, T + 8, 8), shape(bf16, T, D), shape(bf16, T + HALO, E)] + arrays + [
            shape(f32, T, 128), shape(f32, T // TC, N, TC), shape(f32, T // TC, N, TC),
            shape(bf16, T, TC * N), shape(bf16, T, TC * N),
        ],
        scratch_shapes=[
            pltpu.VMEM((HALO, D), bf16),
            pltpu.VMEM((T + HALO, wide), f32),
            pltpu.VMEM((T, wide), bf16),
        ],
        compiler_params=params(),
        name="front",
    )(lengths, tokens, halo, gain, in_weight, in_weight, out_weight, cot, par, wts)


def rates(L, par_ref):
    return -jnp.exp(par_ref[0, L.decay : L.decay + L.N, :]) * LOG2E


def softplus(x):
    return jnp.maximum(x, 0.0) + jnp.log1p(jnp.exp(-jnp.abs(x)))


def pre_kernel(
    L, count, proj_ref, par_ref, wts_ref, act_ref, g_ref, marks_ref, b_ref, c_ref,
    spre_ref, step_ref, u_ref, a_ref, enter_ref, arrive_ref, dtk_ref, ahead_ref, behind_ref, got_ref,
    send_sem, recv_sem,
):
    T, E = act_ref.shape[0], enter_ref.shape[1]
    N = L.N
    i = pl.program_id(0)
    blocks = E // EB
    si, ci = lax.axis_index("seq"), lax.axis_index("chan")

    @pl.when(i == 0)
    def _():
        barrier = pltpu.get_barrier_semaphore()
        for k in range(1, count):
            pl.semaphore_signal(
                barrier, inc=1, device_id=(si, lax.rem(ci + k, count)),
                device_id_type=pl.DeviceIdType.MESH,
            )
        pl.semaphore_wait(barrier, count - 1)

    low = proj_ref[:, 0 : L.R].astype(bf16)
    weights = wts_ref[0, L.step : L.step + L.R, :]
    bias = par_ref[0, L.step_b : L.step_b + 1, :]
    spre_ref[...] = jnp.dot(low, weights, preferred_element_type=f32) + bias

    def tile(r):
        rows = pl.ds(r, RT)
        step = softplus(spre_ref[rows, :])
        u_ref[rows, :] = step * act_ref[rows, :]
        step_ref[rows, :] = step
        dtk_ref[rows, :] = step + marks_ref[rows, 3:4]

    row_tiles(T, tile)
    rate = rates(L, par_ref)

    def chunk(c, carry):
        h, through, head = carry
        base = pl.multiple_of(c * TC, TC)
        b_cols, c_cols = b_ref[c], c_ref[c]
        for j in range(TC):
            d = dtk_ref[pl.ds(base + j, 1), :]
            u = u_ref[pl.ds(base + j, 1), :]
            g = g_ref[pl.ds(base + j, 1), :]
            factor = jnp.exp2(d * rate)
            a_ref[pl.ds(pl.multiple_of((base + j) * N, N), N), :] = factor
            h = factor * h + b_cols[:, j : j + 1] * u
            through = factor * through
            head = head + through * (c_cols[:, j : j + 1] * g)
        return h, through, head

    zero = jnp.zeros(rate.shape, f32)
    h, through, head = lax.fori_loop(0, T // TC, chunk, (zero, zero + 1.0, zero))
    ahead_ref[i, 0:N, :] = h
    ahead_ref[i, N:, :] = through
    behind_ref[i, 0:N, :] = head
    behind_ref[i, N:, :] = through

    def send(b, k, forward):
        return pltpu.make_async_remote_copy(
            src_ref=(ahead_ref if forward else behind_ref).at[b], dst_ref=got_ref.at[count - k, b],
            send_sem=send_sem.at[k, b], recv_sem=recv_sem.at[count - k, b],
            device_id=(si, lax.rem(ci + k, count)), device_id_type=pl.DeviceIdType.MESH,
        )

    for k in range(1, count):
        @pl.when(ci + k < count)
        def _(k=k):
            send(i, k, True).start()

        @pl.when(ci + k >= count)
        def _(k=k):
            send(i, k, False).start()

    @pl.when(i == blocks - 1)
    def _():
        for b in range(blocks):
            for k in range(1, count):
                send(b, k, True).wait()
        for b in range(blocks):
            span = slice(b * EB, (b + 1) * EB)
            entering, arriving = zero, zero
            for k in range(1, count):
                before = ci + k >= count
                got = got_ref[k, b]
                entering = jnp.where(before, got[0:N] + got[N:] * entering, entering)
            for k in range(count - 1, 0, -1):
                behind = ci + k < count
                got = got_ref[k, b]
                arriving = jnp.where(behind, got[0:N] + got[N:] * arriving, arriving)
            enter_ref[:, span] = entering
            arrive_ref[:, span] = arriving


def pre_scan(L, count, proj, par, wts, act, g, marks, b_cols, c_cols):
    T, E = act.shape
    N = L.N
    blocks = E // EB
    state = shape(f32, N, E)
    return pl.pallas_call(
        functools.partial(pre_kernel, L, count),
        grid=(blocks,),
        in_specs=[
            whole(T, 128), lead(PAR, EB), lead(WTS, EB), cols(T), cols(T), whole(*marks.shape),
            whole(*b_cols.shape), whole(*c_cols.shape),
        ],
        out_specs=[cols(T)] * 3 + [cols(T * N)] + [whole(N, E)] * 2,
        out_shape=[shape(f32, T, E)] * 3 + [shape(f32, T * N, E)] + [state] * 2,
        scratch_shapes=[
            pltpu.VMEM((T, EB), f32),
            pltpu.VMEM((blocks, 2 * N, EB), f32),
            pltpu.VMEM((blocks, 2 * N, EB), f32),
            pltpu.VMEM((count, blocks, 2 * N, EB), f32),
            pltpu.SemaphoreType.DMA((count, blocks)),
            pltpu.SemaphoreType.DMA((count, blocks)),
        ],
        compiler_params=params(collective_id=2, has_side_effects=True),
        name="pre_scan",
    )(proj, par, wts, act, g, marks, b_cols, c_cols)


def halves(values):
    return values[0:8] + values[8:16]


def fwd_kernel(
    L, a_ref, u_ref, b_ref, cd_ref, g_ref, par_ref, hin_ref, act_ref, gate_ref, gg_ref,
    wo_ref, cot_ref, tok_ref, normed_ref, wg_ref,
    h_ref, gc_ref, block_ref, gout_ref, gin_ref, gn_ref, y_ref, gated_ref, ggate_ref, branch_ref,
):
    chunks, states = b_ref.shape[0], b_ref.shape[1]
    T = chunks * TC
    width = TC * states
    i = pl.program_id(0)

    @pl.when(i == 0)
    def _():
        gc_ref[...] = jnp.zeros_like(gc_ref)
        gn_ref[...] = jnp.zeros_like(gn_ref)
        branch_ref[...] = jnp.zeros_like(branch_ref)

    h_ref[0:states, :] = hin_ref[...].astype(bf16)

    def contract(c):
        rows = pl.ds(pl.multiple_of(c * TC, TC), TC)
        held = h_ref[pl.ds(pl.multiple_of(c * width, width) + states, width), :]
        y_ref[rows, :] = jnp.dot(cd_ref[rows, :], held, preferred_element_type=f32)
        g_low = g_ref[rows, :].astype(bf16)
        gc_ref[rows, :] += lax.dot_general(g_low, held, NT, preferred_element_type=f32)

    def advance(c, h):
        base = pl.multiple_of(c * TC, TC)
        row = pl.multiple_of(c * width, width)
        b_cols = b_ref[c]
        for j in range(TC):
            u = u_ref[pl.ds(base + j, 1), :]
            h = a_ref[pl.ds(row + j * states, states), :] * h + b_cols[:, j : j + 1] * u
            h_ref[pl.ds(row + (j + 1) * states, states), :] = h.astype(bf16)
        return h

    def chunk(c, h):
        contract(c - 1)
        return advance(c, h)

    lax.fori_loop(1, chunks, chunk, advance(0, hin_ref[...]))
    contract(chunks - 1)
    skip = par_ref[0, L.skip : L.skip + 1, :]

    def tile(r):
        rows = pl.ds(r, RT)
        mixer = (y_ref[rows, :] + skip * act_ref[rows, :]).astype(bf16).astype(f32)
        gate = gate_ref[rows, :]
        sig = jax.nn.sigmoid(gate)
        gated_ref[rows, :] = (mixer * (gate * sig)).astype(bf16)
        ggate_ref[rows, :] = (gg_ref[rows, :] * mixer * sig * (1.0 + gate * (1.0 - sig))).astype(bf16)

    row_tiles(T, tile)
    branch_ref[...] += jnp.dot(gated_ref[...], wo_ref[...], preferred_element_type=f32)
    gout_ref[...] = lax.dot_general(
        gated_ref[...], cot_ref[...], TN, preferred_element_type=f32
    ).astype(bf16)
    gin_ref[...] = lax.dot_general(
        ggate_ref[...], normed_ref[...], TN, preferred_element_type=f32
    ).astype(bf16)
    gn_ref[...] += lax.dot_general(ggate_ref[...], wg_ref[...], NT, preferred_element_type=f32)

    @pl.when(i == pl.num_programs(0) - 1)
    def _():
        block_ref[...] = (tok_ref[...].astype(f32) + branch_ref[...]).astype(bf16)


def fwd_scan(L, factors, u, b_cols, c_diag, g, par, entering, act, gate, gg, out_weight, cot, tokens, normed, in_weight):
    T, E = u.shape
    D = tokens.shape[1]
    N = L.N
    rows = (T + 1) * N
    blocks = E // EB
    return pl.pallas_call(
        functools.partial(fwd_kernel, L),
        grid=(blocks,),
        in_specs=[
            cols(T * N), cols(T), whole(*b_cols.shape), whole(T, TC * N), cols(T), lead(PAR, EB), cols(N),
            cols(T), cols(T), cols(T), tall(EB, D), whole(T, D), whole(T, D), whole(T, D),
            cols(D, EB, blocks),
        ],
        out_specs=[
            cols(rows), whole(T, TC * N), whole(T, D), tall(EB, D), tall(EB, D, blocks), whole(T, D),
        ],
        out_shape=[
            shape(bf16, rows, E), shape(f32, T, TC * N), shape(bf16, T, D), shape(bf16, E, D),
            shape(bf16, 2 * E, D), shape(f32, T, D),
        ],
        scratch_shapes=[
            pltpu.VMEM((T, EB), f32), pltpu.VMEM((T, EB), bf16), pltpu.VMEM((T, EB), bf16),
            pltpu.VMEM((T, D), f32),
        ],
        compiler_params=params(),
        name="fwd_scan",
    )(factors, u, b_cols, c_diag, g, par, entering, act, gate, gg, out_weight, cot, tokens, normed, in_weight)


def bwd_kernel(
    L, a_ref, step_ref, u_ref, g_ref, bd_ref, c_ref, par_ref, wts_ref, fin_ref, h_ref, spre_ref, act_ref, proj_ref,
    gc_ref, gap_ref, chan_ref, gproj_ref, adj_ref, wr_ref, bsum_ref, wsum_ref, gb_ref, rank_ref, pre_ref,
):
    rate = -jnp.exp(par_ref[0, L.decay : L.decay + L.N, :])
    chunks, states = c_ref.shape[0], c_ref.shape[1]
    T = chunks * TC
    width = TC * states
    i = pl.program_id(0)
    ones = same_step(states, TC).astype(f32).astype(bf16)

    @pl.when(i == 0)
    def _():
        gb_ref[...] = jnp.zeros_like(gb_ref)
        rank_ref[...] = jnp.zeros_like(rank_ref)

    def slot(c):
        return pl.multiple_of(lax.rem(c, 2) * width, width)

    def contract(c):
        rows = pl.ds(pl.multiple_of(c * TC, TC), TC)
        span = pl.ds(slot(c), width)
        held = adj_ref[span, :]
        bsum_ref[rows, :] = jnp.dot(bd_ref[rows, :], held, preferred_element_type=f32)
        wsum_ref[rows, :] = jnp.dot(ones, wr_ref[span, :], preferred_element_type=f32)
        u_low = u_ref[rows, :].astype(bf16)
        gb_ref[rows, :] += lax.dot_general(u_low, held, NT, preferred_element_type=f32)

    def retreat(c, carry):
        flow, acc = carry
        base = pl.multiple_of(c * TC, TC)
        row = pl.multiple_of(c * width, width)
        place = slot(c)
        c_cols = c_ref[c]
        for j in reversed(range(TC)):
            d = step_ref[pl.ds(base + j, 1), :]
            g = g_ref[pl.ds(base + j, 1), :]
            at = pl.ds(row + j * states, states)
            adj = c_cols[:, j : j + 1] * g + flow
            flow = a_ref[at, :] * adj
            wr = flow * h_ref[at, :].astype(f32) * rate
            acc = acc + wr * d
            adj_ref[pl.ds(place + j * states, states), :] = adj.astype(bf16)
            wr_ref[pl.ds(place + j * states, states), :] = wr.astype(bf16)
        return flow, acc

    def chunk(k, carry):
        c = chunks - 1 - k
        contract(c + 1)
        return retreat(c, carry)

    carry = retreat(chunks - 1, (fin_ref[...], jnp.zeros(rate.shape, f32)))
    unused, acc = lax.fori_loop(1, chunks, chunk, carry)
    contract(0)
    skip = par_ref[0, L.skip : L.skip + 1, :]

    def tile(k, carry):
        bias_sum, skip_sum = carry
        rows = pl.ds(pl.multiple_of(k * 16, 16), 16)
        spre, act, g, bsum = spre_ref[rows, :], act_ref[rows, :], g_ref[rows, :], bsum_ref[rows, :]
        grad = (wsum_ref[rows, :] + act * bsum) * jax.nn.sigmoid(spre)
        gap_ref[rows, :] = g * skip + step_ref[rows, :] * bsum
        pre_ref[rows, :] = grad.astype(bf16)
        bias_sum = bias_sum + halves(grad)
        skip_sum = skip_sum + halves(g * act)
        return bias_sum, skip_sum

    none = jnp.zeros((8, EB), f32)
    bias_sum, skip_sum = lax.fori_loop(0, T // 16, tile, (none, none))
    R = L.R
    pre = pre_ref[...]
    step_low = proj_ref[...].astype(bf16)
    grad_step_w = lax.dot_general(step_low, pre, TN, preferred_element_type=f32)
    chan_ref[0] = jnp.concatenate(
        [
            grad_step_w[0:R],
            acc,
            jnp.sum(bias_sum, axis=0, keepdims=True),
            jnp.sum(skip_sum, axis=0, keepdims=True),
            jnp.zeros((128 - R - states - 2, EB), f32),
        ],
        axis=0,
    ).astype(bf16)
    weights = wts_ref[0, L.step : L.step + R, :].astype(f32)
    weights = jnp.concatenate([weights, jnp.zeros((128 - R, EB), f32)], axis=0).astype(bf16)
    rank_ref[...] += lax.dot_general(pre, weights, NT, preferred_element_type=f32)

    @pl.when(i == pl.num_programs(0) - 1)
    def _():
        dims = (width, 128)
        state = lax.rem(lax.broadcasted_iota(jnp.int32, dims, 0), states)
        target = lax.broadcasted_iota(jnp.int32, dims, 1)
        diag = same_step(states, T)
        total = rank_ref[...]
        for ref, start in ((gb_ref, R), (gc_ref, R + states)):
            fold = (target == state + start).astype(f32)
            kept = jnp.where(diag, ref[...], 0.0)
            total = total + jnp.dot(
                kept, fold, precision=lax.Precision.HIGHEST, preferred_element_type=f32
            )
        gproj_ref[...] = total.astype(bf16)


def bwd_scan(L, factors, step, u, g, b_diag, c_cols, par, wts, arriving, held, spre, act, proj, grad_c):
    T, E = u.shape
    N = L.N
    blocks = E // EB
    return pl.pallas_call(
        functools.partial(bwd_kernel, L),
        grid=(blocks,),
        in_specs=[
            cols(T * N), cols(T), cols(T), cols(T), whole(T, TC * N), whole(*c_cols.shape), lead(PAR, EB),
            lead(WTS, EB), cols(N), cols(held.shape[0]), cols(T), cols(T), whole(T, 128), whole(T, TC * N),
        ],
        out_specs=[cols(T), lead(128, EB), whole(T, 128)],
        out_shape=[shape(f32, T, E), shape(bf16, blocks, 128, EB), shape(bf16, T, 128)],
        scratch_shapes=[
            pltpu.VMEM((2 * TC * N, EB), bf16), pltpu.VMEM((2 * TC * N, EB), bf16),
            pltpu.VMEM((T, EB), f32), pltpu.VMEM((T, EB), f32),
            pltpu.VMEM((T, TC * N), f32), pltpu.VMEM((T, 128), f32), pltpu.VMEM((T, EB), bf16),
        ],
        compiler_params=params(),
        name="bwd_scan",
    )(factors, step, u, g, b_diag, c_cols, par, wts, arriving, held, spre, act, proj, grad_c)


def conv_kernel(L, gap_ref, gproj_ref, wts_ref, act_ref, cs_ref, inner_ref, marks_ref, gc_ref, chan_ref, xs_ref):
    T = gap_ref.shape[0]
    K, wide = L.K, L.R + 2 * L.N
    weights = wts_ref[0].astype(f32)
    row = lax.broadcasted_iota(jnp.int32, weights.shape, 0)
    weights = jnp.where(row < wide, weights, 0.0).astype(bf16)
    gc_ref[...] = jnp.dot(gproj_ref[...], weights, preferred_element_type=f32)
    act_low = act_ref[...].astype(bf16)
    grad_proj = lax.dot_general(gproj_ref[...], act_low, TN, preferred_element_type=f32)
    xs_ref[...] = inner_ref[...].astype(f32)

    def tile(k, carry):
        r = pl.multiple_of(k * RT, RT)
        rows = pl.ds(r, RT)
        total = cs_ref[rows, :]
        sig = jax.nn.sigmoid(total)
        grad = (gc_ref[rows, :] + gap_ref[rows, :]) * sig * (1.0 + total * (1.0 - sig))
        gc_ref[rows, :] = grad
        block = xs_ref[pl.ds(pl.multiple_of(r + HALO - 8, 8), RT + 8), :]
        out = [carry[K] + jnp.sum(grad.reshape(RT // 8, 8, EB), axis=0)]
        for j in range(K):
            part = grad * block[8 - j : RT + 8 - j]
            if j > 0:
                part = part * marks_ref[rows, j - 1 : j]
            out.insert(0, carry[K - 1 - j] + jnp.sum(part.reshape(RT // 8, 8, EB), axis=0))
        return tuple(out)

    none = jnp.zeros((8, EB), f32)
    sums = lax.fori_loop(0, T // RT, tile, (none,) * (K + 1))
    chan_ref[0] = jnp.concatenate(
        [grad_proj[0:wide]]
        + [jnp.sum(s, axis=0, keepdims=True) for s in sums]
        + [jnp.zeros((128 - wide - K - 1, EB), f32)],
        axis=0,
    ).astype(bf16)


def conv_back(L, gap, gproj, wts, act, cs, inner, marks):
    T, E = gap.shape
    blocks = E // EB
    return pl.pallas_call(
        functools.partial(conv_kernel, L),
        grid=(blocks,),
        in_specs=[
            cols(T), whole(T, 128), lead(WTS, EB), cols(T), cols(T), cols(T + HALO), whole(*marks.shape),
        ],
        out_specs=[cols(T), lead(128, EB)],
        out_shape=[shape(f32, T, E), shape(bf16, blocks, 128, EB)],
        scratch_shapes=[pltpu.VMEM((T + HALO, EB), f32)],
        compiler_params=params(),
        name="conv_back",
    )(gap, gproj, wts, act, cs, inner, marks)


def tail_kernel(
    L, gc_ref, after_ref, par_ref, marks_ref, normed_ref, wi_ref, gn_ref, tok_ref, cot_ref, gain_ref,
    held_ref, gin_ref, gtok_ref, ggain_ref, ext_ref, low_ref, sum_ref,
):
    T, D = tok_ref.shape
    K = L.K
    i = pl.program_id(0)
    ext_ref[0:T, :] = gc_ref[...]
    ext_ref[T : T + 8, :] = after_ref[...]
    taps = [par_ref[0, L.conv + j : L.conv + j + 1, :] for j in range(K)]

    def tile(r):
        block = ext_ref[pl.ds(r, RT + 8), :]
        marks = marks_ref[pl.ds(r, RT + 8), :]
        total = taps[K - 1] * block[0:RT]
        for j in range(1, K):
            masked = block * marks[:, j - 1 : j]
            total = total + taps[K - 1 - j] * masked[j : RT + j]
        low_ref[pl.ds(r, RT), :] = total.astype(bf16)

    row_tiles(T, tile)
    gin_ref[...] = lax.dot_general(
        low_ref[...], normed_ref[...], TN, preferred_element_type=f32
    ).astype(bf16)
    part = lax.dot_general(low_ref[...], wi_ref[...], NT, preferred_element_type=f32)

    @pl.when(i == 0)
    def _():
        sum_ref[...] = gn_ref[...] + part

    @pl.when(i > 0)
    def _():
        sum_ref[...] += part

    @pl.when(i == pl.num_programs(0) - 1)
    def _():
        gain = gain_ref[...].reshape(1, D)

        def last(k, total):
            rows = pl.ds(pl.multiple_of(k * 16, 16), 16)
            x = tok_ref[rows, :].astype(f32)
            grad = sum_ref[rows, :]
            inv = lax.rsqrt(jnp.mean(x * x, axis=1, keepdims=True) + epsilon)
            scaled = grad * gain
            mean = jnp.mean(x * scaled, axis=1, keepdims=True)
            gtok_ref[rows, :] = (
                cot_ref[rows, :].astype(f32) + inv * scaled - x * (inv * inv * inv * mean)
            )
            return total + jnp.sum((grad * x * inv).reshape(2, 8, D), axis=0)

        total = lax.fori_loop(0, T // 16, last, jnp.zeros((8, D), f32))
        ggain_ref[...] = jnp.sum(total, axis=0, keepdims=True)


def tail(L, gc, after, par, marks, normed, in_weight, gn, tokens, cot, gain, held):
    T, E = gc.shape
    D = tokens.shape[1]
    blocks = E // EB
    return pl.pallas_call(
        functools.partial(tail_kernel, L),
        grid=(blocks,),
        in_specs=[
            cols(T), cols(8), lead(PAR, EB), whole(*marks.shape), whole(T, D), cols(D), whole(T, D),
            whole(T, D), whole(T, D), whole(D), pl.BlockSpec(memory_space=pl.ANY),
        ],
        out_specs=[tall(EB, D), whole(T, D), whole(1, D)],
        out_shape=[shape(bf16, 2 * E, D), shape(f32, T, D), shape(f32, 1, D)],
        scratch_shapes=[
            pltpu.VMEM((T + 8, EB), f32), pltpu.VMEM((T, EB), bf16), pltpu.VMEM((T, D), f32),
        ],
        input_output_aliases={10: 0},
        compiler_params=params(),
        name="tail",
    )(gc, after, par, marks, normed, in_weight, gn, tokens, cot, gain, held)


def sum_plan(chan_count, seq_count):
    chan_bits = [("chan", 1 << i) for i in range(chan_count.bit_length() - 1)]
    seq_bits = [("seq", 1 << i) for i in range(seq_count.bit_length() - 1)]
    return chan_bits, seq_bits


def sum_kernel(chan_count, seq_count, pieces, arrays, *refs):
    piece_rows = 16 * seq_count
    x_refs, o_refs = refs[:arrays], refs[arrays : 2 * arrays]
    chan_bits, seq_bits = sum_plan(chan_count, seq_count)
    nc, ns = len(chan_bits), len(seq_bits)
    stages = nc + ns
    count = len(pieces)
    scratch = refs[2 * arrays :]
    held = [scratch[p * stages : (p + 1) * stages] for p in range(count)]
    send_sem, recv_sem = scratch[count * stages :]
    mine = {"seq": lax.axis_index("seq"), "chan": lax.axis_index("chan")}

    def bit_of(name, bit):
        return (mine[name] // bit) % 2

    def partner(name, bit):
        other = dict(mine)
        other[name] = mine[name] + bit - 2 * bit * bit_of(name, bit)
        return (other["seq"], other["chan"])

    def order(p):
        inner = chan_bits if p % 2 == 0 else chan_bits[::-1]
        return seq_bits[:1] + inner + seq_bits[1:]

    barrier = pltpu.get_barrier_semaphore()
    for name, bit in chan_bits + seq_bits:
        pl.semaphore_signal(
            barrier, inc=1, device_id=partner(name, bit), device_id_type=pl.DeviceIdType.MESH
        )
    pl.semaphore_wait(barrier, stages)

    def parts(p, s, keep):
        name, bit = order(p)[s]
        side = bit_of(name, bit) if keep else 1 - bit_of(name, bit)
        done = order(p)[:s]
        size = piece_rows >> sum(1 for n, b in done if n == "seq")
        ref, start = (x_refs[pieces[p][0]], pieces[p][1]) if s == 0 else (held[p][s - 1], 0)
        if name == "seq":
            rows = pl.ds(pl.multiple_of(start + side * (size // 2), 16), size // 2)
            return [ref.at[:, rows, :]]
        left = [b for n, b in chan_bits if ("chan", b) not in done]
        low = 1 << left.index(bit)
        return [
            ref.at[pl.ds((i // low) * 2 * low + side * low + i % low, 1), pl.ds(start, size), :]
            for i in range((1 << len(left)) // 2)
        ]

    def landing(p, s):
        dst = held[p][s]
        if order(p)[s][0] == "seq":
            return [dst]
        return [dst.at[pl.ds(i, 1)] for i in range(dst.shape[0])]

    def copies(p, s):
        return [
            pltpu.make_async_remote_copy(
                src_ref=src, dst_ref=dst, send_sem=send_sem.at[p, s, i], recv_sem=recv_sem.at[p, s, i],
                device_id=partner(*order(p)[s]), device_id_type=pl.DeviceIdType.MESH,
            )
            for i, (src, dst) in enumerate(zip(parts(p, s, False), landing(p, s)))
        ]

    def my_rows(p, done):
        start, size = pieces[p][1], piece_rows
        for name, bit in seq_bits[:done]:
            size //= 2
            start = start + bit_of(name, bit) * size
        return pl.ds(pl.multiple_of(start, 16), size)

    def gather_copy(p, k):
        place = o_refs[pieces[p][0]].at[my_rows(p, ns - k), :]
        return pltpu.make_async_remote_copy(
            src_ref=place, dst_ref=place,
            send_sem=send_sem.at[p, stages + k, 0], recv_sem=recv_sem.at[p, stages + k, 0],
            device_id=partner(*seq_bits[ns - 1 - k]), device_id_type=pl.DeviceIdType.MESH,
        )

    total = stages + ns
    for tick in range((count + 1) // 2 + total):
        for p in range(count):
            s = tick - p // 2
            if not 0 <= s <= total:
                continue
            if 1 <= s <= stages:
                for copy in copies(p, s - 1):
                    copy.wait_recv()
                for src, dst in zip(parts(p, s - 1, True), landing(p, s - 1)):
                    dst[...] = (dst[...].astype(f32) + src[...].astype(f32)).astype(bf16)
                if s == stages:
                    o_refs[pieces[p][0]][my_rows(p, ns), :] = held[p][stages - 1][0]
            elif s > stages:
                gather_copy(p, s - 1 - stages).wait_recv()
            if s < stages:
                for copy in copies(p, s):
                    copy.start()
            elif s < total:
                gather_copy(p, s - stages).start()
    for p in range(count):
        for s in range(stages):
            for copy in copies(p, s):
                copy.wait_send()
        for k in range(ns):
            gather_copy(p, k).wait_send()


def sum_owned(arrays, seq_count):
    chan_count = arrays[0].shape[0]
    chan_bits, seq_bits = sum_plan(chan_count, seq_count)
    piece_rows = 16 * seq_count
    pieces = [(a, r) for a, v in enumerate(arrays) for r in range(0, v.shape[1], piece_rows)]
    ordered = seq_bits[:1] + chan_bits + seq_bits[1:]
    scratch = []
    for a, r in pieces:
        owners, size = chan_count, piece_rows
        for name, bit in ordered:
            if name == "chan":
                owners //= 2
            else:
                size //= 2
            scratch.append(pltpu.VMEM((owners, size, arrays[a].shape[2]), bf16))
    total = len(ordered) + len(seq_bits)
    sems = pltpu.SemaphoreType.DMA((len(pieces), total, max(1, chan_count // 2)))
    vmem = pl.BlockSpec(memory_space=pltpu.VMEM)
    return pl.pallas_call(
        functools.partial(sum_kernel, chan_count, seq_count, pieces, len(arrays)),
        in_specs=[vmem] * len(arrays),
        out_specs=[vmem] * len(arrays),
        out_shape=[shape(bf16, *v.shape[1:]) for v in arrays],
        scratch_shapes=scratch + [sems, sems],
        compiler_params=params(collective_id=0, has_side_effects=True),
        name="sum_owned",
    )(*arrays)


def unpack_kernel(L, in_ref, out_ref, d_ref, e_ref, gin_ref, gout_ref, *refs):
    gin_ref[...] = in_ref[...].astype(f32).T
    gout_ref[...] = out_ref[...].astype(f32)
    d, e = d_ref[...].astype(f32), e_ref[...].astype(f32)
    R, N, K = L.R, L.N, L.K
    wide = R + 2 * N
    conv_w, conv_b, proj, step_w, step_b, decay, skip, gain = refs
    width = d.shape[1]
    step_w[...] = d[0:R]
    decay[...] = d[R : R + N]
    step_b[...] = d[R + N].reshape(width)
    skip[...] = d[R + N + 1].reshape(width)
    proj[...] = e[0:wide]
    conv_w[...] = e[wide : wide + K]
    conv_b[...] = e[wide + K].reshape(width)
    gain[...] = e[wide + K + 1].reshape(width)


def unpack(L, sums):
    width = sums[2].shape[1]
    rows, D = sums[0].shape
    R, N, K = L.R, L.N, L.K
    return pl.pallas_call(
        functools.partial(unpack_kernel, L),
        out_shape=[
            shape(f32, D, rows), shape(f32, *sums[1].shape), shape(f32, K, width), shape(f32, width),
            shape(f32, R + 2 * N, width), shape(f32, R, width), shape(f32, width),
            shape(f32, N, width), shape(f32, width), shape(f32, width),
        ],
        compiler_params=params(),
        name="unpack",
    )(*sums)


def local(
    tokens, norm_gain, in_weight, conv_weight, conv_bias, proj_weight, step_weight,
    step_bias, decay_log, skip_gain, out_weight, cotangent, lengths,
):
    T, D = tokens.shape
    E = in_weight.shape[1] // 2
    L = Layout(step_weight.shape[0], decay_log.shape[0], conv_weight.shape[0])
    ci = lax.axis_index("chan")
    cc = lax.axis_size("chan")
    sc = lax.axis_size("seq")
    blocks, share = E // EB, E // cc

    parts = (conv_weight, conv_bias, proj_weight.T, step_weight, step_bias, decay_log, skip_gain)
    wts, par, halo = gather_params(L, cc, parts, tokens)

    def by_block(values):
        if share == EB:
            return values
        values = jnp.moveaxis(values, 0, 1).reshape(-1, blocks, EB)
        return jnp.moveaxis(values, 1, 0)

    wts, par = by_block(wts), by_block(par)
    marks, normed, inner, gate, gg, g, cs, act, proj, b_cols, c_cols, b_diag, c_diag = front(
        L, lengths, tokens, halo, norm_gain, in_weight, out_weight, cotangent, par, wts
    )
    spre, step, u, factors, entering, arriving = pre_scan(L, cc, proj, par, wts, act, g, marks, b_cols, c_cols)
    held, grad_c, block_out, grad_out, grad_in, gn = fwd_scan(
        L, factors, u, b_cols, c_diag, g, par, entering, act, gate, gg, out_weight, cotangent, tokens,
        normed, in_weight,
    )
    gap, chan_d, gproj = bwd_scan(
        L, factors, step, u, g, b_diag, c_cols, par, wts, arriving, held, spre, act, proj, grad_c
    )
    gc, chan_e = conv_back(L, gap, gproj, wts, act, cs, inner, marks)
    after = lax.ppermute(gc[0:8], "chan", [(k, k - 1) for k in range(1, cc)])
    grad_in, grad_tokens, grad_gain = tail(
        L, gc, after, par, marks, normed, in_weight, gn, tokens, cotangent, norm_gain, grad_in
    )

    def by_owner(values):
        if share == EB:
            return values
        values = jnp.moveaxis(values, 0, 1).reshape(128, cc, share)
        return jnp.moveaxis(values, 1, 0)

    chan_d, chan_e = by_owner(chan_d), by_owner(chan_e)
    row = L.R + 2 * L.N + L.K + 1
    owned_gain = jnp.pad(grad_gain.reshape(cc, 1, D // cc), ((0, 0), (0, 0), (0, share - D // cc)))
    chan_e = lax.dynamic_update_slice(chan_e, owned_gain.astype(bf16), (0, row, 0))
    arrays = [grad_in.reshape(cc, 2 * E // cc, D), grad_out.reshape(cc, share, D), chan_d, chan_e]
    piece = 16 * sc
    rows = [v.shape[1] for v in arrays]
    arrays = [jnp.pad(v, ((0, 0), (0, -v.shape[1] % piece), (0, 0))) for v in arrays]
    sums = sum_owned(arrays, sc)
    sums = [v[:r] for v, r in zip(sums, rows)]
    g_in, g_out, conv_w, conv_b, proj_w, step_w, step_b, decay, skip, g_gain = unpack(L, sums)
    return (
        block_out, grad_tokens, g_gain[: D // cc], g_in, conv_w, conv_b, proj_w.T, step_w,
        step_b, decay, skip, g_out,
    )


def solution(mesh):
    tok, row, vec = P(("seq", "chan"), None), P(None, "chan"), P("chan")
    in_specs = (
        tok, P(), P(), row, vec, P("chan", None), row, vec, row, vec, P(), tok, P("seq", None),
    )
    out_specs = (
        tok, tok, vec, row, row, vec, P("chan", None), row, vec, row, vec, P("chan", None),
    )
    return jax.shard_map(local, mesh=mesh, in_specs=in_specs, out_specs=out_specs, check_vma=False)
```

```python
import functools
import math

import jax
import jax.numpy as jnp
from jax import lax
from jax.experimental import pallas as pl
from jax.experimental.pallas import tpu as pltpu
from jax.sharding import PartitionSpec as P

epsilon = 1e-05
LOG2E = math.log2(math.e)
CUT = 1e30
TC = 16
EB = 384
RT = 32
HALO = 16
PAR = 24
WTS = 128
f32 = jnp.float32
bf16 = jnp.bfloat16
NT = (((1,), (1,)), ((), ()))
TN = (((0,), (0,)), ((), ()))


def params(**more):
    return pltpu.CompilerParams(vmem_limit_bytes=63 * 1024 * 1024, **more)


def cols(rows, width=EB, shift=0):
    return pl.BlockSpec((rows, width), lambda i: (0, i + shift))


def tall(rows, width, shift=0):
    return pl.BlockSpec((rows, width), lambda i: (i + shift, 0))


def lead(rows, width, count=1):
    return pl.BlockSpec((count, rows, width), lambda i: (i, 0, 0))


def whole(*shape):
    return pl.BlockSpec(shape, lambda i: (0,) * len(shape))


def shape(dtype, *dims):
    return jax.ShapeDtypeStruct(dims, dtype)


def row_tiles(count, body):
    def step(i, unused):
        body(pl.multiple_of(i * RT, RT))
        return unused

    lax.fori_loop(0, count // RT, step, 0)


def same_step(states, rows):
    dims = (rows, TC * states)
    here = lax.rem(lax.broadcasted_iota(jnp.int32, dims, 0), TC) * states
    place = lax.broadcasted_iota(jnp.int32, dims, 1)
    return (place >= here) & (place < here + states)


class Layout:
    def __init__(self, R, N, K):
        self.R, self.N, self.K = R, N, K
        self.step = R + 2 * N
        self.decay = 0
        self.conv = self.decay + N
        self.conv_b = self.conv + K
        self.step_b = self.conv_b + 1
        self.skip = self.step_b + 1
        self.end = self.skip + 1


def gather_kernel(
    L, count, cw_ref, cb_ref, pw_ref, sw_ref, sb_ref, dl_ref, sk_ref, tok_ref,
    wts_ref, par_ref, halo_ref, send_sem, recv_sem, halo_sems,
):
    si, ci = lax.axis_index("seq"), lax.axis_index("chan")
    T = tok_ref.shape[0]
    width = par_ref.shape[2]
    barrier = pltpu.get_barrier_semaphore()
    for k in range(1, count):
        pl.semaphore_signal(
            barrier, inc=1, device_id=(si, lax.rem(ci + k, count)),
            device_id_type=pl.DeviceIdType.MESH,
        )
    own, weights = par_ref.at[ci], wts_ref.at[ci]
    weights[...] = jnp.concatenate(
        [pw_ref[...].astype(f32), sw_ref[...].astype(f32)], axis=0
    ).astype(bf16)
    own[...] = jnp.concatenate(
        [
            dl_ref[...], cw_ref[...], cb_ref[...].reshape(1, width), sb_ref[...].reshape(1, width),
            sk_ref[...].reshape(1, width), jnp.zeros((PAR - L.end, width), f32),
        ],
        axis=0,
    )
    pl.semaphore_wait(barrier, count - 1)

    def share(ref, j, k):
        return pltpu.make_async_remote_copy(
            src_ref=ref, dst_ref=ref, send_sem=send_sem.at[j, k], recv_sem=recv_sem.at[j, k],
            device_id=(si, lax.rem(ci + k, count)), device_id_type=pl.DeviceIdType.MESH,
        )

    edge = pltpu.make_async_remote_copy(
        src_ref=tok_ref.at[pl.ds(T - HALO, HALO)], dst_ref=halo_ref,
        send_sem=halo_sems.at[0], recv_sem=halo_sems.at[1],
        device_id=(si, lax.rem(ci + 1, count)), device_id_type=pl.DeviceIdType.MESH,
    )
    edge.start()
    for j, ref in enumerate((own, weights)):
        for k in range(1, count):
            share(ref, j, k).start()
    edge.wait()
    for j, ref in enumerate((own, weights)):
        for k in range(1, count):
            share(ref, j, k).wait()


def gather_params(L, count, parts, tokens):
    width = parts[0].shape[1]
    T, D = tokens.shape
    vmem = pl.BlockSpec(memory_space=pltpu.VMEM)
    return pl.pallas_call(
        functools.partial(gather_kernel, L, count),
        in_specs=[vmem] * 8,
        out_specs=[vmem] * 3,
        out_shape=[shape(bf16, count, WTS, width), shape(f32, count, PAR, width), shape(bf16, HALO, D)],
        scratch_shapes=[
            pltpu.SemaphoreType.DMA((2, count)),
            pltpu.SemaphoreType.DMA((2, count)),
            pltpu.SemaphoreType.DMA((2,)),
        ],
        compiler_params=params(collective_id=1, has_side_effects=True),
        name="gather_params",
    )(*parts, tokens)


def front_kernel(
    L, len_ref, tok_ref, halo_ref, gain_ref, wi_ref, wg_ref, wo_ref, cot_ref, par_ref, wts_ref,
    marks_ref, normed_ref, inner_ref, gate_ref, gg_ref, g_ref, cs_ref, act_ref, proj_ref,
    bch_ref, cch_ref, bd_ref, cd_ref, hn_ref, xs_ref, low_ref,
):
    T = tok_ref.shape[0]
    N, K = L.N, L.K
    i = pl.program_id(0)

    def norm(x):
        x = x.astype(f32)
        inv = lax.rsqrt(jnp.mean(x * x, axis=1, keepdims=True) + epsilon)
        return (x * inv * gain_ref[...].reshape(1, x.shape[1])).astype(bf16)

    @pl.when(i == 0)
    def _():
        first = lax.axis_index("chan") == 0
        halo = jnp.where(first, jnp.zeros(halo_ref.shape, f32), halo_ref[...].astype(f32))
        hn_ref[...] = norm(halo)

        def tile(r):
            normed_ref[pl.ds(r, RT), :] = norm(tok_ref[pl.ds(r, RT), :])

        row_tiles(T, tile)
        proj_ref[...] = jnp.zeros_like(proj_ref)
        dims = marks_ref.shape
        place = lax.broadcasted_iota(jnp.int32, dims, 0) + lax.axis_index("chan") * T
        lane = lax.broadcasted_iota(jnp.int32, dims, 1)
        reach = jnp.where(lane < K - 1, lane + 1, 1)
        inside = jnp.zeros(dims, f32)
        start = jnp.int32(0)
        for k in range(len_ref.shape[1]):
            inside = jnp.where((start > place - reach) & (start <= place), 1.0, inside)
            start = start + len_ref[0, k]
        marks_ref[...] = jnp.where(lane < K - 1, 1.0 - inside, inside * CUT)

    low = jnp.dot(hn_ref[...], wi_ref[...], preferred_element_type=f32).astype(bf16)
    inner_ref[0:HALO, :] = low
    xs_ref[0:HALO, :] = low.astype(f32)
    low = jnp.dot(normed_ref[...], wi_ref[...], preferred_element_type=f32).astype(bf16)
    inner_ref[HALO:, :] = low
    xs_ref[HALO:, :] = low.astype(f32)
    gate_ref[...] = jnp.dot(normed_ref[...], wg_ref[...], preferred_element_type=f32)
    gg_ref[...] = lax.dot_general(cot_ref[...], wo_ref[...], NT, preferred_element_type=f32)

    for k in range(par_ref.shape[0]):
        c = slice(k * EB, (k + 1) * EB)
        taps = [par_ref[k, L.conv + j : L.conv + j + 1, :] for j in range(K)]
        bias = par_ref[k, L.conv_b : L.conv_b + 1, :]

        def tile(r, c=c, taps=taps, bias=bias):
            rows = pl.ds(r, RT)
            block = xs_ref[pl.ds(pl.multiple_of(r + HALO - 8, 8), RT + 8), c]
            total = bias + taps[K - 1] * block[8:]
            for j in range(1, K):
                usable = marks_ref[rows, j - 1 : j]
                total = total + taps[K - 1 - j] * (block[8 - j : RT + 8 - j] * usable)
            act = total * jax.nn.sigmoid(total)
            cs_ref[rows, c] = total
            act_ref[rows, c] = act
            low_ref[rows, c] = act.astype(bf16)
            gate = gate_ref[rows, c]
            passed = gg_ref[rows, c] * (gate * jax.nn.sigmoid(gate))
            g_ref[rows, c] = passed.astype(bf16).astype(f32)

        row_tiles(T, tile)
        proj_ref[...] += lax.dot_general(low_ref[:, c], wts_ref[k], NT, preferred_element_type=f32)

    @pl.when(i == pl.num_programs(0) - 1)
    def _():
        turned = proj_ref[...].T
        for ref, start in ((bch_ref, L.R), (cch_ref, L.R + N)):
            for j in range(T // TC):
                ref[j] = turned[start : start + N, j * TC : (j + 1) * TC]
        dims = (128, TC * N)
        source = lax.broadcasted_iota(jnp.int32, dims, 0)
        state = lax.rem(lax.broadcasted_iota(jnp.int32, dims, 1), N)
        diag = same_step(N, T)
        small = proj_ref[...].astype(bf16)
        for ref, start in ((bd_ref, L.R), (cd_ref, L.R + N)):
            spread = (source == state + start).astype(f32).astype(bf16)
            wide = jnp.dot(small, spread, preferred_element_type=f32)
            ref[...] = jnp.where(diag, wide, 0.0).astype(bf16)


def front(L, lengths, tokens, halo, gain, in_weight, out_weight, cot, par, wts):
    T, D = tokens.shape
    E = out_weight.shape[0]
    sub = 2
    wide = EB * sub
    steps = E // wide
    N = L.N
    arrays = [shape(f32, T, E)] * 5
    return pl.pallas_call(
        functools.partial(front_kernel, L),
        grid=(steps,),
        in_specs=[
            pl.BlockSpec(memory_space=pltpu.SMEM),
            whole(T, D), whole(HALO, D), whole(D), cols(D, wide), cols(D, wide, steps),
            tall(wide, D), whole(T, D), lead(PAR, EB, sub), lead(WTS, EB, sub),
        ],
        out_specs=[whole(T + 8, 8), whole(T, D), cols(T + HALO, wide)] + [cols(T, wide)] * 5 + [
            whole(T, 128), whole(T // TC, N, TC), whole(T // TC, N, TC),
            whole(T, TC * N), whole(T, TC * N),
        ],
        out_shape=[shape(f32, T + 8, 8), shape(bf16, T, D), shape(bf16, T + HALO, E)] + arrays + [
            shape(f32, T, 128), shape(f32, T // TC, N, TC), shape(f32, T // TC, N, TC),
            shape(bf16, T, TC * N), shape(bf16, T, TC * N),
        ],
        scratch_shapes=[
            pltpu.VMEM((HALO, D), bf16),
            pltpu.VMEM((T + HALO, wide), f32),
            pltpu.VMEM((T, wide), bf16),
        ],
        compiler_params=params(),
        name="front",
    )(lengths, tokens, halo, gain, in_weight, in_weight, out_weight, cot, par, wts)


def rates(L, par_ref):
    return -jnp.exp(par_ref[0, L.decay : L.decay + L.N, :]) * LOG2E


def softplus(x):
    return jnp.maximum(x, 0.0) + jnp.log1p(jnp.exp(-jnp.abs(x)))


def pre_kernel(
    L, count, proj_ref, par_ref, wts_ref, act_ref, g_ref, marks_ref, b_ref, c_ref,
    spre_ref, step_ref, u_ref, a_ref, enter_ref, arrive_ref, dtk_ref, ahead_ref, behind_ref, got_ref,
    send_sem, recv_sem,
):
    T, E = act_ref.shape[0], enter_ref.shape[1]
    N = L.N
    i = pl.program_id(0)
    blocks = E // EB
    si, ci = lax.axis_index("seq"), lax.axis_index("chan")

    @pl.when(i == 0)
    def _():
        barrier = pltpu.get_barrier_semaphore()
        for k in range(1, count):
            pl.semaphore_signal(
                barrier, inc=1, device_id=(si, lax.rem(ci + k, count)),
                device_id_type=pl.DeviceIdType.MESH,
            )
        pl.semaphore_wait(barrier, count - 1)

    low = proj_ref[:, 0 : L.R].astype(bf16)
    weights = wts_ref[0, L.step : L.step + L.R, :]
    bias = par_ref[0, L.step_b : L.step_b + 1, :]
    spre_ref[...] = jnp.dot(low, weights, preferred_element_type=f32) + bias

    def tile(r):
        rows = pl.ds(r, RT)
        step = softplus(spre_ref[rows, :])
        u_ref[rows, :] = step * act_ref[rows, :]
        step_ref[rows, :] = step
        dtk_ref[rows, :] = step + marks_ref[rows, 3:4]

    row_tiles(T, tile)
    rate = rates(L, par_ref)

    def ahead(c, h):
        base = pl.multiple_of(c * TC, TC)
        row = pl.multiple_of(c * TC * N, TC * N)
        b_cols = b_ref[c]
        for j in range(TC):
            d = dtk_ref[pl.ds(base + j, 1), :]
            u = u_ref[pl.ds(base + j, 1), :]
            factor = jnp.exp2(d * rate)
            a_ref[pl.ds(row + j * N, N), :] = factor
            h = factor * h + b_cols[:, j : j + 1] * u
        return h

    def back(k, head):
        c = T // TC - 1 - k
        base = pl.multiple_of(c * TC, TC)
        row = pl.multiple_of(c * TC * N, TC * N)
        c_cols = c_ref[c]
        for j in reversed(range(TC)):
            g = g_ref[pl.ds(base + j, 1), :]
            head = a_ref[pl.ds(row + j * N, N), :] * (c_cols[:, j : j + 1] * g + head)
        return head

    zero = jnp.zeros(rate.shape, f32)
    h = lax.fori_loop(0, T // TC, ahead, zero)
    head = lax.fori_loop(0, T // TC, back, zero)
    through = jnp.exp2(jnp.sum(dtk_ref[...], axis=0, keepdims=True) * rate)
    ahead_ref[i, 0:N, :] = h
    ahead_ref[i, N:, :] = through
    behind_ref[i, 0:N, :] = head
    behind_ref[i, N:, :] = through

    def send(b, k, forward):
        return pltpu.make_async_remote_copy(
            src_ref=(ahead_ref if forward else behind_ref).at[b], dst_ref=got_ref.at[count - k, b],
            send_sem=send_sem.at[k, b], recv_sem=recv_sem.at[count - k, b],
            device_id=(si, lax.rem(ci + k, count)), device_id_type=pl.DeviceIdType.MESH,
        )

    for k in range(1, count):
        @pl.when(ci + k < count)
        def _(k=k):
            send(i, k, True).start()

        @pl.when(ci + k >= count)
        def _(k=k):
            send(i, k, False).start()

    @pl.when(i == blocks - 1)
    def _():
        for b in range(blocks):
            for k in range(1, count):
                send(b, k, True).wait()
        for b in range(blocks):
            span = slice(b * EB, (b + 1) * EB)
            entering, arriving = zero, zero
            for k in range(1, count):
                before = ci + k >= count
                got = got_ref[k, b]
                entering = jnp.where(before, got[0:N] + got[N:] * entering, entering)
            for k in range(count - 1, 0, -1):
                behind = ci + k < count
                got = got_ref[k, b]
                arriving = jnp.where(behind, got[0:N] + got[N:] * arriving, arriving)
            enter_ref[:, span] = entering
            arrive_ref[:, span] = arriving


def pre_scan(L, count, proj, par, wts, act, g, marks, b_cols, c_cols):
    T, E = act.shape
    N = L.N
    blocks = E // EB
    state = shape(f32, N, E)
    return pl.pallas_call(
        functools.partial(pre_kernel, L, count),
        grid=(blocks,),
        in_specs=[
            whole(T, 128), lead(PAR, EB), lead(WTS, EB), cols(T), cols(T), whole(*marks.shape),
            whole(*b_cols.shape), whole(*c_cols.shape),
        ],
        out_specs=[cols(T)] * 3 + [cols(T * N)] + [whole(N, E)] * 2,
        out_shape=[shape(f32, T, E)] * 3 + [shape(f32, T * N, E)] + [state] * 2,
        scratch_shapes=[
            pltpu.VMEM((T, EB), f32),
            pltpu.VMEM((blocks, 2 * N, EB), f32),
            pltpu.VMEM((blocks, 2 * N, EB), f32),
            pltpu.VMEM((count, blocks, 2 * N, EB), f32),
            pltpu.SemaphoreType.DMA((count, blocks)),
            pltpu.SemaphoreType.DMA((count, blocks)),
        ],
        compiler_params=params(collective_id=2, has_side_effects=True),
        name="pre_scan",
    )(proj, par, wts, act, g, marks, b_cols, c_cols)


def halves(values):
    return values[0:8] + values[8:16]


def lane_tiles(values):
    return [values[:, k * 128 : (k + 1) * 128] for k in range(EB // 128)]


def fold_rows(refs, r):
    sums = []
    for ref in refs:
        parts = [ref[pl.ds(r * 8 + k, 8, stride=8), :] for k in range(8)]
        while len(parts) > 1:
            parts = [x + y for x, y in zip(parts[::2], parts[1::2])]
        sums.append(parts[0])
    return jnp.concatenate(sums, axis=1)


def lane_sums(states, acc_ref, out_ref, chunks):
    width = TC * states
    ones = jnp.ones((TC, 128), bf16)

    def step(c, unused):
        rows = pl.ds(pl.multiple_of(c * width, width), width)
        out_ref[pl.ds(pl.multiple_of(c * TC, TC), TC), :] = lax.dot_general(
            ones, acc_ref[rows, :].astype(bf16), NT, preferred_element_type=f32
        )
        return unused

    lax.fori_loop(0, chunks, step, 0)


def fwd_kernel(
    L, a_ref, u_ref, b_ref, cd_ref, g_ref, par_ref, hin_ref, act_ref, gate_ref, gg_ref,
    wo_ref, cot_ref, tok_ref, normed_ref, wg_ref,
    h_ref, gc_ref, block_ref, gout_ref, gin_ref, gn_ref, y_ref, gated_ref, ggate_ref, branch_ref, acc_ref,
):
    chunks, states = b_ref.shape[0], b_ref.shape[1]
    T = chunks * TC
    width = TC * states
    i = pl.program_id(0)

    @pl.when(i == 0)
    def _():
        acc_ref[...] = jnp.zeros_like(acc_ref)
        gn_ref[...] = jnp.zeros_like(gn_ref)
        branch_ref[...] = jnp.zeros_like(branch_ref)

    h_ref[0:states, :] = hin_ref[...].astype(bf16)

    def contract(c):
        rows = pl.ds(pl.multiple_of(c * TC, TC), TC)
        held = h_ref[pl.ds(pl.multiple_of(c * width, width) + states, width), :]
        y_ref[rows, :] = jnp.dot(cd_ref[rows, :], held, preferred_element_type=f32)

    def advance(c, h):
        base = pl.multiple_of(c * TC, TC)
        row = pl.multiple_of(c * width, width)
        b_cols = b_ref[c]
        for j in range(TC):
            u = u_ref[pl.ds(base + j, 1), :]
            g = g_ref[pl.ds(base + j, 1), :]
            at = pl.ds(row + j * states, states)
            h = a_ref[at, :] * h + b_cols[:, j : j + 1] * u
            h_ref[pl.ds(row + (j + 1) * states, states), :] = h.astype(bf16)
            acc_ref[at, :] += sum(lane_tiles(h * g))
        return h

    def chunk(c, h):
        contract(c - 1)
        return advance(c, h)

    lax.fori_loop(1, chunks, chunk, advance(0, hin_ref[...]))
    contract(chunks - 1)
    skip = par_ref[0, L.skip : L.skip + 1, :]

    def tile(r):
        rows = pl.ds(r, RT)
        mixer = (y_ref[rows, :] + skip * act_ref[rows, :]).astype(bf16).astype(f32)
        gate = gate_ref[rows, :]
        sig = jax.nn.sigmoid(gate)
        gated_ref[rows, :] = (mixer * (gate * sig)).astype(bf16)
        ggate_ref[rows, :] = (gg_ref[rows, :] * mixer * sig * (1.0 + gate * (1.0 - sig))).astype(bf16)

    row_tiles(T, tile)
    branch_ref[...] += jnp.dot(gated_ref[...], wo_ref[...], preferred_element_type=f32)
    gout_ref[...] = lax.dot_general(
        gated_ref[...], cot_ref[...], TN, preferred_element_type=f32
    ).astype(bf16)
    gin_ref[...] = lax.dot_general(
        ggate_ref[...], normed_ref[...], TN, preferred_element_type=f32
    ).astype(bf16)
    gn_ref[...] += lax.dot_general(ggate_ref[...], wg_ref[...], NT, preferred_element_type=f32)

    @pl.when(i == pl.num_programs(0) - 1)
    def _():
        block_ref[...] = (tok_ref[...].astype(f32) + branch_ref[...]).astype(bf16)
        lane_sums(states, acc_ref, gc_ref, chunks)


def fwd_scan(L, factors, u, b_cols, c_diag, g, par, entering, act, gate, gg, out_weight, cot, tokens, normed, in_weight):
    T, E = u.shape
    D = tokens.shape[1]
    N = L.N
    rows = (T + 1) * N
    blocks = E // EB
    return pl.pallas_call(
        functools.partial(fwd_kernel, L),
        grid=(blocks,),
        in_specs=[
            cols(T * N), cols(T), whole(*b_cols.shape), whole(T, TC * N), cols(T), lead(PAR, EB), cols(N),
            cols(T), cols(T), cols(T), tall(EB, D), whole(T, D), whole(T, D), whole(T, D),
            cols(D, EB, blocks),
        ],
        out_specs=[
            cols(rows), whole(T, TC * N), whole(T, D), tall(EB, D), tall(EB, D, blocks), whole(T, D),
        ],
        out_shape=[
            shape(bf16, rows, E), shape(f32, T, TC * N), shape(bf16, T, D), shape(bf16, E, D),
            shape(bf16, 2 * E, D), shape(f32, T, D),
        ],
        scratch_shapes=[
            pltpu.VMEM((T, EB), f32), pltpu.VMEM((T, EB), bf16), pltpu.VMEM((T, EB), bf16),
            pltpu.VMEM((T, D), f32), pltpu.VMEM((T * N, 128), f32),
        ],
        compiler_params=params(),
        name="fwd_scan",
    )(factors, u, b_cols, c_diag, g, par, entering, act, gate, gg, out_weight, cot, tokens, normed, in_weight)


def bwd_kernel(
    L, a_ref, step_ref, u_ref, g_ref, bd_ref, c_ref, par_ref, wts_ref, fin_ref, h_ref, spre_ref, act_ref, proj_ref,
    gc_ref, gap_ref, chan_ref, gproj_ref, adj_ref, acc_ref, bsum_ref, gb_ref, rank_ref, pre_ref, *wsum_refs,
):
    rate = -jnp.exp(par_ref[0, L.decay : L.decay + L.N, :])
    chunks, states = c_ref.shape[0], c_ref.shape[1]
    T = chunks * TC
    width = TC * states
    i = pl.program_id(0)

    @pl.when(i == 0)
    def _():
        acc_ref[...] = jnp.zeros_like(acc_ref)
        rank_ref[...] = jnp.zeros_like(rank_ref)

    def slot(c):
        return pl.multiple_of(lax.rem(c, 2) * width, width)

    def contract(c):
        rows = pl.ds(pl.multiple_of(c * TC, TC), TC)
        held = adj_ref[pl.ds(slot(c), width), :]
        bsum_ref[rows, :] = jnp.dot(bd_ref[rows, :], held, preferred_element_type=f32)

    def retreat(c, carry):
        flow, acc = carry
        base = pl.multiple_of(c * TC, TC)
        row = pl.multiple_of(c * width, width)
        place = slot(c)
        c_cols = c_ref[c]
        for j in reversed(range(TC)):
            d = step_ref[pl.ds(base + j, 1), :]
            g = g_ref[pl.ds(base + j, 1), :]
            u = u_ref[pl.ds(base + j, 1), :]
            at = pl.ds(row + j * states, states)
            adj = c_cols[:, j : j + 1] * g + flow
            flow = a_ref[at, :] * adj
            wr = flow * h_ref[at, :].astype(f32) * rate
            acc = acc + wr * d
            adj_ref[pl.ds(place + j * states, states), :] = adj.astype(bf16)
            for ref, part in zip(wsum_refs, lane_tiles(halves(wr))):
                ref[pl.ds((base + j) * 8, 8), :] = part
            acc_ref[at, :] += sum(lane_tiles(adj * u))
        return flow, acc

    def chunk(k, carry):
        c = chunks - 1 - k
        contract(c + 1)
        return retreat(c, carry)

    carry = retreat(chunks - 1, (fin_ref[...], jnp.zeros(rate.shape, f32)))
    unused, acc = lax.fori_loop(1, chunks, chunk, carry)
    contract(0)
    skip = par_ref[0, L.skip : L.skip + 1, :]

    def tile(k, carry):
        bias_sum, skip_sum = carry
        rows = pl.ds(pl.multiple_of(k * 16, 16), 16)
        spre, act, g, bsum = spre_ref[rows, :], act_ref[rows, :], g_ref[rows, :], bsum_ref[rows, :]
        wsum = jnp.concatenate([fold_rows(wsum_refs, k * 16), fold_rows(wsum_refs, k * 16 + 8)], axis=0)
        grad = (wsum + act * bsum) * jax.nn.sigmoid(spre)
        gap_ref[rows, :] = g * skip + step_ref[rows, :] * bsum
        pre_ref[rows, :] = grad.astype(bf16)
        bias_sum = bias_sum + halves(grad)
        skip_sum = skip_sum + halves(g * act)
        return bias_sum, skip_sum

    none = jnp.zeros((8, EB), f32)
    bias_sum, skip_sum = lax.fori_loop(0, T // 16, tile, (none, none))
    R = L.R
    pre = pre_ref[...]
    step_low = proj_ref[...].astype(bf16)
    grad_step_w = lax.dot_general(step_low, pre, TN, preferred_element_type=f32)
    chan_ref[0] = jnp.concatenate(
        [
            grad_step_w[0:R],
            acc,
            jnp.sum(bias_sum, axis=0, keepdims=True),
            jnp.sum(skip_sum, axis=0, keepdims=True),
            jnp.zeros((128 - R - states - 2, EB), f32),
        ],
        axis=0,
    ).astype(bf16)
    weights = wts_ref[0, L.step : L.step + R, :].astype(f32)
    weights = jnp.concatenate([weights, jnp.zeros((128 - R, EB), f32)], axis=0).astype(bf16)
    rank_ref[...] += lax.dot_general(pre, weights, NT, preferred_element_type=f32)

    @pl.when(i == pl.num_programs(0) - 1)
    def _():
        lane_sums(states, acc_ref, gb_ref, chunks)
        dims = (width, 128)
        state = lax.rem(lax.broadcasted_iota(jnp.int32, dims, 0), states)
        target = lax.broadcasted_iota(jnp.int32, dims, 1)
        diag = same_step(states, T)
        total = rank_ref[...]
        for ref, start in ((gb_ref, R), (gc_ref, R + states)):
            fold = (target == state + start).astype(f32)
            kept = jnp.where(diag, ref[...], 0.0)
            total = total + jnp.dot(
                kept, fold, precision=lax.Precision.HIGHEST, preferred_element_type=f32
            )
        gproj_ref[...] = total.astype(bf16)


def bwd_scan(L, factors, step, u, g, b_diag, c_cols, par, wts, arriving, held, spre, act, proj, grad_c):
    T, E = u.shape
    N = L.N
    blocks = E // EB
    return pl.pallas_call(
        functools.partial(bwd_kernel, L),
        grid=(blocks,),
        in_specs=[
            cols(T * N), cols(T), cols(T), cols(T), whole(T, TC * N), whole(*c_cols.shape), lead(PAR, EB),
            lead(WTS, EB), cols(N), cols(held.shape[0]), cols(T), cols(T), whole(T, 128), whole(T, TC * N),
        ],
        out_specs=[cols(T), lead(128, EB), whole(T, 128)],
        out_shape=[shape(f32, T, E), shape(bf16, blocks, 128, EB), shape(bf16, T, 128)],
        scratch_shapes=[
            pltpu.VMEM((2 * TC * N, EB), bf16), pltpu.VMEM((T * N, 128), f32), pltpu.VMEM((T, EB), f32),
            pltpu.VMEM((T, TC * N), f32), pltpu.VMEM((T, 128), f32), pltpu.VMEM((T, EB), bf16),
        ] + [pltpu.VMEM((T * 8, 128), f32)] * (EB // 128),
        compiler_params=params(),
        name="bwd_scan",
    )(factors, step, u, g, b_diag, c_cols, par, wts, arriving, held, spre, act, proj, grad_c)


def conv_kernel(L, gap_ref, gproj_ref, wts_ref, act_ref, cs_ref, inner_ref, marks_ref, gc_ref, chan_ref, xs_ref):
    T = gap_ref.shape[0]
    K, wide = L.K, L.R + 2 * L.N
    weights = wts_ref[0].astype(f32)
    row = lax.broadcasted_iota(jnp.int32, weights.shape, 0)
    weights = jnp.where(row < wide, weights, 0.0).astype(bf16)
    gc_ref[...] = jnp.dot(gproj_ref[...], weights, preferred_element_type=f32)
    act_low = act_ref[...].astype(bf16)
    grad_proj = lax.dot_general(gproj_ref[...], act_low, TN, preferred_element_type=f32)
    xs_ref[...] = inner_ref[...].astype(f32)

    def tile(k, carry):
        r = pl.multiple_of(k * RT, RT)
        rows = pl.ds(r, RT)
        total = cs_ref[rows, :]
        sig = jax.nn.sigmoid(total)
        grad = (gc_ref[rows, :] + gap_ref[rows, :]) * sig * (1.0 + total * (1.0 - sig))
        gc_ref[rows, :] = grad
        block = xs_ref[pl.ds(pl.multiple_of(r + HALO - 8, 8), RT + 8), :]
        out = [carry[K] + jnp.sum(grad.reshape(RT // 8, 8, EB), axis=0)]
        for j in range(K):
            part = grad * block[8 - j : RT + 8 - j]
            if j > 0:
                part = part * marks_ref[rows, j - 1 : j]
            out.insert(0, carry[K - 1 - j] + jnp.sum(part.reshape(RT // 8, 8, EB), axis=0))
        return tuple(out)

    none = jnp.zeros((8, EB), f32)
    sums = lax.fori_loop(0, T // RT, tile, (none,) * (K + 1))
    chan_ref[0] = jnp.concatenate(
        [grad_proj[0:wide]]
        + [jnp.sum(s, axis=0, keepdims=True) for s in sums]
        + [jnp.zeros((128 - wide - K - 1, EB), f32)],
        axis=0,
    ).astype(bf16)


def conv_back(L, gap, gproj, wts, act, cs, inner, marks):
    T, E = gap.shape
    blocks = E // EB
    return pl.pallas_call(
        functools.partial(conv_kernel, L),
        grid=(blocks,),
        in_specs=[
            cols(T), whole(T, 128), lead(WTS, EB), cols(T), cols(T), cols(T + HALO), whole(*marks.shape),
        ],
        out_specs=[cols(T), lead(128, EB)],
        out_shape=[shape(f32, T, E), shape(bf16, blocks, 128, EB)],
        scratch_shapes=[pltpu.VMEM((T + HALO, EB), f32)],
        compiler_params=params(),
        name="conv_back",
    )(gap, gproj, wts, act, cs, inner, marks)


def tail_kernel(
    L, gc_ref, after_ref, par_ref, marks_ref, normed_ref, wi_ref, gn_ref, tok_ref, cot_ref, gain_ref,
    held_ref, gin_ref, gtok_ref, ggain_ref, ext_ref, low_ref, sum_ref,
):
    T, D = tok_ref.shape
    K = L.K
    i = pl.program_id(0)
    ext_ref[0:T, :] = gc_ref[...]
    ext_ref[T : T + 8, :] = after_ref[...]
    taps = [par_ref[0, L.conv + j : L.conv + j + 1, :] for j in range(K)]

    def tile(r):
        block = ext_ref[pl.ds(r, RT + 8), :]
        marks = marks_ref[pl.ds(r, RT + 8), :]
        total = taps[K - 1] * block[0:RT]
        for j in range(1, K):
            masked = block * marks[:, j - 1 : j]
            total = total + taps[K - 1 - j] * masked[j : RT + j]
        low_ref[pl.ds(r, RT), :] = total.astype(bf16)

    row_tiles(T, tile)
    gin_ref[...] = lax.dot_general(
        low_ref[...], normed_ref[...], TN, preferred_element_type=f32
    ).astype(bf16)
    part = lax.dot_general(low_ref[...], wi_ref[...], NT, preferred_element_type=f32)

    @pl.when(i == 0)
    def _():
        sum_ref[...] = gn_ref[...] + part

    @pl.when(i > 0)
    def _():
        sum_ref[...] += part

    @pl.when(i == pl.num_programs(0) - 1)
    def _():
        gain = gain_ref[...].reshape(1, D)

        def last(k, total):
            rows = pl.ds(pl.multiple_of(k * 16, 16), 16)
            x = tok_ref[rows, :].astype(f32)
            grad = sum_ref[rows, :]
            inv = lax.rsqrt(jnp.mean(x * x, axis=1, keepdims=True) + epsilon)
            scaled = grad * gain
            mean = jnp.mean(x * scaled, axis=1, keepdims=True)
            gtok_ref[rows, :] = (
                cot_ref[rows, :].astype(f32) + inv * scaled - x * (inv * inv * inv * mean)
            )
            return total + jnp.sum((grad * x * inv).reshape(2, 8, D), axis=0)

        total = lax.fori_loop(0, T // 16, last, jnp.zeros((8, D), f32))
        ggain_ref[...] = jnp.sum(total, axis=0, keepdims=True)


def tail(L, gc, after, par, marks, normed, in_weight, gn, tokens, cot, gain, held):
    T, E = gc.shape
    D = tokens.shape[1]
    blocks = E // EB
    return pl.pallas_call(
        functools.partial(tail_kernel, L),
        grid=(blocks,),
        in_specs=[
            cols(T), cols(8), lead(PAR, EB), whole(*marks.shape), whole(T, D), cols(D), whole(T, D),
            whole(T, D), whole(T, D), whole(D), pl.BlockSpec(memory_space=pl.ANY),
        ],
        out_specs=[tall(EB, D), whole(T, D), whole(1, D)],
        out_shape=[shape(bf16, 2 * E, D), shape(f32, T, D), shape(f32, 1, D)],
        scratch_shapes=[
            pltpu.VMEM((T + 8, EB), f32), pltpu.VMEM((T, EB), bf16), pltpu.VMEM((T, D), f32),
        ],
        input_output_aliases={10: 0},
        compiler_params=params(),
        name="tail",
    )(gc, after, par, marks, normed, in_weight, gn, tokens, cot, gain, held)


def sum_plan(chan_count, seq_count):
    chan_bits = [("chan", 1 << i) for i in range(chan_count.bit_length() - 1)]
    seq_bits = [("seq", 1 << i) for i in range(seq_count.bit_length() - 1)]
    return chan_bits, seq_bits


def sum_kernel(chan_count, seq_count, pieces, arrays, *refs):
    piece_rows = 16 * seq_count
    x_refs, o_refs = refs[:arrays], refs[arrays : 2 * arrays]
    chan_bits, seq_bits = sum_plan(chan_count, seq_count)
    nc, ns = len(chan_bits), len(seq_bits)
    stages = nc + ns
    count = len(pieces)
    scratch = refs[2 * arrays :]
    held = [scratch[p * stages : (p + 1) * stages] for p in range(count)]
    send_sem, recv_sem = scratch[count * stages :]
    mine = {"seq": lax.axis_index("seq"), "chan": lax.axis_index("chan")}

    def bit_of(name, bit):
        return (mine[name] // bit) % 2

    def partner(name, bit):
        other = dict(mine)
        other[name] = mine[name] + bit - 2 * bit * bit_of(name, bit)
        return (other["seq"], other["chan"])

    def order(p):
        inner = chan_bits if p % 2 == 0 else chan_bits[::-1]
        return seq_bits[:1] + inner + seq_bits[1:]

    barrier = pltpu.get_barrier_semaphore()
    for name, bit in chan_bits + seq_bits:
        pl.semaphore_signal(
            barrier, inc=1, device_id=partner(name, bit), device_id_type=pl.DeviceIdType.MESH
        )
    pl.semaphore_wait(barrier, stages)

    def parts(p, s, keep):
        name, bit = order(p)[s]
        side = bit_of(name, bit) if keep else 1 - bit_of(name, bit)
        done = order(p)[:s]
        size = piece_rows >> sum(1 for n, b in done if n == "seq")
        ref, start = (x_refs[pieces[p][0]], pieces[p][1]) if s == 0 else (held[p][s - 1], 0)
        if name == "seq":
            rows = pl.ds(pl.multiple_of(start + side * (size // 2), 16), size // 2)
            return [ref.at[:, rows, :]]
        left = [b for n, b in chan_bits if ("chan", b) not in done]
        low = 1 << left.index(bit)
        return [
            ref.at[pl.ds((i // low) * 2 * low + side * low + i % low, 1), pl.ds(start, size), :]
            for i in range((1 << len(left)) // 2)
        ]

    def landing(p, s):
        dst = held[p][s]
        if order(p)[s][0] == "seq":
            return [dst]
        return [dst.at[pl.ds(i, 1)] for i in range(dst.shape[0])]

    def copies(p, s):
        return [
            pltpu.make_async_remote_copy(
                src_ref=src, dst_ref=dst, send_sem=send_sem.at[p, s, i], recv_sem=recv_sem.at[p, s, i],
                device_id=partner(*order(p)[s]), device_id_type=pl.DeviceIdType.MESH,
            )
            for i, (src, dst) in enumerate(zip(parts(p, s, False), landing(p, s)))
        ]

    def my_rows(p, done):
        start, size = pieces[p][1], piece_rows
        for name, bit in seq_bits[:done]:
            size //= 2
            start = start + bit_of(name, bit) * size
        return pl.ds(pl.multiple_of(start, 16), size)

    def gather_copy(p, k):
        place = o_refs[pieces[p][0]].at[my_rows(p, ns - k), :]
        return pltpu.make_async_remote_copy(
            src_ref=place, dst_ref=place,
            send_sem=send_sem.at[p, stages + k, 0], recv_sem=recv_sem.at[p, stages + k, 0],
            device_id=partner(*seq_bits[ns - 1 - k]), device_id_type=pl.DeviceIdType.MESH,
        )

    total = stages + ns
    for tick in range((count + 1) // 2 + total):
        for p in range(count):
            s = tick - p // 2
            if not 0 <= s <= total:
                continue
            if 1 <= s <= stages:
                for copy in copies(p, s - 1):
                    copy.wait_recv()
                for src, dst in zip(parts(p, s - 1, True), landing(p, s - 1)):
                    dst[...] = (dst[...].astype(f32) + src[...].astype(f32)).astype(bf16)
                if s == stages:
                    o_refs[pieces[p][0]][my_rows(p, ns), :] = held[p][stages - 1][0]
            elif s > stages:
                gather_copy(p, s - 1 - stages).wait_recv()
            if s < stages:
                for copy in copies(p, s):
                    copy.start()
            elif s < total:
                gather_copy(p, s - stages).start()
    for p in range(count):
        for s in range(stages):
            for copy in copies(p, s):
                copy.wait_send()
        for k in range(ns):
            gather_copy(p, k).wait_send()


def sum_owned(arrays, seq_count):
    chan_count = arrays[0].shape[0]
    chan_bits, seq_bits = sum_plan(chan_count, seq_count)
    piece_rows = 16 * seq_count
    pieces = [(a, r) for a, v in enumerate(arrays) for r in range(0, v.shape[1], piece_rows)]
    ordered = seq_bits[:1] + chan_bits + seq_bits[1:]
    scratch = []
    for a, r in pieces:
        owners, size = chan_count, piece_rows
        for name, bit in ordered:
            if name == "chan":
                owners //= 2
            else:
                size //= 2
            scratch.append(pltpu.VMEM((owners, size, arrays[a].shape[2]), bf16))
    total = len(ordered) + len(seq_bits)
    sems = pltpu.SemaphoreType.DMA((len(pieces), total, max(1, chan_count // 2)))
    vmem = pl.BlockSpec(memory_space=pltpu.VMEM)
    return pl.pallas_call(
        functools.partial(sum_kernel, chan_count, seq_count, pieces, len(arrays)),
        in_specs=[vmem] * len(arrays),
        out_specs=[vmem] * len(arrays),
        out_shape=[shape(bf16, *v.shape[1:]) for v in arrays],
        scratch_shapes=scratch + [sems, sems],
        compiler_params=params(collective_id=0, has_side_effects=True),
        name="sum_owned",
    )(*arrays)


def unpack_kernel(L, in_ref, out_ref, d_ref, e_ref, gin_ref, gout_ref, *refs):
    gin_ref[...] = in_ref[...].astype(f32).T
    gout_ref[...] = out_ref[...].astype(f32)
    d, e = d_ref[...].astype(f32), e_ref[...].astype(f32)
    R, N, K = L.R, L.N, L.K
    wide = R + 2 * N
    conv_w, conv_b, proj, step_w, step_b, decay, skip, gain = refs
    width = d.shape[1]
    step_w[...] = d[0:R]
    decay[...] = d[R : R + N]
    step_b[...] = d[R + N].reshape(width)
    skip[...] = d[R + N + 1].reshape(width)
    proj[...] = e[0:wide]
    conv_w[...] = e[wide : wide + K]
    conv_b[...] = e[wide + K].reshape(width)
    gain[...] = e[wide + K + 1].reshape(width)


def unpack(L, sums):
    width = sums[2].shape[1]
    rows, D = sums[0].shape
    R, N, K = L.R, L.N, L.K
    return pl.pallas_call(
        functools.partial(unpack_kernel, L),
        out_shape=[
            shape(f32, D, rows), shape(f32, *sums[1].shape), shape(f32, K, width), shape(f32, width),
            shape(f32, R + 2 * N, width), shape(f32, R, width), shape(f32, width),
            shape(f32, N, width), shape(f32, width), shape(f32, width),
        ],
        compiler_params=params(),
        name="unpack",
    )(*sums)


def local(
    tokens, norm_gain, in_weight, conv_weight, conv_bias, proj_weight, step_weight,
    step_bias, decay_log, skip_gain, out_weight, cotangent, lengths,
):
    T, D = tokens.shape
    E = in_weight.shape[1] // 2
    L = Layout(step_weight.shape[0], decay_log.shape[0], conv_weight.shape[0])
    ci = lax.axis_index("chan")
    cc = lax.axis_size("chan")
    sc = lax.axis_size("seq")
    blocks, share = E // EB, E // cc

    parts = (conv_weight, conv_bias, proj_weight.T, step_weight, step_bias, decay_log, skip_gain)
    wts, par, halo = gather_params(L, cc, parts, tokens)

    def by_block(values):
        if share == EB:
            return values
        values = jnp.moveaxis(values, 0, 1).reshape(-1, blocks, EB)
        return jnp.moveaxis(values, 1, 0)

    wts, par = by_block(wts), by_block(par)
    marks, normed, inner, gate, gg, g, cs, act, proj, b_cols, c_cols, b_diag, c_diag = front(
        L, lengths, tokens, halo, norm_gain, in_weight, out_weight, cotangent, par, wts
    )
    spre, step, u, factors, entering, arriving = pre_scan(L, cc, proj, par, wts, act, g, marks, b_cols, c_cols)
    held, grad_c, block_out, grad_out, grad_in, gn = fwd_scan(
        L, factors, u, b_cols, c_diag, g, par, entering, act, gate, gg, out_weight, cotangent, tokens,
        normed, in_weight,
    )
    gap, chan_d, gproj = bwd_scan(
        L, factors, step, u, g, b_diag, c_cols, par, wts, arriving, held, spre, act, proj, grad_c
    )
    gc, chan_e = conv_back(L, gap, gproj, wts, act, cs, inner, marks)
    after = lax.ppermute(gc[0:8], "chan", [(k, k - 1) for k in range(1, cc)])
    grad_in, grad_tokens, grad_gain = tail(
        L, gc, after, par, marks, normed, in_weight, gn, tokens, cotangent, norm_gain, grad_in
    )

    def by_owner(values):
        if share == EB:
            return values
        values = jnp.moveaxis(values, 0, 1).reshape(128, cc, share)
        return jnp.moveaxis(values, 1, 0)

    chan_d, chan_e = by_owner(chan_d), by_owner(chan_e)
    row = L.R + 2 * L.N + L.K + 1
    owned_gain = jnp.pad(grad_gain.reshape(cc, 1, D // cc), ((0, 0), (0, 0), (0, share - D // cc)))
    chan_e = lax.dynamic_update_slice(chan_e, owned_gain.astype(bf16), (0, row, 0))
    arrays = [grad_in.reshape(cc, 2 * E // cc, D), grad_out.reshape(cc, share, D), chan_d, chan_e]
    piece = 16 * sc
    rows = [v.shape[1] for v in arrays]
    arrays = [jnp.pad(v, ((0, 0), (0, -v.shape[1] % piece), (0, 0))) for v in arrays]
    sums = sum_owned(arrays, sc)
    sums = [v[:r] for v, r in zip(sums, rows)]
    g_in, g_out, conv_w, conv_b, proj_w, step_w, step_b, decay, skip, g_gain = unpack(L, sums)
    return (
        block_out, grad_tokens, g_gain[: D // cc], g_in, conv_w, conv_b, proj_w.T, step_w,
        step_b, decay, skip, g_out,
    )


def solution(mesh):
    tok, row, vec = P(("seq", "chan"), None), P(None, "chan"), P("chan")
    in_specs = (
        tok, P(), P(), row, vec, P("chan", None), row, vec, row, vec, P(), tok, P("seq", None),
    )
    out_specs = (
        tok, tok, vec, row, row, vec, P("chan", None), row, vec, row, vec, P("chan", None),
    )
    return jax.shard_map(local, mesh=mesh, in_specs=in_specs, out_specs=out_specs, check_vma=False)
```

```python
import functools
import math

import jax
import jax.numpy as jnp
from jax import lax
from jax.experimental import pallas as pl
from jax.experimental.pallas import tpu as pltpu
from jax.sharding import PartitionSpec as P

epsilon = 1e-05
LOG2E = math.log2(math.e)
CUT = 1e30
TC = 16
EB = 384
RT = 32
HALO = 16
PAR = 24
WTS = 128
f32 = jnp.float32
bf16 = jnp.bfloat16
NT = (((1,), (1,)), ((), ()))
TN = (((0,), (0,)), ((), ()))


def params(**more):
    return pltpu.CompilerParams(vmem_limit_bytes=60 * 1024 * 1024, **more)


def cols(rows, width=EB, shift=0):
    return pl.BlockSpec((rows, width), lambda i: (0, i + shift))


def tall(rows, width, shift=0):
    return pl.BlockSpec((rows, width), lambda i: (i + shift, 0))


def lead(rows, width, count=1):
    return pl.BlockSpec((count, rows, width), lambda i: (i, 0, 0))


def whole(*shape):
    return pl.BlockSpec(shape, lambda i: (0,) * len(shape))


def once(*shape):
    return pl.BlockSpec(shape, lambda i: (0,) * len(shape), pipeline_mode=pl.Buffered(1))


def shape(dtype, *dims):
    return jax.ShapeDtypeStruct(dims, dtype)


def row_tiles(count, body):
    def step(i, unused):
        body(pl.multiple_of(i * RT, RT))
        return unused

    lax.fori_loop(0, count // RT, step, 0)


def same_step(states, rows):
    dims = (rows, TC * states)
    here = lax.rem(lax.broadcasted_iota(jnp.int32, dims, 0), TC) * states
    place = lax.broadcasted_iota(jnp.int32, dims, 1)
    return (place >= here) & (place < here + states)


class Layout:
    def __init__(self, R, N, K):
        self.R, self.N, self.K = R, N, K
        self.step = R + 2 * N
        self.decay = 0
        self.conv = self.decay + N
        self.conv_b = self.conv + K
        self.step_b = self.conv_b + 1
        self.skip = self.step_b + 1
        self.end = self.skip + 1


def gather_kernel(
    L, count, cw_ref, cb_ref, pw_ref, sw_ref, sb_ref, dl_ref, sk_ref, tok_ref,
    wts_ref, par_ref, halo_ref, send_sem, recv_sem, halo_sems,
):
    si, ci = lax.axis_index("seq"), lax.axis_index("chan")
    T = tok_ref.shape[0]
    width = par_ref.shape[2]
    barrier = pltpu.get_barrier_semaphore()
    for k in range(1, count):
        pl.semaphore_signal(
            barrier, inc=1, device_id=(si, lax.rem(ci + k, count)),
            device_id_type=pl.DeviceIdType.MESH,
        )
    own, weights = par_ref.at[ci], wts_ref.at[ci]
    weights[...] = jnp.concatenate(
        [pw_ref[...].astype(f32), sw_ref[...].astype(f32)], axis=0
    ).astype(bf16)
    own[...] = jnp.concatenate(
        [
            dl_ref[...], cw_ref[...], cb_ref[...].reshape(1, width), sb_ref[...].reshape(1, width),
            sk_ref[...].reshape(1, width), jnp.zeros((PAR - L.end, width), f32),
        ],
        axis=0,
    )
    pl.semaphore_wait(barrier, count - 1)

    def share(ref, j, k):
        return pltpu.make_async_remote_copy(
            src_ref=ref, dst_ref=ref, send_sem=send_sem.at[j, k], recv_sem=recv_sem.at[j, k],
            device_id=(si, lax.rem(ci + k, count)), device_id_type=pl.DeviceIdType.MESH,
        )

    edge = pltpu.make_async_remote_copy(
        src_ref=tok_ref.at[pl.ds(T - HALO, HALO)], dst_ref=halo_ref,
        send_sem=halo_sems.at[0], recv_sem=halo_sems.at[1],
        device_id=(si, lax.rem(ci + 1, count)), device_id_type=pl.DeviceIdType.MESH,
    )
    edge.start()
    for j, ref in enumerate((own, weights)):
        for k in range(1, count):
            share(ref, j, k).start()
    edge.wait()
    for j, ref in enumerate((own, weights)):
        for k in range(1, count):
            share(ref, j, k).wait()


def gather_params(L, count, parts, tokens):
    width = parts[0].shape[1]
    T, D = tokens.shape
    vmem = pl.BlockSpec(memory_space=pltpu.VMEM)
    return pl.pallas_call(
        functools.partial(gather_kernel, L, count),
        in_specs=[vmem] * 8,
        out_specs=[vmem] * 3,
        out_shape=[shape(bf16, count, WTS, width), shape(f32, count, PAR, width), shape(bf16, HALO, D)],
        scratch_shapes=[
            pltpu.SemaphoreType.DMA((2, count)),
            pltpu.SemaphoreType.DMA((2, count)),
            pltpu.SemaphoreType.DMA((2,)),
        ],
        compiler_params=params(collective_id=1, has_side_effects=True),
        name="gather_params",
    )(*parts, tokens)


def front_kernel(
    L, len_ref, tok_ref, halo_ref, gain_ref, wi_ref, wg_ref, wo_ref, cot_ref, par_ref, wts_ref,
    marks_ref, normed_ref, inner_ref, gate_ref, gg_ref, g_ref, cs_ref, act_ref, proj_ref,
    bb_ref, cc_ref, hn_ref, xs_ref, low_ref, hi_ref, lo_ref,
):
    T = tok_ref.shape[0]
    N, K = L.N, L.K
    i = pl.program_id(0)

    def norm(x):
        x = x.astype(f32)
        inv = lax.rsqrt(jnp.mean(x * x, axis=1, keepdims=True) + epsilon)
        return (x * inv * gain_ref[...].reshape(1, x.shape[1])).astype(bf16)

    @pl.when(i == 0)
    def _():
        first = lax.axis_index("chan") == 0
        halo = jnp.where(first, jnp.zeros(halo_ref.shape, f32), halo_ref[...].astype(f32))
        hn_ref[...] = norm(halo)

        def tile(r):
            normed_ref[pl.ds(r, RT), :] = norm(tok_ref[pl.ds(r, RT), :])

        row_tiles(T, tile)
        proj_ref[...] = jnp.zeros_like(proj_ref)
        dims = marks_ref.shape
        place = lax.broadcasted_iota(jnp.int32, dims, 0) + lax.axis_index("chan") * T
        lane = lax.broadcasted_iota(jnp.int32, dims, 1)
        reach = jnp.where(lane < K - 1, lane + 1, 1)
        inside = jnp.zeros(dims, f32)
        start = jnp.int32(0)
        for k in range(len_ref.shape[1]):
            inside = jnp.where((start > place - reach) & (start <= place), 1.0, inside)
            start = start + len_ref[0, k]
        marks_ref[...] = jnp.where(lane < K - 1, 1.0 - inside, inside * CUT)

    low = jnp.dot(hn_ref[...], wi_ref[...], preferred_element_type=f32).astype(bf16)
    inner_ref[0:HALO, :] = low
    xs_ref[0:HALO, :] = low.astype(f32)
    low = jnp.dot(normed_ref[...], wi_ref[...], preferred_element_type=f32).astype(bf16)
    inner_ref[HALO:, :] = low
    xs_ref[HALO:, :] = low.astype(f32)
    gate_ref[...] = jnp.dot(normed_ref[...], wg_ref[...], preferred_element_type=f32)
    gg_ref[...] = lax.dot_general(cot_ref[...], wo_ref[...], NT, preferred_element_type=f32)

    for k in range(par_ref.shape[0]):
        c = slice(k * EB, (k + 1) * EB)
        taps = [par_ref[k, L.conv + j : L.conv + j + 1, :] for j in range(K)]
        bias = par_ref[k, L.conv_b : L.conv_b + 1, :]

        def tile(r, c=c, taps=taps, bias=bias):
            rows = pl.ds(r, RT)
            block = xs_ref[pl.ds(pl.multiple_of(r + HALO - 8, 8), RT + 8), c]
            total = bias + taps[K - 1] * block[8:]
            for j in range(1, K):
                usable = marks_ref[rows, j - 1 : j]
                total = total + taps[K - 1 - j] * (block[8 - j : RT + 8 - j] * usable)
            act = total * jax.nn.sigmoid(total)
            cs_ref[rows, c] = total
            act_ref[rows, c] = act
            low_ref[rows, c] = act.astype(bf16)
            gate = gate_ref[rows, c]
            passed = gg_ref[rows, c] * (gate * jax.nn.sigmoid(gate))
            g_ref[rows, c] = passed.astype(bf16).astype(f32)

        row_tiles(T, tile)
        proj_ref[...] += lax.dot_general(low_ref[:, c], wts_ref[k], NT, preferred_element_type=f32)

    @pl.when(i == pl.num_programs(0) - 1)
    def _():
        dims = (128, TC * N)
        source = lax.broadcasted_iota(jnp.int32, dims, 0)
        state = lax.rem(lax.broadcasted_iota(jnp.int32, dims, 1), N)
        diag = same_step(N, T)
        high = proj_ref[...].astype(bf16)
        low = (proj_ref[...] - high.astype(f32)).astype(bf16)
        ones = jnp.ones((TC, 128), bf16)
        for ref, start in ((bb_ref, L.R), (cc_ref, L.R + N)):
            spread = (source == state + start).astype(f32).astype(bf16)
            for part, held in ((high, hi_ref), (low, lo_ref)):
                wide = jnp.dot(part, spread, preferred_element_type=f32)
                held[...] = jnp.where(diag, wide, 0.0).astype(bf16)

            def expand(c, unused, ref=ref):
                rows = pl.ds(pl.multiple_of(c * TC, TC), TC)
                total = lax.dot_general(hi_ref[rows, :], ones, TN, preferred_element_type=f32)
                total = total + lax.dot_general(lo_ref[rows, :], ones, TN, preferred_element_type=f32)
                ref[pl.ds(pl.multiple_of(c * TC * N, TC * N), TC * N), :] = total
                return unused

            lax.fori_loop(0, T // TC, expand, 0)


def front(L, lengths, tokens, halo, gain, in_weight, out_weight, cot, par, wts):
    T, D = tokens.shape
    E = out_weight.shape[0]
    sub = 2
    wide = EB * sub
    steps = E // wide
    N = L.N
    arrays = [shape(f32, T, E)] * 5
    return pl.pallas_call(
        functools.partial(front_kernel, L),
        grid=(steps,),
        in_specs=[
            pl.BlockSpec(memory_space=pltpu.SMEM),
            whole(T, D), whole(HALO, D), whole(D), cols(D, wide), cols(D, wide, steps),
            tall(wide, D), whole(T, D), lead(PAR, EB, sub), lead(WTS, EB, sub),
        ],
        out_specs=[whole(T + 8, 8), whole(T, D), cols(T + HALO, wide)] + [cols(T, wide)] * 5 + [
            whole(T, 128), whole(T * N, 128), whole(T * N, 128),
        ],
        out_shape=[shape(f32, T + 8, 8), shape(bf16, T, D), shape(bf16, T + HALO, E)] + arrays + [
            shape(f32, T, 128), shape(f32, T * N, 128), shape(f32, T * N, 128),
        ],
        scratch_shapes=[
            pltpu.VMEM((HALO, D), bf16),
            pltpu.VMEM((T + HALO, wide), f32),
            pltpu.VMEM((T, wide), bf16),
            pltpu.VMEM((T, TC * N), bf16),
            pltpu.VMEM((T, TC * N), bf16),
        ],
        compiler_params=params(),
        name="front",
    )(lengths, tokens, halo, gain, in_weight, in_weight, out_weight, cot, par, wts)


def rates(L, par_ref):
    return -jnp.exp(par_ref[0, L.decay : L.decay + L.N, :]) * LOG2E


def lane_tiles(values):
    return [values[:, k * 128 : (k + 1) * 128] for k in range(EB // 128)]


def row_at(ref, t):
    return lane_tiles(ref[pl.ds(t, 1), :])


def ahead_of(steps, fetch):
    steps = list(steps)
    loaded = [fetch(j) for j in steps[:2]]
    for k, j in enumerate(steps):
        if k + 2 < len(steps):
            loaded.append(fetch(steps[k + 2]))
        yield j, loaded[k]


def softplus(x):
    return jnp.maximum(x, 0.0) + jnp.log1p(jnp.exp(-jnp.abs(x)))


def pre_kernel(
    L, count, proj_ref, par_ref, wts_ref, act_ref, g_ref, marks_ref, b_ref, c_ref,
    spre_ref, dtk_ref, u_ref, enter_ref, arrive_ref, ahead_ref, behind_ref, got_ref,
    send_sem, recv_sem,
):
    T, E = act_ref.shape[0], enter_ref.shape[1]
    N = L.N
    i = pl.program_id(0)
    blocks = E // EB
    si, ci = lax.axis_index("seq"), lax.axis_index("chan")

    @pl.when(i == 0)
    def _():
        barrier = pltpu.get_barrier_semaphore()
        for k in range(1, count):
            pl.semaphore_signal(
                barrier, inc=1, device_id=(si, lax.rem(ci + k, count)),
                device_id_type=pl.DeviceIdType.MESH,
            )
        pl.semaphore_wait(barrier, count - 1)

    low = proj_ref[:, 0 : L.R].astype(bf16)
    weights = wts_ref[0, L.step : L.step + L.R, :]
    bias = par_ref[0, L.step_b : L.step_b + 1, :]
    spre_ref[...] = jnp.dot(low, weights, preferred_element_type=f32) + bias

    def tile(r):
        rows = pl.ds(r, RT)
        step = softplus(spre_ref[rows, :])
        u_ref[rows, :] = step * act_ref[rows, :]
        dtk_ref[rows, :] = step + marks_ref[rows, 3:4]

    row_tiles(T, tile)
    rate = lane_tiles(rates(L, par_ref))
    tiles = len(rate)

    def chunk(c, carry):
        h, through, head = (list(carry[k * tiles : (k + 1) * tiles]) for k in range(3))
        base = pl.multiple_of(c * TC, TC)

        def fetch(j):
            at = pl.ds(pl.multiple_of((base + j) * N, N), N)
            return [row_at(ref, base + j) for ref in (dtk_ref, u_ref, g_ref)] + [b_ref[at, :], c_ref[at, :]]

        for j, (d, u, g, b_now, c_now) in ahead_of(range(TC), fetch):
            for k in range(tiles):
                factor = jnp.exp2(d[k] * rate[k])
                h[k] = factor * h[k] + b_now * u[k]
                through[k] = factor * through[k]
                head[k] = head[k] + through[k] * (c_now * g[k])
        return tuple(h + through + head)

    zero = jnp.zeros((N, 128), f32)
    out = lax.fori_loop(0, T // TC, chunk, (zero,) * tiles + (zero + 1.0,) * tiles + (zero,) * tiles)
    h, through, head = (jnp.concatenate(out[k * tiles : (k + 1) * tiles], axis=1) for k in range(3))
    zero = jnp.zeros((N, EB), f32)
    ahead_ref[i, 0:N, :] = h
    ahead_ref[i, N:, :] = through
    behind_ref[i, 0:N, :] = head
    behind_ref[i, N:, :] = through

    def send(b, k, forward):
        return pltpu.make_async_remote_copy(
            src_ref=(ahead_ref if forward else behind_ref).at[b], dst_ref=got_ref.at[count - k, b],
            send_sem=send_sem.at[k, b], recv_sem=recv_sem.at[count - k, b],
            device_id=(si, lax.rem(ci + k, count)), device_id_type=pl.DeviceIdType.MESH,
        )

    for k in range(1, count):
        @pl.when(ci + k < count)
        def _(k=k):
            send(i, k, True).start()

        @pl.when(ci + k >= count)
        def _(k=k):
            send(i, k, False).start()

    @pl.when(i == blocks - 1)
    def _():
        for b in range(blocks):
            for k in range(1, count):
                send(b, k, True).wait()
        for b in range(blocks):
            span = slice(b * EB, (b + 1) * EB)
            entering, arriving = zero, zero
            for k in range(1, count):
                before = ci + k >= count
                got = got_ref[k, b]
                entering = jnp.where(before, got[0:N] + got[N:] * entering, entering)
            for k in range(count - 1, 0, -1):
                behind = ci + k < count
                got = got_ref[k, b]
                arriving = jnp.where(behind, got[0:N] + got[N:] * arriving, arriving)
            enter_ref[:, span] = entering
            arrive_ref[:, span] = arriving


def pre_scan(L, count, proj, par, wts, act, g, marks, b_cols, c_cols):
    T, E = act.shape
    N = L.N
    blocks = E // EB
    state = shape(f32, N, E)
    return pl.pallas_call(
        functools.partial(pre_kernel, L, count),
        grid=(blocks,),
        in_specs=[
            whole(T, 128), lead(PAR, EB), lead(WTS, EB), cols(T), cols(T), whole(*marks.shape),
            once(*b_cols.shape), once(*c_cols.shape),
        ],
        out_specs=[cols(T)] * 3 + [whole(N, E)] * 2,
        out_shape=[shape(f32, T, E)] * 3 + [state] * 2,
        scratch_shapes=[
            pltpu.VMEM((blocks, 2 * N, EB), f32),
            pltpu.VMEM((blocks, 2 * N, EB), f32),
            pltpu.VMEM((count, blocks, 2 * N, EB), f32),
            pltpu.SemaphoreType.DMA((count, blocks)),
            pltpu.SemaphoreType.DMA((count, blocks)),
        ],
        compiler_params=params(collective_id=2, has_side_effects=True),
        name="pre_scan",
    )(proj, par, wts, act, g, marks, b_cols, c_cols)


def fold_rows(refs, r):
    sums = []
    for ref in refs:
        parts = [ref[pl.ds(r * 8 + k, 8, stride=8), :] for k in range(8)]
        while len(parts) > 1:
            parts = [x + y for x, y in zip(parts[::2], parts[1::2])]
        sums.append(parts[0])
    return jnp.concatenate(sums, axis=1)


def halves(values):
    return values[0:8] + values[8:16]


def lane_sums(states, acc_ref, out_ref, chunks):
    width = TC * states
    ones = jnp.ones((TC, 128), bf16)

    def step(c, unused):
        rows = pl.ds(pl.multiple_of(c * width, width), width)
        out_ref[pl.ds(pl.multiple_of(c * TC, TC), TC), :] = lax.dot_general(
            ones, acc_ref[rows, :].astype(bf16), NT, preferred_element_type=f32
        )
        return unused

    lax.fori_loop(0, chunks, step, 0)


def fwd_kernel(
    L, dtk_ref, u_ref, b_ref, c_ref, g_ref, par_ref, hin_ref, act_ref, gate_ref, gg_ref,
    wo_ref, cot_ref, tok_ref, normed_ref, wg_ref,
    h_ref, gc_ref, block_ref, gout_ref, gin_ref, gn_ref,
    acc_ref, gated_ref, ggate_ref, branch_ref, *y_refs,
):
    rate = lane_tiles(rates(L, par_ref))
    T, states = u_ref.shape[0], L.N
    chunks = T // TC
    width = TC * states
    i = pl.program_id(0)

    @pl.when(i == 0)
    def _():
        acc_ref[...] = jnp.zeros_like(acc_ref)
        gn_ref[...] = jnp.zeros_like(gn_ref)
        branch_ref[...] = jnp.zeros_like(branch_ref)

    h_ref[0:states, :] = hin_ref[...].astype(bf16)

    def chunk(c, carry):
        h = list(carry)
        base = pl.multiple_of(c * TC, TC)
        row = pl.multiple_of(c * width, width)

        def fetch(j):
            at = pl.ds(row + j * states, states)
            rows = [row_at(ref, base + j) for ref in (dtk_ref, u_ref, g_ref)]
            return rows + [b_ref[at, :], c_ref[at, :], acc_ref[at, :]]

        for j, (d, u, g, b_now, c_now, acc) in ahead_of(range(TC), fetch):
            for k in range(len(h)):
                h[k] = jnp.exp2(d[k] * rate[k]) * h[k] + b_now * u[k]
                h_ref[pl.ds(row + (j + 1) * states, states), k * 128 : (k + 1) * 128] = h[k].astype(bf16)
                y_refs[k][pl.ds((base + j) * 8, 8), :] = halves(c_now * h[k])
                acc = acc + h[k] * g[k]
            acc_ref[pl.ds(row + j * states, states), :] = acc
        return tuple(h)

    lax.fori_loop(0, chunks, chunk, tuple(lane_tiles(hin_ref[...])))
    skip = par_ref[0, L.skip : L.skip + 1, :]

    def tile(k, unused):
        rows = pl.ds(pl.multiple_of(k * 16, 16), 16)
        y = jnp.concatenate([fold_rows(y_refs, k * 16), fold_rows(y_refs, k * 16 + 8)], axis=0)
        mixer = (y + skip * act_ref[rows, :]).astype(bf16).astype(f32)
        gate = gate_ref[rows, :]
        sig = jax.nn.sigmoid(gate)
        gated_ref[rows, :] = (mixer * (gate * sig)).astype(bf16)
        ggate_ref[rows, :] = (gg_ref[rows, :] * mixer * sig * (1.0 + gate * (1.0 - sig))).astype(bf16)
        return unused

    lax.fori_loop(0, T // 16, tile, 0)
    branch_ref[...] += jnp.dot(gated_ref[...], wo_ref[...], preferred_element_type=f32)
    gout_ref[...] = lax.dot_general(
        gated_ref[...], cot_ref[...], TN, preferred_element_type=f32
    ).astype(bf16)
    gin_ref[...] = lax.dot_general(
        ggate_ref[...], normed_ref[...], TN, preferred_element_type=f32
    ).astype(bf16)
    gn_ref[...] += lax.dot_general(ggate_ref[...], wg_ref[...], NT, preferred_element_type=f32)

    @pl.when(i == pl.num_programs(0) - 1)
    def _():
        block_ref[...] = (tok_ref[...].astype(f32) + branch_ref[...]).astype(bf16)
        lane_sums(states, acc_ref, gc_ref, chunks)


def fwd_scan(L, dtk, u, b_cols, c_cols, g, par, entering, act, gate, gg, out_weight, cot, tokens, normed, in_weight):
    T, E = dtk.shape
    D = tokens.shape[1]
    N = L.N
    rows = (T + 1) * N
    blocks = E // EB
    return pl.pallas_call(
        functools.partial(fwd_kernel, L),
        grid=(blocks,),
        in_specs=[
            cols(T), cols(T), once(*b_cols.shape), once(*c_cols.shape), cols(T), lead(PAR, EB), cols(N),
            cols(T), cols(T), cols(T), tall(EB, D), whole(T, D), whole(T, D), whole(T, D),
            cols(D, EB, blocks),
        ],
        out_specs=[
            cols(rows), whole(T, TC * N), whole(T, D), tall(EB, D), tall(EB, D, blocks), whole(T, D),
        ],
        out_shape=[
            shape(bf16, rows, E), shape(f32, T, TC * N), shape(bf16, T, D), shape(bf16, E, D),
            shape(bf16, 2 * E, D), shape(f32, T, D),
        ],
        scratch_shapes=[
            pltpu.VMEM((T * N, 128), f32), pltpu.VMEM((T, EB), bf16), pltpu.VMEM((T, EB), bf16),
            pltpu.VMEM((T, D), f32),
        ] + [pltpu.VMEM((T * 8, 128), f32)] * (EB // 128),
        compiler_params=params(),
        name="fwd_scan",
    )(dtk, u, b_cols, c_cols, g, par, entering, act, gate, gg, out_weight, cot, tokens, normed, in_weight)


def bwd_kernel(
    L, dtk_ref, u_ref, g_ref, b_ref, c_ref, par_ref, wts_ref, fin_ref, h_ref, spre_ref, act_ref, proj_ref,
    gc_ref, gap_ref, chan_ref, gproj_ref, acc_ref, gb_ref, rank_ref, pre_ref, *part_refs,
):
    rate = lane_tiles(rates(L, par_ref))
    tiles = len(rate)
    bsum_refs, wsum_refs = part_refs[:tiles], part_refs[tiles:]
    T, states = u_ref.shape[0], L.N
    chunks = T // TC
    width = TC * states
    i = pl.program_id(0)

    @pl.when(i == 0)
    def _():
        acc_ref[...] = jnp.zeros_like(acc_ref)
        rank_ref[...] = jnp.zeros_like(rank_ref)

    def chunk(i, carry):
        flow, total = list(carry[:tiles]), list(carry[tiles:])
        c = chunks - 1 - i
        base = pl.multiple_of(c * TC, TC)
        row = pl.multiple_of(c * width, width)

        def fetch(j):
            at = pl.ds(row + j * states, states)
            rows = [row_at(ref, base + j) for ref in (dtk_ref, u_ref, g_ref)]
            return rows + [b_ref[at, :], c_ref[at, :], acc_ref[at, :], lane_tiles(h_ref[at, :])]

        for j, (d, u, g, b_now, c_now, acc, before) in ahead_of(reversed(range(TC)), fetch):
            part = pl.ds((base + j) * 8, 8)
            for k in range(tiles):
                adj = c_now * g[k] + flow[k]
                flow[k] = jnp.exp2(d[k] * rate[k]) * adj
                wr = flow[k] * before[k].astype(f32) * rate[k]
                total[k] = total[k] + wr * d[k]
                wsum_refs[k][part, :] = halves(wr)
                bsum_refs[k][part, :] = halves(adj * b_now)
                acc = acc + adj * u[k]
            acc_ref[pl.ds(row + j * states, states), :] = acc
        return tuple(flow) + tuple(total)

    none = jnp.zeros((states, 128), f32)
    out = lax.fori_loop(0, chunks, chunk, tuple(lane_tiles(fin_ref[...])) + (none,) * tiles)
    total = jnp.concatenate(out[tiles:], axis=1)
    skip = par_ref[0, L.skip : L.skip + 1, :]

    def tile(k, carry):
        bias_sum, skip_sum = carry
        rows = pl.ds(pl.multiple_of(k * 16, 16), 16)
        bsum, wsum = (
            jnp.concatenate([fold_rows(refs, k * 16), fold_rows(refs, k * 16 + 8)], axis=0)
            for refs in (bsum_refs, wsum_refs)
        )
        spre, act, g = spre_ref[rows, :], act_ref[rows, :], g_ref[rows, :]
        grad = (wsum * (1.0 / LOG2E) + act * bsum) * jax.nn.sigmoid(spre)
        gap_ref[rows, :] = g * skip + softplus(spre) * bsum
        pre_ref[rows, :] = grad.astype(bf16)
        bias_sum = bias_sum + halves(grad)
        skip_sum = skip_sum + halves(g * act)
        return bias_sum, skip_sum

    none = jnp.zeros((8, EB), f32)
    bias_sum, skip_sum = lax.fori_loop(0, T // 16, tile, (none, none))
    R = L.R
    pre = pre_ref[...]
    step_low = proj_ref[...].astype(bf16)
    grad_step_w = lax.dot_general(step_low, pre, TN, preferred_element_type=f32)
    chan_ref[0] = jnp.concatenate(
        [
            grad_step_w[0:R],
            total * (1.0 / LOG2E),
            jnp.sum(bias_sum, axis=0, keepdims=True),
            jnp.sum(skip_sum, axis=0, keepdims=True),
            jnp.zeros((128 - R - states - 2, EB), f32),
        ],
        axis=0,
    ).astype(bf16)
    weights = wts_ref[0, L.step : L.step + R, :].astype(f32)
    weights = jnp.concatenate([weights, jnp.zeros((128 - R, EB), f32)], axis=0).astype(bf16)
    rank_ref[...] += lax.dot_general(pre, weights, NT, preferred_element_type=f32)

    @pl.when(i == pl.num_programs(0) - 1)
    def _():
        lane_sums(states, acc_ref, gb_ref, chunks)
        dims = (width, 128)
        state = lax.rem(lax.broadcasted_iota(jnp.int32, dims, 0), states)
        target = lax.broadcasted_iota(jnp.int32, dims, 1)
        diag = same_step(states, T)
        sums = rank_ref[...]
        for ref, start in ((gb_ref, R), (gc_ref, R + states)):
            fold = (target == state + start).astype(f32)
            kept = jnp.where(diag, ref[...], 0.0)
            sums = sums + jnp.dot(
                kept, fold, precision=lax.Precision.HIGHEST, preferred_element_type=f32
            )
        gproj_ref[...] = sums.astype(bf16)


def bwd_scan(L, dtk, u, g, b_cols, c_cols, par, wts, arriving, held, spre, act, proj, grad_c):
    T, E = dtk.shape
    N = L.N
    blocks = E // EB
    return pl.pallas_call(
        functools.partial(bwd_kernel, L),
        grid=(blocks,),
        in_specs=[
            cols(T), cols(T), cols(T), once(*b_cols.shape), once(*c_cols.shape), lead(PAR, EB),
            lead(WTS, EB), cols(N), cols(held.shape[0]), cols(T), cols(T), whole(T, 128), whole(T, TC * N),
        ],
        out_specs=[cols(T), lead(128, EB), whole(T, 128)],
        out_shape=[shape(f32, T, E), shape(bf16, blocks, 128, EB), shape(bf16, T, 128)],
        scratch_shapes=[
            pltpu.VMEM((T * N, 128), f32),
            pltpu.VMEM((T, TC * N), f32), pltpu.VMEM((T, 128), f32), pltpu.VMEM((T, EB), bf16),
        ] + [pltpu.VMEM((T * 8, 128), f32)] * (2 * EB // 128),
        compiler_params=params(),
        name="bwd_scan",
    )(dtk, u, g, b_cols, c_cols, par, wts, arriving, held, spre, act, proj, grad_c)


def conv_kernel(L, gap_ref, gproj_ref, wts_ref, act_ref, cs_ref, inner_ref, marks_ref, gc_ref, chan_ref, xs_ref):
    T = gap_ref.shape[0]
    K, wide = L.K, L.R + 2 * L.N
    weights = wts_ref[0].astype(f32)
    row = lax.broadcasted_iota(jnp.int32, weights.shape, 0)
    weights = jnp.where(row < wide, weights, 0.0).astype(bf16)
    gc_ref[...] = jnp.dot(gproj_ref[...], weights, preferred_element_type=f32)
    act_low = act_ref[...].astype(bf16)
    grad_proj = lax.dot_general(gproj_ref[...], act_low, TN, preferred_element_type=f32)
    xs_ref[...] = inner_ref[...].astype(f32)

    def tile(k, carry):
        r = pl.multiple_of(k * RT, RT)
        rows = pl.ds(r, RT)
        total = cs_ref[rows, :]
        sig = jax.nn.sigmoid(total)
        grad = (gc_ref[rows, :] + gap_ref[rows, :]) * sig * (1.0 + total * (1.0 - sig))
        gc_ref[rows, :] = grad
        block = xs_ref[pl.ds(pl.multiple_of(r + HALO - 8, 8), RT + 8), :]
        out = [carry[K] + jnp.sum(grad.reshape(RT // 8, 8, EB), axis=0)]
        for j in range(K):
            part = grad * block[8 - j : RT + 8 - j]
            if j > 0:
                part = part * marks_ref[rows, j - 1 : j]
            out.insert(0, carry[K - 1 - j] + jnp.sum(part.reshape(RT // 8, 8, EB), axis=0))
        return tuple(out)

    none = jnp.zeros((8, EB), f32)
    sums = lax.fori_loop(0, T // RT, tile, (none,) * (K + 1))
    chan_ref[0] = jnp.concatenate(
        [grad_proj[0:wide]]
        + [jnp.sum(s, axis=0, keepdims=True) for s in sums]
        + [jnp.zeros((128 - wide - K - 1, EB), f32)],
        axis=0,
    ).astype(bf16)


def conv_back(L, gap, gproj, wts, act, cs, inner, marks):
    T, E = gap.shape
    blocks = E // EB
    return pl.pallas_call(
        functools.partial(conv_kernel, L),
        grid=(blocks,),
        in_specs=[
            cols(T), whole(T, 128), lead(WTS, EB), cols(T), cols(T), cols(T + HALO), whole(*marks.shape),
        ],
        out_specs=[cols(T), lead(128, EB)],
        out_shape=[shape(f32, T, E), shape(bf16, blocks, 128, EB)],
        scratch_shapes=[pltpu.VMEM((T + HALO, EB), f32)],
        compiler_params=params(),
        name="conv_back",
    )(gap, gproj, wts, act, cs, inner, marks)


def tail_kernel(
    L, gc_ref, after_ref, par_ref, marks_ref, normed_ref, wi_ref, gn_ref, tok_ref, cot_ref, gain_ref,
    held_ref, gin_ref, gtok_ref, ggain_ref, ext_ref, low_ref, sum_ref,
):
    T, D = tok_ref.shape
    K = L.K
    i = pl.program_id(0)
    ext_ref[0:T, :] = gc_ref[...]
    ext_ref[T : T + 8, :] = after_ref[...]
    taps = [par_ref[0, L.conv + j : L.conv + j + 1, :] for j in range(K)]

    def tile(r):
        block = ext_ref[pl.ds(r, RT + 8), :]
        marks = marks_ref[pl.ds(r, RT + 8), :]
        total = taps[K - 1] * block[0:RT]
        for j in range(1, K):
            masked = block * marks[:, j - 1 : j]
            total = total + taps[K - 1 - j] * masked[j : RT + j]
        low_ref[pl.ds(r, RT), :] = total.astype(bf16)

    row_tiles(T, tile)
    gin_ref[...] = lax.dot_general(
        low_ref[...], normed_ref[...], TN, preferred_element_type=f32
    ).astype(bf16)
    part = lax.dot_general(low_ref[...], wi_ref[...], NT, preferred_element_type=f32)

    @pl.when(i == 0)
    def _():
        sum_ref[...] = gn_ref[...] + part

    @pl.when(i > 0)
    def _():
        sum_ref[...] += part

    @pl.when(i == pl.num_programs(0) - 1)
    def _():
        gain = gain_ref[...].reshape(1, D)

        def last(k, total):
            rows = pl.ds(pl.multiple_of(k * 16, 16), 16)
            x = tok_ref[rows, :].astype(f32)
            grad = sum_ref[rows, :]
            inv = lax.rsqrt(jnp.mean(x * x, axis=1, keepdims=True) + epsilon)
            scaled = grad * gain
            mean = jnp.mean(x * scaled, axis=1, keepdims=True)
            gtok_ref[rows, :] = (
                cot_ref[rows, :].astype(f32) + inv * scaled - x * (inv * inv * inv * mean)
            )
            return total + jnp.sum((grad * x * inv).reshape(2, 8, D), axis=0)

        total = lax.fori_loop(0, T // 16, last, jnp.zeros((8, D), f32))
        ggain_ref[...] = jnp.sum(total, axis=0, keepdims=True)


def tail(L, gc, after, par, marks, normed, in_weight, gn, tokens, cot, gain, held):
    T, E = gc.shape
    D = tokens.shape[1]
    blocks = E // EB
    return pl.pallas_call(
        functools.partial(tail_kernel, L),
        grid=(blocks,),
        in_specs=[
            cols(T), cols(8), lead(PAR, EB), whole(*marks.shape), whole(T, D), cols(D), whole(T, D),
            whole(T, D), whole(T, D), whole(D), pl.BlockSpec(memory_space=pl.ANY),
        ],
        out_specs=[tall(EB, D), whole(T, D), whole(1, D)],
        out_shape=[shape(bf16, 2 * E, D), shape(f32, T, D), shape(f32, 1, D)],
        scratch_shapes=[
            pltpu.VMEM((T + 8, EB), f32), pltpu.VMEM((T, EB), bf16), pltpu.VMEM((T, D), f32),
        ],
        input_output_aliases={10: 0},
        compiler_params=params(),
        name="tail",
    )(gc, after, par, marks, normed, in_weight, gn, tokens, cot, gain, held)


def sum_plan(chan_count, seq_count):
    chan_bits = [("chan", 1 << i) for i in range(chan_count.bit_length() - 1)]
    seq_bits = [("seq", 1 << i) for i in range(seq_count.bit_length() - 1)]
    return chan_bits, seq_bits


def sum_kernel(chan_count, seq_count, pieces, arrays, *refs):
    piece_rows = 16 * seq_count
    x_refs, o_refs = refs[:arrays], refs[arrays : 2 * arrays]
    chan_bits, seq_bits = sum_plan(chan_count, seq_count)
    nc, ns = len(chan_bits), len(seq_bits)
    stages = nc + ns
    count = len(pieces)
    scratch = refs[2 * arrays :]
    held = [scratch[p * stages : (p + 1) * stages] for p in range(count)]
    send_sem, recv_sem = scratch[count * stages :]
    mine = {"seq": lax.axis_index("seq"), "chan": lax.axis_index("chan")}

    def bit_of(name, bit):
        return (mine[name] // bit) % 2

    def partner(name, bit):
        other = dict(mine)
        other[name] = mine[name] + bit - 2 * bit * bit_of(name, bit)
        return (other["seq"], other["chan"])

    def order(p):
        inner = chan_bits if p % 2 == 0 else chan_bits[::-1]
        return seq_bits[:1] + inner + seq_bits[1:]

    barrier = pltpu.get_barrier_semaphore()
    for name, bit in chan_bits + seq_bits:
        pl.semaphore_signal(
            barrier, inc=1, device_id=partner(name, bit), device_id_type=pl.DeviceIdType.MESH
        )
    pl.semaphore_wait(barrier, stages)

    def parts(p, s, keep):
        name, bit = order(p)[s]
        side = bit_of(name, bit) if keep else 1 - bit_of(name, bit)
        done = order(p)[:s]
        size = piece_rows >> sum(1 for n, b in done if n == "seq")
        ref, start = (x_refs[pieces[p][0]], pieces[p][1]) if s == 0 else (held[p][s - 1], 0)
        if name == "seq":
            rows = pl.ds(pl.multiple_of(start + side * (size // 2), 16), size // 2)
            return [ref.at[:, rows, :]]
        left = [b for n, b in chan_bits if ("chan", b) not in done]
        low = 1 << left.index(bit)
        return [
            ref.at[pl.ds((i // low) * 2 * low + side * low + i % low, 1), pl.ds(start, size), :]
            for i in range((1 << len(left)) // 2)
        ]

    def landing(p, s):
        dst = held[p][s]
        if order(p)[s][0] == "seq":
            return [dst]
        return [dst.at[pl.ds(i, 1)] for i in range(dst.shape[0])]

    def copies(p, s):
        return [
            pltpu.make_async_remote_copy(
                src_ref=src, dst_ref=dst, send_sem=send_sem.at[p, s, i], recv_sem=recv_sem.at[p, s, i],
                device_id=partner(*order(p)[s]), device_id_type=pl.DeviceIdType.MESH,
            )
            for i, (src, dst) in enumerate(zip(parts(p, s, False), landing(p, s)))
        ]

    def my_rows(p, done):
        start, size = pieces[p][1], piece_rows
        for name, bit in seq_bits[:done]:
            size //= 2
            start = start + bit_of(name, bit) * size
        return pl.ds(pl.multiple_of(start, 16), size)

    def gather_copy(p, k):
        place = o_refs[pieces[p][0]].at[my_rows(p, ns - k), :]
        return pltpu.make_async_remote_copy(
            src_ref=place, dst_ref=place,
            send_sem=send_sem.at[p, stages + k, 0], recv_sem=recv_sem.at[p, stages + k, 0],
            device_id=partner(*seq_bits[ns - 1 - k]), device_id_type=pl.DeviceIdType.MESH,
        )

    total = stages + ns
    for tick in range((count + 1) // 2 + total):
        for p in range(count):
            s = tick - p // 2
            if not 0 <= s <= total:
                continue
            if 1 <= s <= stages:
                for copy in copies(p, s - 1):
                    copy.wait_recv()
                for src, dst in zip(parts(p, s - 1, True), landing(p, s - 1)):
                    dst[...] = (dst[...].astype(f32) + src[...].astype(f32)).astype(bf16)
                if s == stages:
                    o_refs[pieces[p][0]][my_rows(p, ns), :] = held[p][stages - 1][0]
            elif s > stages:
                gather_copy(p, s - 1 - stages).wait_recv()
            if s < stages:
                for copy in copies(p, s):
                    copy.start()
            elif s < total:
                gather_copy(p, s - stages).start()
    for p in range(count):
        for s in range(stages):
            for copy in copies(p, s):
                copy.wait_send()
        for k in range(ns):
            gather_copy(p, k).wait_send()


def sum_owned(arrays, seq_count):
    chan_count = arrays[0].shape[0]
    chan_bits, seq_bits = sum_plan(chan_count, seq_count)
    piece_rows = 16 * seq_count
    pieces = [(a, r) for a, v in enumerate(arrays) for r in range(0, v.shape[1], piece_rows)]
    ordered = seq_bits[:1] + chan_bits + seq_bits[1:]
    scratch = []
    for a, r in pieces:
        owners, size = chan_count, piece_rows
        for name, bit in ordered:
            if name == "chan":
                owners //= 2
            else:
                size //= 2
            scratch.append(pltpu.VMEM((owners, size, arrays[a].shape[2]), bf16))
    total = len(ordered) + len(seq_bits)
    sems = pltpu.SemaphoreType.DMA((len(pieces), total, max(1, chan_count // 2)))
    vmem = pl.BlockSpec(memory_space=pltpu.VMEM)
    return pl.pallas_call(
        functools.partial(sum_kernel, chan_count, seq_count, pieces, len(arrays)),
        in_specs=[vmem] * len(arrays),
        out_specs=[vmem] * len(arrays),
        out_shape=[shape(bf16, *v.shape[1:]) for v in arrays],
        scratch_shapes=scratch + [sems, sems],
        compiler_params=params(collective_id=0, has_side_effects=True),
        name="sum_owned",
    )(*arrays)


def unpack_kernel(L, in_ref, out_ref, d_ref, e_ref, gin_ref, gout_ref, *refs):
    gin_ref[...] = in_ref[...].astype(f32).T
    gout_ref[...] = out_ref[...].astype(f32)
    d, e = d_ref[...].astype(f32), e_ref[...].astype(f32)
    R, N, K = L.R, L.N, L.K
    wide = R + 2 * N
    conv_w, conv_b, proj, step_w, step_b, decay, skip, gain = refs
    width = d.shape[1]
    step_w[...] = d[0:R]
    decay[...] = d[R : R + N]
    step_b[...] = d[R + N].reshape(width)
    skip[...] = d[R + N + 1].reshape(width)
    proj[...] = e[0:wide]
    conv_w[...] = e[wide : wide + K]
    conv_b[...] = e[wide + K].reshape(width)
    gain[...] = e[wide + K + 1].reshape(width)


def unpack(L, sums):
    width = sums[2].shape[1]
    rows, D = sums[0].shape
    R, N, K = L.R, L.N, L.K
    return pl.pallas_call(
        functools.partial(unpack_kernel, L),
        out_shape=[
            shape(f32, D, rows), shape(f32, *sums[1].shape), shape(f32, K, width), shape(f32, width),
            shape(f32, R + 2 * N, width), shape(f32, R, width), shape(f32, width),
            shape(f32, N, width), shape(f32, width), shape(f32, width),
        ],
        compiler_params=params(),
        name="unpack",
    )(*sums)


def local(
    tokens, norm_gain, in_weight, conv_weight, conv_bias, proj_weight, step_weight,
    step_bias, decay_log, skip_gain, out_weight, cotangent, lengths,
):
    T, D = tokens.shape
    E = in_weight.shape[1] // 2
    L = Layout(step_weight.shape[0], decay_log.shape[0], conv_weight.shape[0])
    ci = lax.axis_index("chan")
    cc = lax.axis_size("chan")
    sc = lax.axis_size("seq")
    blocks, share = E // EB, E // cc

    parts = (conv_weight, conv_bias, proj_weight.T, step_weight, step_bias, decay_log, skip_gain)
    wts, par, halo = gather_params(L, cc, parts, tokens)

    def by_block(values):
        if share == EB:
            return values
        values = jnp.moveaxis(values, 0, 1).reshape(-1, blocks, EB)
        return jnp.moveaxis(values, 1, 0)

    wts, par = by_block(wts), by_block(par)
    marks, normed, inner, gate, gg, g, cs, act, proj, b_cols, c_cols = front(
        L, lengths, tokens, halo, norm_gain, in_weight, out_weight, cotangent, par, wts
    )
    spre, dtk, u, entering, arriving = pre_scan(L, cc, proj, par, wts, act, g, marks, b_cols, c_cols)
    held, grad_c, block_out, grad_out, grad_in, gn = fwd_scan(
        L, dtk, u, b_cols, c_cols, g, par, entering, act, gate, gg, out_weight, cotangent, tokens,
        normed, in_weight,
    )
    gap, chan_d, gproj = bwd_scan(
        L, dtk, u, g, b_cols, c_cols, par, wts, arriving, held, spre, act, proj, grad_c
    )
    gc, chan_e = conv_back(L, gap, gproj, wts, act, cs, inner, marks)
    after = lax.ppermute(gc[0:8], "chan", [(k, k - 1) for k in range(1, cc)])
    grad_in, grad_tokens, grad_gain = tail(
        L, gc, after, par, marks, normed, in_weight, gn, tokens, cotangent, norm_gain, grad_in
    )

    def by_owner(values):
        if share == EB:
            return values
        values = jnp.moveaxis(values, 0, 1).reshape(128, cc, share)
        return jnp.moveaxis(values, 1, 0)

    chan_d, chan_e = by_owner(chan_d), by_owner(chan_e)
    row = L.R + 2 * L.N + L.K + 1
    owned_gain = jnp.pad(grad_gain.reshape(cc, 1, D // cc), ((0, 0), (0, 0), (0, share - D // cc)))
    chan_e = lax.dynamic_update_slice(chan_e, owned_gain.astype(bf16), (0, row, 0))
    arrays = [grad_in.reshape(cc, 2 * E // cc, D), grad_out.reshape(cc, share, D), chan_d, chan_e]
    piece = 16 * sc
    rows = [v.shape[1] for v in arrays]
    arrays = [jnp.pad(v, ((0, 0), (0, -v.shape[1] % piece), (0, 0))) for v in arrays]
    sums = sum_owned(arrays, sc)
    sums = [v[:r] for v, r in zip(sums, rows)]
    g_in, g_out, conv_w, conv_b, proj_w, step_w, step_b, decay, skip, g_gain = unpack(L, sums)
    return (
        block_out, grad_tokens, g_gain[: D // cc], g_in, conv_w, conv_b, proj_w.T, step_w,
        step_b, decay, skip, g_out,
    )


def solution(mesh):
    tok, row, vec = P(("seq", "chan"), None), P(None, "chan"), P("chan")
    in_specs = (
        tok, P(), P(), row, vec, P("chan", None), row, vec, row, vec, P(), tok, P("seq", None),
    )
    out_specs = (
        tok, tok, vec, row, row, vec, P("chan", None), row, vec, row, vec, P("chan", None),
    )
    return jax.shard_map(local, mesh=mesh, in_specs=in_specs, out_specs=out_specs, check_vma=False)
```

```python
import functools
import math

import jax
import jax.numpy as jnp
from jax import lax
from jax.experimental import pallas as pl
from jax.experimental.pallas import tpu as pltpu
from jax.sharding import PartitionSpec as P

epsilon = 1e-05
LOG2E = math.log2(math.e)
CUT = 1e30
TC = 16
EB = 384
RT = 32
BLOCK_SLOTS = 4
HALO = 16
PAR = 24
WTS = 128
f32 = jnp.float32
bf16 = jnp.bfloat16
NT = (((1,), (1,)), ((), ()))
TN = (((0,), (0,)), ((), ()))


def params(**more):
    return pltpu.CompilerParams(vmem_limit_bytes=60 * 1024 * 1024, **more)


def cols(rows, width=EB, shift=0):
    return pl.BlockSpec((rows, width), lambda i: (0, i + shift))


def tall(rows, width, shift=0):
    return pl.BlockSpec((rows, width), lambda i: (i + shift, 0))


def lead(rows, width, count=1):
    return pl.BlockSpec((count, rows, width), lambda i: (i, 0, 0))


def whole(*shape):
    return pl.BlockSpec(shape, lambda i: (0,) * len(shape))


def once(*shape):
    return pl.BlockSpec(shape, lambda i: (0,) * len(shape), pipeline_mode=pl.Buffered(1))


def shape(dtype, *dims):
    return jax.ShapeDtypeStruct(dims, dtype)


def row_tiles(count, body):
    def step(i, unused):
        body(pl.multiple_of(i * RT, RT))
        return unused

    lax.fori_loop(0, count // RT, step, 0)


def same_step(states, rows):
    dims = (rows, TC * states)
    here = lax.rem(lax.broadcasted_iota(jnp.int32, dims, 0), TC) * states
    place = lax.broadcasted_iota(jnp.int32, dims, 1)
    return (place >= here) & (place < here + states)


class Layout:
    def __init__(self, R, N, K):
        self.R, self.N, self.K = R, N, K
        self.step = R + 2 * N
        self.decay = 0
        self.conv = self.decay + N
        self.conv_b = self.conv + K
        self.step_b = self.conv_b + 1
        self.skip = self.step_b + 1
        self.end = self.skip + 1


def gather_kernel(
    L, count, cw_ref, cb_ref, pw_ref, sw_ref, sb_ref, dl_ref, sk_ref, tok_ref,
    wts_ref, par_ref, halo_ref, send_sem, recv_sem, halo_sems,
):
    si, ci = lax.axis_index("seq"), lax.axis_index("chan")
    T = tok_ref.shape[0]
    width = par_ref.shape[2]
    barrier = pltpu.get_barrier_semaphore()
    for k in range(1, count):
        pl.semaphore_signal(
            barrier, inc=1, device_id=(si, lax.rem(ci + k, count)),
            device_id_type=pl.DeviceIdType.MESH,
        )
    own, weights = par_ref.at[ci], wts_ref.at[ci]
    weights[...] = jnp.concatenate(
        [pw_ref[...].astype(f32), sw_ref[...].astype(f32)], axis=0
    ).astype(bf16)
    own[...] = jnp.concatenate(
        [
            dl_ref[...], cw_ref[...], cb_ref[...].reshape(1, width), sb_ref[...].reshape(1, width),
            sk_ref[...].reshape(1, width), jnp.zeros((PAR - L.end, width), f32),
        ],
        axis=0,
    )
    pl.semaphore_wait(barrier, count - 1)

    def share(ref, j, k):
        return pltpu.make_async_remote_copy(
            src_ref=ref, dst_ref=ref, send_sem=send_sem.at[j, k], recv_sem=recv_sem.at[j, k],
            device_id=(si, lax.rem(ci + k, count)), device_id_type=pl.DeviceIdType.MESH,
        )

    edge = pltpu.make_async_remote_copy(
        src_ref=tok_ref.at[pl.ds(T - HALO, HALO)], dst_ref=halo_ref,
        send_sem=halo_sems.at[0], recv_sem=halo_sems.at[1],
        device_id=(si, lax.rem(ci + 1, count)), device_id_type=pl.DeviceIdType.MESH,
    )
    edge.start()
    for j, ref in enumerate((own, weights)):
        for k in range(1, count):
            share(ref, j, k).start()
    edge.wait()
    for j, ref in enumerate((own, weights)):
        for k in range(1, count):
            share(ref, j, k).wait()


def gather_params(L, count, parts, tokens):
    width = parts[0].shape[1]
    T, D = tokens.shape
    vmem = pl.BlockSpec(memory_space=pltpu.VMEM)
    return pl.pallas_call(
        functools.partial(gather_kernel, L, count),
        in_specs=[vmem] * 8,
        out_specs=[vmem] * 3,
        out_shape=[shape(bf16, count, WTS, width), shape(f32, count, PAR, width), shape(bf16, HALO, D)],
        scratch_shapes=[
            pltpu.SemaphoreType.DMA((2, count)),
            pltpu.SemaphoreType.DMA((2, count)),
            pltpu.SemaphoreType.DMA((2,)),
        ],
        compiler_params=params(collective_id=1, has_side_effects=True),
        name="gather_params",
    )(*parts, tokens)


def front_kernel(
    L, len_ref, tok_ref, halo_ref, gain_ref, wi_ref, wg_ref, wo_ref, cot_ref, par_ref, wts_ref,
    marks_ref, normed_ref, inner_ref, gate_ref, gg_ref, g_ref, cs_ref, act_ref, proj_ref,
    bch_ref, cch_ref, hn_ref, xs_ref, low_ref,
):
    T = tok_ref.shape[0]
    N, K = L.N, L.K
    i = pl.program_id(0)

    def norm(x):
        x = x.astype(f32)
        inv = lax.rsqrt(jnp.mean(x * x, axis=1, keepdims=True) + epsilon)
        return (x * inv * gain_ref[...].reshape(1, x.shape[1])).astype(bf16)

    @pl.when(i == 0)
    def _():
        first = lax.axis_index("chan") == 0
        halo = jnp.where(first, jnp.zeros(halo_ref.shape, f32), halo_ref[...].astype(f32))
        hn_ref[...] = norm(halo)

        def tile(r):
            normed_ref[pl.ds(r, RT), :] = norm(tok_ref[pl.ds(r, RT), :])

        row_tiles(T, tile)
        proj_ref[...] = jnp.zeros_like(proj_ref)
        dims = marks_ref.shape
        place = lax.broadcasted_iota(jnp.int32, dims, 0) + lax.axis_index("chan") * T
        lane = lax.broadcasted_iota(jnp.int32, dims, 1)
        reach = jnp.where(lane < K - 1, lane + 1, 1)
        inside = jnp.zeros(dims, f32)
        start = jnp.int32(0)
        for k in range(len_ref.shape[1]):
            inside = jnp.where((start > place - reach) & (start <= place), 1.0, inside)
            start = start + len_ref[0, k]
        marks_ref[...] = jnp.where(lane < K - 1, 1.0 - inside, inside * CUT)

    low = jnp.dot(hn_ref[...], wi_ref[...], preferred_element_type=f32).astype(bf16)
    inner_ref[0:HALO, :] = low
    xs_ref[0:HALO, :] = low.astype(f32)
    low = jnp.dot(normed_ref[...], wi_ref[...], preferred_element_type=f32).astype(bf16)
    inner_ref[HALO:, :] = low
    xs_ref[HALO:, :] = low.astype(f32)
    gate_ref[...] = jnp.dot(normed_ref[...], wg_ref[...], preferred_element_type=f32)
    gg_ref[...] = lax.dot_general(cot_ref[...], wo_ref[...], NT, preferred_element_type=f32)

    for k in range(par_ref.shape[0]):
        c = slice(k * EB, (k + 1) * EB)
        taps = [par_ref[k, L.conv + j : L.conv + j + 1, :] for j in range(K)]
        bias = par_ref[k, L.conv_b : L.conv_b + 1, :]

        def tile(r, c=c, taps=taps, bias=bias):
            rows = pl.ds(r, RT)
            block = xs_ref[pl.ds(pl.multiple_of(r + HALO - 8, 8), RT + 8), c]
            total = bias + taps[K - 1] * block[8:]
            for j in range(1, K):
                usable = marks_ref[rows, j - 1 : j]
                total = total + taps[K - 1 - j] * (block[8 - j : RT + 8 - j] * usable)
            act = total * jax.nn.sigmoid(total)
            cs_ref[rows, c] = total
            act_ref[rows, c] = act
            low_ref[rows, c] = act.astype(bf16)
            gate = gate_ref[rows, c]
            passed = gg_ref[rows, c] * (gate * jax.nn.sigmoid(gate))
            g_ref[rows, c] = passed.astype(bf16).astype(f32)

        row_tiles(T, tile)
        proj_ref[...] += lax.dot_general(low_ref[:, c], wts_ref[k], NT, preferred_element_type=f32)

    @pl.when(i == pl.num_programs(0) - 1)
    def _():
        turned = proj_ref[...].T
        for ref, start in ((bch_ref, L.R), (cch_ref, L.R + N)):
            for j in range(T // TC):
                ref[j] = turned[start : start + N, j * TC : (j + 1) * TC]


def front(L, lengths, tokens, halo, gain, in_weight, out_weight, cot, par, wts):
    T, D = tokens.shape
    E = out_weight.shape[0]
    sub = 2
    wide = EB * sub
    steps = E // wide
    N = L.N
    arrays = [shape(f32, T, E)] * 5
    return pl.pallas_call(
        functools.partial(front_kernel, L),
        grid=(steps,),
        in_specs=[
            pl.BlockSpec(memory_space=pltpu.SMEM),
            whole(T, D), whole(HALO, D), whole(D), cols(D, wide), cols(D, wide, steps),
            tall(wide, D), whole(T, D), lead(PAR, EB, sub), lead(WTS, EB, sub),
        ],
        out_specs=[whole(T + 8, 8), whole(T, D), cols(T + HALO, wide)] + [cols(T, wide)] * 5 + [
            whole(T, 128), whole(T // TC, N, TC), whole(T // TC, N, TC),
        ],
        out_shape=[shape(f32, T + 8, 8), shape(bf16, T, D), shape(bf16, T + HALO, E)] + arrays + [
            shape(f32, T, 128), shape(f32, T // TC, N, TC), shape(f32, T // TC, N, TC),
        ],
        scratch_shapes=[
            pltpu.VMEM((HALO, D), bf16),
            pltpu.VMEM((T + HALO, wide), f32),
            pltpu.VMEM((T, wide), bf16),
        ],
        compiler_params=params(),
        name="front",
    )(lengths, tokens, halo, gain, in_weight, in_weight, out_weight, cot, par, wts)


def rates(L, par_ref):
    return -jnp.exp(par_ref[0, L.decay : L.decay + L.N, :]) * LOG2E


def lane_tiles(values):
    return [values[:, k * 128 : (k + 1) * 128] for k in range(EB // 128)]


def row_at(ref, t):
    return lane_tiles(ref[pl.ds(t, 1), :])


def spread(columns, j):
    return jnp.broadcast_to(columns[:, j : j + 1], (columns.shape[0], 128))


def ahead_of(steps, fetch):
    steps = list(steps)
    loaded = [fetch(j) for j in steps[:2]]
    for k, j in enumerate(steps):
        if k + 2 < len(steps):
            loaded.append(fetch(steps[k + 2]))
        yield j, loaded[k]


def softplus(x):
    return jnp.maximum(x, 0.0) + jnp.log1p(jnp.exp(-jnp.abs(x)))


def pre_kernel(
    L, count, proj_ref, par_ref, wts_ref, act_ref, g_ref, marks_ref, b_ref, c_ref,
    spre_ref, dtk_ref, u_ref, enter_ref, arrive_ref, ahead_ref, behind_ref, got_ref,
    send_sem, recv_sem,
):
    T, E = act_ref.shape[0], enter_ref.shape[1]
    N = L.N
    i = pl.program_id(0)
    blocks = E // EB
    si, ci = lax.axis_index("seq"), lax.axis_index("chan")

    @pl.when(i == 0)
    def _():
        barrier = pltpu.get_barrier_semaphore()
        for k in range(1, count):
            pl.semaphore_signal(
                barrier, inc=1, device_id=(si, lax.rem(ci + k, count)),
                device_id_type=pl.DeviceIdType.MESH,
            )
        pl.semaphore_wait(barrier, count - 1)

    low = proj_ref[:, 0 : L.R].astype(bf16)
    weights = wts_ref[0, L.step : L.step + L.R, :]
    bias = par_ref[0, L.step_b : L.step_b + 1, :]
    spre_ref[...] = jnp.dot(low, weights, preferred_element_type=f32) + bias

    def tile(r):
        rows = pl.ds(r, RT)
        step = softplus(spre_ref[rows, :])
        u_ref[rows, :] = step * act_ref[rows, :]
        dtk_ref[rows, :] = step + marks_ref[rows, 3:4]

    row_tiles(T, tile)
    rate = lane_tiles(rates(L, par_ref))
    tiles = len(rate)

    def chunk(c, carry):
        h, through, head = (list(carry[k * tiles : (k + 1) * tiles]) for k in range(3))
        base = pl.multiple_of(c * TC, TC)
        b_cols, c_cols = b_ref[c], c_ref[c]

        def fetch(j):
            rows = [row_at(ref, base + j) for ref in (dtk_ref, u_ref, g_ref)]
            return rows + [spread(b_cols, j), spread(c_cols, j)]

        for j, (d, u, g, b_now, c_now) in ahead_of(range(TC), fetch):
            for k in range(tiles):
                factor = jnp.exp2(d[k] * rate[k])
                h[k] = factor * h[k] + b_now * u[k]
                through[k] = factor * through[k]
                head[k] = head[k] + through[k] * (c_now * g[k])
        return tuple(h + through + head)

    zero = jnp.zeros((N, 128), f32)
    out = lax.fori_loop(0, T // TC, chunk, (zero,) * tiles + (zero + 1.0,) * tiles + (zero,) * tiles)
    h, through, head = (jnp.concatenate(out[k * tiles : (k + 1) * tiles], axis=1) for k in range(3))
    zero = jnp.zeros((N, EB), f32)
    ahead_ref[i, 0:N, :] = h
    ahead_ref[i, N:, :] = through
    behind_ref[i, 0:N, :] = head
    behind_ref[i, N:, :] = through

    def send(b, k, forward):
        return pltpu.make_async_remote_copy(
            src_ref=(ahead_ref if forward else behind_ref).at[b], dst_ref=got_ref.at[count - k, b],
            send_sem=send_sem.at[k, b], recv_sem=recv_sem.at[count - k, b],
            device_id=(si, lax.rem(ci + k, count)), device_id_type=pl.DeviceIdType.MESH,
        )

    for k in range(1, count):
        @pl.when(ci + k < count)
        def _(k=k):
            send(i, k, True).start()

        @pl.when(ci + k >= count)
        def _(k=k):
            send(i, k, False).start()

    @pl.when(i == blocks - 1)
    def _():
        for b in range(blocks):
            for k in range(1, count):
                send(b, k, True).wait()
        for b in range(blocks):
            span = slice(b * EB, (b + 1) * EB)
            entering, arriving = zero, zero
            for k in range(1, count):
                before = ci + k >= count
                got = got_ref[k, b]
                entering = jnp.where(before, got[0:N] + got[N:] * entering, entering)
            for k in range(count - 1, 0, -1):
                behind = ci + k < count
                got = got_ref[k, b]
                arriving = jnp.where(behind, got[0:N] + got[N:] * arriving, arriving)
            enter_ref[:, span] = entering
            arrive_ref[:, span] = arriving


def pre_scan(L, count, proj, par, wts, act, g, marks, b_cols, c_cols):
    T, E = act.shape
    N = L.N
    blocks = E // EB
    state = shape(f32, N, E)
    return pl.pallas_call(
        functools.partial(pre_kernel, L, count),
        grid=(blocks,),
        in_specs=[
            whole(T, 128), lead(PAR, EB), lead(WTS, EB), cols(T), cols(T), whole(*marks.shape),
            once(*b_cols.shape), once(*c_cols.shape),
        ],
        out_specs=[cols(T)] * 3 + [whole(N, E)] * 2,
        out_shape=[shape(f32, T, E)] * 3 + [state] * 2,
        scratch_shapes=[
            pltpu.VMEM((blocks, 2 * N, EB), f32),
            pltpu.VMEM((blocks, 2 * N, EB), f32),
            pltpu.VMEM((count, blocks, 2 * N, EB), f32),
            pltpu.SemaphoreType.DMA((count, blocks)),
            pltpu.SemaphoreType.DMA((count, blocks)),
        ],
        compiler_params=params(collective_id=2, has_side_effects=True),
        name="pre_scan",
    )(proj, par, wts, act, g, marks, b_cols, c_cols)


def fold_rows(refs, r):
    sums = []
    for ref in refs:
        parts = [ref[pl.ds(r * 8 + k, 8, stride=8), :] for k in range(8)]
        while len(parts) > 1:
            parts = [x + y for x, y in zip(parts[::2], parts[1::2])]
        sums.append(parts[0])
    return jnp.concatenate(sums, axis=1)


def halves(values):
    return values[0:8] + values[8:16]


def lane_sums(states, acc_ref, out_ref, chunks):
    width = TC * states
    ones = jnp.ones((TC, 128), bf16)
    group = chunks // 4
    for k in range(4):
        part = acc_ref[k * group * width : (k + 1) * group * width, :].astype(bf16)
        sums = lax.dot_general(ones, part, NT, preferred_element_type=f32)
        for c in range(group):
            row = (k * group + c) * TC
            out_ref[row : row + TC, :] = sums[:, c * width : (c + 1) * width]


def fwd_kernel(
    L, dtk_ref, u_ref, b_ref, c_ref, g_ref, par_ref, hin_ref, act_ref, gate_ref, gg_ref,
    wo_ref, cot_ref, tok_ref, normed_ref, wg_ref,
    h_ref, gc_ref, block_ref, gout_ref, gin_ref, gn_ref,
    acc_ref, gated_ref, ggate_ref, branch_ref, *y_refs,
):
    rate = lane_tiles(rates(L, par_ref))
    T, states = u_ref.shape[0], L.N
    chunks = T // TC
    width = TC * states
    i = pl.program_id(0)

    @pl.when(i == 0)
    def _():
        acc_ref[...] = jnp.zeros_like(acc_ref)
        gn_ref[...] = jnp.zeros_like(gn_ref)
        branch_ref[...] = jnp.zeros_like(branch_ref)

    h_ref[0:states, :] = hin_ref[...].astype(bf16)

    def chunk(c, carry):
        h = list(carry)
        base = pl.multiple_of(c * TC, TC)
        row = pl.multiple_of(c * width, width)
        b_cols, c_cols = b_ref[c], c_ref[c]

        def fetch(j):
            at = pl.ds(row + j * states, states)
            rows = [row_at(ref, base + j) for ref in (dtk_ref, u_ref, g_ref)]
            return rows + [spread(b_cols, j), spread(c_cols, j), acc_ref[at, :]]

        for j, (d, u, g, b_now, c_now, acc) in ahead_of(range(TC), fetch):
            for k in range(len(h)):
                h[k] = jnp.exp2(d[k] * rate[k]) * h[k] + b_now * u[k]
                h_ref[pl.ds(row + (j + 1) * states, states), k * 128 : (k + 1) * 128] = h[k].astype(bf16)
                y_refs[k][pl.ds((base + j) * 8, 8), :] = halves(c_now * h[k])
                acc = acc + h[k] * g[k]
            acc_ref[pl.ds(row + j * states, states), :] = acc
        return tuple(h)

    lax.fori_loop(0, chunks, chunk, tuple(lane_tiles(hin_ref[...])))
    skip = par_ref[0, L.skip : L.skip + 1, :]

    def tile(k, unused):
        rows = pl.ds(pl.multiple_of(k * 16, 16), 16)
        y = jnp.concatenate([fold_rows(y_refs, k * 16), fold_rows(y_refs, k * 16 + 8)], axis=0)
        mixer = (y + skip * act_ref[rows, :]).astype(bf16).astype(f32)
        gate = gate_ref[rows, :]
        sig = jax.nn.sigmoid(gate)
        gated_ref[rows, :] = (mixer * (gate * sig)).astype(bf16)
        ggate_ref[rows, :] = (gg_ref[rows, :] * mixer * sig * (1.0 + gate * (1.0 - sig))).astype(bf16)
        return unused

    lax.fori_loop(0, T // 16, tile, 0)
    branch_ref[...] += jnp.dot(gated_ref[...], wo_ref[...], preferred_element_type=f32)
    gout_ref[...] = lax.dot_general(
        gated_ref[...], cot_ref[...], TN, preferred_element_type=f32
    ).astype(bf16)
    gin_ref[...] = lax.dot_general(
        ggate_ref[...], normed_ref[...], TN, preferred_element_type=f32
    ).astype(bf16)
    gn_ref[...] += lax.dot_general(ggate_ref[...], wg_ref[...], NT, preferred_element_type=f32)

    @pl.when(i == pl.num_programs(0) - 1)
    def _():
        block_ref[...] = (tok_ref[...].astype(f32) + branch_ref[...]).astype(bf16)
        lane_sums(states, acc_ref, gc_ref, chunks)


def fwd_scan(L, dtk, u, b_cols, c_cols, g, par, entering, act, gate, gg, out_weight, cot, tokens, normed, in_weight):
    T, E = dtk.shape
    D = tokens.shape[1]
    N = L.N
    rows = (T + 1) * N
    blocks = E // EB
    return pl.pallas_call(
        functools.partial(fwd_kernel, L),
        grid=(blocks,),
        in_specs=[
            cols(T), cols(T), once(*b_cols.shape), once(*c_cols.shape), cols(T), lead(PAR, EB), cols(N),
            cols(T), cols(T), cols(T), tall(EB, D), whole(T, D), whole(T, D), whole(T, D),
            cols(D, EB, blocks),
        ],
        out_specs=[
            cols(rows), whole(T, TC * N), whole(T, D), tall(EB, D), tall(EB, D), whole(T, D),
        ],
        out_shape=[
            shape(bf16, rows, E), shape(f32, T, TC * N), shape(bf16, T, D), shape(bf16, E, D),
            shape(bf16, E, D), shape(f32, T, D),
        ],
        scratch_shapes=[
            pltpu.VMEM((T * N, 128), f32), pltpu.VMEM((T, EB), bf16), pltpu.VMEM((T, EB), bf16),
            pltpu.VMEM((T, D), f32),
        ] + [pltpu.VMEM((T * 8, 128), f32)] * (EB // 128),
        compiler_params=params(),
        name="fwd_scan",
    )(dtk, u, b_cols, c_cols, g, par, entering, act, gate, gg, out_weight, cot, tokens, normed, in_weight)


def bwd_kernel(
    L, sums, blocks, dtk_ref, u_ref, g_ref, b_ref, c_ref, par_ref, wts_ref, fin_ref, h_ref, spre_ref, act_ref, proj_ref,
    gc_ref, *refs,
):
    arrays = len(sums.kinds)
    x_refs, refs = refs[:arrays], refs[arrays:]
    gap_ref, chan_ref, gproj_ref = refs[:3]
    o_refs, refs = refs[3 : 3 + arrays], refs[3 + arrays :]
    acc_ref, gb_ref, rank_ref, pre_ref = refs[:4]
    rate = lane_tiles(rates(L, par_ref))
    tiles = len(rate)
    bsum_refs, wsum_refs = refs[4 : 4 + tiles], refs[4 + tiles : 4 + 2 * tiles]
    sums.bind(x_refs, o_refs, refs[4 + 2 * tiles :])
    T, states = u_ref.shape[0], L.N
    chunks = T // TC
    width = TC * states
    i = pl.program_id(0)

    @pl.when(i == 0)
    def _():
        acc_ref[...] = jnp.zeros_like(acc_ref)
        rank_ref[...] = jnp.zeros_like(rank_ref)
        sums.barrier()

    def chunk(i, carry):
        flow, total = list(carry[:tiles]), list(carry[tiles:])
        c = chunks - 1 - i
        base = pl.multiple_of(c * TC, TC)
        row = pl.multiple_of(c * width, width)
        b_cols, c_cols = b_ref[c], c_ref[c]

        def fetch(j):
            at = pl.ds(row + j * states, states)
            rows = [row_at(ref, base + j) for ref in (dtk_ref, u_ref, g_ref)]
            return rows + [spread(b_cols, j), spread(c_cols, j), acc_ref[at, :], lane_tiles(h_ref[at, :])]

        for j, (d, u, g, b_now, c_now, acc, before) in ahead_of(reversed(range(TC)), fetch):
            part = pl.ds((base + j) * 8, 8)
            for k in range(tiles):
                adj = c_now * g[k] + flow[k]
                flow[k] = jnp.exp2(d[k] * rate[k]) * adj
                wr = flow[k] * before[k].astype(f32) * rate[k]
                total[k] = total[k] + wr * d[k]
                wsum_refs[k][part, :] = halves(wr)
                bsum_refs[k][part, :] = halves(adj * b_now)
                acc = acc + adj * u[k]
            acc_ref[pl.ds(row + j * states, states), :] = acc
        return tuple(flow) + tuple(total)

    none = jnp.zeros((states, 128), f32)
    out = tuple(lane_tiles(fin_ref[...])) + (none,) * tiles
    for q in range(BLOCK_SLOTS):
        for n in range(sums.ticks()):
            block, quarter = divmod(n, BLOCK_SLOTS)
            if quarter == q and block < blocks:
                pl.when(i == block)(functools.partial(sums.tick, n))
        out = lax.fori_loop(q * chunks // BLOCK_SLOTS, (q + 1) * chunks // BLOCK_SLOTS, chunk, out)
    total = jnp.concatenate(out[tiles:], axis=1)
    skip = par_ref[0, L.skip : L.skip + 1, :]

    def tile(k, carry):
        bias_sum, skip_sum = carry
        rows = pl.ds(pl.multiple_of(k * 16, 16), 16)
        bsum, wsum = (
            jnp.concatenate([fold_rows(refs, k * 16), fold_rows(refs, k * 16 + 8)], axis=0)
            for refs in (bsum_refs, wsum_refs)
        )
        spre, act, g = spre_ref[rows, :], act_ref[rows, :], g_ref[rows, :]
        grad = (wsum * (1.0 / LOG2E) + act * bsum) * jax.nn.sigmoid(spre)
        gap_ref[rows, :] = g * skip + softplus(spre) * bsum
        pre_ref[rows, :] = grad.astype(bf16)
        bias_sum = bias_sum + halves(grad)
        skip_sum = skip_sum + halves(g * act)
        return bias_sum, skip_sum

    none = jnp.zeros((8, EB), f32)
    bias_sum, skip_sum = lax.fori_loop(0, T // 16, tile, (none, none))
    R = L.R
    pre = pre_ref[...]
    step_low = proj_ref[...].astype(bf16)
    grad_step_w = lax.dot_general(step_low, pre, TN, preferred_element_type=f32)
    chan_ref[0] = jnp.concatenate(
        [
            grad_step_w[0:R],
            total * (1.0 / LOG2E),
            jnp.sum(bias_sum, axis=0, keepdims=True),
            jnp.sum(skip_sum, axis=0, keepdims=True),
            jnp.zeros((128 - R - states - 2, EB), f32),
        ],
        axis=0,
    ).astype(bf16)
    weights = wts_ref[0, L.step : L.step + R, :].astype(f32)
    weights = jnp.concatenate([weights, jnp.zeros((128 - R, EB), f32)], axis=0).astype(bf16)
    rank_ref[...] += lax.dot_general(pre, weights, NT, preferred_element_type=f32)

    @pl.when(i == pl.num_programs(0) - 1)
    def _():
        lane_sums(states, acc_ref, gb_ref, chunks)
        dims = (width, 128)
        state = lax.rem(lax.broadcasted_iota(jnp.int32, dims, 0), states)
        target = lax.broadcasted_iota(jnp.int32, dims, 1)
        diag = same_step(states, T)
        total = rank_ref[...]
        for ref, start in ((gb_ref, R), (gc_ref, R + states)):
            fold = (target == state + start).astype(f32)
            kept = jnp.where(diag, ref[...], 0.0)
            total = total + jnp.dot(
                kept, fold, precision=lax.Precision.HIGHEST, preferred_element_type=f32
            )
        gproj_ref[...] = total.astype(bf16)
        for n in range(blocks * BLOCK_SLOTS, sums.ticks()):
            sums.tick(n)
        sums.drain()


def bwd_scan(L, dtk, u, g, b_cols, c_cols, par, wts, arriving, held, spre, act, proj, grad_c, arrays, sums):
    T, E = dtk.shape
    N = L.N
    blocks = E // EB
    return pl.pallas_call(
        functools.partial(bwd_kernel, L, sums, blocks),
        grid=(blocks,),
        in_specs=[
            cols(T), cols(T), cols(T), once(*b_cols.shape), once(*c_cols.shape), lead(PAR, EB),
            lead(WTS, EB), cols(N), cols(held.shape[0]), cols(T), cols(T), whole(T, 128), whole(T, TC * N),
        ] + [once(*v.shape) for v in arrays],
        out_specs=[cols(T), lead(128, EB), whole(T, 128)] + [whole(*o.shape) for o in sums.outs()],
        out_shape=[shape(f32, T, E), shape(bf16, blocks, 128, EB), shape(bf16, T, 128)] + sums.outs(),
        scratch_shapes=[
            pltpu.VMEM((T * N, 128), f32),
            pltpu.VMEM((T, TC * N), f32), pltpu.VMEM((T, 128), f32), pltpu.VMEM((T, EB), bf16),
        ] + [pltpu.VMEM((T * 8, 128), f32)] * (2 * EB // 128) + sums.scratch(),
        compiler_params=params(collective_id=3, has_side_effects=True),
        name="bwd_scan",
    )(dtk, u, g, b_cols, c_cols, par, wts, arriving, held, spre, act, proj, grad_c, *arrays)


def conv_kernel(L, gap_ref, gproj_ref, wts_ref, act_ref, cs_ref, inner_ref, marks_ref, gc_ref, chan_ref, xs_ref):
    T = gap_ref.shape[0]
    K, wide = L.K, L.R + 2 * L.N
    weights = wts_ref[0].astype(f32)
    row = lax.broadcasted_iota(jnp.int32, weights.shape, 0)
    weights = jnp.where(row < wide, weights, 0.0).astype(bf16)
    gc_ref[...] = jnp.dot(gproj_ref[...], weights, preferred_element_type=f32)
    act_low = act_ref[...].astype(bf16)
    grad_proj = lax.dot_general(gproj_ref[...], act_low, TN, preferred_element_type=f32)
    xs_ref[...] = inner_ref[...].astype(f32)

    def tile(k, carry):
        r = pl.multiple_of(k * RT, RT)
        rows = pl.ds(r, RT)
        total = cs_ref[rows, :]
        sig = jax.nn.sigmoid(total)
        grad = (gc_ref[rows, :] + gap_ref[rows, :]) * sig * (1.0 + total * (1.0 - sig))
        gc_ref[rows, :] = grad
        block = xs_ref[pl.ds(pl.multiple_of(r + HALO - 8, 8), RT + 8), :]
        out = [carry[K] + jnp.sum(grad.reshape(RT // 8, 8, EB), axis=0)]
        for j in range(K):
            part = grad * block[8 - j : RT + 8 - j]
            if j > 0:
                part = part * marks_ref[rows, j - 1 : j]
            out.insert(0, carry[K - 1 - j] + jnp.sum(part.reshape(RT // 8, 8, EB), axis=0))
        return tuple(out)

    none = jnp.zeros((8, EB), f32)
    sums = lax.fori_loop(0, T // RT, tile, (none,) * (K + 1))
    chan_ref[0] = jnp.concatenate(
        [grad_proj[0:wide]]
        + [jnp.sum(s, axis=0, keepdims=True) for s in sums]
        + [jnp.zeros((128 - wide - K - 1, EB), f32)],
        axis=0,
    ).astype(bf16)


def conv_back(L, gap, gproj, wts, act, cs, inner, marks):
    T, E = gap.shape
    blocks = E // EB
    return pl.pallas_call(
        functools.partial(conv_kernel, L),
        grid=(blocks,),
        in_specs=[
            cols(T), whole(T, 128), lead(WTS, EB), cols(T), cols(T), cols(T + HALO), whole(*marks.shape),
        ],
        out_specs=[cols(T), lead(128, EB)],
        out_shape=[shape(f32, T, E), shape(bf16, blocks, 128, EB)],
        scratch_shapes=[pltpu.VMEM((T + HALO, EB), f32)],
        compiler_params=params(),
        name="conv_back",
    )(gap, gproj, wts, act, cs, inner, marks)


def tail_kernel(
    L, gc_ref, after_ref, par_ref, marks_ref, normed_ref, wi_ref, gn_ref, tok_ref, cot_ref, gain_ref,
    gin_ref, gtok_ref, ggain_ref, ext_ref, low_ref, sum_ref,
):
    T, D = tok_ref.shape
    K = L.K
    i = pl.program_id(0)
    ext_ref[0:T, :] = gc_ref[...]
    ext_ref[T : T + 8, :] = after_ref[...]
    taps = [par_ref[0, L.conv + j : L.conv + j + 1, :] for j in range(K)]

    def tile(r):
        block = ext_ref[pl.ds(r, RT + 8), :]
        marks = marks_ref[pl.ds(r, RT + 8), :]
        total = taps[K - 1] * block[0:RT]
        for j in range(1, K):
            masked = block * marks[:, j - 1 : j]
            total = total + taps[K - 1 - j] * masked[j : RT + j]
        low_ref[pl.ds(r, RT), :] = total.astype(bf16)

    row_tiles(T, tile)
    gin_ref[...] = lax.dot_general(
        low_ref[...], normed_ref[...], TN, preferred_element_type=f32
    ).astype(bf16)
    part = lax.dot_general(low_ref[...], wi_ref[...], NT, preferred_element_type=f32)

    @pl.when(i == 0)
    def _():
        sum_ref[...] = gn_ref[...] + part

    @pl.when(i > 0)
    def _():
        sum_ref[...] += part

    @pl.when(i == pl.num_programs(0) - 1)
    def _():
        gain = gain_ref[...].reshape(1, D)

        def last(k, total):
            rows = pl.ds(pl.multiple_of(k * 16, 16), 16)
            x = tok_ref[rows, :].astype(f32)
            grad = sum_ref[rows, :]
            inv = lax.rsqrt(jnp.mean(x * x, axis=1, keepdims=True) + epsilon)
            scaled = grad * gain
            mean = jnp.mean(x * scaled, axis=1, keepdims=True)
            gtok_ref[rows, :] = (
                cot_ref[rows, :].astype(f32) + inv * scaled - x * (inv * inv * inv * mean)
            )
            return total + jnp.sum((grad * x * inv).reshape(2, 8, D), axis=0)

        total = lax.fori_loop(0, T // 16, last, jnp.zeros((8, D), f32))
        ggain_ref[...] = jnp.sum(total, axis=0, keepdims=True)


def tail(L, gc, after, par, marks, normed, in_weight, gn, tokens, cot, gain):
    T, E = gc.shape
    D = tokens.shape[1]
    blocks = E // EB
    return pl.pallas_call(
        functools.partial(tail_kernel, L),
        grid=(blocks,),
        in_specs=[
            cols(T), cols(8), lead(PAR, EB), whole(*marks.shape), whole(T, D), cols(D), whole(T, D),
            whole(T, D), whole(T, D), whole(D),
        ],
        out_specs=[tall(EB, D), whole(T, D), whole(1, D)],
        out_shape=[shape(bf16, E, D), shape(f32, T, D), shape(f32, 1, D)],
        scratch_shapes=[
            pltpu.VMEM((T + 8, EB), f32), pltpu.VMEM((T, EB), bf16), pltpu.VMEM((T, D), f32),
        ],
        compiler_params=params(),
        name="tail",
    )(gc, after, par, marks, normed, in_weight, gn, tokens, cot, gain)


class Sums:
    def __init__(self, chan_count, seq_count, kinds, shapes, phases, skew=1, pace=1):
        self.cc, self.sc = chan_count, seq_count
        self.kinds = kinds
        self.phases, self.skew, self.pace = phases, skew, pace
        self.size = 8 * seq_count
        self.bits = [1 << i for i in range(chan_count.bit_length() - 1)]
        self.z_bits = [2 << i for i in range(seq_count.bit_length() - 2)]
        self.pieces = [
            (a, r, dims[2]) for a, dims in enumerate(shapes) for r in range(0, dims[1], 2 * self.size)
        ]
        self.shapes = shapes

    def half(self, p):
        return self.kinds[self.pieces[p][0]] is not None

    def stages(self, p):
        bits = self.bits if p % 2 == 0 else self.bits[::-1]
        return (
            [("core", 1)] + [("chan", b) for b in bits] + [("z", b) for b in self.z_bits]
            + [("zgather", b) for b in self.z_bits[::-1]] + ([("move", 0)] if self.half(p) else [])
            + [("cgather", 1)]
        )

    def span(self, p):
        halvings = 1 + len(self.bits) + len(self.z_bits)
        phase = self.phases[self.pieces[p][0]]
        first = halvings if phase == "gather" else 0
        return first, halvings if phase == "halve" else len(self.stages(p))

    def begin(self, p):
        phase = self.phases[self.pieces[p][0]]
        before = [q for q in range(p) if self.phases[self.pieces[q][0]] == phase]
        return self.skew * (len(before) // 2)

    def ticks(self):
        return max(
            self.begin(p) + self.pace * (self.span(p)[1] - self.span(p)[0]) for p in range(len(self.pieces))
        ) + 1

    def final(self, p):
        a, first, width = self.pieces[p]
        return pl.ds(first // (2 * self.size) * 16, 16)

    def outs(self):
        found = []
        for kind, dims, phase in zip(self.kinds, self.shapes, self.phases):
            if phase == "halve":
                found.append(shape(bf16, dims[1] // (2 * self.size) * 16, dims[2]))
            else:
                found.append(shape(bf16, *(dims[1:] if kind is None else (2,) + tuple(dims[1:]))))
        return found

    def scratch(self):
        found = []
        for p, (a, r, width) in enumerate(self.pieces):
            small = self.span(p)[0] > 0
            for k in range(len(self.bits) + 1):
                dims = (self.cc >> k, self.size, width)
                found.append(pltpu.VMEM((1, 16, 128) if small else dims, bf16))
            for k in range(len(self.z_bits)):
                dims = (self.size >> (k + 1), width)
                found.append(pltpu.VMEM((16, 128) if small else dims, bf16))
            found.append(pltpu.VMEM((self.size, width), bf16))
        dims = (len(self.pieces), len(self.bits) + 2 * len(self.z_bits) + 3, max(2, self.cc // 2))
        return found + [pltpu.SemaphoreType.DMA(dims), pltpu.SemaphoreType.DMA(dims)]

    def bind(self, x_refs, o_refs, scratch):
        self.x, self.o = x_refs, o_refs
        each = len(self.bits) + len(self.z_bits) + 2
        self.held = [scratch[p * each : (p + 1) * each] for p in range(len(self.pieces))]
        self.send_sem, self.recv_sem = scratch[-2:]
        self.si, self.ci = lax.axis_index("seq"), lax.axis_index("chan")
        self.core = lax.rem(self.si, 2)

    def side(self, bit):
        return lax.rem(self.si // bit, 2)

    def across(self, bit):
        return (self.si + bit - 2 * bit * self.side(bit), self.ci)

    def barrier(self):
        barrier = pltpu.get_barrier_semaphore()
        others = [(self.si, lax.rem(self.ci + k, self.cc)) for k in range(1, self.cc)]
        others += [self.across(bit) for bit in [1] + self.z_bits]
        for other in others:
            pl.semaphore_signal(barrier, inc=1, device_id=other, device_id_type=pl.DeviceIdType.MESH)
        pl.semaphore_wait(barrier, len(others))

    def copy(self, p, s, slot, src, dst, device):
        return pltpu.make_async_remote_copy(
            src_ref=src, dst_ref=dst, send_sem=self.send_sem.at[p, s, slot],
            recv_sem=self.recv_sem.at[p, s, slot], device_id=device, device_id_type=pl.DeviceIdType.MESH,
        )

    def kept(self, p, s, keep):
        name, bit = self.stages(p)[s]
        if name == "core":
            a, start, width = self.pieces[p]
            side = self.core if keep else 1 - self.core
            return [self.x[a].at[:, pl.ds(pl.multiple_of(start + side * self.size, 16), self.size), :]]
        ref = self.held[p][s - 1]
        if name == "z":
            side = self.side(bit) if keep else 1 - self.side(bit)
            k = self.z_bits.index(bit)
            rows = self.size >> (k + 1)
            rows = pl.ds(pl.multiple_of(side * rows, 16), rows)
            return [ref.at[0, rows, :] if k == 0 else ref.at[rows, :]]
        mine = lax.rem(self.ci // bit, 2)
        side = mine if keep else 1 - mine
        left = sorted(b for n, b in self.stages(p)[s : 1 + len(self.bits)])
        low = 1 << left.index(bit)
        return [
            ref.at[pl.ds((i // low) * 2 * low + side * low + i % low, 1)]
            for i in range((1 << len(left)) // 2)
        ]

    def landing(self, p, s):
        dst = self.held[p][s]
        return [dst.at[pl.ds(i, 1)] for i in range(dst.shape[0])] if self.stages(p)[s][0] == "chan" else [dst]

    def gathered(self, p, done):
        start, rows = 0, self.size
        for bit in self.z_bits[:done]:
            rows //= 2
            start = start + self.side(bit) * rows
        if self.half(p):
            return self.held[p][-1].at[pl.ds(pl.multiple_of(start, 16), rows), :]
        start = start + self.pieces[p][1] + self.core * self.size
        return self.o[self.pieces[p][0]].at[pl.ds(pl.multiple_of(start, 16), rows), :]

    def places(self, p):
        a, first, width = self.pieces[p]
        rows = pl.ds(pl.multiple_of(first + self.core * self.size, 16), self.size)
        return [self.o[a].at[b, rows, :] for b in range(2)] if self.half(p) else [self.o[a].at[rows, :]]

    def move(self, p, s, v):
        goal = self.kinds[self.pieces[p][0]] + v // 2
        place = self.places(p)[v % 2]
        return goal, place, self.copy(p, s, v % 2, self.held[p][-1], place, (self.si, goal))

    def copies(self, p, s):
        name, bit = self.stages(p)[s]
        if name in ("core", "chan", "z"):
            device = (self.si, self.ci + bit - 2 * bit * lax.rem(self.ci // bit, 2))
            device = device if name == "chan" else self.across(bit)
            pairs = zip(self.kept(p, s, False), self.landing(p, s))
            return [self.copy(p, s, i, src, dst, device) for i, (src, dst) in enumerate(pairs)]
        places = self.places(p)
        if name == "zgather":
            places = [self.gathered(p, self.z_bits.index(bit) + 1)]
        return [self.copy(p, s, b, place, place, self.across(bit)) for b, place in enumerate(places)]

    def taking_part(self, p, s, work):
        if self.half(p) and self.stages(p)[s][0] == "cgather":
            base = self.kinds[self.pieces[p][0]]
            pl.when((self.ci >= base) & (self.ci < base + self.cc // 2))(work)
        else:
            work()

    def start(self, p, s):
        if self.stages(p)[s][0] == "move":
            for v in range(self.cc):
                @pl.when(self.ci == v)
                def _(v=v):
                    goal, place, copy = self.move(p, s, v)
                    if goal == v:
                        place[...] = self.held[p][-1][...]
                    else:
                        copy.start()
            return

        def work():
            for copy in self.copies(p, s):
                copy.start()

        self.taking_part(p, s, work)

    def finish(self, p, s):
        name, bit = self.stages(p)[s]
        if name == "move":
            for v in range(self.cc):
                goal, place, copy = self.move(p, s, v)
                if goal != v:
                    pl.when(self.ci == goal)(copy.wait_recv)
            return

        def work():
            for copy in self.copies(p, s):
                copy.wait_recv()

        self.taking_part(p, s, work)
        if name in ("core", "chan", "z"):
            last = s == len(self.bits) + len(self.z_bits)
            for src, dst in zip(self.kept(p, s, True), self.landing(p, s)):
                total = (dst[...].astype(f32) + src[...].astype(f32)).astype(bf16)
                if last and self.span(p)[1] == s + 1:
                    dst = self.o[self.pieces[p][0]].at[self.final(p), :]
                elif last:
                    dst = self.gathered(p, len(self.z_bits))
                dst[...] = total

    def tick(self, n):
        for p in range(len(self.pieces)):
            first, end = self.span(p)
            s, rest = divmod(n - self.begin(p), self.pace)
            s += first
            if rest != 0:
                continue
            if first + 1 <= s <= end:
                self.finish(p, s - 1)
            if first > 0 and s == first:
                self.gathered(p, len(self.z_bits))[...] = self.x[self.pieces[p][0]][self.final(p), :]
            if first <= s < end:
                self.start(p, s)

    def drain(self):
        for p in range(len(self.pieces)):
            for s in range(*self.span(p)):
                if self.stages(p)[s][0] == "move":
                    for v in range(self.cc):
                        goal, place, copy = self.move(p, s, v)
                        if goal != v:
                            pl.when(self.ci == v)(copy.wait_send)
                    continue

                def work(p=p, s=s):
                    for copy in self.copies(p, s):
                        copy.wait_send()

                self.taking_part(p, s, work)


def sum_kernel(sums, *refs):
    arrays = len(sums.kinds)
    sums.bind(refs[:arrays], refs[arrays : 2 * arrays], refs[2 * arrays :])
    sums.barrier()
    for n in range(sums.ticks()):
        sums.tick(n)
    sums.drain()


def sum_owned(arrays, shapes, kinds, phases, chan_count, seq_count):
    sums = Sums(chan_count, seq_count, kinds, shapes, phases)
    vmem = pl.BlockSpec(memory_space=pltpu.VMEM)
    return pl.pallas_call(
        functools.partial(sum_kernel, sums),
        in_specs=[vmem] * len(arrays),
        out_specs=[vmem] * len(arrays),
        out_shape=sums.outs(),
        scratch_shapes=sums.scratch(),
        compiler_params=params(collective_id=0, has_side_effects=True),
        name="sum_owned",
    )(*arrays)


def unpack_kernel(L, inner_ref, gate_ref, out_ref, d_ref, e_ref, gin_ref, gout_ref, *refs):
    first = lax.axis_index("chan") < lax.axis_size("chan") // 2

    @pl.when(first)
    def _():
        gin_ref[...] = inner_ref[...].astype(f32).T

    @pl.when(jnp.logical_not(first))
    def _():
        gin_ref[...] = gate_ref[...].astype(f32).T

    gout_ref[...] = out_ref[...].astype(f32)
    d, e = d_ref[...].astype(f32), e_ref[...].astype(f32)
    R, N, K = L.R, L.N, L.K
    wide = R + 2 * N
    conv_w, conv_b, proj, step_w, step_b, decay, skip, gain = refs
    width = d.shape[1]
    step_w[...] = d[0:R]
    decay[...] = d[R : R + N]
    step_b[...] = d[R + N].reshape(width)
    skip[...] = d[R + N + 1].reshape(width)
    proj[...] = e[0:wide]
    conv_w[...] = e[wide : wide + K]
    conv_b[...] = e[wide + K].reshape(width)
    gain[...] = e[wide + K + 1].reshape(width)


def unpack(L, sums):
    width = sums[3].shape[1]
    rows, D = sums[0].shape
    R, N, K = L.R, L.N, L.K
    return pl.pallas_call(
        functools.partial(unpack_kernel, L),
        out_shape=[
            shape(f32, D, rows), shape(f32, *sums[2].shape), shape(f32, K, width), shape(f32, width),
            shape(f32, R + 2 * N, width), shape(f32, R, width), shape(f32, width),
            shape(f32, N, width), shape(f32, width), shape(f32, width),
        ],
        compiler_params=params(),
        name="unpack",
    )(*sums)


def local(
    tokens, norm_gain, in_weight, conv_weight, conv_bias, proj_weight, step_weight,
    step_bias, decay_log, skip_gain, out_weight, cotangent, lengths,
):
    T, D = tokens.shape
    E = in_weight.shape[1] // 2
    L = Layout(step_weight.shape[0], decay_log.shape[0], conv_weight.shape[0])
    ci = lax.axis_index("chan")
    cc = lax.axis_size("chan")
    sc = lax.axis_size("seq")
    blocks, share = E // EB, E // cc

    parts = (conv_weight, conv_bias, proj_weight.T, step_weight, step_bias, decay_log, skip_gain)
    wts, par, halo = gather_params(L, cc, parts, tokens)

    def by_block(values):
        if share == EB:
            return values
        values = jnp.moveaxis(values, 0, 1).reshape(-1, blocks, EB)
        return jnp.moveaxis(values, 1, 0)

    wts, par = by_block(wts), by_block(par)
    marks, normed, inner, gate, gg, g, cs, act, proj, b_cols, c_cols = front(
        L, lengths, tokens, halo, norm_gain, in_weight, out_weight, cotangent, par, wts
    )
    spre, dtk, u, entering, arriving = pre_scan(L, cc, proj, par, wts, act, g, marks, b_cols, c_cols)
    held, grad_c, block_out, grad_out, grad_in_gate, gn = fwd_scan(
        L, dtk, u, b_cols, c_cols, g, par, entering, act, gate, gg, out_weight, cotangent, tokens,
        normed, in_weight,
    )

    piece = 16 * sc
    fold = 2 if 2 * share <= piece else 1

    def owned(values):
        values = values.reshape(cc, -1, values.shape[-1] // fold)
        return jnp.pad(values, ((0, 0), (0, -values.shape[1] % piece), (0, 0)))

    def unfolded(values):
        if values.ndim == 2:
            return values[: share * fold].reshape(share, D)
        return values[:, : share * fold].reshape(2 * share, D)

    def by_owner(values):
        if share != EB:
            values = jnp.moveaxis(values, 0, 1).reshape(values.shape[1], cc, share)
            values = jnp.moveaxis(values, 1, 0)
        return jnp.pad(values, ((0, 0), (0, -values.shape[1] % piece), (0, 0)))

    early = [owned(grad_out), owned(grad_in_gate)]
    early_shapes = [v.shape for v in early]
    kinds = [None, cc // 2]
    sums = Sums(cc, sc, kinds, early_shapes, ["halve"] * 2, skew=3, pace=2)
    gap, chan_d, gproj, *early = bwd_scan(
        L, dtk, u, g, b_cols, c_cols, par, wts, arriving, held, spre, act, proj, grad_c, early, sums
    )
    gc, chan_e = conv_back(L, gap, gproj, wts, act, cs, inner, marks)
    after = lax.ppermute(gc[0:8], "chan", [(k, k - 1) for k in range(1, cc)])
    grad_in_inner, grad_tokens, grad_gain = tail(
        L, gc, after, par, marks, normed, in_weight, gn, tokens, cotangent, norm_gain
    )
    row = L.R + 2 * L.N + L.K + 1
    gain_part = jnp.pad(grad_gain.reshape(cc, 1, D // cc), ((0, 0), (0, 0), (0, share - D // cc)))
    chan_e = lax.dynamic_update_slice(by_owner(chan_e), gain_part.astype(bf16), (0, row, 0))
    late = [owned(grad_in_inner), by_owner(chan_d), chan_e]
    sum_inner, sum_d, sum_e, sum_out, sum_gate = sum_owned(
        late + early, [v.shape for v in late] + early_shapes, [0, None, None] + kinds,
        ["all"] * 3 + ["gather"] * 2, cc, sc,
    )
    sums = [unfolded(v) for v in (sum_inner, sum_gate, sum_out)] + [sum_d, sum_e]
    g_in, g_out, conv_w, conv_b, proj_w, step_w, step_b, decay, skip, g_gain = unpack(L, sums)
    return (
        block_out, grad_tokens, g_gain[: D // cc], g_in, conv_w, conv_b, proj_w.T, step_w,
        step_b, decay, skip, g_out,
    )


def solution(mesh):
    tok, row, vec = P(("seq", "chan"), None), P(None, "chan"), P("chan")
    in_specs = (
        tok, P(), P(), row, vec, P("chan", None), row, vec, row, vec, P(), tok, P("seq", None),
    )
    out_specs = (
        tok, tok, vec, row, row, vec, P("chan", None), row, vec, row, vec, P("chan", None),
    )
    return jax.shard_map(local, mesh=mesh, in_specs=in_specs, out_specs=out_specs, check_vma=False)
```

```python
import functools
import math

import jax
import jax.numpy as jnp
from jax import lax
from jax.experimental import pallas as pl
from jax.experimental.pallas import tpu as pltpu
from jax.sharding import PartitionSpec as P

epsilon = 1e-05
LOG2E = math.log2(math.e)
CUT = 1e30
TC = 16
EB = 384
RT = 32
BLOCK_SLOTS = 4
HALO = 16
PAR = 24
WTS = 128
f32 = jnp.float32
bf16 = jnp.bfloat16
NT = (((1,), (1,)), ((), ()))
TN = (((0,), (0,)), ((), ()))


def params(**more):
    return pltpu.CompilerParams(vmem_limit_bytes=60 * 1024 * 1024, **more)


def cols(rows, width=EB, shift=0):
    return pl.BlockSpec((rows, width), lambda i: (0, i + shift))


def tall(rows, width, shift=0):
    return pl.BlockSpec((rows, width), lambda i: (i + shift, 0))


def lead(rows, width, count=1):
    return pl.BlockSpec((count, rows, width), lambda i: (i, 0, 0))


def whole(*shape):
    return pl.BlockSpec(shape, lambda i: (0,) * len(shape))


def once(*shape):
    return pl.BlockSpec(shape, lambda i: (0,) * len(shape), pipeline_mode=pl.Buffered(1))


def shape(dtype, *dims):
    return jax.ShapeDtypeStruct(dims, dtype)


def row_tiles(count, body):
    def step(i, unused):
        body(pl.multiple_of(i * RT, RT))
        return unused

    lax.fori_loop(0, count // RT, step, 0)


def same_step(states, rows):
    dims = (rows, TC * states)
    here = lax.rem(lax.broadcasted_iota(jnp.int32, dims, 0), TC) * states
    place = lax.broadcasted_iota(jnp.int32, dims, 1)
    return (place >= here) & (place < here + states)


class Layout:
    def __init__(self, R, N, K):
        self.R, self.N, self.K = R, N, K
        self.step = R + 2 * N
        self.decay = 0
        self.conv = self.decay + N
        self.conv_b = self.conv + K
        self.step_b = self.conv_b + 1
        self.skip = self.step_b + 1
        self.end = self.skip + 1


def start_gather(
    L, count, cw_ref, cb_ref, pw_ref, sw_ref, sb_ref, dl_ref, sk_ref, tok_ref,
    wts_ref, par_ref, halo_ref, send_sem, recv_sem, halo_sems,
):
    si, ci = lax.axis_index("seq"), lax.axis_index("chan")
    T = tok_ref.shape[0]
    width = par_ref.shape[2]
    barrier = pltpu.get_barrier_semaphore()
    for k in range(1, count):
        pl.semaphore_signal(
            barrier, inc=1, device_id=(si, lax.rem(ci + k, count)),
            device_id_type=pl.DeviceIdType.MESH,
        )
    own, weights = par_ref.at[ci], wts_ref.at[ci]
    weights[...] = jnp.concatenate(
        [pw_ref[...].astype(f32), sw_ref[...].astype(f32)], axis=0
    ).astype(bf16)
    own[...] = jnp.concatenate(
        [
            dl_ref[...], cw_ref[...], cb_ref[...].reshape(1, width), sb_ref[...].reshape(1, width),
            sk_ref[...].reshape(1, width), jnp.zeros((PAR - L.end, width), f32),
        ],
        axis=0,
    )
    pl.semaphore_wait(barrier, count - 1)

    def share(ref, j, k):
        return pltpu.make_async_remote_copy(
            src_ref=ref, dst_ref=ref, send_sem=send_sem.at[j, k], recv_sem=recv_sem.at[j, k],
            device_id=(si, lax.rem(ci + k, count)), device_id_type=pl.DeviceIdType.MESH,
        )

    edge = pltpu.make_async_remote_copy(
        src_ref=tok_ref.at[pl.ds(T - HALO, HALO)], dst_ref=halo_ref,
        send_sem=halo_sems.at[0], recv_sem=halo_sems.at[1],
        device_id=(si, lax.rem(ci + 1, count)), device_id_type=pl.DeviceIdType.MESH,
    )
    edge.start()
    for j, ref in enumerate((own, weights)):
        for k in range(1, count):
            share(ref, j, k).start()

    def wait():
        edge.wait()
        for j, ref in enumerate((own, weights)):
            for k in range(1, count):
                share(ref, j, k).wait()

    return wait


def gather_kernel(L, count, *refs):
    start_gather(L, count, *refs)()


def gather_scratch(count):
    return [
        pltpu.SemaphoreType.DMA((2, count)),
        pltpu.SemaphoreType.DMA((2, count)),
        pltpu.SemaphoreType.DMA((2,)),
    ]


def gather_params(L, count, parts, tokens):
    width = parts[0].shape[1]
    T, D = tokens.shape
    vmem = pl.BlockSpec(memory_space=pltpu.VMEM)
    return pl.pallas_call(
        functools.partial(gather_kernel, L, count),
        in_specs=[vmem] * 8,
        out_specs=[vmem] * 3,
        out_shape=[shape(bf16, count, WTS, width), shape(f32, count, PAR, width), shape(bf16, HALO, D)],
        scratch_shapes=gather_scratch(count),
        compiler_params=params(collective_id=1, has_side_effects=True),
        name="gather_params",
    )(*parts, tokens)


def front_kernel(
    L, count, inside, len_ref, tok_ref, gain_ref, wi_ref, wg_ref, wo_ref, cot_ref, *refs,
):
    given, refs = refs[: 7 if inside else 3], refs[7 if inside else 3 :]
    (
        marks_ref, normed_ref, inner_ref, gate_ref, gg_ref, g_ref, cs_ref, act_ref, proj_ref, bch_ref, cch_ref,
    ) = refs[:11]
    results, refs = refs[11 : 13 if inside else 11], refs[13 if inside else 11 :]
    hn_ref, xs_ref, low_ref = refs[:3]
    T = tok_ref.shape[0]
    N, K = L.N, L.K
    i = pl.program_id(0)
    sub = low_ref.shape[1] // EB
    if inside:
        wts_ref, par_ref, halo_ref, *sems = refs[3:]
        first = i * sub
    else:
        wts_ref, par_ref, halo_ref = given
        first = 0

    def norm(x):
        x = x.astype(f32)
        inv = lax.rsqrt(jnp.mean(x * x, axis=1, keepdims=True) + epsilon)
        return (x * inv * gain_ref[...].reshape(1, x.shape[1])).astype(bf16)

    def products():
        low = jnp.dot(normed_ref[...], wi_ref[...], preferred_element_type=f32).astype(bf16)
        inner_ref[HALO:, :] = low
        xs_ref[HALO:, :] = low.astype(f32)
        gate_ref[...] = jnp.dot(normed_ref[...], wg_ref[...], preferred_element_type=f32)
        gg_ref[...] = lax.dot_general(cot_ref[...], wo_ref[...], NT, preferred_element_type=f32)

    @pl.when(i == 0)
    def _():
        if inside:
            wait = start_gather(L, count, *given, tok_ref, wts_ref, par_ref, halo_ref, *sems)

        def tile(r):
            normed_ref[pl.ds(r, RT), :] = norm(tok_ref[pl.ds(r, RT), :])

        row_tiles(T, tile)
        proj_ref[...] = jnp.zeros_like(proj_ref)
        dims = marks_ref.shape
        place = lax.broadcasted_iota(jnp.int32, dims, 0) + lax.axis_index("chan") * T
        lane = lax.broadcasted_iota(jnp.int32, dims, 1)
        reach = jnp.where(lane < K - 1, lane + 1, 1)
        found = jnp.zeros(dims, f32)
        start = jnp.int32(0)
        for k in range(len_ref.shape[1]):
            found = jnp.where((start > place - reach) & (start <= place), 1.0, found)
            start = start + len_ref[0, k]
        marks_ref[...] = jnp.where(lane < K - 1, 1.0 - found, found * CUT)
        products()
        if inside:
            wait()
            results[0][...] = wts_ref[...]
            results[1][...] = par_ref[...]
        lead_device = lax.axis_index("chan") == 0
        halo = jnp.where(lead_device, jnp.zeros(halo_ref.shape, f32), halo_ref[...].astype(f32))
        hn_ref[...] = norm(halo)

    pl.when(i > 0)(products)
    low = jnp.dot(hn_ref[...], wi_ref[...], preferred_element_type=f32).astype(bf16)
    inner_ref[0:HALO, :] = low
    xs_ref[0:HALO, :] = low.astype(f32)

    for k in range(sub):
        c = slice(k * EB, (k + 1) * EB)
        taps = [par_ref[first + k, L.conv + j : L.conv + j + 1, :] for j in range(K)]
        bias = par_ref[first + k, L.conv_b : L.conv_b + 1, :]

        def tile(r, c=c, taps=taps, bias=bias):
            rows = pl.ds(r, RT)
            block = xs_ref[pl.ds(pl.multiple_of(r + HALO - 8, 8), RT + 8), c]
            total = bias + taps[K - 1] * block[8:]
            for j in range(1, K):
                usable = marks_ref[rows, j - 1 : j]
                total = total + taps[K - 1 - j] * (block[8 - j : RT + 8 - j] * usable)
            act = total * jax.nn.sigmoid(total)
            cs_ref[rows, c] = total
            act_ref[rows, c] = act
            low_ref[rows, c] = act.astype(bf16)
            gate = gate_ref[rows, c]
            passed = gg_ref[rows, c] * (gate * jax.nn.sigmoid(gate))
            g_ref[rows, c] = passed.astype(bf16).astype(f32)

        row_tiles(T, tile)
        proj_ref[...] += lax.dot_general(low_ref[:, c], wts_ref[first + k], NT, preferred_element_type=f32)

    @pl.when(i == pl.num_programs(0) - 1)
    def _():
        turned = proj_ref[...].T
        for ref, start in ((bch_ref, L.R), (cch_ref, L.R + N)):
            for j in range(T // TC):
                ref[j] = turned[start : start + N, j * TC : (j + 1) * TC]


def front(L, count, lengths, tokens, gain, in_weight, out_weight, cot, parts, gathered):
    T, D = tokens.shape
    E = out_weight.shape[0]
    sub = 2
    wide = EB * sub
    steps = E // wide
    N = L.N
    inside = parts is not None
    more_out, scratch, options = [], [], {}
    if inside:
        given, given_specs = parts, [whole(*v.shape) for v in parts]
        more_out = [shape(bf16, count, WTS, EB), shape(f32, count, PAR, EB)]
        scratch = [pltpu.VMEM(o.shape, o.dtype) for o in more_out] + [pltpu.VMEM((HALO, D), bf16)]
        scratch += gather_scratch(count)
        options = dict(collective_id=1, has_side_effects=True)
    else:
        given, given_specs = gathered, [lead(WTS, EB, sub), lead(PAR, EB, sub), whole(HALO, D)]
    return pl.pallas_call(
        functools.partial(front_kernel, L, count, inside),
        grid=(steps,),
        in_specs=[
            pl.BlockSpec(memory_space=pltpu.SMEM),
            whole(T, D), whole(D), cols(D, wide), cols(D, wide, steps), tall(wide, D), whole(T, D),
        ] + given_specs,
        out_specs=[whole(T + 8, 8), whole(T, D), cols(T + HALO, wide)] + [cols(T, wide)] * 5 + [
            whole(T, 128), whole(T // TC, N, TC), whole(T // TC, N, TC),
        ] + [whole(*o.shape) for o in more_out],
        out_shape=[shape(f32, T + 8, 8), shape(bf16, T, D), shape(bf16, T + HALO, E)]
        + [shape(f32, T, E)] * 5
        + [shape(f32, T, 128), shape(f32, T // TC, N, TC), shape(f32, T // TC, N, TC)]
        + more_out,
        scratch_shapes=[
            pltpu.VMEM((HALO, D), bf16),
            pltpu.VMEM((T + HALO, wide), f32),
            pltpu.VMEM((T, wide), bf16),
        ] + scratch,
        compiler_params=params(**options),
        name="front",
    )(lengths, tokens, gain, in_weight, in_weight, out_weight, cot, *given)


def rates(L, par_ref):
    return -jnp.exp(par_ref[0, L.decay : L.decay + L.N, :]) * LOG2E


def lane_tiles(values):
    return [values[:, k * 128 : (k + 1) * 128] for k in range(EB // 128)]


def row_at(ref, t):
    return lane_tiles(ref[pl.ds(t, 1), :])


def spread(columns, j):
    return jnp.broadcast_to(columns[:, j : j + 1], (columns.shape[0], 128))


def ahead_of(steps, fetch):
    steps = list(steps)
    loaded = [fetch(j) for j in steps[:2]]
    for k, j in enumerate(steps):
        if k + 2 < len(steps):
            loaded.append(fetch(steps[k + 2]))
        yield j, loaded[k]


def softplus(x):
    return jnp.maximum(x, 0.0) + jnp.log1p(jnp.exp(-jnp.abs(x)))


def pre_kernel(
    L, count, proj_ref, par_ref, wts_ref, act_ref, g_ref, marks_ref, b_ref, c_ref,
    spre_ref, dtk_ref, u_ref, enter_ref, arrive_ref, ahead_ref, behind_ref, got_ref,
    send_sem, recv_sem,
):
    T, E = act_ref.shape[0], enter_ref.shape[1]
    N = L.N
    i = pl.program_id(0)
    blocks = E // EB
    si, ci = lax.axis_index("seq"), lax.axis_index("chan")

    @pl.when(i == 0)
    def _():
        barrier = pltpu.get_barrier_semaphore()
        for k in range(1, count):
            pl.semaphore_signal(
                barrier, inc=1, device_id=(si, lax.rem(ci + k, count)),
                device_id_type=pl.DeviceIdType.MESH,
            )
        pl.semaphore_wait(barrier, count - 1)

    low = proj_ref[:, 0 : L.R].astype(bf16)
    weights = wts_ref[0, L.step : L.step + L.R, :]
    bias = par_ref[0, L.step_b : L.step_b + 1, :]
    spre_ref[...] = jnp.dot(low, weights, preferred_element_type=f32) + bias

    def tile(r):
        rows = pl.ds(r, RT)
        step = softplus(spre_ref[rows, :])
        u_ref[rows, :] = step * act_ref[rows, :]
        dtk_ref[rows, :] = step + marks_ref[rows, 3:4]

    row_tiles(T, tile)
    rate = lane_tiles(rates(L, par_ref))
    tiles = len(rate)

    def chunk(c, carry):
        h, through, head = (list(carry[k * tiles : (k + 1) * tiles]) for k in range(3))
        base = pl.multiple_of(c * TC, TC)
        b_cols, c_cols = b_ref[c], c_ref[c]

        def fetch(j):
            rows = [row_at(ref, base + j) for ref in (dtk_ref, u_ref, g_ref)]
            return rows + [spread(b_cols, j), spread(c_cols, j)]

        for j, (d, u, g, b_now, c_now) in ahead_of(range(TC), fetch):
            for k in range(tiles):
                factor = jnp.exp2(d[k] * rate[k])
                h[k] = factor * h[k] + b_now * u[k]
                through[k] = factor * through[k]
                head[k] = head[k] + through[k] * (c_now * g[k])
        return tuple(h + through + head)

    zero = jnp.zeros((N, 128), f32)
    out = lax.fori_loop(0, T // TC, chunk, (zero,) * tiles + (zero + 1.0,) * tiles + (zero,) * tiles)
    h, through, head = (jnp.concatenate(out[k * tiles : (k + 1) * tiles], axis=1) for k in range(3))
    zero = jnp.zeros((N, EB), f32)
    ahead_ref[i, 0:N, :] = h
    ahead_ref[i, N:, :] = through
    behind_ref[i, 0:N, :] = head
    behind_ref[i, N:, :] = through

    def send(b, k, forward):
        return pltpu.make_async_remote_copy(
            src_ref=(ahead_ref if forward else behind_ref).at[b], dst_ref=got_ref.at[count - k, b],
            send_sem=send_sem.at[k, b], recv_sem=recv_sem.at[count - k, b],
            device_id=(si, lax.rem(ci + k, count)), device_id_type=pl.DeviceIdType.MESH,
        )

    for k in range(1, count):
        @pl.when(ci + k < count)
        def _(k=k):
            send(i, k, True).start()

        @pl.when(ci + k >= count)
        def _(k=k):
            send(i, k, False).start()

    @pl.when(i == blocks - 1)
    def _():
        for b in range(blocks):
            for k in range(1, count):
                send(b, k, True).wait()
        for b in range(blocks):
            span = slice(b * EB, (b + 1) * EB)
            entering, arriving = zero, zero
            for k in range(1, count):
                before = ci + k >= count
                got = got_ref[k, b]
                entering = jnp.where(before, got[0:N] + got[N:] * entering, entering)
            for k in range(count - 1, 0, -1):
                behind = ci + k < count
                got = got_ref[k, b]
                arriving = jnp.where(behind, got[0:N] + got[N:] * arriving, arriving)
            enter_ref[:, span] = entering
            arrive_ref[:, span] = arriving


def pre_scan(L, count, proj, par, wts, act, g, marks, b_cols, c_cols):
    T, E = act.shape
    N = L.N
    blocks = E // EB
    state = shape(f32, N, E)
    return pl.pallas_call(
        functools.partial(pre_kernel, L, count),
        grid=(blocks,),
        in_specs=[
            whole(T, 128), lead(PAR, EB), lead(WTS, EB), cols(T), cols(T), whole(*marks.shape),
            once(*b_cols.shape), once(*c_cols.shape),
        ],
        out_specs=[cols(T)] * 3 + [whole(N, E)] * 2,
        out_shape=[shape(f32, T, E)] * 3 + [state] * 2,
        scratch_shapes=[
            pltpu.VMEM((blocks, 2 * N, EB), f32),
            pltpu.VMEM((blocks, 2 * N, EB), f32),
            pltpu.VMEM((count, blocks, 2 * N, EB), f32),
            pltpu.SemaphoreType.DMA((count, blocks)),
            pltpu.SemaphoreType.DMA((count, blocks)),
        ],
        compiler_params=params(collective_id=2, has_side_effects=True),
        name="pre_scan",
    )(proj, par, wts, act, g, marks, b_cols, c_cols)


def fold_rows(refs, r):
    sums = []
    for ref in refs:
        parts = [ref[pl.ds(r * 8 + k, 8, stride=8), :] for k in range(8)]
        while len(parts) > 1:
            parts = [x + y for x, y in zip(parts[::2], parts[1::2])]
        sums.append(parts[0])
    return jnp.concatenate(sums, axis=1)


def halves(values):
    return values[0:8] + values[8:16]


def lane_sums(states, acc_ref, out_ref, chunks):
    width = TC * states
    ones = jnp.ones((TC, 128), bf16)
    group = chunks // 4
    for k in range(4):
        part = acc_ref[k * group * width : (k + 1) * group * width, :].astype(bf16)
        sums = lax.dot_general(ones, part, NT, preferred_element_type=f32)
        for c in range(group):
            row = (k * group + c) * TC
            out_ref[row : row + TC, :] = sums[:, c * width : (c + 1) * width]


def fwd_kernel(
    L, dtk_ref, u_ref, b_ref, c_ref, g_ref, par_ref, hin_ref, act_ref, gate_ref, gg_ref,
    wo_ref, cot_ref, tok_ref, normed_ref, wg_ref,
    h_ref, gc_ref, block_ref, gout_ref, gin_ref, gn_ref,
    acc_ref, gated_ref, ggate_ref, branch_ref, *y_refs,
):
    rate = lane_tiles(rates(L, par_ref))
    T, states = u_ref.shape[0], L.N
    chunks = T // TC
    width = TC * states
    i = pl.program_id(0)

    @pl.when(i == 0)
    def _():
        acc_ref[...] = jnp.zeros_like(acc_ref)
        gn_ref[...] = jnp.zeros_like(gn_ref)
        branch_ref[...] = jnp.zeros_like(branch_ref)

    h_ref[0:states, :] = hin_ref[...].astype(bf16)

    def chunk(c, carry):
        h = list(carry)
        base = pl.multiple_of(c * TC, TC)
        row = pl.multiple_of(c * width, width)
        b_cols, c_cols = b_ref[c], c_ref[c]

        def fetch(j):
            at = pl.ds(row + j * states, states)
            rows = [row_at(ref, base + j) for ref in (dtk_ref, u_ref, g_ref)]
            return rows + [spread(b_cols, j), spread(c_cols, j), acc_ref[at, :]]

        for j, (d, u, g, b_now, c_now, acc) in ahead_of(range(TC), fetch):
            for k in range(len(h)):
                h[k] = jnp.exp2(d[k] * rate[k]) * h[k] + b_now * u[k]
                h_ref[pl.ds(row + (j + 1) * states, states), k * 128 : (k + 1) * 128] = h[k].astype(bf16)
                y_refs[k][pl.ds((base + j) * 8, 8), :] = halves(c_now * h[k])
                acc = acc + h[k] * g[k]
            acc_ref[pl.ds(row + j * states, states), :] = acc
        return tuple(h)

    lax.fori_loop(0, chunks, chunk, tuple(lane_tiles(hin_ref[...])))
    skip = par_ref[0, L.skip : L.skip + 1, :]

    def tile(k, unused):
        rows = pl.ds(pl.multiple_of(k * 16, 16), 16)
        y = jnp.concatenate([fold_rows(y_refs, k * 16), fold_rows(y_refs, k * 16 + 8)], axis=0)
        mixer = (y + skip * act_ref[rows, :]).astype(bf16).astype(f32)
        gate = gate_ref[rows, :]
        sig = jax.nn.sigmoid(gate)
        gated_ref[rows, :] = (mixer * (gate * sig)).astype(bf16)
        ggate_ref[rows, :] = (gg_ref[rows, :] * mixer * sig * (1.0 + gate * (1.0 - sig))).astype(bf16)
        return unused

    lax.fori_loop(0, T // 16, tile, 0)
    branch_ref[...] += jnp.dot(gated_ref[...], wo_ref[...], preferred_element_type=f32)
    gout_ref[...] = lax.dot_general(
        gated_ref[...], cot_ref[...], TN, preferred_element_type=f32
    ).astype(bf16)
    gin_ref[...] = lax.dot_general(
        ggate_ref[...], normed_ref[...], TN, preferred_element_type=f32
    ).astype(bf16)
    gn_ref[...] += lax.dot_general(ggate_ref[...], wg_ref[...], NT, preferred_element_type=f32)

    @pl.when(i == pl.num_programs(0) - 1)
    def _():
        block_ref[...] = (tok_ref[...].astype(f32) + branch_ref[...]).astype(bf16)
        lane_sums(states, acc_ref, gc_ref, chunks)


def fwd_scan(L, dtk, u, b_cols, c_cols, g, par, entering, act, gate, gg, out_weight, cot, tokens, normed, in_weight):
    T, E = dtk.shape
    D = tokens.shape[1]
    N = L.N
    rows = (T + 1) * N
    blocks = E // EB
    return pl.pallas_call(
        functools.partial(fwd_kernel, L),
        grid=(blocks,),
        in_specs=[
            cols(T), cols(T), once(*b_cols.shape), once(*c_cols.shape), cols(T), lead(PAR, EB), cols(N),
            cols(T), cols(T), cols(T), tall(EB, D), whole(T, D), whole(T, D), whole(T, D),
            cols(D, EB, blocks),
        ],
        out_specs=[
            cols(rows), whole(T, TC * N), whole(T, D), tall(EB, D), tall(EB, D), whole(T, D),
        ],
        out_shape=[
            shape(bf16, rows, E), shape(f32, T, TC * N), shape(bf16, T, D), shape(bf16, E, D),
            shape(bf16, E, D), shape(f32, T, D),
        ],
        scratch_shapes=[
            pltpu.VMEM((T * N, 128), f32), pltpu.VMEM((T, EB), bf16), pltpu.VMEM((T, EB), bf16),
            pltpu.VMEM((T, D), f32),
        ] + [pltpu.VMEM((T * 8, 128), f32)] * (EB // 128),
        compiler_params=params(),
        name="fwd_scan",
    )(dtk, u, b_cols, c_cols, g, par, entering, act, gate, gg, out_weight, cot, tokens, normed, in_weight)


def bwd_kernel(
    L, sums, blocks, dtk_ref, u_ref, g_ref, b_ref, c_ref, par_ref, wts_ref, fin_ref, h_ref, spre_ref, act_ref, proj_ref,
    gc_ref, *refs,
):
    arrays = len(sums.kinds)
    x_refs, refs = refs[:arrays], refs[arrays:]
    gap_ref, chan_ref, gproj_ref = refs[:3]
    o_refs, refs = refs[3 : 3 + arrays], refs[3 + arrays :]
    acc_ref, gb_ref, rank_ref, pre_ref = refs[:4]
    rate = lane_tiles(rates(L, par_ref))
    tiles = len(rate)
    bsum_refs, wsum_refs = refs[4 : 4 + tiles], refs[4 + tiles : 4 + 2 * tiles]
    sums.bind(x_refs, o_refs, refs[4 + 2 * tiles :])
    T, states = u_ref.shape[0], L.N
    chunks = T // TC
    width = TC * states
    i = pl.program_id(0)

    @pl.when(i == 0)
    def _():
        acc_ref[...] = jnp.zeros_like(acc_ref)
        rank_ref[...] = jnp.zeros_like(rank_ref)
        sums.barrier()

    def chunk(i, carry):
        flow, total = list(carry[:tiles]), list(carry[tiles:])
        c = chunks - 1 - i
        base = pl.multiple_of(c * TC, TC)
        row = pl.multiple_of(c * width, width)
        b_cols, c_cols = b_ref[c], c_ref[c]

        def fetch(j):
            at = pl.ds(row + j * states, states)
            rows = [row_at(ref, base + j) for ref in (dtk_ref, u_ref, g_ref)]
            return rows + [spread(b_cols, j), spread(c_cols, j), acc_ref[at, :], lane_tiles(h_ref[at, :])]

        for j, (d, u, g, b_now, c_now, acc, before) in ahead_of(reversed(range(TC)), fetch):
            part = pl.ds((base + j) * 8, 8)
            for k in range(tiles):
                adj = c_now * g[k] + flow[k]
                flow[k] = jnp.exp2(d[k] * rate[k]) * adj
                wr = flow[k] * before[k].astype(f32) * rate[k]
                total[k] = total[k] + wr * d[k]
                wsum_refs[k][part, :] = halves(wr)
                bsum_refs[k][part, :] = halves(adj * b_now)
                acc = acc + adj * u[k]
            acc_ref[pl.ds(row + j * states, states), :] = acc
        return tuple(flow) + tuple(total)

    none = jnp.zeros((states, 128), f32)
    out = tuple(lane_tiles(fin_ref[...])) + (none,) * tiles
    for q in range(BLOCK_SLOTS):
        for n in range(sums.ticks()):
            block, quarter = divmod(n, BLOCK_SLOTS)
            if quarter == q and block < blocks:
                pl.when(i == block)(functools.partial(sums.tick, n))
        out = lax.fori_loop(q * chunks // BLOCK_SLOTS, (q + 1) * chunks // BLOCK_SLOTS, chunk, out)
    total = jnp.concatenate(out[tiles:], axis=1)
    skip = par_ref[0, L.skip : L.skip + 1, :]

    def tile(k, carry):
        bias_sum, skip_sum = carry
        rows = pl.ds(pl.multiple_of(k * 16, 16), 16)
        bsum, wsum = (
            jnp.concatenate([fold_rows(refs, k * 16), fold_rows(refs, k * 16 + 8)], axis=0)
            for refs in (bsum_refs, wsum_refs)
        )
        spre, act, g = spre_ref[rows, :], act_ref[rows, :], g_ref[rows, :]
        grad = (wsum * (1.0 / LOG2E) + act * bsum) * jax.nn.sigmoid(spre)
        gap_ref[rows, :] = g * skip + softplus(spre) * bsum
        pre_ref[rows, :] = grad.astype(bf16)
        bias_sum = bias_sum + halves(grad)
        skip_sum = skip_sum + halves(g * act)
        return bias_sum, skip_sum

    none = jnp.zeros((8, EB), f32)
    bias_sum, skip_sum = lax.fori_loop(0, T // 16, tile, (none, none))
    R = L.R
    pre = pre_ref[...]
    step_low = proj_ref[...].astype(bf16)
    grad_step_w = lax.dot_general(step_low, pre, TN, preferred_element_type=f32)
    chan_ref[0] = jnp.concatenate(
        [
            grad_step_w[0:R],
            total * (1.0 / LOG2E),
            jnp.sum(bias_sum, axis=0, keepdims=True),
            jnp.sum(skip_sum, axis=0, keepdims=True),
            jnp.zeros((128 - R - states - 2, EB), f32),
        ],
        axis=0,
    ).astype(bf16)
    weights = wts_ref[0, L.step : L.step + R, :].astype(f32)
    weights = jnp.concatenate([weights, jnp.zeros((128 - R, EB), f32)], axis=0).astype(bf16)
    rank_ref[...] += lax.dot_general(pre, weights, NT, preferred_element_type=f32)

    @pl.when(i == pl.num_programs(0) - 1)
    def _():
        lane_sums(states, acc_ref, gb_ref, chunks)
        dims = (width, 128)
        state = lax.rem(lax.broadcasted_iota(jnp.int32, dims, 0), states)
        target = lax.broadcasted_iota(jnp.int32, dims, 1)
        diag = same_step(states, T)
        total = rank_ref[...]
        for ref, start in ((gb_ref, R), (gc_ref, R + states)):
            fold = (target == state + start).astype(f32)
            kept = jnp.where(diag, ref[...], 0.0)
            total = total + jnp.dot(
                kept, fold, precision=lax.Precision.HIGHEST, preferred_element_type=f32
            )
        gproj_ref[...] = total.astype(bf16)
        for n in range(blocks * BLOCK_SLOTS, sums.ticks()):
            sums.tick(n)
        sums.drain()


def bwd_scan(L, dtk, u, g, b_cols, c_cols, par, wts, arriving, held, spre, act, proj, grad_c, arrays, sums):
    T, E = dtk.shape
    N = L.N
    blocks = E // EB
    return pl.pallas_call(
        functools.partial(bwd_kernel, L, sums, blocks),
        grid=(blocks,),
        in_specs=[
            cols(T), cols(T), cols(T), once(*b_cols.shape), once(*c_cols.shape), lead(PAR, EB),
            lead(WTS, EB), cols(N), cols(held.shape[0]), cols(T), cols(T), whole(T, 128), whole(T, TC * N),
        ] + [once(*v.shape) for v in arrays],
        out_specs=[cols(T), lead(128, EB), whole(T, 128)] + [whole(*o.shape) for o in sums.outs()],
        out_shape=[shape(f32, T, E), shape(bf16, blocks, 128, EB), shape(bf16, T, 128)] + sums.outs(),
        scratch_shapes=[
            pltpu.VMEM((T * N, 128), f32),
            pltpu.VMEM((T, TC * N), f32), pltpu.VMEM((T, 128), f32), pltpu.VMEM((T, EB), bf16),
        ] + [pltpu.VMEM((T * 8, 128), f32)] * (2 * EB // 128) + sums.scratch(),
        compiler_params=params(collective_id=3, has_side_effects=True),
        name="bwd_scan",
    )(dtk, u, g, b_cols, c_cols, par, wts, arriving, held, spre, act, proj, grad_c, *arrays)


def conv_kernel(
    L, count, gap_ref, gproj_ref, wts_ref, act_ref, cs_ref, inner_ref, marks_ref,
    gc_ref, chan_ref, after_ref, xs_ref, edge_ref, got_ref, send_sem, recv_sem,
):
    T = gap_ref.shape[0]
    i = pl.program_id(0)
    blocks = edge_ref.shape[0]
    si, ci = lax.axis_index("seq"), lax.axis_index("chan")
    before = lax.rem(ci + count - 1, count)

    @pl.when(i == 0)
    def _():
        barrier = pltpu.get_barrier_semaphore()
        for other in (before, lax.rem(ci + 1, count)):
            pl.semaphore_signal(barrier, inc=1, device_id=(si, other), device_id_type=pl.DeviceIdType.MESH)
        pl.semaphore_wait(barrier, 2)

    def edge(b):
        return pltpu.make_async_remote_copy(
            src_ref=edge_ref.at[b], dst_ref=got_ref.at[b], send_sem=send_sem.at[b], recv_sem=recv_sem.at[b],
            device_id=(si, before), device_id_type=pl.DeviceIdType.MESH,
        )

    K, wide = L.K, L.R + 2 * L.N
    weights = wts_ref[0].astype(f32)
    row = lax.broadcasted_iota(jnp.int32, weights.shape, 0)
    weights = jnp.where(row < wide, weights, 0.0).astype(bf16)
    gc_ref[...] = jnp.dot(gproj_ref[...], weights, preferred_element_type=f32)
    act_low = act_ref[...].astype(bf16)
    grad_proj = lax.dot_general(gproj_ref[...], act_low, TN, preferred_element_type=f32)
    xs_ref[...] = inner_ref[...].astype(f32)

    def tile(k, carry):
        r = pl.multiple_of(k * RT, RT)
        rows = pl.ds(r, RT)
        total = cs_ref[rows, :]
        sig = jax.nn.sigmoid(total)
        grad = (gc_ref[rows, :] + gap_ref[rows, :]) * sig * (1.0 + total * (1.0 - sig))
        gc_ref[rows, :] = grad
        block = xs_ref[pl.ds(pl.multiple_of(r + HALO - 8, 8), RT + 8), :]
        out = [carry[K] + jnp.sum(grad.reshape(RT // 8, 8, EB), axis=0)]
        for j in range(K):
            part = grad * block[8 - j : RT + 8 - j]
            if j > 0:
                part = part * marks_ref[rows, j - 1 : j]
            out.insert(0, carry[K - 1 - j] + jnp.sum(part.reshape(RT // 8, 8, EB), axis=0))
        return tuple(out)

    none = jnp.zeros((8, EB), f32)
    sums = lax.fori_loop(0, T // RT, tile, (none,) * (K + 1))
    edge_ref[i] = gc_ref[0:8, :]
    edge(i).start()
    chan_ref[0] = jnp.concatenate(
        [grad_proj[0:wide]]
        + [jnp.sum(s, axis=0, keepdims=True) for s in sums]
        + [jnp.zeros((128 - wide - K - 1, EB), f32)],
        axis=0,
    ).astype(bf16)

    @pl.when(i == blocks - 1)
    def _():
        for b in range(blocks):
            edge(b).wait()
            rows = jnp.where(ci == count - 1, 0.0, got_ref[b])
            after_ref[:, b * EB : (b + 1) * EB] = rows


def conv_back(L, count, gap, gproj, wts, act, cs, inner, marks):
    T, E = gap.shape
    blocks = E // EB
    return pl.pallas_call(
        functools.partial(conv_kernel, L, count),
        grid=(blocks,),
        in_specs=[
            cols(T), whole(T, 128), lead(WTS, EB), cols(T), cols(T), cols(T + HALO), whole(*marks.shape),
        ],
        out_specs=[cols(T), lead(128, EB), whole(8, E)],
        out_shape=[shape(f32, T, E), shape(bf16, blocks, 128, EB), shape(f32, 8, E)],
        scratch_shapes=[
            pltpu.VMEM((T + HALO, EB), f32),
            pltpu.VMEM((blocks, 8, EB), f32),
            pltpu.VMEM((blocks, 8, EB), f32),
            pltpu.SemaphoreType.DMA((blocks,)),
            pltpu.SemaphoreType.DMA((blocks,)),
        ],
        compiler_params=params(collective_id=4, has_side_effects=True),
        name="conv_back",
    )(gap, gproj, wts, act, cs, inner, marks)


def tail_kernel(
    L, gc_ref, after_ref, par_ref, marks_ref, normed_ref, wi_ref, gn_ref, tok_ref, cot_ref, gain_ref,
    gin_ref, gtok_ref, ggain_ref, ext_ref, low_ref, sum_ref,
):
    T, D = tok_ref.shape
    K = L.K
    i = pl.program_id(0)
    ext_ref[0:T, :] = gc_ref[...]
    ext_ref[T : T + 8, :] = after_ref[...]
    taps = [par_ref[0, L.conv + j : L.conv + j + 1, :] for j in range(K)]

    def tile(r):
        block = ext_ref[pl.ds(r, RT + 8), :]
        marks = marks_ref[pl.ds(r, RT + 8), :]
        total = taps[K - 1] * block[0:RT]
        for j in range(1, K):
            masked = block * marks[:, j - 1 : j]
            total = total + taps[K - 1 - j] * masked[j : RT + j]
        low_ref[pl.ds(r, RT), :] = total.astype(bf16)

    row_tiles(T, tile)
    gin_ref[...] = lax.dot_general(
        low_ref[...], normed_ref[...], TN, preferred_element_type=f32
    ).astype(bf16)
    part = lax.dot_general(low_ref[...], wi_ref[...], NT, preferred_element_type=f32)

    @pl.when(i == 0)
    def _():
        sum_ref[...] = gn_ref[...] + part

    @pl.when(i > 0)
    def _():
        sum_ref[...] += part

    @pl.when(i == pl.num_programs(0) - 1)
    def _():
        gain = gain_ref[...].reshape(1, D)

        def last(k, total):
            rows = pl.ds(pl.multiple_of(k * 16, 16), 16)
            x = tok_ref[rows, :].astype(f32)
            grad = sum_ref[rows, :]
            inv = lax.rsqrt(jnp.mean(x * x, axis=1, keepdims=True) + epsilon)
            scaled = grad * gain
            mean = jnp.mean(x * scaled, axis=1, keepdims=True)
            gtok_ref[rows, :] = (
                cot_ref[rows, :].astype(f32) + inv * scaled - x * (inv * inv * inv * mean)
            )
            return total + jnp.sum((grad * x * inv).reshape(2, 8, D), axis=0)

        total = lax.fori_loop(0, T // 16, last, jnp.zeros((8, D), f32))
        ggain_ref[...] = jnp.sum(total, axis=0, keepdims=True)


def tail(L, gc, after, par, marks, normed, in_weight, gn, tokens, cot, gain):
    T, E = gc.shape
    D = tokens.shape[1]
    blocks = E // EB
    return pl.pallas_call(
        functools.partial(tail_kernel, L),
        grid=(blocks,),
        in_specs=[
            cols(T), cols(8), lead(PAR, EB), whole(*marks.shape), whole(T, D), cols(D), whole(T, D),
            whole(T, D), whole(T, D), whole(D),
        ],
        out_specs=[tall(EB, D), whole(T, D), whole(1, D)],
        out_shape=[shape(bf16, E, D), shape(f32, T, D), shape(f32, 1, D)],
        scratch_shapes=[
            pltpu.VMEM((T + 8, EB), f32), pltpu.VMEM((T, EB), bf16), pltpu.VMEM((T, D), f32),
        ],
        compiler_params=params(),
        name="tail",
    )(gc, after, par, marks, normed, in_weight, gn, tokens, cot, gain)


class Sums:
    def __init__(self, chan_count, seq_count, kinds, shapes, phases, skew=1, pace=1):
        self.cc, self.sc = chan_count, seq_count
        self.kinds = kinds
        self.phases, self.skew, self.pace = phases, skew, pace
        self.size = 8 * seq_count
        self.bits = [1 << i for i in range(chan_count.bit_length() - 1)]
        self.z_bits = [2 << i for i in range(seq_count.bit_length() - 2)]
        self.pieces = [
            (a, r, dims[2]) for a, dims in enumerate(shapes) for r in range(0, dims[1], 2 * self.size)
        ]
        self.shapes = shapes

    def half(self, p):
        return self.kinds[self.pieces[p][0]] is not None

    def stages(self, p):
        bits = self.bits if p % 2 == 0 else self.bits[::-1]
        return (
            [("core", 1)] + [("chan", b) for b in bits] + [("z", b) for b in self.z_bits]
            + [("zgather", b) for b in self.z_bits[::-1]] + ([("move", 0)] if self.half(p) else [])
            + [("cgather", 1)]
        )

    def span(self, p):
        halvings = 1 + len(self.bits) + len(self.z_bits)
        phase = self.phases[self.pieces[p][0]]
        first = halvings if phase == "gather" else 0
        return first, halvings if phase == "halve" else len(self.stages(p))

    def begin(self, p):
        phase = self.phases[self.pieces[p][0]]
        before = [q for q in range(p) if self.phases[self.pieces[q][0]] == phase]
        return self.skew * (len(before) // 2)

    def ticks(self):
        return max(
            self.begin(p) + self.pace * (self.span(p)[1] - self.span(p)[0]) for p in range(len(self.pieces))
        ) + 1

    def final(self, p):
        a, first, width = self.pieces[p]
        return pl.ds(first // (2 * self.size) * 16, 16)

    def outs(self):
        found = []
        for kind, dims, phase in zip(self.kinds, self.shapes, self.phases):
            if phase == "halve":
                found.append(shape(bf16, dims[1] // (2 * self.size) * 16, dims[2]))
            else:
                found.append(shape(bf16, *(dims[1:] if kind is None else (2,) + tuple(dims[1:]))))
        return found

    def scratch(self):
        found = []
        for p, (a, r, width) in enumerate(self.pieces):
            small = self.span(p)[0] > 0
            for k in range(len(self.bits) + 1):
                dims = (self.cc >> k, self.size, width)
                found.append(pltpu.VMEM((1, 16, 128) if small else dims, bf16))
            for k in range(len(self.z_bits)):
                dims = (self.size >> (k + 1), width)
                found.append(pltpu.VMEM((16, 128) if small else dims, bf16))
            found.append(pltpu.VMEM((self.size, width), bf16))
        dims = (len(self.pieces), len(self.bits) + 2 * len(self.z_bits) + 3, max(2, self.cc // 2))
        return found + [pltpu.SemaphoreType.DMA(dims), pltpu.SemaphoreType.DMA(dims)]

    def bind(self, x_refs, o_refs, scratch):
        self.x, self.o = x_refs, o_refs
        each = len(self.bits) + len(self.z_bits) + 2
        self.held = [scratch[p * each : (p + 1) * each] for p in range(len(self.pieces))]
        self.send_sem, self.recv_sem = scratch[-2:]
        self.si, self.ci = lax.axis_index("seq"), lax.axis_index("chan")
        self.core = lax.rem(self.si, 2)

    def side(self, bit):
        return lax.rem(self.si // bit, 2)

    def across(self, bit):
        return (self.si + bit - 2 * bit * self.side(bit), self.ci)

    def barrier(self):
        barrier = pltpu.get_barrier_semaphore()
        others = [(self.si, lax.rem(self.ci + k, self.cc)) for k in range(1, self.cc)]
        others += [self.across(bit) for bit in [1] + self.z_bits]
        for other in others:
            pl.semaphore_signal(barrier, inc=1, device_id=other, device_id_type=pl.DeviceIdType.MESH)
        pl.semaphore_wait(barrier, len(others))

    def copy(self, p, s, slot, src, dst, device):
        return pltpu.make_async_remote_copy(
            src_ref=src, dst_ref=dst, send_sem=self.send_sem.at[p, s, slot],
            recv_sem=self.recv_sem.at[p, s, slot], device_id=device, device_id_type=pl.DeviceIdType.MESH,
        )

    def kept(self, p, s, keep):
        name, bit = self.stages(p)[s]
        if name == "core":
            a, start, width = self.pieces[p]
            side = self.core if keep else 1 - self.core
            return [self.x[a].at[:, pl.ds(pl.multiple_of(start + side * self.size, 16), self.size), :]]
        ref = self.held[p][s - 1]
        if name == "z":
            side = self.side(bit) if keep else 1 - self.side(bit)
            k = self.z_bits.index(bit)
            rows = self.size >> (k + 1)
            rows = pl.ds(pl.multiple_of(side * rows, 16), rows)
            return [ref.at[0, rows, :] if k == 0 else ref.at[rows, :]]
        mine = lax.rem(self.ci // bit, 2)
        side = mine if keep else 1 - mine
        left = sorted(b for n, b in self.stages(p)[s : 1 + len(self.bits)])
        low = 1 << left.index(bit)
        return [
            ref.at[pl.ds((i // low) * 2 * low + side * low + i % low, 1)]
            for i in range((1 << len(left)) // 2)
        ]

    def landing(self, p, s):
        dst = self.held[p][s]
        return [dst.at[pl.ds(i, 1)] for i in range(dst.shape[0])] if self.stages(p)[s][0] == "chan" else [dst]

    def gathered(self, p, done):
        start, rows = 0, self.size
        for bit in self.z_bits[:done]:
            rows //= 2
            start = start + self.side(bit) * rows
        if self.half(p):
            return self.held[p][-1].at[pl.ds(pl.multiple_of(start, 16), rows), :]
        start = start + self.pieces[p][1] + self.core * self.size
        return self.o[self.pieces[p][0]].at[pl.ds(pl.multiple_of(start, 16), rows), :]

    def places(self, p):
        a, first, width = self.pieces[p]
        rows = pl.ds(pl.multiple_of(first + self.core * self.size, 16), self.size)
        return [self.o[a].at[b, rows, :] for b in range(2)] if self.half(p) else [self.o[a].at[rows, :]]

    def move(self, p, s, v):
        goal = self.kinds[self.pieces[p][0]] + v // 2
        place = self.places(p)[v % 2]
        return goal, place, self.copy(p, s, v % 2, self.held[p][-1], place, (self.si, goal))

    def copies(self, p, s):
        name, bit = self.stages(p)[s]
        if name in ("core", "chan", "z"):
            device = (self.si, self.ci + bit - 2 * bit * lax.rem(self.ci // bit, 2))
            device = device if name == "chan" else self.across(bit)
            pairs = zip(self.kept(p, s, False), self.landing(p, s))
            return [self.copy(p, s, i, src, dst, device) for i, (src, dst) in enumerate(pairs)]
        places = self.places(p)
        if name == "zgather":
            places = [self.gathered(p, self.z_bits.index(bit) + 1)]
        return [self.copy(p, s, b, place, place, self.across(bit)) for b, place in enumerate(places)]

    def taking_part(self, p, s, work):
        if self.half(p) and self.stages(p)[s][0] == "cgather":
            base = self.kinds[self.pieces[p][0]]
            pl.when((self.ci >= base) & (self.ci < base + self.cc // 2))(work)
        else:
            work()

    def start(self, p, s):
        if self.stages(p)[s][0] == "move":
            for v in range(self.cc):
                @pl.when(self.ci == v)
                def _(v=v):
                    goal, place, copy = self.move(p, s, v)
                    if goal == v:
                        place[...] = self.held[p][-1][...]
                    else:
                        copy.start()
            return

        def work():
            for copy in self.copies(p, s):
                copy.start()

        self.taking_part(p, s, work)

    def finish(self, p, s):
        name, bit = self.stages(p)[s]
        if name == "move":
            for v in range(self.cc):
                goal, place, copy = self.move(p, s, v)
                if goal != v:
                    pl.when(self.ci == goal)(copy.wait_recv)
            return

        def work():
            for copy in self.copies(p, s):
                copy.wait_recv()

        self.taking_part(p, s, work)
        if name in ("core", "chan", "z"):
            last = s == len(self.bits) + len(self.z_bits)
            for src, dst in zip(self.kept(p, s, True), self.landing(p, s)):
                total = (dst[...].astype(f32) + src[...].astype(f32)).astype(bf16)
                if last and self.span(p)[1] == s + 1:
                    dst = self.o[self.pieces[p][0]].at[self.final(p), :]
                elif last:
                    dst = self.gathered(p, len(self.z_bits))
                dst[...] = total

    def tick(self, n):
        for p in range(len(self.pieces)):
            first, end = self.span(p)
            s, rest = divmod(n - self.begin(p), self.pace)
            s += first
            if rest != 0:
                continue
            if first + 1 <= s <= end:
                self.finish(p, s - 1)
            if first > 0 and s == first:
                self.gathered(p, len(self.z_bits))[...] = self.x[self.pieces[p][0]][self.final(p), :]
            if first <= s < end:
                self.start(p, s)

    def drain(self):
        for p in range(len(self.pieces)):
            for s in range(*self.span(p)):
                if self.stages(p)[s][0] == "move":
                    for v in range(self.cc):
                        goal, place, copy = self.move(p, s, v)
                        if goal != v:
                            pl.when(self.ci == v)(copy.wait_send)
                    continue

                def work(p=p, s=s):
                    for copy in self.copies(p, s):
                        copy.wait_send()

                self.taking_part(p, s, work)


def sum_kernel(sums, *refs):
    arrays = len(sums.kinds)
    sums.bind(refs[:arrays], refs[arrays : 2 * arrays], refs[2 * arrays :])
    sums.barrier()
    for n in range(sums.ticks()):
        sums.tick(n)
    sums.drain()


def sum_owned(arrays, shapes, kinds, phases, chan_count, seq_count):
    sums = Sums(chan_count, seq_count, kinds, shapes, phases)
    vmem = pl.BlockSpec(memory_space=pltpu.VMEM)
    return pl.pallas_call(
        functools.partial(sum_kernel, sums),
        in_specs=[vmem] * len(arrays),
        out_specs=[vmem] * len(arrays),
        out_shape=sums.outs(),
        scratch_shapes=sums.scratch(),
        compiler_params=params(collective_id=0, has_side_effects=True),
        name="sum_owned",
    )(*arrays)


def unpack_kernel(L, inner_ref, gate_ref, out_ref, d_ref, e_ref, gin_ref, gout_ref, *refs):
    first = lax.axis_index("chan") < lax.axis_size("chan") // 2

    @pl.when(first)
    def _():
        gin_ref[...] = inner_ref[...].astype(f32).T

    @pl.when(jnp.logical_not(first))
    def _():
        gin_ref[...] = gate_ref[...].astype(f32).T

    gout_ref[...] = out_ref[...].astype(f32)
    d, e = d_ref[...].astype(f32), e_ref[...].astype(f32)
    R, N, K = L.R, L.N, L.K
    wide = R + 2 * N
    conv_w, conv_b, proj, step_w, step_b, decay, skip, gain = refs
    width = d.shape[1]
    step_w[...] = d[0:R]
    decay[...] = d[R : R + N]
    step_b[...] = d[R + N].reshape(width)
    skip[...] = d[R + N + 1].reshape(width)
    proj[...] = e[0:wide]
    conv_w[...] = e[wide : wide + K]
    conv_b[...] = e[wide + K].reshape(width)
    gain[...] = e[wide + K + 1].reshape(width)


def unpack(L, sums):
    width = sums[3].shape[1]
    rows, D = sums[0].shape
    R, N, K = L.R, L.N, L.K
    return pl.pallas_call(
        functools.partial(unpack_kernel, L),
        out_shape=[
            shape(f32, D, rows), shape(f32, *sums[2].shape), shape(f32, K, width), shape(f32, width),
            shape(f32, R + 2 * N, width), shape(f32, R, width), shape(f32, width),
            shape(f32, N, width), shape(f32, width), shape(f32, width),
        ],
        compiler_params=params(),
        name="unpack",
    )(*sums)


def local(
    tokens, norm_gain, in_weight, conv_weight, conv_bias, proj_weight, step_weight,
    step_bias, decay_log, skip_gain, out_weight, cotangent, lengths,
):
    T, D = tokens.shape
    E = in_weight.shape[1] // 2
    L = Layout(step_weight.shape[0], decay_log.shape[0], conv_weight.shape[0])
    ci = lax.axis_index("chan")
    cc = lax.axis_size("chan")
    sc = lax.axis_size("seq")
    blocks, share = E // EB, E // cc

    parts = (conv_weight, conv_bias, proj_weight.T, step_weight, step_bias, decay_log, skip_gain)
    gathered = None
    if share != EB:
        wts, par, halo = gather_params(L, cc, parts, tokens)

        def by_block(values):
            values = jnp.moveaxis(values, 0, 1).reshape(-1, blocks, EB)
            return jnp.moveaxis(values, 1, 0)

        parts, gathered = None, (by_block(wts), by_block(par), halo)
    marks, normed, inner, gate, gg, g, cs, act, proj, b_cols, c_cols, *own = front(
        L, cc, lengths, tokens, norm_gain, in_weight, out_weight, cotangent, parts, gathered
    )
    wts, par = gathered[:2] if gathered else own
    spre, dtk, u, entering, arriving = pre_scan(L, cc, proj, par, wts, act, g, marks, b_cols, c_cols)
    held, grad_c, block_out, grad_out, grad_in_gate, gn = fwd_scan(
        L, dtk, u, b_cols, c_cols, g, par, entering, act, gate, gg, out_weight, cotangent, tokens,
        normed, in_weight,
    )

    piece = 16 * sc
    fold = 2 if 2 * share <= piece else 1

    def owned(values):
        values = values.reshape(cc, -1, values.shape[-1] // fold)
        return jnp.pad(values, ((0, 0), (0, -values.shape[1] % piece), (0, 0)))

    def unfolded(values):
        if values.ndim == 2:
            return values[: share * fold].reshape(share, D)
        return values[:, : share * fold].reshape(2 * share, D)

    def by_owner(values):
        if share != EB:
            values = jnp.moveaxis(values, 0, 1).reshape(values.shape[1], cc, share)
            values = jnp.moveaxis(values, 1, 0)
        return jnp.pad(values, ((0, 0), (0, -values.shape[1] % piece), (0, 0)))

    early = [owned(grad_out), owned(grad_in_gate)]
    early_shapes = [v.shape for v in early]
    kinds = [None, cc // 2]
    sums = Sums(cc, sc, kinds, early_shapes, ["halve"] * 2, skew=3, pace=2)
    gap, chan_d, gproj, *early = bwd_scan(
        L, dtk, u, g, b_cols, c_cols, par, wts, arriving, held, spre, act, proj, grad_c, early, sums
    )
    gc, chan_e, after = conv_back(L, cc, gap, gproj, wts, act, cs, inner, marks)
    grad_in_inner, grad_tokens, grad_gain = tail(
        L, gc, after, par, marks, normed, in_weight, gn, tokens, cotangent, norm_gain
    )
    row = L.R + 2 * L.N + L.K + 1
    gain_part = jnp.pad(grad_gain.reshape(cc, 1, D // cc), ((0, 0), (0, 0), (0, share - D // cc)))
    chan_e = lax.dynamic_update_slice(by_owner(chan_e), gain_part.astype(bf16), (0, row, 0))
    late = [owned(grad_in_inner), by_owner(chan_d), chan_e]
    sum_inner, sum_d, sum_e, sum_out, sum_gate = sum_owned(
        late + early, [v.shape for v in late] + early_shapes, [0, None, None] + kinds,
        ["all"] * 3 + ["gather"] * 2, cc, sc,
    )
    sums = [unfolded(v) for v in (sum_inner, sum_gate, sum_out)] + [sum_d, sum_e]
    g_in, g_out, conv_w, conv_b, proj_w, step_w, step_b, decay, skip, g_gain = unpack(L, sums)
    return (
        block_out, grad_tokens, g_gain[: D // cc], g_in, conv_w, conv_b, proj_w.T, step_w,
        step_b, decay, skip, g_out,
    )


def solution(mesh):
    tok, row, vec = P(("seq", "chan"), None), P(None, "chan"), P("chan")
    in_specs = (
        tok, P(), P(), row, vec, P("chan", None), row, vec, row, vec, P(), tok, P("seq", None),
    )
    out_specs = (
        tok, tok, vec, row, row, vec, P("chan", None), row, vec, row, vec, P("chan", None),
    )
    return jax.shard_map(local, mesh=mesh, in_specs=in_specs, out_specs=out_specs, check_vma=False)
```

```python
import functools
import math

import jax
import jax.numpy as jnp
from jax import lax
from jax.experimental import pallas as pl
from jax.experimental.pallas import tpu as pltpu
from jax.sharding import PartitionSpec as P

epsilon = 1e-05
LOG2E = math.log2(math.e)
CUT = 1e30
TC = 32
EB = 384
RT = 32
BLOCK_SLOTS = 4
HALO = 16
PAR = 24
WTS = 128
f32 = jnp.float32
bf16 = jnp.bfloat16
NT = (((1,), (1,)), ((), ()))
TN = (((0,), (0,)), ((), ()))


def params(**more):
    return pltpu.CompilerParams(vmem_limit_bytes=60 * 1024 * 1024, **more)


def cols(rows, width=EB, shift=0):
    return pl.BlockSpec((rows, width), lambda i: (0, i + shift))


def tall(rows, width, shift=0):
    return pl.BlockSpec((rows, width), lambda i: (i + shift, 0))


def lead(rows, width, count=1):
    return pl.BlockSpec((count, rows, width), lambda i: (i, 0, 0))


def whole(*shape):
    return pl.BlockSpec(shape, lambda i: (0,) * len(shape))


def once(*shape):
    return pl.BlockSpec(shape, lambda i: (0,) * len(shape), pipeline_mode=pl.Buffered(1))


def shape(dtype, *dims):
    return jax.ShapeDtypeStruct(dims, dtype)


def row_tiles(count, body):
    def step(i, unused):
        body(pl.multiple_of(i * RT, RT))
        return unused

    lax.fori_loop(0, count // RT, step, 0)


def same_step(states, rows):
    dims = (rows, TC * states)
    here = lax.rem(lax.broadcasted_iota(jnp.int32, dims, 0), TC) * states
    place = lax.broadcasted_iota(jnp.int32, dims, 1)
    return (place >= here) & (place < here + states)


class Layout:
    def __init__(self, R, N, K):
        self.R, self.N, self.K = R, N, K
        self.step = R + 2 * N
        self.decay = 0
        self.conv = self.decay + N
        self.conv_b = self.conv + K
        self.step_b = self.conv_b + 1
        self.skip = self.step_b + 1
        self.end = self.skip + 1


def start_gather(
    L, count, cw_ref, cb_ref, pw_ref, sw_ref, sb_ref, dl_ref, sk_ref, tok_ref,
    wts_ref, par_ref, halo_ref, send_sem, recv_sem, halo_sems,
):
    si, ci = lax.axis_index("seq"), lax.axis_index("chan")
    T = tok_ref.shape[0]
    width = par_ref.shape[2]
    barrier = pltpu.get_barrier_semaphore()
    for k in range(1, count):
        pl.semaphore_signal(
            barrier, inc=1, device_id=(si, lax.rem(ci + k, count)),
            device_id_type=pl.DeviceIdType.MESH,
        )
    own, weights = par_ref.at[ci], wts_ref.at[ci]
    weights[...] = jnp.concatenate(
        [pw_ref[...].astype(f32), sw_ref[...].astype(f32)], axis=0
    ).astype(bf16)
    own[...] = jnp.concatenate(
        [
            dl_ref[...], cw_ref[...], cb_ref[...].reshape(1, width), sb_ref[...].reshape(1, width),
            sk_ref[...].reshape(1, width), jnp.zeros((PAR - L.end, width), f32),
        ],
        axis=0,
    )
    pl.semaphore_wait(barrier, count - 1)

    def share(ref, j, k):
        return pltpu.make_async_remote_copy(
            src_ref=ref, dst_ref=ref, send_sem=send_sem.at[j, k], recv_sem=recv_sem.at[j, k],
            device_id=(si, lax.rem(ci + k, count)), device_id_type=pl.DeviceIdType.MESH,
        )

    edge = pltpu.make_async_remote_copy(
        src_ref=tok_ref.at[pl.ds(T - HALO, HALO)], dst_ref=halo_ref,
        send_sem=halo_sems.at[0], recv_sem=halo_sems.at[1],
        device_id=(si, lax.rem(ci + 1, count)), device_id_type=pl.DeviceIdType.MESH,
    )
    edge.start()
    for j, ref in enumerate((own, weights)):
        for k in range(1, count):
            share(ref, j, k).start()

    def wait():
        edge.wait()
        for j, ref in enumerate((own, weights)):
            for k in range(1, count):
                share(ref, j, k).wait()

    return wait


def gather_kernel(L, count, *refs):
    start_gather(L, count, *refs)()


def gather_scratch(count):
    return [
        pltpu.SemaphoreType.DMA((2, count)),
        pltpu.SemaphoreType.DMA((2, count)),
        pltpu.SemaphoreType.DMA((2,)),
    ]


def gather_params(L, count, parts, tokens):
    width = parts[0].shape[1]
    T, D = tokens.shape
    vmem = pl.BlockSpec(memory_space=pltpu.VMEM)
    return pl.pallas_call(
        functools.partial(gather_kernel, L, count),
        in_specs=[vmem] * 8,
        out_specs=[vmem] * 3,
        out_shape=[shape(bf16, count, WTS, width), shape(f32, count, PAR, width), shape(bf16, HALO, D)],
        scratch_shapes=gather_scratch(count),
        compiler_params=params(collective_id=1, has_side_effects=True),
        name="gather_params",
    )(*parts, tokens)


def front_kernel(
    L, count, inside, len_ref, tok_ref, gain_ref, wi_ref, wg_ref, wo_ref, cot_ref, *refs,
):
    given, refs = refs[: 7 if inside else 3], refs[7 if inside else 3 :]
    (
        marks_ref, normed_ref, inner_ref, gate_ref, gg_ref, g_ref, cs_ref, act_ref, proj_ref, bch_ref, cch_ref,
    ) = refs[:11]
    results, refs = refs[11 : 13 if inside else 11], refs[13 if inside else 11 :]
    hn_ref, xs_ref, low_ref = refs[:3]
    T = tok_ref.shape[0]
    N, K = L.N, L.K
    i = pl.program_id(0)
    sub = low_ref.shape[1] // EB
    if inside:
        wts_ref, par_ref, halo_ref, *sems = refs[3:]
        first = i * sub
    else:
        wts_ref, par_ref, halo_ref = given
        first = 0

    def norm(x):
        x = x.astype(f32)
        inv = lax.rsqrt(jnp.mean(x * x, axis=1, keepdims=True) + epsilon)
        return (x * inv * gain_ref[...].reshape(1, x.shape[1])).astype(bf16)

    def products():
        low = jnp.dot(normed_ref[...], wi_ref[...], preferred_element_type=f32).astype(bf16)
        inner_ref[HALO:, :] = low
        xs_ref[HALO:, :] = low.astype(f32)
        gate_ref[...] = jnp.dot(normed_ref[...], wg_ref[...], preferred_element_type=f32)
        gg_ref[...] = lax.dot_general(cot_ref[...], wo_ref[...], NT, preferred_element_type=f32)

    @pl.when(i == 0)
    def _():
        if inside:
            wait = start_gather(L, count, *given, tok_ref, wts_ref, par_ref, halo_ref, *sems)

        def tile(r):
            normed_ref[pl.ds(r, RT), :] = norm(tok_ref[pl.ds(r, RT), :])

        row_tiles(T, tile)
        proj_ref[...] = jnp.zeros_like(proj_ref)
        dims = marks_ref.shape
        place = lax.broadcasted_iota(jnp.int32, dims, 0) + lax.axis_index("chan") * T
        lane = lax.broadcasted_iota(jnp.int32, dims, 1)
        reach = jnp.where(lane < K - 1, lane + 1, 1)
        found = jnp.zeros(dims, f32)
        start = jnp.int32(0)
        for k in range(len_ref.shape[1]):
            found = jnp.where((start > place - reach) & (start <= place), 1.0, found)
            start = start + len_ref[0, k]
        marks_ref[...] = jnp.where(lane < K - 1, 1.0 - found, found * CUT)
        products()
        if inside:
            wait()
            results[0][...] = wts_ref[...]
            results[1][...] = par_ref[...]
        lead_device = lax.axis_index("chan") == 0
        halo = jnp.where(lead_device, jnp.zeros(halo_ref.shape, f32), halo_ref[...].astype(f32))
        hn_ref[...] = norm(halo)

    pl.when(i > 0)(products)
    low = jnp.dot(hn_ref[...], wi_ref[...], preferred_element_type=f32).astype(bf16)
    inner_ref[0:HALO, :] = low
    xs_ref[0:HALO, :] = low.astype(f32)

    for k in range(sub):
        c = slice(k * EB, (k + 1) * EB)
        taps = [par_ref[first + k, L.conv + j : L.conv + j + 1, :] for j in range(K)]
        bias = par_ref[first + k, L.conv_b : L.conv_b + 1, :]

        def tile(r, c=c, taps=taps, bias=bias):
            rows = pl.ds(r, RT)
            block = xs_ref[pl.ds(pl.multiple_of(r + HALO - 8, 8), RT + 8), c]
            total = bias + taps[K - 1] * block[8:]
            for j in range(1, K):
                usable = marks_ref[rows, j - 1 : j]
                total = total + taps[K - 1 - j] * (block[8 - j : RT + 8 - j] * usable)
            act = total * jax.nn.sigmoid(total)
            cs_ref[rows, c] = total
            act_ref[rows, c] = act
            low_ref[rows, c] = act.astype(bf16)
            gate = gate_ref[rows, c]
            passed = gg_ref[rows, c] * (gate * jax.nn.sigmoid(gate))
            g_ref[rows, c] = passed.astype(bf16).astype(f32)

        row_tiles(T, tile)
        proj_ref[...] += lax.dot_general(low_ref[:, c], wts_ref[first + k], NT, preferred_element_type=f32)

    @pl.when(i == pl.num_programs(0) - 1)
    def _():
        turned = proj_ref[...].T
        for ref, start in ((bch_ref, L.R), (cch_ref, L.R + N)):
            for j in range(T // TC):
                ref[j] = turned[start : start + N, j * TC : (j + 1) * TC]


def front(L, count, lengths, tokens, gain, in_weight, out_weight, cot, parts, gathered):
    T, D = tokens.shape
    E = out_weight.shape[0]
    sub = 2
    wide = EB * sub
    steps = E // wide
    N = L.N
    inside = parts is not None
    more_out, scratch, options = [], [], {}
    if inside:
        given, given_specs = parts, [whole(*v.shape) for v in parts]
        more_out = [shape(bf16, count, WTS, EB), shape(f32, count, PAR, EB)]
        scratch = [pltpu.VMEM(o.shape, o.dtype) for o in more_out] + [pltpu.VMEM((HALO, D), bf16)]
        scratch += gather_scratch(count)
        options = dict(collective_id=1, has_side_effects=True)
    else:
        given, given_specs = gathered, [lead(WTS, EB, sub), lead(PAR, EB, sub), whole(HALO, D)]
    return pl.pallas_call(
        functools.partial(front_kernel, L, count, inside),
        grid=(steps,),
        in_specs=[
            pl.BlockSpec(memory_space=pltpu.SMEM),
            whole(T, D), whole(D), cols(D, wide), cols(D, wide, steps), tall(wide, D), whole(T, D),
        ] + given_specs,
        out_specs=[whole(T + 8, 8), whole(T, D), cols(T + HALO, wide)] + [cols(T, wide)] * 5 + [
            whole(T, 128), whole(T // TC, N, TC), whole(T // TC, N, TC),
        ] + [whole(*o.shape) for o in more_out],
        out_shape=[shape(f32, T + 8, 8), shape(bf16, T, D), shape(bf16, T + HALO, E)]
        + [shape(f32, T, E)] * 5
        + [shape(f32, T, 128), shape(f32, T // TC, N, TC), shape(f32, T // TC, N, TC)]
        + more_out,
        scratch_shapes=[
            pltpu.VMEM((HALO, D), bf16),
            pltpu.VMEM((T + HALO, wide), f32),
            pltpu.VMEM((T, wide), bf16),
        ] + scratch,
        compiler_params=params(**options),
        name="front",
    )(lengths, tokens, gain, in_weight, in_weight, out_weight, cot, *given)


def rates(L, par_ref):
    return -jnp.exp(par_ref[0, L.decay : L.decay + L.N, :]) * LOG2E


def lane_tiles(values):
    return [values[:, k * 128 : (k + 1) * 128] for k in range(EB // 128)]


def row_at(ref, t):
    return lane_tiles(ref[pl.ds(t, 1), :])


def spread(columns, j):
    return jnp.broadcast_to(columns[:, j : j + 1], (columns.shape[0], 128))


def ahead_of(steps, fetch):
    steps = list(steps)
    loaded = [fetch(j) for j in steps[:2]]
    for k, j in enumerate(steps):
        if k + 2 < len(steps):
            loaded.append(fetch(steps[k + 2]))
        yield j, loaded[k]


def softplus(x):
    return jnp.maximum(x, 0.0) + jnp.log1p(jnp.exp(-jnp.abs(x)))


def pre_kernel(
    L, count, proj_ref, par_ref, wts_ref, act_ref, g_ref, marks_ref, b_ref, c_ref,
    spre_ref, dtk_ref, u_ref, enter_ref, arrive_ref, ahead_ref, behind_ref, got_ref,
    send_sem, recv_sem,
):
    T, E = act_ref.shape[0], enter_ref.shape[1]
    N = L.N
    i = pl.program_id(0)
    blocks = E // EB
    si, ci = lax.axis_index("seq"), lax.axis_index("chan")

    @pl.when(i == 0)
    def _():
        barrier = pltpu.get_barrier_semaphore()
        for k in range(1, count):
            pl.semaphore_signal(
                barrier, inc=1, device_id=(si, lax.rem(ci + k, count)),
                device_id_type=pl.DeviceIdType.MESH,
            )
        pl.semaphore_wait(barrier, count - 1)

    low = proj_ref[:, 0 : L.R].astype(bf16)
    weights = wts_ref[0, L.step : L.step + L.R, :]
    bias = par_ref[0, L.step_b : L.step_b + 1, :]
    spre_ref[...] = jnp.dot(low, weights, preferred_element_type=f32) + bias

    def tile(r):
        rows = pl.ds(r, RT)
        step = softplus(spre_ref[rows, :])
        u_ref[rows, :] = step * act_ref[rows, :]
        dtk_ref[rows, :] = step + marks_ref[rows, 3:4]

    row_tiles(T, tile)
    rate = lane_tiles(rates(L, par_ref))
    tiles = len(rate)

    def chunk(c, carry):
        h, through, head = (list(carry[k * tiles : (k + 1) * tiles]) for k in range(3))
        base = pl.multiple_of(c * TC, TC)
        b_cols, c_cols = b_ref[c], c_ref[c]

        def fetch(j):
            rows = [row_at(ref, base + j) for ref in (dtk_ref, u_ref, g_ref)]
            return rows + [spread(b_cols, j), spread(c_cols, j)]

        for j, (d, u, g, b_now, c_now) in ahead_of(range(TC), fetch):
            for k in range(tiles):
                factor = jnp.exp2(d[k] * rate[k])
                h[k] = factor * h[k] + b_now * u[k]
                through[k] = factor * through[k]
                head[k] = head[k] + through[k] * (c_now * g[k])
        return tuple(h + through + head)

    zero = jnp.zeros((N, 128), f32)
    out = lax.fori_loop(0, T // TC, chunk, (zero,) * tiles + (zero + 1.0,) * tiles + (zero,) * tiles)
    h, through, head = (jnp.concatenate(out[k * tiles : (k + 1) * tiles], axis=1) for k in range(3))
    zero = jnp.zeros((N, EB), f32)
    ahead_ref[i, 0:N, :] = h
    ahead_ref[i, N:, :] = through
    behind_ref[i, 0:N, :] = head
    behind_ref[i, N:, :] = through

    def send(b, k, forward):
        return pltpu.make_async_remote_copy(
            src_ref=(ahead_ref if forward else behind_ref).at[b], dst_ref=got_ref.at[count - k, b],
            send_sem=send_sem.at[k, b], recv_sem=recv_sem.at[count - k, b],
            device_id=(si, lax.rem(ci + k, count)), device_id_type=pl.DeviceIdType.MESH,
        )

    for k in range(1, count):
        @pl.when(ci + k < count)
        def _(k=k):
            send(i, k, True).start()

        @pl.when(ci + k >= count)
        def _(k=k):
            send(i, k, False).start()

    @pl.when(i == blocks - 1)
    def _():
        for b in range(blocks):
            for k in range(1, count):
                send(b, k, True).wait()
        for b in range(blocks):
            span = slice(b * EB, (b + 1) * EB)
            entering, arriving = zero, zero
            for k in range(1, count):
                before = ci + k >= count
                got = got_ref[k, b]
                entering = jnp.where(before, got[0:N] + got[N:] * entering, entering)
            for k in range(count - 1, 0, -1):
                behind = ci + k < count
                got = got_ref[k, b]
                arriving = jnp.where(behind, got[0:N] + got[N:] * arriving, arriving)
            enter_ref[:, span] = entering
            arrive_ref[:, span] = arriving


def pre_scan(L, count, proj, par, wts, act, g, marks, b_cols, c_cols):
    T, E = act.shape
    N = L.N
    blocks = E // EB
    state = shape(f32, N, E)
    return pl.pallas_call(
        functools.partial(pre_kernel, L, count),
        grid=(blocks,),
        in_specs=[
            whole(T, 128), lead(PAR, EB), lead(WTS, EB), cols(T), cols(T), whole(*marks.shape),
            once(*b_cols.shape), once(*c_cols.shape),
        ],
        out_specs=[cols(T)] * 3 + [whole(N, E)] * 2,
        out_shape=[shape(f32, T, E)] * 3 + [state] * 2,
        scratch_shapes=[
            pltpu.VMEM((blocks, 2 * N, EB), f32),
            pltpu.VMEM((blocks, 2 * N, EB), f32),
            pltpu.VMEM((count, blocks, 2 * N, EB), f32),
            pltpu.SemaphoreType.DMA((count, blocks)),
            pltpu.SemaphoreType.DMA((count, blocks)),
        ],
        compiler_params=params(collective_id=2, has_side_effects=True),
        name="pre_scan",
    )(proj, par, wts, act, g, marks, b_cols, c_cols)


def fold_rows(refs, r):
    sums = []
    for ref in refs:
        parts = [ref[pl.ds(r * 8 + k, 8, stride=8), :] for k in range(8)]
        while len(parts) > 1:
            parts = [x + y for x, y in zip(parts[::2], parts[1::2])]
        sums.append(parts[0])
    return jnp.concatenate(sums, axis=1)


def halves(values):
    return values[0:8] + values[8:16]


def lane_sums(states, acc_ref, out_ref, chunks):
    width = TC * states
    ones = jnp.ones((TC, 128), bf16)
    group = chunks // 4
    for k in range(4):
        part = acc_ref[k * group * width : (k + 1) * group * width, :].astype(bf16)
        sums = lax.dot_general(ones, part, NT, preferred_element_type=f32)
        for c in range(group):
            row = (k * group + c) * TC
            out_ref[row : row + TC, :] = sums[:, c * width : (c + 1) * width]


def fwd_kernel(
    L, dtk_ref, u_ref, b_ref, c_ref, g_ref, par_ref, hin_ref, act_ref, gate_ref, gg_ref,
    wo_ref, cot_ref, tok_ref, normed_ref, wg_ref,
    h_ref, gc_ref, block_ref, gout_ref, gin_ref, gn_ref,
    acc_ref, gated_ref, ggate_ref, branch_ref, *y_refs,
):
    rate = lane_tiles(rates(L, par_ref))
    T, states = u_ref.shape[0], L.N
    chunks = T // TC
    width = TC * states
    i = pl.program_id(0)

    @pl.when(i == 0)
    def _():
        acc_ref[...] = jnp.zeros_like(acc_ref)
        gn_ref[...] = jnp.zeros_like(gn_ref)
        branch_ref[...] = jnp.zeros_like(branch_ref)

    h_ref[0:states, :] = hin_ref[...].astype(bf16)

    def chunk(c, carry):
        h = list(carry)
        base = pl.multiple_of(c * TC, TC)
        row = pl.multiple_of(c * width, width)
        b_cols, c_cols = b_ref[c], c_ref[c]

        def fetch(j):
            at = pl.ds(row + j * states, states)
            rows = [row_at(ref, base + j) for ref in (dtk_ref, u_ref, g_ref)]
            return rows + [spread(b_cols, j), spread(c_cols, j), acc_ref[at, :]]

        for j, (d, u, g, b_now, c_now, acc) in ahead_of(range(TC), fetch):
            for k in range(len(h)):
                h[k] = jnp.exp2(d[k] * rate[k]) * h[k] + b_now * u[k]
                h_ref[pl.ds(row + (j + 1) * states, states), k * 128 : (k + 1) * 128] = h[k].astype(bf16)
                y_refs[k][pl.ds((base + j) * 8, 8), :] = halves(c_now * h[k])
                acc = acc + h[k] * g[k]
            acc_ref[pl.ds(row + j * states, states), :] = acc
        return tuple(h)

    lax.fori_loop(0, chunks, chunk, tuple(lane_tiles(hin_ref[...])))
    skip = par_ref[0, L.skip : L.skip + 1, :]

    def tile(k, unused):
        rows = pl.ds(pl.multiple_of(k * 16, 16), 16)
        y = jnp.concatenate([fold_rows(y_refs, k * 16), fold_rows(y_refs, k * 16 + 8)], axis=0)
        mixer = (y + skip * act_ref[rows, :]).astype(bf16).astype(f32)
        gate = gate_ref[rows, :]
        sig = jax.nn.sigmoid(gate)
        gated_ref[rows, :] = (mixer * (gate * sig)).astype(bf16)
        ggate_ref[rows, :] = (gg_ref[rows, :] * mixer * sig * (1.0 + gate * (1.0 - sig))).astype(bf16)
        return unused

    lax.fori_loop(0, T // 16, tile, 0)
    branch_ref[...] += jnp.dot(gated_ref[...], wo_ref[...], preferred_element_type=f32)
    gout_ref[...] = lax.dot_general(
        gated_ref[...], cot_ref[...], TN, preferred_element_type=f32
    ).astype(bf16)
    gin_ref[...] = lax.dot_general(
        ggate_ref[...], normed_ref[...], TN, preferred_element_type=f32
    ).astype(bf16)
    gn_ref[...] += lax.dot_general(ggate_ref[...], wg_ref[...], NT, preferred_element_type=f32)

    @pl.when(i == pl.num_programs(0) - 1)
    def _():
        block_ref[...] = (tok_ref[...].astype(f32) + branch_ref[...]).astype(bf16)
        lane_sums(states, acc_ref, gc_ref, chunks)


def fwd_scan(L, dtk, u, b_cols, c_cols, g, par, entering, act, gate, gg, out_weight, cot, tokens, normed, in_weight):
    T, E = dtk.shape
    D = tokens.shape[1]
    N = L.N
    rows = (T + 1) * N
    blocks = E // EB
    return pl.pallas_call(
        functools.partial(fwd_kernel, L),
        grid=(blocks,),
        in_specs=[
            cols(T), cols(T), once(*b_cols.shape), once(*c_cols.shape), cols(T), lead(PAR, EB), cols(N),
            cols(T), cols(T), cols(T), tall(EB, D), whole(T, D), whole(T, D), whole(T, D),
            cols(D, EB, blocks),
        ],
        out_specs=[
            cols(rows), whole(T, TC * N), whole(T, D), tall(EB, D), tall(EB, D), whole(T, D),
        ],
        out_shape=[
            shape(bf16, rows, E), shape(f32, T, TC * N), shape(bf16, T, D), shape(bf16, E, D),
            shape(bf16, E, D), shape(f32, T, D),
        ],
        scratch_shapes=[
            pltpu.VMEM((T * N, 128), f32), pltpu.VMEM((T, EB), bf16), pltpu.VMEM((T, EB), bf16),
            pltpu.VMEM((T, D), f32),
        ] + [pltpu.VMEM((T * 8, 128), f32)] * (EB // 128),
        compiler_params=params(),
        name="fwd_scan",
    )(dtk, u, b_cols, c_cols, g, par, entering, act, gate, gg, out_weight, cot, tokens, normed, in_weight)


def bwd_kernel(
    L, sums, blocks, dtk_ref, u_ref, g_ref, b_ref, c_ref, par_ref, wts_ref, fin_ref, h_ref, spre_ref, act_ref, proj_ref,
    gc_ref, *refs,
):
    arrays = len(sums.kinds)
    x_refs, refs = refs[:arrays], refs[arrays:]
    gap_ref, chan_ref, gproj_ref = refs[:3]
    o_refs, refs = refs[3 : 3 + arrays], refs[3 + arrays :]
    acc_ref, gb_ref, rank_ref, pre_ref = refs[:4]
    rate = lane_tiles(rates(L, par_ref))
    tiles = len(rate)
    bsum_refs, wsum_refs = refs[4 : 4 + tiles], refs[4 + tiles : 4 + 2 * tiles]
    sums.bind(x_refs, o_refs, refs[4 + 2 * tiles :])
    T, states = u_ref.shape[0], L.N
    chunks = T // TC
    width = TC * states
    i = pl.program_id(0)

    @pl.when(i == 0)
    def _():
        acc_ref[...] = jnp.zeros_like(acc_ref)
        rank_ref[...] = jnp.zeros_like(rank_ref)
        sums.barrier()

    def chunk(i, carry):
        flow, total = list(carry[:tiles]), list(carry[tiles:])
        c = chunks - 1 - i
        base = pl.multiple_of(c * TC, TC)
        row = pl.multiple_of(c * width, width)
        b_cols, c_cols = b_ref[c], c_ref[c]

        def fetch(j):
            at = pl.ds(row + j * states, states)
            rows = [row_at(ref, base + j) for ref in (dtk_ref, u_ref, g_ref)]
            return rows + [spread(b_cols, j), spread(c_cols, j), acc_ref[at, :], lane_tiles(h_ref[at, :])]

        for j, (d, u, g, b_now, c_now, acc, before) in ahead_of(reversed(range(TC)), fetch):
            part = pl.ds((base + j) * 8, 8)
            for k in range(tiles):
                adj = c_now * g[k] + flow[k]
                flow[k] = jnp.exp2(d[k] * rate[k]) * adj
                wr = flow[k] * before[k].astype(f32) * rate[k]
                total[k] = total[k] + wr * d[k]
                wsum_refs[k][part, :] = halves(wr)
                bsum_refs[k][part, :] = halves(adj * b_now)
                acc = acc + adj * u[k]
            acc_ref[pl.ds(row + j * states, states), :] = acc
        return tuple(flow) + tuple(total)

    none = jnp.zeros((states, 128), f32)
    out = tuple(lane_tiles(fin_ref[...])) + (none,) * tiles
    for q in range(BLOCK_SLOTS):
        for n in range(sums.ticks()):
            block, quarter = divmod(n, BLOCK_SLOTS)
            if quarter == q and block < blocks:
                pl.when(i == block)(functools.partial(sums.tick, n))
        out = lax.fori_loop(q * chunks // BLOCK_SLOTS, (q + 1) * chunks // BLOCK_SLOTS, chunk, out)
    total = jnp.concatenate(out[tiles:], axis=1)
    skip = par_ref[0, L.skip : L.skip + 1, :]

    def tile(k, carry):
        bias_sum, skip_sum = carry
        rows = pl.ds(pl.multiple_of(k * 16, 16), 16)
        bsum, wsum = (
            jnp.concatenate([fold_rows(refs, k * 16), fold_rows(refs, k * 16 + 8)], axis=0)
            for refs in (bsum_refs, wsum_refs)
        )
        spre, act, g = spre_ref[rows, :], act_ref[rows, :], g_ref[rows, :]
        grad = (wsum * (1.0 / LOG2E) + act * bsum) * jax.nn.sigmoid(spre)
        gap_ref[rows, :] = g * skip + softplus(spre) * bsum
        pre_ref[rows, :] = grad.astype(bf16)
        bias_sum = bias_sum + halves(grad)
        skip_sum = skip_sum + halves(g * act)
        return bias_sum, skip_sum

    none = jnp.zeros((8, EB), f32)
    bias_sum, skip_sum = lax.fori_loop(0, T // 16, tile, (none, none))
    R = L.R
    pre = pre_ref[...]
    step_low = proj_ref[...].astype(bf16)
    grad_step_w = lax.dot_general(step_low, pre, TN, preferred_element_type=f32)
    chan_ref[0] = jnp.concatenate(
        [
            grad_step_w[0:R],
            total * (1.0 / LOG2E),
            jnp.sum(bias_sum, axis=0, keepdims=True),
            jnp.sum(skip_sum, axis=0, keepdims=True),
            jnp.zeros((128 - R - states - 2, EB), f32),
        ],
        axis=0,
    ).astype(bf16)
    weights = wts_ref[0, L.step : L.step + R, :].astype(f32)
    weights = jnp.concatenate([weights, jnp.zeros((128 - R, EB), f32)], axis=0).astype(bf16)
    rank_ref[...] += lax.dot_general(pre, weights, NT, preferred_element_type=f32)

    @pl.when(i == pl.num_programs(0) - 1)
    def _():
        lane_sums(states, acc_ref, gb_ref, chunks)
        dims = (width, 128)
        state = lax.rem(lax.broadcasted_iota(jnp.int32, dims, 0), states)
        target = lax.broadcasted_iota(jnp.int32, dims, 1)
        diag = same_step(states, T)
        total = rank_ref[...]
        for ref, start in ((gb_ref, R), (gc_ref, R + states)):
            fold = (target == state + start).astype(f32)
            kept = jnp.where(diag, ref[...], 0.0)
            total = total + jnp.dot(
                kept, fold, precision=lax.Precision.HIGHEST, preferred_element_type=f32
            )
        gproj_ref[...] = total.astype(bf16)
        for n in range(blocks * BLOCK_SLOTS, sums.ticks()):
            sums.tick(n)
        sums.drain()


def bwd_scan(L, dtk, u, g, b_cols, c_cols, par, wts, arriving, held, spre, act, proj, grad_c, arrays, sums):
    T, E = dtk.shape
    N = L.N
    blocks = E // EB
    return pl.pallas_call(
        functools.partial(bwd_kernel, L, sums, blocks),
        grid=(blocks,),
        in_specs=[
            cols(T), cols(T), cols(T), once(*b_cols.shape), once(*c_cols.shape), lead(PAR, EB),
            lead(WTS, EB), cols(N), cols(held.shape[0]), cols(T), cols(T), whole(T, 128), whole(T, TC * N),
        ] + [once(*v.shape) for v in arrays],
        out_specs=[cols(T), lead(128, EB), whole(T, 128)] + [whole(*o.shape) for o in sums.outs()],
        out_shape=[shape(f32, T, E), shape(bf16, blocks, 128, EB), shape(bf16, T, 128)] + sums.outs(),
        scratch_shapes=[
            pltpu.VMEM((T * N, 128), f32),
            pltpu.VMEM((T, TC * N), f32), pltpu.VMEM((T, 128), f32), pltpu.VMEM((T, EB), bf16),
        ] + [pltpu.VMEM((T * 8, 128), f32)] * (2 * EB // 128) + sums.scratch(),
        compiler_params=params(collective_id=3, has_side_effects=True),
        name="bwd_scan",
    )(dtk, u, g, b_cols, c_cols, par, wts, arriving, held, spre, act, proj, grad_c, *arrays)


def conv_kernel(
    L, count, gap_ref, gproj_ref, wts_ref, act_ref, cs_ref, inner_ref, marks_ref,
    gc_ref, chan_ref, after_ref, xs_ref, edge_ref, got_ref, send_sem, recv_sem,
):
    T = gap_ref.shape[0]
    i = pl.program_id(0)
    blocks = edge_ref.shape[0]
    si, ci = lax.axis_index("seq"), lax.axis_index("chan")
    before = lax.rem(ci + count - 1, count)

    @pl.when(i == 0)
    def _():
        barrier = pltpu.get_barrier_semaphore()
        for other in (before, lax.rem(ci + 1, count)):
            pl.semaphore_signal(barrier, inc=1, device_id=(si, other), device_id_type=pl.DeviceIdType.MESH)
        pl.semaphore_wait(barrier, 2)

    def edge(b):
        return pltpu.make_async_remote_copy(
            src_ref=edge_ref.at[b], dst_ref=got_ref.at[b], send_sem=send_sem.at[b], recv_sem=recv_sem.at[b],
            device_id=(si, before), device_id_type=pl.DeviceIdType.MESH,
        )

    K, wide = L.K, L.R + 2 * L.N
    weights = wts_ref[0].astype(f32)
    row = lax.broadcasted_iota(jnp.int32, weights.shape, 0)
    weights = jnp.where(row < wide, weights, 0.0).astype(bf16)
    gc_ref[...] = jnp.dot(gproj_ref[...], weights, preferred_element_type=f32)
    act_low = act_ref[...].astype(bf16)
    grad_proj = lax.dot_general(gproj_ref[...], act_low, TN, preferred_element_type=f32)
    xs_ref[...] = inner_ref[...].astype(f32)

    def tile(k, carry):
        r = pl.multiple_of(k * RT, RT)
        rows = pl.ds(r, RT)
        total = cs_ref[rows, :]
        sig = jax.nn.sigmoid(total)
        grad = (gc_ref[rows, :] + gap_ref[rows, :]) * sig * (1.0 + total * (1.0 - sig))
        gc_ref[rows, :] = grad
        block = xs_ref[pl.ds(pl.multiple_of(r + HALO - 8, 8), RT + 8), :]
        out = [carry[K] + jnp.sum(grad.reshape(RT // 8, 8, EB), axis=0)]
        for j in range(K):
            part = grad * block[8 - j : RT + 8 - j]
            if j > 0:
                part = part * marks_ref[rows, j - 1 : j]
            out.insert(0, carry[K - 1 - j] + jnp.sum(part.reshape(RT // 8, 8, EB), axis=0))
        return tuple(out)

    none = jnp.zeros((8, EB), f32)
    sums = lax.fori_loop(0, T // RT, tile, (none,) * (K + 1))
    edge_ref[i] = gc_ref[0:8, :]
    edge(i).start()
    chan_ref[0] = jnp.concatenate(
        [grad_proj[0:wide]]
        + [jnp.sum(s, axis=0, keepdims=True) for s in sums]
        + [jnp.zeros((128 - wide - K - 1, EB), f32)],
        axis=0,
    ).astype(bf16)

    @pl.when(i == blocks - 1)
    def _():
        for b in range(blocks):
            edge(b).wait()
            rows = jnp.where(ci == count - 1, 0.0, got_ref[b])
            after_ref[:, b * EB : (b + 1) * EB] = rows


def conv_back(L, count, gap, gproj, wts, act, cs, inner, marks):
    T, E = gap.shape
    blocks = E // EB
    return pl.pallas_call(
        functools.partial(conv_kernel, L, count),
        grid=(blocks,),
        in_specs=[
            cols(T), whole(T, 128), lead(WTS, EB), cols(T), cols(T), cols(T + HALO), whole(*marks.shape),
        ],
        out_specs=[cols(T), lead(128, EB), whole(8, E)],
        out_shape=[shape(f32, T, E), shape(bf16, blocks, 128, EB), shape(f32, 8, E)],
        scratch_shapes=[
            pltpu.VMEM((T + HALO, EB), f32),
            pltpu.VMEM((blocks, 8, EB), f32),
            pltpu.VMEM((blocks, 8, EB), f32),
            pltpu.SemaphoreType.DMA((blocks,)),
            pltpu.SemaphoreType.DMA((blocks,)),
        ],
        compiler_params=params(collective_id=4, has_side_effects=True),
        name="conv_back",
    )(gap, gproj, wts, act, cs, inner, marks)


def tail_kernel(
    L, gc_ref, after_ref, par_ref, marks_ref, normed_ref, wi_ref, gn_ref, tok_ref, cot_ref, gain_ref,
    gin_ref, gtok_ref, ggain_ref, ext_ref, low_ref, sum_ref,
):
    T, D = tok_ref.shape
    K = L.K
    i = pl.program_id(0)
    ext_ref[0:T, :] = gc_ref[...]
    ext_ref[T : T + 8, :] = after_ref[...]
    taps = [par_ref[0, L.conv + j : L.conv + j + 1, :] for j in range(K)]

    def tile(r):
        block = ext_ref[pl.ds(r, RT + 8), :]
        marks = marks_ref[pl.ds(r, RT + 8), :]
        total = taps[K - 1] * block[0:RT]
        for j in range(1, K):
            masked = block * marks[:, j - 1 : j]
            total = total + taps[K - 1 - j] * masked[j : RT + j]
        low_ref[pl.ds(r, RT), :] = total.astype(bf16)

    row_tiles(T, tile)
    gin_ref[...] = lax.dot_general(
        low_ref[...], normed_ref[...], TN, preferred_element_type=f32
    ).astype(bf16)
    part = lax.dot_general(low_ref[...], wi_ref[...], NT, preferred_element_type=f32)

    @pl.when(i == 0)
    def _():
        sum_ref[...] = gn_ref[...] + part

    @pl.when(i > 0)
    def _():
        sum_ref[...] += part

    @pl.when(i == pl.num_programs(0) - 1)
    def _():
        gain = gain_ref[...].reshape(1, D)

        def last(k, total):
            rows = pl.ds(pl.multiple_of(k * 16, 16), 16)
            x = tok_ref[rows, :].astype(f32)
            grad = sum_ref[rows, :]
            inv = lax.rsqrt(jnp.mean(x * x, axis=1, keepdims=True) + epsilon)
            scaled = grad * gain
            mean = jnp.mean(x * scaled, axis=1, keepdims=True)
            gtok_ref[rows, :] = (
                cot_ref[rows, :].astype(f32) + inv * scaled - x * (inv * inv * inv * mean)
            )
            return total + jnp.sum((grad * x * inv).reshape(2, 8, D), axis=0)

        total = lax.fori_loop(0, T // 16, last, jnp.zeros((8, D), f32))
        ggain_ref[...] = jnp.sum(total, axis=0, keepdims=True)


def tail(L, gc, after, par, marks, normed, in_weight, gn, tokens, cot, gain):
    T, E = gc.shape
    D = tokens.shape[1]
    blocks = E // EB
    return pl.pallas_call(
        functools.partial(tail_kernel, L),
        grid=(blocks,),
        in_specs=[
            cols(T), cols(8), lead(PAR, EB), whole(*marks.shape), whole(T, D), cols(D), whole(T, D),
            whole(T, D), whole(T, D), whole(D),
        ],
        out_specs=[tall(EB, D), whole(T, D), whole(1, D)],
        out_shape=[shape(bf16, E, D), shape(f32, T, D), shape(f32, 1, D)],
        scratch_shapes=[
            pltpu.VMEM((T + 8, EB), f32), pltpu.VMEM((T, EB), bf16), pltpu.VMEM((T, D), f32),
        ],
        compiler_params=params(),
        name="tail",
    )(gc, after, par, marks, normed, in_weight, gn, tokens, cot, gain)


class Sums:
    def __init__(self, chan_count, seq_count, kinds, shapes, phases, skew=1, pace=1):
        self.cc, self.sc = chan_count, seq_count
        self.kinds = kinds
        self.phases, self.skew, self.pace = phases, skew, pace
        self.size = 8 * seq_count
        self.bits = [1 << i for i in range(chan_count.bit_length() - 1)]
        self.z_bits = [2 << i for i in range(seq_count.bit_length() - 2)]
        self.pieces = [
            (a, r, dims[2]) for a, dims in enumerate(shapes) for r in range(0, dims[1], 2 * self.size)
        ]
        self.shapes = shapes

    def half(self, p):
        return self.kinds[self.pieces[p][0]] is not None

    def stages(self, p):
        bits = self.bits if p % 2 == 0 else self.bits[::-1]
        return (
            [("core", 1)] + [("chan", b) for b in bits] + [("z", b) for b in self.z_bits]
            + [("zgather", b) for b in self.z_bits[::-1]] + ([("move", 0)] if self.half(p) else [])
            + [("cgather", 1)]
        )

    def span(self, p):
        halvings = 2 + len(self.bits)
        phase = self.phases[self.pieces[p][0]]
        first = halvings if phase == "gather" else 0
        return first, halvings if phase == "halve" else len(self.stages(p))

    def begin(self, p):
        phase = self.phases[self.pieces[p][0]]
        before = [q for q in range(p) if self.phases[self.pieces[q][0]] == phase]
        return self.skew * (len(before) // 2)

    def ticks(self):
        return max(
            self.begin(p) + self.pace * (self.span(p)[1] - self.span(p)[0]) for p in range(len(self.pieces))
        ) + 1

    def final(self, p):
        a, first, width = self.pieces[p]
        return pl.ds(first // 4, self.size // 2)

    def outs(self):
        found = []
        for kind, dims, phase in zip(self.kinds, self.shapes, self.phases):
            if phase == "halve":
                found.append(shape(bf16, dims[1] // 4, dims[2]))
            else:
                found.append(shape(bf16, *(dims[1:] if kind is None else (2,) + tuple(dims[1:]))))
        return found

    def scratch(self):
        found = []
        for p, (a, r, width) in enumerate(self.pieces):
            small = self.span(p)[0] > 0
            for k in range(len(self.bits) + 1):
                dims = (self.cc >> k, self.size, width)
                found.append(pltpu.VMEM((1, 16, 128) if small else dims, bf16))
            for k in range(len(self.z_bits)):
                found.append(pltpu.VMEM((self.size >> (k + 1), width), bf16))
            found.append(pltpu.VMEM((self.size, width), bf16))
        dims = (len(self.pieces), len(self.bits) + 2 * len(self.z_bits) + 3, max(2, self.cc // 2))
        return found + [pltpu.SemaphoreType.DMA(dims), pltpu.SemaphoreType.DMA(dims)]

    def bind(self, x_refs, o_refs, scratch):
        self.x, self.o = x_refs, o_refs
        each = len(self.bits) + len(self.z_bits) + 2
        self.held = [scratch[p * each : (p + 1) * each] for p in range(len(self.pieces))]
        self.send_sem, self.recv_sem = scratch[-2:]
        self.si, self.ci = lax.axis_index("seq"), lax.axis_index("chan")
        self.core = lax.rem(self.si, 2)

    def side(self, bit):
        return lax.rem(self.si // bit, 2)

    def across(self, bit):
        return (self.si + bit - 2 * bit * self.side(bit), self.ci)

    def barrier(self):
        barrier = pltpu.get_barrier_semaphore()
        others = [(self.si, lax.rem(self.ci + k, self.cc)) for k in range(1, self.cc)]
        others += [self.across(bit) for bit in [1] + self.z_bits]
        for other in others:
            pl.semaphore_signal(barrier, inc=1, device_id=other, device_id_type=pl.DeviceIdType.MESH)
        pl.semaphore_wait(barrier, len(others))

    def copy(self, p, s, slot, src, dst, device):
        return pltpu.make_async_remote_copy(
            src_ref=src, dst_ref=dst, send_sem=self.send_sem.at[p, s, slot],
            recv_sem=self.recv_sem.at[p, s, slot], device_id=device, device_id_type=pl.DeviceIdType.MESH,
        )

    def kept(self, p, s, keep):
        name, bit = self.stages(p)[s]
        if name == "core":
            a, start, width = self.pieces[p]
            side = self.core if keep else 1 - self.core
            return [self.x[a].at[:, pl.ds(pl.multiple_of(start + side * self.size, 16), self.size), :]]
        ref = self.held[p][s - 1]
        if name == "z":
            side = self.side(bit) if keep else 1 - self.side(bit)
            k = self.z_bits.index(bit)
            rows = self.size >> (k + 1)
            rows = pl.ds(pl.multiple_of(side * rows, 16), rows)
            return [ref.at[0, rows, :] if k == 0 else ref.at[rows, :]]
        mine = lax.rem(self.ci // bit, 2)
        side = mine if keep else 1 - mine
        left = sorted(b for n, b in self.stages(p)[s : 1 + len(self.bits)])
        low = 1 << left.index(bit)
        return [
            ref.at[pl.ds((i // low) * 2 * low + side * low + i % low, 1)]
            for i in range((1 << len(left)) // 2)
        ]

    def landing(self, p, s):
        dst = self.held[p][s]
        return [dst.at[pl.ds(i, 1)] for i in range(dst.shape[0])] if self.stages(p)[s][0] == "chan" else [dst]

    def gathered(self, p, done):
        start, rows = 0, self.size
        for bit in self.z_bits[:done]:
            rows //= 2
            start = start + self.side(bit) * rows
        if self.half(p):
            return self.held[p][-1].at[pl.ds(pl.multiple_of(start, 16), rows), :]
        start = start + self.pieces[p][1] + self.core * self.size
        return self.o[self.pieces[p][0]].at[pl.ds(pl.multiple_of(start, 16), rows), :]

    def places(self, p):
        a, first, width = self.pieces[p]
        rows = pl.ds(pl.multiple_of(first + self.core * self.size, 16), self.size)
        return [self.o[a].at[b, rows, :] for b in range(2)] if self.half(p) else [self.o[a].at[rows, :]]

    def move(self, p, s, v):
        goal = self.kinds[self.pieces[p][0]] + v // 2
        place = self.places(p)[v % 2]
        return goal, place, self.copy(p, s, v % 2, self.held[p][-1], place, (self.si, goal))

    def copies(self, p, s):
        name, bit = self.stages(p)[s]
        if name in ("core", "chan", "z"):
            device = (self.si, self.ci + bit - 2 * bit * lax.rem(self.ci // bit, 2))
            device = device if name == "chan" else self.across(bit)
            pairs = zip(self.kept(p, s, False), self.landing(p, s))
            return [self.copy(p, s, i, src, dst, device) for i, (src, dst) in enumerate(pairs)]
        places = self.places(p)
        if name == "zgather":
            places = [self.gathered(p, self.z_bits.index(bit) + 1)]
        return [self.copy(p, s, b, place, place, self.across(bit)) for b, place in enumerate(places)]

    def taking_part(self, p, s, work):
        if self.half(p) and self.stages(p)[s][0] == "cgather":
            base = self.kinds[self.pieces[p][0]]
            pl.when((self.ci >= base) & (self.ci < base + self.cc // 2))(work)
        else:
            work()

    def start(self, p, s):
        if self.stages(p)[s][0] == "move":
            for v in range(self.cc):
                @pl.when(self.ci == v)
                def _(v=v):
                    goal, place, copy = self.move(p, s, v)
                    if goal == v:
                        place[...] = self.held[p][-1][...]
                    else:
                        copy.start()
            return

        def work():
            for copy in self.copies(p, s):
                copy.start()

        self.taking_part(p, s, work)

    def finish(self, p, s):
        name, bit = self.stages(p)[s]
        if name == "move":
            for v in range(self.cc):
                goal, place, copy = self.move(p, s, v)
                if goal != v:
                    pl.when(self.ci == goal)(copy.wait_recv)
            return

        def work():
            for copy in self.copies(p, s):
                copy.wait_recv()

        self.taking_part(p, s, work)
        if name in ("core", "chan", "z"):
            last = s == len(self.bits) + len(self.z_bits)
            handed = self.phases[self.pieces[p][0]] == "halve" and self.span(p)[1] == s + 1
            for src, dst in zip(self.kept(p, s, True), self.landing(p, s)):
                total = (dst[...].astype(f32) + src[...].astype(f32)).astype(bf16)
                if handed:
                    dst = self.o[self.pieces[p][0]].at[self.final(p), :]
                elif last:
                    dst = self.gathered(p, len(self.z_bits))
                dst[...] = total

    def tick(self, n):
        for p in range(len(self.pieces)):
            first, end = self.span(p)
            s, rest = divmod(n - self.begin(p), self.pace)
            s += first
            if rest != 0:
                continue
            if first + 1 <= s <= end:
                self.finish(p, s - 1)
            if first > 0 and s == first:
                self.held[p][first - 1][...] = self.x[self.pieces[p][0]][self.final(p), :]
            if first <= s < end:
                self.start(p, s)

    def drain(self):
        for p in range(len(self.pieces)):
            for s in range(*self.span(p)):
                if self.stages(p)[s][0] == "move":
                    for v in range(self.cc):
                        goal, place, copy = self.move(p, s, v)
                        if goal != v:
                            pl.when(self.ci == v)(copy.wait_send)
                    continue

                def work(p=p, s=s):
                    for copy in self.copies(p, s):
                        copy.wait_send()

                self.taking_part(p, s, work)


def sum_kernel(sums, *refs):
    arrays = len(sums.kinds)
    sums.bind(refs[:arrays], refs[arrays : 2 * arrays], refs[2 * arrays :])
    sums.barrier()
    for n in range(sums.ticks()):
        sums.tick(n)
    sums.drain()


def sum_owned(arrays, shapes, kinds, phases, chan_count, seq_count):
    sums = Sums(chan_count, seq_count, kinds, shapes, phases)
    vmem = pl.BlockSpec(memory_space=pltpu.VMEM)
    return pl.pallas_call(
        functools.partial(sum_kernel, sums),
        in_specs=[vmem] * len(arrays),
        out_specs=[vmem] * len(arrays),
        out_shape=sums.outs(),
        scratch_shapes=sums.scratch(),
        compiler_params=params(collective_id=0, has_side_effects=True),
        name="sum_owned",
    )(*arrays)


def unpack_kernel(L, inner_ref, gate_ref, out_ref, d_ref, e_ref, gin_ref, gout_ref, *refs):
    first = lax.axis_index("chan") < lax.axis_size("chan") // 2

    @pl.when(first)
    def _():
        gin_ref[...] = inner_ref[...].astype(f32).T

    @pl.when(jnp.logical_not(first))
    def _():
        gin_ref[...] = gate_ref[...].astype(f32).T

    gout_ref[...] = out_ref[...].astype(f32)
    d, e = d_ref[...].astype(f32), e_ref[...].astype(f32)
    R, N, K = L.R, L.N, L.K
    wide = R + 2 * N
    conv_w, conv_b, proj, step_w, step_b, decay, skip, gain = refs
    width = d.shape[1]
    step_w[...] = d[0:R]
    decay[...] = d[R : R + N]
    step_b[...] = d[R + N].reshape(width)
    skip[...] = d[R + N + 1].reshape(width)
    proj[...] = e[0:wide]
    conv_w[...] = e[wide : wide + K]
    conv_b[...] = e[wide + K].reshape(width)
    gain[...] = e[wide + K + 1].reshape(width)


def unpack(L, sums):
    width = sums[3].shape[1]
    rows, D = sums[0].shape
    R, N, K = L.R, L.N, L.K
    return pl.pallas_call(
        functools.partial(unpack_kernel, L),
        out_shape=[
            shape(f32, D, rows), shape(f32, *sums[2].shape), shape(f32, K, width), shape(f32, width),
            shape(f32, R + 2 * N, width), shape(f32, R, width), shape(f32, width),
            shape(f32, N, width), shape(f32, width), shape(f32, width),
        ],
        compiler_params=params(),
        name="unpack",
    )(*sums)


def local(
    tokens, norm_gain, in_weight, conv_weight, conv_bias, proj_weight, step_weight,
    step_bias, decay_log, skip_gain, out_weight, cotangent, lengths,
):
    T, D = tokens.shape
    E = in_weight.shape[1] // 2
    L = Layout(step_weight.shape[0], decay_log.shape[0], conv_weight.shape[0])
    ci = lax.axis_index("chan")
    cc = lax.axis_size("chan")
    sc = lax.axis_size("seq")
    blocks, share = E // EB, E // cc

    parts = (conv_weight, conv_bias, proj_weight.T, step_weight, step_bias, decay_log, skip_gain)
    gathered = None
    if share != EB:
        wts, par, halo = gather_params(L, cc, parts, tokens)

        def by_block(values):
            values = jnp.moveaxis(values, 0, 1).reshape(-1, blocks, EB)
            return jnp.moveaxis(values, 1, 0)

        parts, gathered = None, (by_block(wts), by_block(par), halo)
    marks, normed, inner, gate, gg, g, cs, act, proj, b_cols, c_cols, *own = front(
        L, cc, lengths, tokens, norm_gain, in_weight, out_weight, cotangent, parts, gathered
    )
    wts, par = gathered[:2] if gathered else own
    spre, dtk, u, entering, arriving = pre_scan(L, cc, proj, par, wts, act, g, marks, b_cols, c_cols)
    held, grad_c, block_out, grad_out, grad_in_gate, gn = fwd_scan(
        L, dtk, u, b_cols, c_cols, g, par, entering, act, gate, gg, out_weight, cotangent, tokens,
        normed, in_weight,
    )

    piece = 16 * sc
    fold = 2 if 2 * share <= piece else 1

    def owned(values):
        values = values.reshape(cc, -1, values.shape[-1] // fold)
        return jnp.pad(values, ((0, 0), (0, -values.shape[1] % piece), (0, 0)))

    def unfolded(values):
        if values.ndim == 2:
            return values[: share * fold].reshape(share, D)
        return values[:, : share * fold].reshape(2 * share, D)

    def by_owner(values):
        if share != EB:
            values = jnp.moveaxis(values, 0, 1).reshape(values.shape[1], cc, share)
            values = jnp.moveaxis(values, 1, 0)
        return jnp.pad(values, ((0, 0), (0, -values.shape[1] % piece), (0, 0)))

    early = [owned(grad_out), owned(grad_in_gate)]
    early_shapes = [v.shape for v in early]
    kinds = [None, cc // 2]
    sums = Sums(cc, sc, kinds, early_shapes, ["halve"] * 2, skew=1, pace=3)
    gap, chan_d, gproj, *early = bwd_scan(
        L, dtk, u, g, b_cols, c_cols, par, wts, arriving, held, spre, act, proj, grad_c, early, sums
    )
    gc, chan_e, after = conv_back(L, cc, gap, gproj, wts, act, cs, inner, marks)
    grad_in_inner, grad_tokens, grad_gain = tail(
        L, gc, after, par, marks, normed, in_weight, gn, tokens, cotangent, norm_gain
    )
    row = L.R + 2 * L.N + L.K + 1
    gain_part = jnp.pad(grad_gain.reshape(cc, 1, D // cc), ((0, 0), (0, 0), (0, share - D // cc)))
    chan_e = lax.dynamic_update_slice(by_owner(chan_e), gain_part.astype(bf16), (0, row, 0))
    late = [owned(grad_in_inner), by_owner(chan_d), chan_e]
    sum_inner, sum_d, sum_e, sum_out, sum_gate = sum_owned(
        late + early, [v.shape for v in late] + early_shapes, [0, None, None] + kinds,
        ["all"] * 3 + ["gather"] * 2, cc, sc,
    )
    sums = [unfolded(v) for v in (sum_inner, sum_gate, sum_out)] + [sum_d, sum_e]
    g_in, g_out, conv_w, conv_b, proj_w, step_w, step_b, decay, skip, g_gain = unpack(L, sums)
    return (
        block_out, grad_tokens, g_gain[: D // cc], g_in, conv_w, conv_b, proj_w.T, step_w,
        step_b, decay, skip, g_out,
    )


def solution(mesh):
    tok, row, vec = P(("seq", "chan"), None), P(None, "chan"), P("chan")
    in_specs = (
        tok, P(), P(), row, vec, P("chan", None), row, vec, row, vec, P(), tok, P("seq", None),
    )
    out_specs = (
        tok, tok, vec, row, row, vec, P("chan", None), row, vec, row, vec, P("chan", None),
    )
    return jax.shard_map(local, mesh=mesh, in_specs=in_specs, out_specs=out_specs, check_vma=False)
```

```python
import functools
import math

import jax
import jax.numpy as jnp
from jax import lax
from jax.experimental import pallas as pl
from jax.experimental.pallas import tpu as pltpu
from jax.sharding import PartitionSpec as P

epsilon = 1e-05
LOG2E = math.log2(math.e)
CUT = 1e30
TC = 64
EB = 384
RT = 32
BLOCK_SLOTS = 4
HALO = 16
PAR = 24
WTS = 128
f32 = jnp.float32
bf16 = jnp.bfloat16
NT = (((1,), (1,)), ((), ()))
TN = (((0,), (0,)), ((), ()))


def params(**more):
    return pltpu.CompilerParams(vmem_limit_bytes=60 * 1024 * 1024, **more)


def cols(rows, width=EB, shift=0):
    return pl.BlockSpec((rows, width), lambda i: (0, i + shift))


def tall(rows, width, shift=0):
    return pl.BlockSpec((rows, width), lambda i: (i + shift, 0))


def lead(rows, width, count=1):
    return pl.BlockSpec((count, rows, width), lambda i: (i, 0, 0))


def whole(*shape):
    return pl.BlockSpec(shape, lambda i: (0,) * len(shape))


def once(*shape):
    return pl.BlockSpec(shape, lambda i: (0,) * len(shape), pipeline_mode=pl.Buffered(1))


def shape(dtype, *dims):
    return jax.ShapeDtypeStruct(dims, dtype)


def row_tiles(count, body):
    def step(i, unused):
        body(pl.multiple_of(i * RT, RT))
        return unused

    lax.fori_loop(0, count // RT, step, 0)


def same_step(states, rows):
    dims = (rows, TC * states)
    here = lax.rem(lax.broadcasted_iota(jnp.int32, dims, 0), TC) * states
    place = lax.broadcasted_iota(jnp.int32, dims, 1)
    return (place >= here) & (place < here + states)


class Layout:
    def __init__(self, R, N, K):
        self.R, self.N, self.K = R, N, K
        self.step = R + 2 * N
        self.decay = 0
        self.conv = self.decay + N
        self.conv_b = self.conv + K
        self.step_b = self.conv_b + 1
        self.skip = self.step_b + 1
        self.end = self.skip + 1


def start_gather(
    L, count, cw_ref, cb_ref, pw_ref, sw_ref, sb_ref, dl_ref, sk_ref, tok_ref,
    wts_ref, par_ref, halo_ref, send_sem, recv_sem, halo_sems,
):
    si, ci = lax.axis_index("seq"), lax.axis_index("chan")
    T = tok_ref.shape[0]
    width = par_ref.shape[2]
    barrier = pltpu.get_barrier_semaphore()
    for k in range(1, count):
        pl.semaphore_signal(
            barrier, inc=1, device_id=(si, lax.rem(ci + k, count)),
            device_id_type=pl.DeviceIdType.MESH,
        )
    own, weights = par_ref.at[ci], wts_ref.at[ci]
    weights[...] = jnp.concatenate(
        [pw_ref[...].astype(f32), sw_ref[...].astype(f32)], axis=0
    ).astype(bf16)
    own[...] = jnp.concatenate(
        [
            dl_ref[...], cw_ref[...], cb_ref[...].reshape(1, width), sb_ref[...].reshape(1, width),
            sk_ref[...].reshape(1, width), jnp.zeros((PAR - L.end, width), f32),
        ],
        axis=0,
    )
    pl.semaphore_wait(barrier, count - 1)

    def share(ref, j, k):
        return pltpu.make_async_remote_copy(
            src_ref=ref, dst_ref=ref, send_sem=send_sem.at[j, k], recv_sem=recv_sem.at[j, k],
            device_id=(si, lax.rem(ci + k, count)), device_id_type=pl.DeviceIdType.MESH,
        )

    edge = pltpu.make_async_remote_copy(
        src_ref=tok_ref.at[pl.ds(T - HALO, HALO)], dst_ref=halo_ref,
        send_sem=halo_sems.at[0], recv_sem=halo_sems.at[1],
        device_id=(si, lax.rem(ci + 1, count)), device_id_type=pl.DeviceIdType.MESH,
    )
    edge.start()
    for j, ref in enumerate((own, weights)):
        for k in range(1, count):
            share(ref, j, k).start()

    def wait():
        edge.wait()
        for j, ref in enumerate((own, weights)):
            for k in range(1, count):
                share(ref, j, k).wait()

    return wait


def gather_kernel(L, count, *refs):
    start_gather(L, count, *refs)()


def gather_scratch(count):
    return [
        pltpu.SemaphoreType.DMA((2, count)),
        pltpu.SemaphoreType.DMA((2, count)),
        pltpu.SemaphoreType.DMA((2,)),
    ]


def gather_params(L, count, parts, tokens):
    width = parts[0].shape[1]
    T, D = tokens.shape
    vmem = pl.BlockSpec(memory_space=pltpu.VMEM)
    return pl.pallas_call(
        functools.partial(gather_kernel, L, count),
        in_specs=[vmem] * 8,
        out_specs=[vmem] * 3,
        out_shape=[shape(bf16, count, WTS, width), shape(f32, count, PAR, width), shape(bf16, HALO, D)],
        scratch_shapes=gather_scratch(count),
        compiler_params=params(collective_id=1, has_side_effects=True),
        name="gather_params",
    )(*parts, tokens)


def front_kernel(
    L, count, inside, len_ref, tok_ref, gain_ref, wi_ref, wg_ref, wo_ref, cot_ref, *refs,
):
    given, refs = refs[: 7 if inside else 3], refs[7 if inside else 3 :]
    (
        marks_ref, normed_ref, inner_ref, gate_ref, gg_ref, g_ref, cs_ref, act_ref, proj_ref, bch_ref, cch_ref,
        taps_ref,
    ) = refs[:12]
    results, refs = refs[12 : 14 if inside else 12], refs[14 if inside else 12 :]
    hn_ref, xs_ref, low_ref = refs[:3]
    T = tok_ref.shape[0]
    N, K = L.N, L.K
    i = pl.program_id(0)
    sub = low_ref.shape[1] // EB
    if inside:
        wts_ref, par_ref, halo_ref, *sems = refs[3:]
        first = i * sub
    else:
        wts_ref, par_ref, halo_ref = given
        first = 0

    def norm(x):
        x = x.astype(f32)
        inv = lax.rsqrt(jnp.mean(x * x, axis=1, keepdims=True) + epsilon)
        return (x * inv * gain_ref[...].reshape(1, x.shape[1])).astype(bf16)

    def products():
        low = jnp.dot(normed_ref[...], wi_ref[...], preferred_element_type=f32).astype(bf16)
        inner_ref[HALO:, :] = low
        xs_ref[HALO:, :] = low.astype(f32)
        gate_ref[...] = jnp.dot(normed_ref[...], wg_ref[...], preferred_element_type=f32)
        gg_ref[...] = lax.dot_general(cot_ref[...], wo_ref[...], NT, preferred_element_type=f32)

    @pl.when(i == 0)
    def _():
        if inside:
            wait = start_gather(L, count, *given, tok_ref, wts_ref, par_ref, halo_ref, *sems)

        def tile(r):
            normed_ref[pl.ds(r, RT), :] = norm(tok_ref[pl.ds(r, RT), :])

        row_tiles(T, tile)
        proj_ref[...] = jnp.zeros_like(proj_ref)
        dims = marks_ref.shape
        place = lax.broadcasted_iota(jnp.int32, dims, 0) + lax.axis_index("chan") * T
        lane = lax.broadcasted_iota(jnp.int32, dims, 1)
        reach = jnp.where(lane < K - 1, lane + 1, 1)
        found = jnp.zeros(dims, f32)
        start = jnp.int32(0)
        for k in range(len_ref.shape[1]):
            found = jnp.where((start > place - reach) & (start <= place), 1.0, found)
            start = start + len_ref[0, k]
        marks_ref[...] = jnp.where(lane < K - 1, 1.0 - found, found * CUT)
        products()
        if inside:
            wait()
            results[0][...] = wts_ref[...]
            results[1][...] = par_ref[...]
        lead_device = lax.axis_index("chan") == 0
        halo = jnp.where(lead_device, jnp.zeros(halo_ref.shape, f32), halo_ref[...].astype(f32))
        hn_ref[...] = norm(halo)

    pl.when(i > 0)(products)
    low = jnp.dot(hn_ref[...], wi_ref[...], preferred_element_type=f32).astype(bf16)
    inner_ref[0:HALO, :] = low
    xs_ref[0:HALO, :] = low.astype(f32)

    for k in range(sub):
        c = slice(k * EB, (k + 1) * EB)
        taps = [par_ref[first + k, L.conv + j : L.conv + j + 1, :] for j in range(K)]
        bias = par_ref[first + k, L.conv_b : L.conv_b + 1, :]
        taps_ref[:, c] = par_ref[first + k, L.conv : L.conv + 8, :]

        def tile(r, c=c, taps=taps, bias=bias):
            rows = pl.ds(r, RT)
            block = xs_ref[pl.ds(pl.multiple_of(r + HALO - 8, 8), RT + 8), c]
            total = bias + taps[K - 1] * block[8:]
            for j in range(1, K):
                usable = marks_ref[rows, j - 1 : j]
                total = total + taps[K - 1 - j] * (block[8 - j : RT + 8 - j] * usable)
            act = total * jax.nn.sigmoid(total)
            cs_ref[rows, c] = total
            act_ref[rows, c] = act
            low_ref[rows, c] = act.astype(bf16)
            gate = gate_ref[rows, c]
            passed = gg_ref[rows, c] * (gate * jax.nn.sigmoid(gate))
            g_ref[rows, c] = passed.astype(bf16).astype(f32)

        row_tiles(T, tile)
        proj_ref[...] += lax.dot_general(low_ref[:, c], wts_ref[first + k], NT, preferred_element_type=f32)

    @pl.when(i == pl.num_programs(0) - 1)
    def _():
        turned = proj_ref[...].T
        for ref, start in ((bch_ref, L.R), (cch_ref, L.R + N)):
            for j in range(T // TC):
                ref[j] = turned[start : start + N, j * TC : (j + 1) * TC]


def front(L, count, lengths, tokens, gain, in_weight, out_weight, cot, parts, gathered):
    T, D = tokens.shape
    E = out_weight.shape[0]
    sub = 2
    wide = EB * sub
    steps = E // wide
    N = L.N
    inside = parts is not None
    more_out, scratch, options = [], [], {}
    if inside:
        given, given_specs = parts, [whole(*v.shape) for v in parts]
        more_out = [shape(bf16, count, WTS, EB), shape(f32, count, PAR, EB)]
        scratch = [pltpu.VMEM(o.shape, o.dtype) for o in more_out] + [pltpu.VMEM((HALO, D), bf16)]
        scratch += gather_scratch(count)
        options = dict(collective_id=1, has_side_effects=True)
    else:
        given, given_specs = gathered, [lead(WTS, EB, sub), lead(PAR, EB, sub), whole(HALO, D)]
    return pl.pallas_call(
        functools.partial(front_kernel, L, count, inside),
        grid=(steps,),
        in_specs=[
            pl.BlockSpec(memory_space=pltpu.SMEM),
            whole(T, D), whole(D), cols(D, wide), cols(D, wide, steps), tall(wide, D), whole(T, D),
        ] + given_specs,
        out_specs=[whole(T + 8, 8), whole(T, D), cols(T + HALO, wide)] + [cols(T, wide)] * 5 + [
            whole(T, 128), whole(T // TC, N, TC), whole(T // TC, N, TC), cols(8, wide),
        ] + [whole(*o.shape) for o in more_out],
        out_shape=[shape(f32, T + 8, 8), shape(bf16, T, D), shape(bf16, T + HALO, E)]
        + [shape(f32, T, E)] * 5
        + [shape(f32, T, 128), shape(f32, T // TC, N, TC), shape(f32, T // TC, N, TC), shape(f32, 8, E)]
        + more_out,
        scratch_shapes=[
            pltpu.VMEM((HALO, D), bf16),
            pltpu.VMEM((T + HALO, wide), f32),
            pltpu.VMEM((T, wide), bf16),
        ] + scratch,
        compiler_params=params(**options),
        name="front",
    )(lengths, tokens, gain, in_weight, in_weight, out_weight, cot, *given)


def rates(L, par_ref):
    return -jnp.exp(par_ref[0, L.decay : L.decay + L.N, :]) * LOG2E


def lane_tiles(values):
    return [values[:, k * 128 : (k + 1) * 128] for k in range(EB // 128)]


def row_at(ref, t):
    return lane_tiles(ref[pl.ds(t, 1), :])


def spread(columns, j):
    return jnp.broadcast_to(columns[:, j : j + 1], (columns.shape[0], 128))


def ahead_of(steps, fetch):
    steps = list(steps)
    loaded = [fetch(j) for j in steps[:2]]
    for k, j in enumerate(steps):
        if k + 2 < len(steps):
            loaded.append(fetch(steps[k + 2]))
        yield j, loaded[k]


def softplus(x):
    return jnp.maximum(x, 0.0) + jnp.log1p(jnp.exp(-jnp.abs(x)))


def pre_kernel(
    L, count, proj_ref, par_ref, wts_ref, act_ref, g_ref, marks_ref, b_ref, c_ref,
    spre_ref, dtk_ref, u_ref, enter_ref, arrive_ref, ahead_ref, behind_ref, got_ref,
    send_sem, recv_sem,
):
    T, E = act_ref.shape[0], enter_ref.shape[1]
    N = L.N
    i = pl.program_id(0)
    blocks = E // EB
    si, ci = lax.axis_index("seq"), lax.axis_index("chan")

    @pl.when(i == 0)
    def _():
        barrier = pltpu.get_barrier_semaphore()
        for k in range(1, count):
            pl.semaphore_signal(
                barrier, inc=1, device_id=(si, lax.rem(ci + k, count)),
                device_id_type=pl.DeviceIdType.MESH,
            )
        pl.semaphore_wait(barrier, count - 1)

    low = proj_ref[:, 0 : L.R].astype(bf16)
    weights = wts_ref[0, L.step : L.step + L.R, :]
    bias = par_ref[0, L.step_b : L.step_b + 1, :]
    spre_ref[...] = jnp.dot(low, weights, preferred_element_type=f32) + bias

    def tile(r):
        rows = pl.ds(r, RT)
        step = softplus(spre_ref[rows, :])
        u_ref[rows, :] = step * act_ref[rows, :]
        dtk_ref[rows, :] = step + marks_ref[rows, 3:4]

    row_tiles(T, tile)
    rate = lane_tiles(rates(L, par_ref))
    tiles = len(rate)

    def chunk(c, carry):
        h, through, head = (list(carry[k * tiles : (k + 1) * tiles]) for k in range(3))
        base = pl.multiple_of(c * TC, TC)
        b_cols, c_cols = b_ref[c], c_ref[c]

        def fetch(j):
            rows = [row_at(ref, base + j) for ref in (dtk_ref, u_ref, g_ref)]
            return rows + [spread(b_cols, j), spread(c_cols, j)]

        for j, (d, u, g, b_now, c_now) in ahead_of(range(TC), fetch):
            for k in range(tiles):
                factor = jnp.exp2(d[k] * rate[k])
                h[k] = factor * h[k] + b_now * u[k]
                through[k] = factor * through[k]
                head[k] = head[k] + through[k] * (c_now * g[k])
        return tuple(h + through + head)

    zero = jnp.zeros((N, 128), f32)
    out = lax.fori_loop(0, T // TC, chunk, (zero,) * tiles + (zero + 1.0,) * tiles + (zero,) * tiles)
    h, through, head = (jnp.concatenate(out[k * tiles : (k + 1) * tiles], axis=1) for k in range(3))
    zero = jnp.zeros((N, EB), f32)
    ahead_ref[i, 0:N, :] = h
    ahead_ref[i, N:, :] = through
    behind_ref[i, 0:N, :] = head
    behind_ref[i, N:, :] = through

    def send(b, k, forward):
        return pltpu.make_async_remote_copy(
            src_ref=(ahead_ref if forward else behind_ref).at[b], dst_ref=got_ref.at[count - k, b],
            send_sem=send_sem.at[k, b], recv_sem=recv_sem.at[count - k, b],
            device_id=(si, lax.rem(ci + k, count)), device_id_type=pl.DeviceIdType.MESH,
        )

    for k in range(1, count):
        @pl.when(ci + k < count)
        def _(k=k):
            send(i, k, True).start()

        @pl.when(ci + k >= count)
        def _(k=k):
            send(i, k, False).start()

    @pl.when(i == blocks - 1)
    def _():
        for b in range(blocks):
            for k in range(1, count):
                send(b, k, True).wait()
        for b in range(blocks):
            span = slice(b * EB, (b + 1) * EB)
            entering, arriving = zero, zero
            for k in range(1, count):
                before = ci + k >= count
                got = got_ref[k, b]
                entering = jnp.where(before, got[0:N] + got[N:] * entering, entering)
            for k in range(count - 1, 0, -1):
                behind = ci + k < count
                got = got_ref[k, b]
                arriving = jnp.where(behind, got[0:N] + got[N:] * arriving, arriving)
            enter_ref[:, span] = entering
            arrive_ref[:, span] = arriving


def pre_scan(L, count, proj, par, wts, act, g, marks, b_cols, c_cols):
    T, E = act.shape
    N = L.N
    blocks = E // EB
    state = shape(f32, N, E)
    return pl.pallas_call(
        functools.partial(pre_kernel, L, count),
        grid=(blocks,),
        in_specs=[
            whole(T, 128), lead(PAR, EB), lead(WTS, EB), cols(T), cols(T), whole(*marks.shape),
            once(*b_cols.shape), once(*c_cols.shape),
        ],
        out_specs=[cols(T)] * 3 + [whole(N, E)] * 2,
        out_shape=[shape(f32, T, E)] * 3 + [state] * 2,
        scratch_shapes=[
            pltpu.VMEM((blocks, 2 * N, EB), f32),
            pltpu.VMEM((blocks, 2 * N, EB), f32),
            pltpu.VMEM((count, blocks, 2 * N, EB), f32),
            pltpu.SemaphoreType.DMA((count, blocks)),
            pltpu.SemaphoreType.DMA((count, blocks)),
        ],
        compiler_params=params(collective_id=2, has_side_effects=True),
        name="pre_scan",
    )(proj, par, wts, act, g, marks, b_cols, c_cols)


def fold_rows(refs, r):
    sums = []
    for ref in refs:
        parts = [ref[pl.ds(r * 8 + k, 8, stride=8), :] for k in range(8)]
        while len(parts) > 1:
            parts = [x + y for x, y in zip(parts[::2], parts[1::2])]
        sums.append(parts[0])
    return jnp.concatenate(sums, axis=1)


def halves(values):
    return values[0:8] + values[8:16]


def lane_sums(states, acc_ref, out_ref, chunks):
    width = TC * states
    ones = jnp.ones((TC, 128), bf16)
    group = chunks // 4
    for k in range(4):
        part = acc_ref[k * group * width : (k + 1) * group * width, :].astype(bf16)
        sums = lax.dot_general(ones, part, NT, preferred_element_type=f32)
        for c in range(group):
            row = (k * group + c) * TC
            out_ref[row : row + TC, :] = sums[:, c * width : (c + 1) * width]


def fwd_kernel(
    L, dtk_ref, u_ref, b_ref, c_ref, g_ref, par_ref, hin_ref, act_ref, gate_ref, gg_ref,
    wo_ref, cot_ref, tok_ref, normed_ref, wg_ref,
    h_ref, gc_ref, block_ref, gout_ref, gin_ref, gn_ref,
    acc_ref, gated_ref, ggate_ref, branch_ref, *y_refs,
):
    rate = lane_tiles(rates(L, par_ref))
    T, states = u_ref.shape[0], L.N
    chunks = T // TC
    width = TC * states
    i = pl.program_id(0)

    @pl.when(i == 0)
    def _():
        acc_ref[...] = jnp.zeros_like(acc_ref)
        gn_ref[...] = jnp.zeros_like(gn_ref)
        branch_ref[...] = jnp.zeros_like(branch_ref)

    h_ref[0:states, :] = hin_ref[...].astype(bf16)

    def chunk(c, carry):
        h = list(carry)
        base = pl.multiple_of(c * TC, TC)
        row = pl.multiple_of(c * width, width)
        b_cols, c_cols = b_ref[c], c_ref[c]

        def fetch(j):
            at = pl.ds(row + j * states, states)
            rows = [row_at(ref, base + j) for ref in (dtk_ref, u_ref, g_ref)]
            return rows + [spread(b_cols, j), spread(c_cols, j), acc_ref[at, :]]

        for j, (d, u, g, b_now, c_now, acc) in ahead_of(range(TC), fetch):
            for k in range(len(h)):
                h[k] = jnp.exp2(d[k] * rate[k]) * h[k] + b_now * u[k]
                h_ref[pl.ds(row + (j + 1) * states, states), k * 128 : (k + 1) * 128] = h[k].astype(bf16)
                y_refs[k][pl.ds((base + j) * 8, 8), :] = halves(c_now * h[k])
                acc = acc + h[k] * g[k]
            acc_ref[pl.ds(row + j * states, states), :] = acc
        return tuple(h)

    lax.fori_loop(0, chunks, chunk, tuple(lane_tiles(hin_ref[...])))
    skip = par_ref[0, L.skip : L.skip + 1, :]

    def tile(k, unused):
        rows = pl.ds(pl.multiple_of(k * 16, 16), 16)
        y = jnp.concatenate([fold_rows(y_refs, k * 16), fold_rows(y_refs, k * 16 + 8)], axis=0)
        mixer = (y + skip * act_ref[rows, :]).astype(bf16).astype(f32)
        gate = gate_ref[rows, :]
        sig = jax.nn.sigmoid(gate)
        gated_ref[rows, :] = (mixer * (gate * sig)).astype(bf16)
        ggate_ref[rows, :] = (gg_ref[rows, :] * mixer * sig * (1.0 + gate * (1.0 - sig))).astype(bf16)
        return unused

    lax.fori_loop(0, T // 16, tile, 0)
    branch_ref[...] += jnp.dot(gated_ref[...], wo_ref[...], preferred_element_type=f32)
    gout_ref[...] = lax.dot_general(
        gated_ref[...], cot_ref[...], TN, preferred_element_type=f32
    ).astype(bf16)
    gin_ref[...] = lax.dot_general(
        ggate_ref[...], normed_ref[...], TN, preferred_element_type=f32
    ).astype(bf16)
    gn_ref[...] += lax.dot_general(ggate_ref[...], wg_ref[...], NT, preferred_element_type=f32)

    @pl.when(i == pl.num_programs(0) - 1)
    def _():
        block_ref[...] = (tok_ref[...].astype(f32) + branch_ref[...]).astype(bf16)
        lane_sums(states, acc_ref, gc_ref, chunks)


def fwd_scan(L, dtk, u, b_cols, c_cols, g, par, entering, act, gate, gg, out_weight, cot, tokens, normed, in_weight):
    T, E = dtk.shape
    D = tokens.shape[1]
    N = L.N
    rows = (T + 1) * N
    blocks = E // EB
    return pl.pallas_call(
        functools.partial(fwd_kernel, L),
        grid=(blocks,),
        in_specs=[
            cols(T), cols(T), once(*b_cols.shape), once(*c_cols.shape), cols(T), lead(PAR, EB), cols(N),
            cols(T), cols(T), cols(T), tall(EB, D), whole(T, D), whole(T, D), whole(T, D),
            cols(D, EB, blocks),
        ],
        out_specs=[
            cols(rows), whole(T, TC * N), whole(T, D), tall(EB, D), tall(EB, D), whole(T, D),
        ],
        out_shape=[
            shape(bf16, rows, E), shape(f32, T, TC * N), shape(bf16, T, D), shape(bf16, E, D),
            shape(bf16, E, D), shape(f32, T, D),
        ],
        scratch_shapes=[
            pltpu.VMEM((T * N, 128), f32), pltpu.VMEM((T, EB), bf16), pltpu.VMEM((T, EB), bf16),
            pltpu.VMEM((T, D), f32),
        ] + [pltpu.VMEM((T * 8, 128), f32)] * (EB // 128),
        compiler_params=params(),
        name="fwd_scan",
    )(dtk, u, b_cols, c_cols, g, par, entering, act, gate, gg, out_weight, cot, tokens, normed, in_weight)


def bwd_kernel(
    L, sums, blocks, dtk_ref, u_ref, g_ref, b_ref, c_ref, par_ref, wts_ref, fin_ref, h_ref, spre_ref, act_ref, proj_ref,
    gc_ref, *refs,
):
    arrays = len(sums.kinds)
    x_refs, refs = refs[:arrays], refs[arrays:]
    gap_ref, chan_ref, gproj_ref = refs[:3]
    o_refs, refs = refs[3 : 3 + arrays], refs[3 + arrays :]
    acc_ref, gb_ref, rank_ref, pre_ref = refs[:4]
    rate = lane_tiles(rates(L, par_ref))
    tiles = len(rate)
    bsum_refs, wsum_refs = refs[4 : 4 + tiles], refs[4 + tiles : 4 + 2 * tiles]
    sums.bind(x_refs, o_refs, refs[4 + 2 * tiles :])
    T, states = u_ref.shape[0], L.N
    chunks = T // TC
    width = TC * states
    i = pl.program_id(0)

    @pl.when(i == 0)
    def _():
        acc_ref[...] = jnp.zeros_like(acc_ref)
        rank_ref[...] = jnp.zeros_like(rank_ref)
        sums.barrier()

    def chunk(i, carry):
        flow, total = list(carry[:tiles]), list(carry[tiles:])
        c = chunks - 1 - i
        base = pl.multiple_of(c * TC, TC)
        row = pl.multiple_of(c * width, width)
        b_cols, c_cols = b_ref[c], c_ref[c]

        def fetch(j):
            at = pl.ds(row + j * states, states)
            rows = [row_at(ref, base + j) for ref in (dtk_ref, u_ref, g_ref)]
            return rows + [spread(b_cols, j), spread(c_cols, j), acc_ref[at, :], lane_tiles(h_ref[at, :])]

        for j, (d, u, g, b_now, c_now, acc, before) in ahead_of(reversed(range(TC)), fetch):
            part = pl.ds((base + j) * 8, 8)
            for k in range(tiles):
                adj = c_now * g[k] + flow[k]
                flow[k] = jnp.exp2(d[k] * rate[k]) * adj
                wr = flow[k] * before[k].astype(f32) * rate[k]
                total[k] = total[k] + wr * d[k]
                wsum_refs[k][part, :] = halves(wr)
                bsum_refs[k][part, :] = halves(adj * b_now)
                acc = acc + adj * u[k]
            acc_ref[pl.ds(row + j * states, states), :] = acc
        return tuple(flow) + tuple(total)

    none = jnp.zeros((states, 128), f32)
    out = tuple(lane_tiles(fin_ref[...])) + (none,) * tiles
    for q in range(BLOCK_SLOTS):
        for n in range(sums.ticks()):
            block, quarter = divmod(n, BLOCK_SLOTS)
            if quarter == q and block < blocks:
                pl.when(i == block)(functools.partial(sums.tick, n))
        out = lax.fori_loop(q * chunks // BLOCK_SLOTS, (q + 1) * chunks // BLOCK_SLOTS, chunk, out)
    total = jnp.concatenate(out[tiles:], axis=1)
    skip = par_ref[0, L.skip : L.skip + 1, :]

    def tile(k, carry):
        bias_sum, skip_sum = carry
        rows = pl.ds(pl.multiple_of(k * 16, 16), 16)
        bsum, wsum = (
            jnp.concatenate([fold_rows(refs, k * 16), fold_rows(refs, k * 16 + 8)], axis=0)
            for refs in (bsum_refs, wsum_refs)
        )
        spre, act, g = spre_ref[rows, :], act_ref[rows, :], g_ref[rows, :]
        grad = (wsum * (1.0 / LOG2E) + act * bsum) * jax.nn.sigmoid(spre)
        gap_ref[rows, :] = g * skip + softplus(spre) * bsum
        pre_ref[rows, :] = grad.astype(bf16)
        bias_sum = bias_sum + halves(grad)
        skip_sum = skip_sum + halves(g * act)
        return bias_sum, skip_sum

    none = jnp.zeros((8, EB), f32)
    bias_sum, skip_sum = lax.fori_loop(0, T // 16, tile, (none, none))
    R = L.R
    pre = pre_ref[...]
    step_low = proj_ref[...].astype(bf16)
    grad_step_w = lax.dot_general(step_low, pre, TN, preferred_element_type=f32)
    chan_ref[0] = jnp.concatenate(
        [
            grad_step_w[0:R],
            total * (1.0 / LOG2E),
            jnp.sum(bias_sum, axis=0, keepdims=True),
            jnp.sum(skip_sum, axis=0, keepdims=True),
            jnp.zeros((128 - R - states - 2, EB), f32),
        ],
        axis=0,
    ).astype(bf16)
    weights = wts_ref[0, L.step : L.step + R, :].astype(f32)
    weights = jnp.concatenate([weights, jnp.zeros((128 - R, EB), f32)], axis=0).astype(bf16)
    rank_ref[...] += lax.dot_general(pre, weights, NT, preferred_element_type=f32)

    @pl.when(i == pl.num_programs(0) - 1)
    def _():
        lane_sums(states, acc_ref, gb_ref, chunks)
        dims = (width, 128)
        state = lax.rem(lax.broadcasted_iota(jnp.int32, dims, 0), states)
        target = lax.broadcasted_iota(jnp.int32, dims, 1)
        diag = same_step(states, T)
        total = rank_ref[...]
        for ref, start in ((gb_ref, R), (gc_ref, R + states)):
            fold = (target == state + start).astype(f32)
            kept = jnp.where(diag, ref[...], 0.0)
            total = total + jnp.dot(
                kept, fold, precision=lax.Precision.HIGHEST, preferred_element_type=f32
            )
        gproj_ref[...] = total.astype(bf16)
        for n in range(blocks * BLOCK_SLOTS, sums.ticks()):
            sums.tick(n)
        sums.drain()


def bwd_scan(L, dtk, u, g, b_cols, c_cols, par, wts, arriving, held, spre, act, proj, grad_c, arrays, sums):
    T, E = dtk.shape
    N = L.N
    blocks = E // EB
    return pl.pallas_call(
        functools.partial(bwd_kernel, L, sums, blocks),
        grid=(blocks,),
        in_specs=[
            cols(T), cols(T), cols(T), once(*b_cols.shape), once(*c_cols.shape), lead(PAR, EB),
            lead(WTS, EB), cols(N), cols(held.shape[0]), cols(T), cols(T), whole(T, 128), whole(T, TC * N),
        ] + [once(*v.shape) for v in arrays],
        out_specs=[cols(T), lead(128, EB), whole(T, 128)] + [whole(*o.shape) for o in sums.outs()],
        out_shape=[shape(f32, T, E), shape(bf16, blocks, 128, EB), shape(bf16, T, 128)] + sums.outs(),
        scratch_shapes=[
            pltpu.VMEM((T * N, 128), f32),
            pltpu.VMEM((T, TC * N), f32), pltpu.VMEM((T, 128), f32), pltpu.VMEM((T, EB), bf16),
        ] + [pltpu.VMEM((T * 8, 128), f32)] * (2 * EB // 128) + sums.scratch(),
        compiler_params=params(collective_id=3, has_side_effects=True),
        name="bwd_scan",
    )(dtk, u, g, b_cols, c_cols, par, wts, arriving, held, spre, act, proj, grad_c, *arrays)


def conv_kernel(
    L, count, gap_ref, gproj_ref, wts_ref, act_ref, cs_ref, inner_ref, marks_ref,
    gc_ref, chan_ref, after_ref, xs_ref, edge_ref, got_ref, send_sem, recv_sem,
):
    T = gap_ref.shape[0]
    i = pl.program_id(0)
    blocks = edge_ref.shape[0]
    si, ci = lax.axis_index("seq"), lax.axis_index("chan")
    before = lax.rem(ci + count - 1, count)

    @pl.when(i == 0)
    def _():
        barrier = pltpu.get_barrier_semaphore()
        for other in (before, lax.rem(ci + 1, count)):
            pl.semaphore_signal(barrier, inc=1, device_id=(si, other), device_id_type=pl.DeviceIdType.MESH)
        pl.semaphore_wait(barrier, 2)

    def edge(b):
        return pltpu.make_async_remote_copy(
            src_ref=edge_ref.at[b], dst_ref=got_ref.at[b], send_sem=send_sem.at[b], recv_sem=recv_sem.at[b],
            device_id=(si, before), device_id_type=pl.DeviceIdType.MESH,
        )

    K, wide = L.K, L.R + 2 * L.N
    weights = wts_ref[0].astype(f32)
    row = lax.broadcasted_iota(jnp.int32, weights.shape, 0)
    weights = jnp.where(row < wide, weights, 0.0).astype(bf16)
    gc_ref[...] = jnp.dot(gproj_ref[...], weights, preferred_element_type=f32)
    act_low = act_ref[...].astype(bf16)
    grad_proj = lax.dot_general(gproj_ref[...], act_low, TN, preferred_element_type=f32)
    xs_ref[...] = inner_ref[...].astype(f32)

    def tile(k, carry):
        r = pl.multiple_of(k * RT, RT)
        rows = pl.ds(r, RT)
        total = cs_ref[rows, :]
        sig = jax.nn.sigmoid(total)
        grad = (gc_ref[rows, :] + gap_ref[rows, :]) * sig * (1.0 + total * (1.0 - sig))
        gc_ref[rows, :] = grad
        block = xs_ref[pl.ds(pl.multiple_of(r + HALO - 8, 8), RT + 8), :]
        out = [carry[K] + jnp.sum(grad.reshape(RT // 8, 8, EB), axis=0)]
        for j in range(K):
            part = grad * block[8 - j : RT + 8 - j]
            if j > 0:
                part = part * marks_ref[rows, j - 1 : j]
            out.insert(0, carry[K - 1 - j] + jnp.sum(part.reshape(RT // 8, 8, EB), axis=0))
        return tuple(out)

    none = jnp.zeros((8, EB), f32)
    sums = lax.fori_loop(0, T // RT, tile, (none,) * (K + 1))
    edge_ref[i] = gc_ref[0:8, :]
    edge(i).start()
    chan_ref[0] = jnp.concatenate(
        [grad_proj[0:wide]]
        + [jnp.sum(s, axis=0, keepdims=True) for s in sums]
        + [jnp.zeros((128 - wide - K - 1, EB), f32)],
        axis=0,
    ).astype(bf16)

    @pl.when(i == blocks - 1)
    def _():
        for b in range(blocks):
            edge(b).wait()
            rows = jnp.where(ci == count - 1, 0.0, got_ref[b])
            after_ref[:, b * EB : (b + 1) * EB] = rows


def conv_back(L, count, gap, gproj, wts, act, cs, inner, marks):
    T, E = gap.shape
    blocks = E // EB
    return pl.pallas_call(
        functools.partial(conv_kernel, L, count),
        grid=(blocks,),
        in_specs=[
            cols(T), whole(T, 128), lead(WTS, EB), cols(T), cols(T), cols(T + HALO), whole(*marks.shape),
        ],
        out_specs=[cols(T), lead(128, EB), whole(8, E)],
        out_shape=[shape(f32, T, E), shape(bf16, blocks, 128, EB), shape(f32, 8, E)],
        scratch_shapes=[
            pltpu.VMEM((T + HALO, EB), f32),
            pltpu.VMEM((blocks, 8, EB), f32),
            pltpu.VMEM((blocks, 8, EB), f32),
            pltpu.SemaphoreType.DMA((blocks,)),
            pltpu.SemaphoreType.DMA((blocks,)),
        ],
        compiler_params=params(collective_id=4, has_side_effects=True),
        name="conv_back",
    )(gap, gproj, wts, act, cs, inner, marks)


def tail_kernel(
    L, gc_ref, after_ref, par_ref, marks_ref, normed_ref, wi_ref, gn_ref, tok_ref, cot_ref, gain_ref,
    gin_ref, gtok_ref, ggain_ref, ext_ref, low_ref, sum_ref,
):
    T, D = tok_ref.shape
    K = L.K
    i = pl.program_id(0)
    ext_ref[0:T, :] = gc_ref[...]
    ext_ref[T : T + 8, :] = after_ref[...]
    taps = [par_ref[0, L.conv + j : L.conv + j + 1, :] for j in range(K)]

    def tile(r):
        block = ext_ref[pl.ds(r, RT + 8), :]
        marks = marks_ref[pl.ds(r, RT + 8), :]
        total = taps[K - 1] * block[0:RT]
        for j in range(1, K):
            masked = block * marks[:, j - 1 : j]
            total = total + taps[K - 1 - j] * masked[j : RT + j]
        low_ref[pl.ds(r, RT), :] = total.astype(bf16)

    row_tiles(T, tile)
    gin_ref[...] = lax.dot_general(
        low_ref[...], normed_ref[...], TN, preferred_element_type=f32
    ).astype(bf16)
    part = lax.dot_general(low_ref[...], wi_ref[...], NT, preferred_element_type=f32)

    @pl.when(i == 0)
    def _():
        sum_ref[...] = gn_ref[...] + part

    @pl.when(i > 0)
    def _():
        sum_ref[...] += part

    @pl.when(i == pl.num_programs(0) - 1)
    def _():
        gain = gain_ref[...].reshape(1, D)

        def last(k, total):
            rows = pl.ds(pl.multiple_of(k * 16, 16), 16)
            x = tok_ref[rows, :].astype(f32)
            grad = sum_ref[rows, :]
            inv = lax.rsqrt(jnp.mean(x * x, axis=1, keepdims=True) + epsilon)
            scaled = grad * gain
            mean = jnp.mean(x * scaled, axis=1, keepdims=True)
            gtok_ref[rows, :] = (
                cot_ref[rows, :].astype(f32) + inv * scaled - x * (inv * inv * inv * mean)
            )
            return total + jnp.sum((grad * x * inv).reshape(2, 8, D), axis=0)

        total = lax.fori_loop(0, T // 16, last, jnp.zeros((8, D), f32))
        ggain_ref[...] = jnp.sum(total, axis=0, keepdims=True)


def tail(L, gc, after, par, marks, normed, in_weight, gn, tokens, cot, gain):
    T, E = gc.shape
    D = tokens.shape[1]
    blocks = E // EB
    return pl.pallas_call(
        functools.partial(tail_kernel, L),
        grid=(blocks,),
        in_specs=[
            cols(T), cols(8), lead(PAR, EB), whole(*marks.shape), whole(T, D), cols(D), whole(T, D),
            whole(T, D), whole(T, D), whole(D),
        ],
        out_specs=[tall(EB, D), whole(T, D), whole(1, D)],
        out_shape=[shape(bf16, E, D), shape(f32, T, D), shape(f32, 1, D)],
        scratch_shapes=[
            pltpu.VMEM((T + 8, EB), f32), pltpu.VMEM((T, EB), bf16), pltpu.VMEM((T, D), f32),
        ],
        compiler_params=params(),
        name="tail",
    )(gc, after, par, marks, normed, in_weight, gn, tokens, cot, gain)


class Sums:
    def __init__(self, chan_count, seq_count, kinds, shapes, phases, skew=1, pace=1, begins=None, blocked=()):
        self.cc, self.sc = chan_count, seq_count
        self.kinds = kinds
        self.phases, self.skew, self.pace = phases, skew, pace
        self.begins = begins
        self.blocked = blocked
        self.size = 8 * seq_count
        self.bits = [1 << i for i in range(chan_count.bit_length() - 1)]
        self.z_bits = [2 << i for i in range(seq_count.bit_length() - 2)]
        self.pieces = [
            (a, r, dims[2]) for a, dims in enumerate(shapes) for r in range(0, dims[1], 2 * self.size)
        ]
        self.shapes = shapes

    def half(self, p):
        return self.kinds[self.pieces[p][0]] is not None

    def stages(self, p):
        bits = self.bits if p % 2 == 0 else self.bits[::-1]
        return (
            [("core", 1)] + [("chan", b) for b in bits] + [("z", b) for b in self.z_bits]
            + [("zgather", b) for b in self.z_bits[::-1]] + ([("move", 0)] if self.half(p) else [])
            + [("cgather", 1)]
        )

    def span(self, p):
        halvings = 2 + len(self.bits)
        phase = self.phases[self.pieces[p][0]]
        first = halvings if phase == "gather" else 0
        return first, halvings if phase == "halve" else len(self.stages(p))

    def begin(self, p):
        if self.begins is not None:
            return self.begins[p]
        phase = self.phases[self.pieces[p][0]]
        before = [q for q in range(p) if self.phases[self.pieces[q][0]] == phase]
        return self.skew * (len(before) // 2)

    def ticks(self):
        return max(
            self.begin(p) + self.pace * (self.span(p)[1] - self.span(p)[0]) for p in range(len(self.pieces))
        ) + 1

    def final(self, p):
        a, first, width = self.pieces[p]
        return pl.ds(first // 4, self.size // 2)

    def outs(self):
        found = []
        for kind, dims, phase in zip(self.kinds, self.shapes, self.phases):
            if phase == "halve":
                found.append(shape(bf16, dims[1] // 4, dims[2]))
            elif len(found) in self.blocked:
                found.append(shape(bf16, 2 * dims[1], dims[2]))
            else:
                found.append(shape(bf16, *(dims[1:] if kind is None else (2,) + tuple(dims[1:]))))
        return found

    def scratch(self):
        found = []
        for p, (a, r, width) in enumerate(self.pieces):
            small = self.span(p)[0] > 0
            for k in range(len(self.bits) + 1):
                dims = (self.cc >> k, self.size, width)
                found.append(pltpu.VMEM((1, 16, 128) if small else dims, bf16))
            for k in range(len(self.z_bits)):
                found.append(pltpu.VMEM((self.size >> (k + 1), width), bf16))
            found.append(pltpu.VMEM((self.size, width), bf16))
        dims = (len(self.pieces), len(self.bits) + 2 * len(self.z_bits) + 3, self.cc)
        return found + [pltpu.SemaphoreType.DMA(dims), pltpu.SemaphoreType.DMA(dims)]

    def bind(self, x_refs, o_refs, scratch):
        self.x, self.o = x_refs, o_refs
        each = len(self.bits) + len(self.z_bits) + 2
        self.held = [scratch[p * each : (p + 1) * each] for p in range(len(self.pieces))]
        self.send_sem, self.recv_sem = scratch[-2:]
        self.si, self.ci = lax.axis_index("seq"), lax.axis_index("chan")
        self.core = lax.rem(self.si, 2)

    def side(self, bit):
        return lax.rem(self.si // bit, 2)

    def across(self, bit):
        return (self.si + bit - 2 * bit * self.side(bit), self.ci)

    def barrier(self):
        barrier = pltpu.get_barrier_semaphore()
        others = [(self.si, lax.rem(self.ci + k, self.cc)) for k in range(1, self.cc)]
        others += [self.across(bit) for bit in [1] + self.z_bits]
        for other in others:
            pl.semaphore_signal(barrier, inc=1, device_id=other, device_id_type=pl.DeviceIdType.MESH)
        pl.semaphore_wait(barrier, len(others))

    def copy(self, p, s, slot, src, dst, device):
        return pltpu.make_async_remote_copy(
            src_ref=src, dst_ref=dst, send_sem=self.send_sem.at[p, s, slot],
            recv_sem=self.recv_sem.at[p, s, slot], device_id=device, device_id_type=pl.DeviceIdType.MESH,
        )

    def kept(self, p, s, keep):
        name, bit = self.stages(p)[s]
        if name == "core":
            a, start, width = self.pieces[p]
            side = self.core if keep else 1 - self.core
            return [self.x[a].at[:, pl.ds(pl.multiple_of(start + side * self.size, 16), self.size), :]]
        ref = self.held[p][s - 1]
        if name == "z":
            side = self.side(bit) if keep else 1 - self.side(bit)
            k = self.z_bits.index(bit)
            rows = self.size >> (k + 1)
            rows = pl.ds(pl.multiple_of(side * rows, 16), rows)
            return [ref.at[0, rows, :] if k == 0 else ref.at[rows, :]]
        mine = lax.rem(self.ci // bit, 2)
        side = mine if keep else 1 - mine
        left = sorted(b for n, b in self.stages(p)[s : 1 + len(self.bits)])
        low = 1 << left.index(bit)
        return [
            ref.at[pl.ds((i // low) * 2 * low + side * low + i % low, 1)]
            for i in range((1 << len(left)) // 2)
        ]

    def landing(self, p, s):
        dst = self.held[p][s]
        return [dst.at[pl.ds(i, 1)] for i in range(dst.shape[0])] if self.stages(p)[s][0] == "chan" else [dst]

    def gathered(self, p, done):
        start, rows = 0, self.size
        for bit in self.z_bits[:done]:
            rows //= 2
            start = start + self.side(bit) * rows
        if self.half(p):
            return self.held[p][-1].at[pl.ds(pl.multiple_of(start, 16), rows), :]
        start = start + self.pieces[p][1] + self.core * self.size
        return self.o[self.pieces[p][0]].at[pl.ds(pl.multiple_of(start, 16), rows), :]

    def target(self, p, v):
        a, first, width = self.pieces[p]
        base = self.kinds[a]
        if a in self.blocked:
            row = first * self.cc + v * 2 * self.size
            owner_rows = 2 * self.shapes[a][1]
            rows = pl.ds(pl.multiple_of(row % owner_rows + self.core * self.size, 16), self.size)
            return base + row // owner_rows, self.o[a].at[rows, :]
        rows = pl.ds(pl.multiple_of(first + self.core * self.size, 16), self.size)
        return base + v // 2, self.o[a].at[v % 2, rows, :]

    def move(self, p, s, v):
        goal, place = self.target(p, v)
        return goal, place, self.copy(p, s, v, self.held[p][-1], place, (self.si, goal))

    def pass_on(self, p, s, v):
        goal, place = self.target(p, v)
        return goal, self.copy(p, s, v, place, place, self.across(1))

    def copies(self, p, s):
        name, bit = self.stages(p)[s]
        if name in ("core", "chan", "z"):
            device = (self.si, self.ci + bit - 2 * bit * lax.rem(self.ci // bit, 2))
            device = device if name == "chan" else self.across(bit)
            pairs = zip(self.kept(p, s, False), self.landing(p, s))
            return [self.copy(p, s, i, src, dst, device) for i, (src, dst) in enumerate(pairs)]
        if name == "zgather":
            place = self.gathered(p, self.z_bits.index(bit) + 1)
        else:
            a, first, width = self.pieces[p]
            rows = pl.ds(pl.multiple_of(first + self.core * self.size, 16), self.size)
            place = self.o[a].at[rows, :]
        return [self.copy(p, s, 0, place, place, self.across(bit))]

    def last_of_half(self, p, s):
        return self.half(p) and self.stages(p)[s][0] == "cgather"

    def start(self, p, s):
        if self.stages(p)[s][0] == "move":
            for v in range(self.cc):
                @pl.when(self.ci == v)
                def _(v=v):
                    goal, place, copy = self.move(p, s, v)
                    if goal == v:
                        place[...] = self.held[p][-1][...]
                    else:
                        copy.start()
        elif self.last_of_half(p, s):
            for v in range(self.cc):
                goal, copy = self.pass_on(p, s, v)
                pl.when(self.ci == goal)(copy.start)
        else:
            for copy in self.copies(p, s):
                copy.start()

    def finish(self, p, s):
        name, bit = self.stages(p)[s]
        if name == "move":
            for v in range(self.cc):
                goal, place, copy = self.move(p, s, v)
                if goal != v:
                    pl.when(self.ci == goal)(copy.wait_recv)
            return
        if self.last_of_half(p, s):
            for v in range(self.cc):
                goal, copy = self.pass_on(p, s, v)
                pl.when(self.ci == goal)(copy.wait_recv)
            return
        for copy in self.copies(p, s):
            copy.wait_recv()
        if name in ("core", "chan", "z"):
            last = s == len(self.bits) + len(self.z_bits)
            handed = self.phases[self.pieces[p][0]] == "halve" and self.span(p)[1] == s + 1
            for src, dst in zip(self.kept(p, s, True), self.landing(p, s)):
                total = (dst[...].astype(f32) + src[...].astype(f32)).astype(bf16)
                if handed:
                    dst = self.o[self.pieces[p][0]].at[self.final(p), :]
                elif last:
                    dst = self.gathered(p, len(self.z_bits))
                dst[...] = total

    def tick(self, n):
        for p in range(len(self.pieces)):
            first, end = self.span(p)
            s, rest = divmod(n - self.begin(p), self.pace)
            s += first
            if rest != 0:
                continue
            if first + 1 <= s <= end:
                self.finish(p, s - 1)
            if first > 0 and s == first:
                self.held[p][first - 1][...] = self.x[self.pieces[p][0]][self.final(p), :]
            if first <= s < end:
                self.start(p, s)

    def drain(self):
        for p in range(len(self.pieces)):
            for s in range(*self.span(p)):
                if self.stages(p)[s][0] == "move":
                    for v in range(self.cc):
                        goal, place, copy = self.move(p, s, v)
                        if goal != v:
                            pl.when(self.ci == v)(copy.wait_send)
                elif self.last_of_half(p, s):
                    for v in range(self.cc):
                        goal, copy = self.pass_on(p, s, v)
                        pl.when(self.ci == goal)(copy.wait_send)
                else:
                    for copy in self.copies(p, s):
                        copy.wait_send()

    def hand_over(self, refs):
        for kind, src, dst in zip(self.kinds, self.o, refs):
            def work(src=src, dst=dst):
                dst[...] = src[...]

            if kind is None:
                work()
            else:
                pl.when((self.ci >= kind) & (self.ci < kind + self.cc // 2))(work)


def sum_kernel(sums, *refs):
    arrays = len(sums.kinds)
    sums.bind(refs[:arrays], refs[arrays : 2 * arrays], refs[2 * arrays :])
    sums.barrier()
    for n in range(sums.ticks()):
        sums.tick(n)
    sums.drain()


def sum_owned(arrays, shapes, kinds, phases, chan_count, seq_count):
    sums = Sums(chan_count, seq_count, kinds, shapes, phases)
    vmem = pl.BlockSpec(memory_space=pltpu.VMEM)
    return pl.pallas_call(
        functools.partial(sum_kernel, sums),
        in_specs=[vmem] * len(arrays),
        out_specs=[vmem] * len(arrays),
        out_shape=sums.outs(),
        scratch_shapes=sums.scratch(),
        compiler_params=params(collective_id=0, has_side_effects=True),
        name="sum_owned",
    )(*arrays)


def tail_sum_kernel(
    L, sums, gain_row, gc_ref, after_ref, taps_ref, marks_ref, normed_ref, wi_ref, gn_ref, tok_ref, cot_ref, gain_ref,
    d_ref, e_ref, *refs,
):
    early_refs, gtok_ref, refs = refs[:2], refs[2], refs[3:]
    arrays = len(sums.kinds)
    out_refs, held_refs, refs = refs[:arrays], refs[arrays : 2 * arrays], refs[2 * arrays :]
    ext_ref, low_ref, sum_ref, xin_ref, xe_ref = refs[:5]
    sums.bind((xin_ref, d_ref, xe_ref) + early_refs, held_refs, refs[5:])
    T, D = tok_ref.shape
    K, cc = L.K, sums.cc
    i = pl.program_id(0)
    blocks = xin_ref.shape[1] // (2 * sums.size)
    width = low_ref.shape[1]

    def tick_at(place):
        for b in range(blocks):
            pl.when(i == b)(functools.partial(sums.tick, 2 * b + place))

    @pl.when(i == 0)
    def _():
        sums.barrier()
        xe_ref[...] = e_ref[...]

    tick_at(0)
    ext_ref[0:T, :] = gc_ref[...]
    ext_ref[T : T + 8, :] = after_ref[...]
    taps = [taps_ref[j : j + 1, :] for j in range(K)]

    def tile(r):
        block = ext_ref[pl.ds(r, RT + 8), :]
        marks = marks_ref[pl.ds(r, RT + 8), :]
        total = taps[K - 1] * block[0:RT]
        for j in range(1, K):
            masked = block * marks[:, j - 1 : j]
            total = total + taps[K - 1 - j] * masked[j : RT + j]
        low_ref[pl.ds(r, RT), :] = total.astype(bf16)

    row_tiles(T, tile)
    tick_at(1)
    grad = lax.dot_general(
        low_ref[...], normed_ref[...], TN, preferred_element_type=f32
    ).astype(bf16)
    rows = pl.ds(pl.multiple_of(i * 2 * sums.size, 16), 2 * sums.size)
    for v in range(cc):
        xin_ref[v, rows, :] = grad[v * 2 * sums.size : (v + 1) * 2 * sums.size]
    pl.when(i == blocks - 1)(functools.partial(sums.tick, 2 * blocks))
    part = lax.dot_general(low_ref[...], wi_ref[...], NT, preferred_element_type=f32)

    @pl.when(i == 0)
    def _():
        sum_ref[...] = gn_ref[...] + part

    @pl.when(i > 0)
    def _():
        sum_ref[...] += part

    @pl.when(i == blocks - 1)
    def _():
        gain = gain_ref[...].reshape(1, D)

        def last(k, total):
            rows = pl.ds(pl.multiple_of(k * 16, 16), 16)
            x = tok_ref[rows, :].astype(f32)
            grad = sum_ref[rows, :]
            inv = lax.rsqrt(jnp.mean(x * x, axis=1, keepdims=True) + epsilon)
            scaled = grad * gain
            mean = jnp.mean(x * scaled, axis=1, keepdims=True)
            gtok_ref[rows, :] = (
                cot_ref[rows, :].astype(f32) + inv * scaled - x * (inv * inv * inv * mean)
            )
            return total + jnp.sum((grad * x * inv).reshape(2, 8, D), axis=0)

        total = lax.fori_loop(0, T // 16, last, jnp.zeros((8, D), f32))
        total = jnp.broadcast_to(jnp.sum(total, axis=0, keepdims=True), (16, D))
        share, start = D // cc, gain_row // 16 * 16
        dims = (16, xe_ref.shape[2])
        here = lax.broadcasted_iota(jnp.int32, dims, 0) == gain_row - start
        here = here & (lax.broadcasted_iota(jnp.int32, dims, 1) < share)
        for q in range(cc):
            turned = total if q == 0 else pltpu.roll(total, D - q * share, 1)
            old = xe_ref[q, start : start + 16, :].astype(f32)
            xe_ref[q, start : start + 16, :] = jnp.where(here, turned[:, : dims[1]], old).astype(bf16)
        for n in range(2 * blocks + 1, sums.ticks()):
            sums.tick(n)
        sums.drain()
        sums.hand_over(out_refs)


def tail_sum(
    L, counts, gc, after, taps, marks, normed, in_weight, gn, tokens, cot, gain, d, e, early, early_shapes, kinds,
    gain_row,
):
    T, E = gc.shape
    D = tokens.shape[1]
    cc, sc = counts
    piece = 16 * sc
    wide = cc * piece
    blocks = E // wide
    shapes = [(cc, E // cc, D), d.shape, e.shape] + early_shapes
    pieces = [v[1] // piece for v in shapes]
    begins = [2 * (b + 1) for b in range(pieces[0])] + [0] * pieces[1] + [2 * blocks + 1] * pieces[2]
    begins += [k // 2 for k in range(pieces[3] + pieces[4])]
    sums = Sums(
        cc, sc, [0, None, None] + kinds, shapes, ["all"] * 3 + ["gather"] * 2, begins=begins, blocked=(0,)
    )
    return pl.pallas_call(
        functools.partial(tail_sum_kernel, L, sums, gain_row),
        grid=(blocks,),
        in_specs=[
            cols(T, wide), cols(8, wide), cols(8, wide), whole(*marks.shape), whole(T, D), cols(D, wide),
            whole(T, D), whole(T, D), whole(T, D), whole(D), once(*d.shape), once(*e.shape),
        ] + [once(*v.shape) for v in early],
        out_specs=[whole(T, D)] + [whole(*o.shape) for o in sums.outs()],
        out_shape=[shape(f32, T, D)] + sums.outs(),
        scratch_shapes=[pltpu.VMEM(o.shape, o.dtype) for o in sums.outs()] + [
            pltpu.VMEM((T + 8, wide), f32), pltpu.VMEM((T, wide), bf16), pltpu.VMEM((T, D), f32),
            pltpu.VMEM(shapes[0], bf16), pltpu.VMEM(e.shape, bf16),
        ] + sums.scratch(),
        compiler_params=params(collective_id=5, has_side_effects=True),
        name="tail_sum",
    )(gc, after, taps, marks, normed, in_weight, gn, tokens, cot, gain, d, e, *early)


def unpack_kernel(L, inner_ref, gate_ref, out_ref, d_ref, e_ref, gin_ref, gout_ref, *refs):
    first = lax.axis_index("chan") < lax.axis_size("chan") // 2

    @pl.when(first)
    def _():
        gin_ref[...] = inner_ref[...].astype(f32).T

    @pl.when(jnp.logical_not(first))
    def _():
        gin_ref[...] = gate_ref[...].astype(f32).T

    gout_ref[...] = out_ref[...].astype(f32)
    d, e = d_ref[...].astype(f32), e_ref[...].astype(f32)
    R, N, K = L.R, L.N, L.K
    wide = R + 2 * N
    conv_w, conv_b, proj, step_w, step_b, decay, skip, gain = refs
    width = d.shape[1]
    step_w[...] = d[0:R]
    decay[...] = d[R : R + N]
    step_b[...] = d[R + N].reshape(width)
    skip[...] = d[R + N + 1].reshape(width)
    proj[...] = e[0:wide]
    conv_w[...] = e[wide : wide + K]
    conv_b[...] = e[wide + K].reshape(width)
    gain[...] = e[wide + K + 1].reshape(width)


def unpack(L, sums):
    width = sums[3].shape[1]
    rows, D = sums[0].shape
    R, N, K = L.R, L.N, L.K
    return pl.pallas_call(
        functools.partial(unpack_kernel, L),
        out_shape=[
            shape(f32, D, rows), shape(f32, *sums[2].shape), shape(f32, K, width), shape(f32, width),
            shape(f32, R + 2 * N, width), shape(f32, R, width), shape(f32, width),
            shape(f32, N, width), shape(f32, width), shape(f32, width),
        ],
        compiler_params=params(),
        name="unpack",
    )(*sums)


def local(
    tokens, norm_gain, in_weight, conv_weight, conv_bias, proj_weight, step_weight,
    step_bias, decay_log, skip_gain, out_weight, cotangent, lengths,
):
    T, D = tokens.shape
    E = in_weight.shape[1] // 2
    L = Layout(step_weight.shape[0], decay_log.shape[0], conv_weight.shape[0])
    ci = lax.axis_index("chan")
    cc = lax.axis_size("chan")
    sc = lax.axis_size("seq")
    blocks, share = E // EB, E // cc

    parts = (conv_weight, conv_bias, proj_weight.T, step_weight, step_bias, decay_log, skip_gain)
    gathered = None
    if share != EB:
        wts, par, halo = gather_params(L, cc, parts, tokens)

        def by_block(values):
            values = jnp.moveaxis(values, 0, 1).reshape(-1, blocks, EB)
            return jnp.moveaxis(values, 1, 0)

        parts, gathered = None, (by_block(wts), by_block(par), halo)
    marks, normed, inner, gate, gg, g, cs, act, proj, b_cols, c_cols, taps, *own = front(
        L, cc, lengths, tokens, norm_gain, in_weight, out_weight, cotangent, parts, gathered
    )
    wts, par = gathered[:2] if gathered else own
    spre, dtk, u, entering, arriving = pre_scan(L, cc, proj, par, wts, act, g, marks, b_cols, c_cols)
    held, grad_c, block_out, grad_out, grad_in_gate, gn = fwd_scan(
        L, dtk, u, b_cols, c_cols, g, par, entering, act, gate, gg, out_weight, cotangent, tokens,
        normed, in_weight,
    )

    piece = 16 * sc
    fold = 2 if 2 * share <= piece else 1

    def owned(values):
        values = values.reshape(cc, -1, values.shape[-1] // fold)
        return jnp.pad(values, ((0, 0), (0, -values.shape[1] % piece), (0, 0)))

    def unfolded(values):
        if values.ndim == 2:
            return values[: share * fold].reshape(share, D)
        return values[:, : share * fold].reshape(2 * share, D)

    def by_owner(values):
        if share != EB:
            values = jnp.moveaxis(values, 0, 1).reshape(values.shape[1], cc, share)
            values = jnp.moveaxis(values, 1, 0)
        return jnp.pad(values, ((0, 0), (0, -values.shape[1] % piece), (0, 0)))

    early = [owned(grad_out), owned(grad_in_gate)]
    early_shapes = [v.shape for v in early]
    kinds = [None, cc // 2]
    sums = Sums(cc, sc, kinds, early_shapes, ["halve"] * 2, skew=1, pace=3)
    gap, chan_d, gproj, *early = bwd_scan(
        L, dtk, u, g, b_cols, c_cols, par, wts, arriving, held, spre, act, proj, grad_c, early, sums
    )
    gc, chan_e, after = conv_back(L, cc, gap, gproj, wts, act, cs, inner, marks)
    row = L.R + 2 * L.N + L.K + 1
    chan_d, chan_e = by_owner(chan_d), by_owner(chan_e)
    if share == EB and fold == 1 and E % (cc * piece) == 0:
        grad_tokens, sum_inner, sum_d, sum_e, sum_out, sum_gate = tail_sum(
            L, (cc, sc), gc, after, taps, marks, normed, in_weight, gn, tokens, cotangent, norm_gain,
            chan_d, chan_e, early, early_shapes, kinds, row,
        )
    else:
        grad_in_inner, grad_tokens, grad_gain = tail(
            L, gc, after, par, marks, normed, in_weight, gn, tokens, cotangent, norm_gain
        )
        gain_part = jnp.pad(grad_gain.reshape(cc, 1, D // cc), ((0, 0), (0, 0), (0, share - D // cc)))
        chan_e = lax.dynamic_update_slice(chan_e, gain_part.astype(bf16), (0, row, 0))
        late = [owned(grad_in_inner), chan_d, chan_e]
        sum_inner, sum_d, sum_e, sum_out, sum_gate = sum_owned(
            late + early, [v.shape for v in late] + early_shapes, [0, None, None] + kinds,
            ["all"] * 3 + ["gather"] * 2, cc, sc,
        )
        sum_inner = unfolded(sum_inner)
    sums = [sum_inner, unfolded(sum_gate), unfolded(sum_out), sum_d, sum_e]
    g_in, g_out, conv_w, conv_b, proj_w, step_w, step_b, decay, skip, g_gain = unpack(L, sums)
    return (
        block_out, grad_tokens, g_gain[: D // cc], g_in, conv_w, conv_b, proj_w.T, step_w,
        step_b, decay, skip, g_out,
    )


def solution(mesh):
    tok, row, vec = P(("seq", "chan"), None), P(None, "chan"), P("chan")
    in_specs = (
        tok, P(), P(), row, vec, P("chan", None), row, vec, row, vec, P(), tok, P("seq", None),
    )
    out_specs = (
        tok, tok, vec, row, row, vec, P("chan", None), row, vec, row, vec, P("chan", None),
    )
    return jax.shard_map(local, mesh=mesh, in_specs=in_specs, out_specs=out_specs, check_vma=False)
```

```python
import functools
import math

import jax
import jax.numpy as jnp
from jax import lax
from jax.experimental import pallas as pl
from jax.experimental.pallas import tpu as pltpu
from jax.sharding import PartitionSpec as P

epsilon = 1e-05
LOG2E = math.log2(math.e)
CUT = 1e30
TC = 64
EB = 384
RT = 32
BLOCK_SLOTS = 4
HALO = 16
PAR = 24
WTS = 128
f32 = jnp.float32
bf16 = jnp.bfloat16
NT = (((1,), (1,)), ((), ()))
TN = (((0,), (0,)), ((), ()))


def params(**more):
    return pltpu.CompilerParams(vmem_limit_bytes=60 * 1024 * 1024, **more)


def cols(rows, width=EB, shift=0):
    return pl.BlockSpec((rows, width), lambda i: (0, i + shift))


def tall(rows, width, shift=0):
    return pl.BlockSpec((rows, width), lambda i: (i + shift, 0))


def lead(rows, width, count=1):
    return pl.BlockSpec((count, rows, width), lambda i: (i, 0, 0))


def whole(*shape):
    return pl.BlockSpec(shape, lambda i: (0,) * len(shape))


def once(*shape):
    return pl.BlockSpec(shape, lambda i: (0,) * len(shape), pipeline_mode=pl.Buffered(1))


def shape(dtype, *dims):
    return jax.ShapeDtypeStruct(dims, dtype)


def row_tiles(count, body):
    def step(i, unused):
        body(pl.multiple_of(i * RT, RT))
        return unused

    lax.fori_loop(0, count // RT, step, 0)


def same_step(states, rows):
    dims = (rows, TC * states)
    here = lax.rem(lax.broadcasted_iota(jnp.int32, dims, 0), TC) * states
    place = lax.broadcasted_iota(jnp.int32, dims, 1)
    return (place >= here) & (place < here + states)


class Layout:
    def __init__(self, R, N, K):
        self.R, self.N, self.K = R, N, K
        self.step = R + 2 * N
        self.decay = 0
        self.conv = self.decay + N
        self.conv_b = self.conv + K
        self.step_b = self.conv_b + 1
        self.skip = self.step_b + 1
        self.end = self.skip + 1


def start_gather(
    L, count, cw_ref, cb_ref, pw_ref, sw_ref, sb_ref, dl_ref, sk_ref, tok_ref,
    wts_ref, par_ref, halo_ref, send_sem, recv_sem, halo_sems,
):
    si, ci = lax.axis_index("seq"), lax.axis_index("chan")
    T = tok_ref.shape[0]
    width = par_ref.shape[2]
    barrier = pltpu.get_barrier_semaphore()
    for k in range(1, count):
        pl.semaphore_signal(
            barrier, inc=1, device_id=(si, lax.rem(ci + k, count)),
            device_id_type=pl.DeviceIdType.MESH,
        )
    own, weights = par_ref.at[ci], wts_ref.at[ci]
    weights[...] = jnp.concatenate(
        [pw_ref[...].astype(f32), sw_ref[...].astype(f32)], axis=0
    ).astype(bf16)
    own[...] = jnp.concatenate(
        [
            dl_ref[...], cw_ref[...], cb_ref[...].reshape(1, width), sb_ref[...].reshape(1, width),
            sk_ref[...].reshape(1, width), jnp.zeros((PAR - L.end, width), f32),
        ],
        axis=0,
    )
    pl.semaphore_wait(barrier, count - 1)

    def share(ref, j, k):
        return pltpu.make_async_remote_copy(
            src_ref=ref, dst_ref=ref, send_sem=send_sem.at[j, k], recv_sem=recv_sem.at[j, k],
            device_id=(si, lax.rem(ci + k, count)), device_id_type=pl.DeviceIdType.MESH,
        )

    edge = pltpu.make_async_remote_copy(
        src_ref=tok_ref.at[pl.ds(T - HALO, HALO)], dst_ref=halo_ref,
        send_sem=halo_sems.at[0], recv_sem=halo_sems.at[1],
        device_id=(si, lax.rem(ci + 1, count)), device_id_type=pl.DeviceIdType.MESH,
    )
    edge.start()
    for j, ref in enumerate((own, weights)):
        for k in range(1, count):
            share(ref, j, k).start()

    def wait():
        edge.wait()
        for j, ref in enumerate((own, weights)):
            for k in range(1, count):
                share(ref, j, k).wait()

    return wait


def gather_kernel(L, count, *refs):
    start_gather(L, count, *refs)()


def gather_scratch(count):
    return [
        pltpu.SemaphoreType.DMA((2, count)),
        pltpu.SemaphoreType.DMA((2, count)),
        pltpu.SemaphoreType.DMA((2,)),
    ]


def gather_params(L, count, parts, tokens):
    width = parts[0].shape[1]
    T, D = tokens.shape
    vmem = pl.BlockSpec(memory_space=pltpu.VMEM)
    return pl.pallas_call(
        functools.partial(gather_kernel, L, count),
        in_specs=[vmem] * 8,
        out_specs=[vmem] * 3,
        out_shape=[shape(bf16, count, WTS, width), shape(f32, count, PAR, width), shape(bf16, HALO, D)],
        scratch_shapes=gather_scratch(count),
        compiler_params=params(collective_id=1, has_side_effects=True),
        name="gather_params",
    )(*parts, tokens)


def front_kernel(
    L, count, inside, len_ref, tok_ref, gain_ref, wi_ref, wg_ref, wo_ref, cot_ref, *refs,
):
    given, refs = refs[: 7 if inside else 3], refs[7 if inside else 3 :]
    (
        marks_ref, normed_ref, inner_ref, gate_ref, gg_ref, g_ref, cs_ref, act_ref, proj_ref, bch_ref, cch_ref,
        taps_ref,
    ) = refs[:12]
    results, refs = refs[12 : 14 if inside else 12], refs[14 if inside else 12 :]
    hn_ref, xs_ref, low_ref = refs[:3]
    T = tok_ref.shape[0]
    N, K = L.N, L.K
    i = pl.program_id(0)
    sub = low_ref.shape[1] // EB
    if inside:
        wts_ref, par_ref, halo_ref, *sems = refs[3:]
        first = i * sub
    else:
        wts_ref, par_ref, halo_ref = given
        first = 0

    def norm(x):
        x = x.astype(f32)
        inv = lax.rsqrt(jnp.mean(x * x, axis=1, keepdims=True) + epsilon)
        return (x * inv * gain_ref[...].reshape(1, x.shape[1])).astype(bf16)

    def products():
        low = jnp.dot(normed_ref[...], wi_ref[...], preferred_element_type=f32).astype(bf16)
        inner_ref[HALO:, :] = low
        xs_ref[HALO:, :] = low.astype(f32)
        gate_ref[...] = jnp.dot(normed_ref[...], wg_ref[...], preferred_element_type=f32)
        gg_ref[...] = lax.dot_general(cot_ref[...], wo_ref[...], NT, preferred_element_type=f32)

    @pl.when(i == 0)
    def _():
        if inside:
            wait = start_gather(L, count, *given, tok_ref, wts_ref, par_ref, halo_ref, *sems)

        def tile(r):
            normed_ref[pl.ds(r, RT), :] = norm(tok_ref[pl.ds(r, RT), :])

        row_tiles(T, tile)
        proj_ref[...] = jnp.zeros_like(proj_ref)
        dims = marks_ref.shape
        place = lax.broadcasted_iota(jnp.int32, dims, 0) + lax.axis_index("chan") * T
        lane = lax.broadcasted_iota(jnp.int32, dims, 1)
        reach = jnp.where(lane < K - 1, lane + 1, 1)
        found = jnp.zeros(dims, f32)
        start = jnp.int32(0)
        for k in range(len_ref.shape[1]):
            found = jnp.where((start > place - reach) & (start <= place), 1.0, found)
            start = start + len_ref[0, k]
        marks_ref[...] = jnp.where(lane < K - 1, 1.0 - found, found * CUT)
        products()
        if inside:
            wait()
            results[0][...] = wts_ref[...]
            results[1][...] = par_ref[...]
        lead_device = lax.axis_index("chan") == 0
        halo = jnp.where(lead_device, jnp.zeros(halo_ref.shape, f32), halo_ref[...].astype(f32))
        hn_ref[...] = norm(halo)

    pl.when(i > 0)(products)
    low = jnp.dot(hn_ref[...], wi_ref[...], preferred_element_type=f32).astype(bf16)
    inner_ref[0:HALO, :] = low
    xs_ref[0:HALO, :] = low.astype(f32)

    for k in range(sub):
        c = slice(k * EB, (k + 1) * EB)
        taps = [par_ref[first + k, L.conv + j : L.conv + j + 1, :] for j in range(K)]
        bias = par_ref[first + k, L.conv_b : L.conv_b + 1, :]
        taps_ref[:, c] = par_ref[first + k, L.conv : L.conv + 8, :]

        def tile(r, c=c, taps=taps, bias=bias):
            rows = pl.ds(r, RT)
            block = xs_ref[pl.ds(pl.multiple_of(r + HALO - 8, 8), RT + 8), c]
            total = bias + taps[K - 1] * block[8:]
            for j in range(1, K):
                usable = marks_ref[rows, j - 1 : j]
                total = total + taps[K - 1 - j] * (block[8 - j : RT + 8 - j] * usable)
            act = total * jax.nn.sigmoid(total)
            cs_ref[rows, c] = total
            act_ref[rows, c] = act
            low_ref[rows, c] = act.astype(bf16)
            gate = gate_ref[rows, c]
            passed = gg_ref[rows, c] * (gate * jax.nn.sigmoid(gate))
            g_ref[rows, c] = passed.astype(bf16).astype(f32)

        row_tiles(T, tile)
        proj_ref[...] += lax.dot_general(low_ref[:, c], wts_ref[first + k], NT, preferred_element_type=f32)

    @pl.when(i == pl.num_programs(0) - 1)
    def _():
        turned = proj_ref[...].T
        for ref, start in ((bch_ref, L.R), (cch_ref, L.R + N)):
            for j in range(T // TC):
                ref[j] = turned[start : start + N, j * TC : (j + 1) * TC]


def front(L, count, lengths, tokens, gain, in_weight, out_weight, cot, parts, gathered):
    T, D = tokens.shape
    E = out_weight.shape[0]
    sub = 2
    wide = EB * sub
    steps = E // wide
    N = L.N
    inside = parts is not None
    more_out, scratch, options = [], [], {}
    if inside:
        given, given_specs = parts, [whole(*v.shape) for v in parts]
        more_out = [shape(bf16, count, WTS, EB), shape(f32, count, PAR, EB)]
        scratch = [pltpu.VMEM(o.shape, o.dtype) for o in more_out] + [pltpu.VMEM((HALO, D), bf16)]
        scratch += gather_scratch(count)
        options = dict(collective_id=1, has_side_effects=True)
    else:
        given, given_specs = gathered, [lead(WTS, EB, sub), lead(PAR, EB, sub), whole(HALO, D)]
    return pl.pallas_call(
        functools.partial(front_kernel, L, count, inside),
        grid=(steps,),
        in_specs=[
            pl.BlockSpec(memory_space=pltpu.SMEM),
            whole(T, D), whole(D), cols(D, wide), cols(D, wide, steps), tall(wide, D), whole(T, D),
        ] + given_specs,
        out_specs=[whole(T + 8, 8), whole(T, D), cols(T + HALO, wide)] + [cols(T, wide)] * 5 + [
            whole(T, 128), whole(T // TC, N, TC), whole(T // TC, N, TC), cols(8, wide),
        ] + [whole(*o.shape) for o in more_out],
        out_shape=[shape(f32, T + 8, 8), shape(bf16, T, D), shape(bf16, T + HALO, E)]
        + [shape(f32, T, E)] * 5
        + [shape(f32, T, 128), shape(f32, T // TC, N, TC), shape(f32, T // TC, N, TC), shape(f32, 8, E)]
        + more_out,
        scratch_shapes=[
            pltpu.VMEM((HALO, D), bf16),
            pltpu.VMEM((T + HALO, wide), f32),
            pltpu.VMEM((T, wide), bf16),
        ] + scratch,
        compiler_params=params(**options),
        name="front",
    )(lengths, tokens, gain, in_weight, in_weight, out_weight, cot, *given)


def rates(L, par_ref):
    return -jnp.exp(par_ref[0, L.decay : L.decay + L.N, :]) * LOG2E


def lane_tiles(values):
    return [values[:, k * 128 : (k + 1) * 128] for k in range(EB // 128)]


def row_at(ref, t):
    return lane_tiles(ref[pl.ds(t, 1), :])


def spread(columns, j):
    return jnp.broadcast_to(columns[:, j : j + 1], (columns.shape[0], 128))


def ahead_of(steps, fetch):
    steps = list(steps)
    loaded = [fetch(j) for j in steps[:2]]
    for k, j in enumerate(steps):
        if k + 2 < len(steps):
            loaded.append(fetch(steps[k + 2]))
        yield j, loaded[k]


def softplus(x):
    return jnp.maximum(x, 0.0) + jnp.log1p(jnp.exp(-jnp.abs(x)))


def pre_kernel(
    L, count, proj_ref, par_ref, wts_ref, act_ref, g_ref, marks_ref, b_ref, c_ref,
    spre_ref, dtk_ref, u_ref, enter_ref, arrive_ref, ahead_ref, behind_ref, got_ref,
    send_sem, recv_sem,
):
    T, E = act_ref.shape[0], enter_ref.shape[1]
    N = L.N
    i = pl.program_id(0)
    blocks = E // EB
    si, ci = lax.axis_index("seq"), lax.axis_index("chan")

    @pl.when(i == 0)
    def _():
        barrier = pltpu.get_barrier_semaphore()
        for k in range(1, count):
            pl.semaphore_signal(
                barrier, inc=1, device_id=(si, lax.rem(ci + k, count)),
                device_id_type=pl.DeviceIdType.MESH,
            )
        pl.semaphore_wait(barrier, count - 1)

    low = proj_ref[:, 0 : L.R].astype(bf16)
    weights = wts_ref[0, L.step : L.step + L.R, :]
    bias = par_ref[0, L.step_b : L.step_b + 1, :]
    spre_ref[...] = jnp.dot(low, weights, preferred_element_type=f32) + bias

    def tile(r):
        rows = pl.ds(r, RT)
        step = softplus(spre_ref[rows, :])
        u_ref[rows, :] = step * act_ref[rows, :]
        dtk_ref[rows, :] = step + marks_ref[rows, 3:4]

    row_tiles(T, tile)
    rate = lane_tiles(rates(L, par_ref))
    tiles = len(rate)

    def chunk(c, carry):
        h, through, head = (list(carry[k * tiles : (k + 1) * tiles]) for k in range(3))
        base = pl.multiple_of(c * TC, TC)
        b_cols, c_cols = b_ref[c], c_ref[c]

        def fetch(j):
            rows = [row_at(ref, base + j) for ref in (dtk_ref, u_ref, g_ref)]
            return rows + [spread(b_cols, j), spread(c_cols, j)]

        for j, (d, u, g, b_now, c_now) in ahead_of(range(TC), fetch):
            for k in range(tiles):
                factor = jnp.exp2(d[k] * rate[k])
                h[k] = factor * h[k] + b_now * u[k]
                through[k] = factor * through[k]
                head[k] = head[k] + through[k] * (c_now * g[k])
        return tuple(h + through + head)

    zero = jnp.zeros((N, 128), f32)
    out = lax.fori_loop(0, T // TC, chunk, (zero,) * tiles + (zero + 1.0,) * tiles + (zero,) * tiles)
    h, through, head = (jnp.concatenate(out[k * tiles : (k + 1) * tiles], axis=1) for k in range(3))
    zero = jnp.zeros((N, EB), f32)
    ahead_ref[i, 0:N, :] = h
    ahead_ref[i, N:, :] = through
    behind_ref[i, 0:N, :] = head
    behind_ref[i, N:, :] = through

    def send(b, k, forward):
        return pltpu.make_async_remote_copy(
            src_ref=(ahead_ref if forward else behind_ref).at[b], dst_ref=got_ref.at[count - k, b],
            send_sem=send_sem.at[k, b], recv_sem=recv_sem.at[count - k, b],
            device_id=(si, lax.rem(ci + k, count)), device_id_type=pl.DeviceIdType.MESH,
        )

    for k in range(1, count):
        @pl.when(ci + k < count)
        def _(k=k):
            send(i, k, True).start()

        @pl.when(ci + k >= count)
        def _(k=k):
            send(i, k, False).start()

    @pl.when(i == blocks - 1)
    def _():
        for b in range(blocks):
            for k in range(1, count):
                send(b, k, True).wait()
        for b in range(blocks):
            span = slice(b * EB, (b + 1) * EB)
            entering, arriving = zero, zero
            for k in range(1, count):
                before = ci + k >= count
                got = got_ref[k, b]
                entering = jnp.where(before, got[0:N] + got[N:] * entering, entering)
            for k in range(count - 1, 0, -1):
                behind = ci + k < count
                got = got_ref[k, b]
                arriving = jnp.where(behind, got[0:N] + got[N:] * arriving, arriving)
            enter_ref[:, span] = entering
            arrive_ref[:, span] = arriving


def pre_scan(L, count, proj, par, wts, act, g, marks, b_cols, c_cols):
    T, E = act.shape
    N = L.N
    blocks = E // EB
    state = shape(f32, N, E)
    return pl.pallas_call(
        functools.partial(pre_kernel, L, count),
        grid=(blocks,),
        in_specs=[
            whole(T, 128), lead(PAR, EB), lead(WTS, EB), cols(T), cols(T), whole(*marks.shape),
            once(*b_cols.shape), once(*c_cols.shape),
        ],
        out_specs=[cols(T)] * 3 + [whole(N, E)] * 2,
        out_shape=[shape(f32, T, E)] * 3 + [state] * 2,
        scratch_shapes=[
            pltpu.VMEM((blocks, 2 * N, EB), f32),
            pltpu.VMEM((blocks, 2 * N, EB), f32),
            pltpu.VMEM((count, blocks, 2 * N, EB), f32),
            pltpu.SemaphoreType.DMA((count, blocks)),
            pltpu.SemaphoreType.DMA((count, blocks)),
        ],
        compiler_params=params(collective_id=2, has_side_effects=True),
        name="pre_scan",
    )(proj, par, wts, act, g, marks, b_cols, c_cols)


def fold_rows(refs, r):
    sums = []
    for ref in refs:
        parts = [ref[pl.ds(r * 8 + k, 8, stride=8), :] for k in range(8)]
        while len(parts) > 1:
            parts = [x + y for x, y in zip(parts[::2], parts[1::2])]
        sums.append(parts[0])
    return jnp.concatenate(sums, axis=1)


def halves(values):
    return values[0:8] + values[8:16]


def lane_sums(states, acc_ref, out_ref, chunks):
    width = TC * states
    ones = jnp.ones((TC, 128), bf16)
    group = chunks // 4
    for k in range(4):
        part = acc_ref[k * group * width : (k + 1) * group * width, :].astype(bf16)
        sums = lax.dot_general(ones, part, NT, preferred_element_type=f32)
        for c in range(group):
            row = (k * group + c) * TC
            out_ref[row : row + TC, :] = sums[:, c * width : (c + 1) * width]


def fwd_kernel(
    L, dtk_ref, u_ref, b_ref, c_ref, g_ref, par_ref, hin_ref, act_ref, gate_ref, gg_ref,
    wo_ref, cot_ref, tok_ref, normed_ref, wg_ref,
    h_ref, gc_ref, block_ref, gout_ref, gin_ref, gn_ref,
    acc_ref, gated_ref, ggate_ref, branch_ref, *y_refs,
):
    rate = lane_tiles(rates(L, par_ref))
    T, states = u_ref.shape[0], L.N
    chunks = T // TC
    width = TC * states
    i = pl.program_id(0)

    @pl.when(i == 0)
    def _():
        acc_ref[...] = jnp.zeros_like(acc_ref)
        gn_ref[...] = jnp.zeros_like(gn_ref)
        branch_ref[...] = jnp.zeros_like(branch_ref)

    h_ref[0:states, :] = hin_ref[...].astype(bf16)

    def chunk(c, carry):
        h = list(carry)
        base = pl.multiple_of(c * TC, TC)
        row = pl.multiple_of(c * width, width)
        b_cols, c_cols = b_ref[c], c_ref[c]

        def fetch(j):
            at = pl.ds(row + j * states, states)
            rows = [row_at(ref, base + j) for ref in (dtk_ref, u_ref, g_ref)]
            return rows + [spread(b_cols, j), spread(c_cols, j), acc_ref[at, :]]

        for j, (d, u, g, b_now, c_now, acc) in ahead_of(range(TC), fetch):
            for k in range(len(h)):
                h[k] = jnp.exp2(d[k] * rate[k]) * h[k] + b_now * u[k]
                h_ref[pl.ds(row + (j + 1) * states, states), k * 128 : (k + 1) * 128] = h[k].astype(bf16)
                y_refs[k][pl.ds((base + j) * 8, 8), :] = halves(c_now * h[k])
                acc = acc + h[k] * g[k]
            acc_ref[pl.ds(row + j * states, states), :] = acc
        return tuple(h)

    lax.fori_loop(0, chunks, chunk, tuple(lane_tiles(hin_ref[...])))
    skip = par_ref[0, L.skip : L.skip + 1, :]

    def tile(k, unused):
        rows = pl.ds(pl.multiple_of(k * 16, 16), 16)
        y = jnp.concatenate([fold_rows(y_refs, k * 16), fold_rows(y_refs, k * 16 + 8)], axis=0)
        mixer = (y + skip * act_ref[rows, :]).astype(bf16).astype(f32)
        gate = gate_ref[rows, :]
        sig = jax.nn.sigmoid(gate)
        gated_ref[rows, :] = (mixer * (gate * sig)).astype(bf16)
        ggate_ref[rows, :] = (gg_ref[rows, :] * mixer * sig * (1.0 + gate * (1.0 - sig))).astype(bf16)
        return unused

    lax.fori_loop(0, T // 16, tile, 0)
    branch_ref[...] += jnp.dot(gated_ref[...], wo_ref[...], preferred_element_type=f32)
    gout_ref[...] = lax.dot_general(
        gated_ref[...], cot_ref[...], TN, preferred_element_type=f32
    ).astype(bf16)
    gin_ref[...] = lax.dot_general(
        ggate_ref[...], normed_ref[...], TN, preferred_element_type=f32
    ).astype(bf16)
    gn_ref[...] += lax.dot_general(ggate_ref[...], wg_ref[...], NT, preferred_element_type=f32)

    @pl.when(i == pl.num_programs(0) - 1)
    def _():
        block_ref[...] = (tok_ref[...].astype(f32) + branch_ref[...]).astype(bf16)
        lane_sums(states, acc_ref, gc_ref, chunks)


def fwd_scan(L, dtk, u, b_cols, c_cols, g, par, entering, act, gate, gg, out_weight, cot, tokens, normed, in_weight):
    T, E = dtk.shape
    D = tokens.shape[1]
    N = L.N
    rows = (T + 1) * N
    blocks = E // EB
    return pl.pallas_call(
        functools.partial(fwd_kernel, L),
        grid=(blocks,),
        in_specs=[
            cols(T), cols(T), once(*b_cols.shape), once(*c_cols.shape), cols(T), lead(PAR, EB), cols(N),
            cols(T), cols(T), cols(T), tall(EB, D), whole(T, D), whole(T, D), whole(T, D),
            cols(D, EB, blocks),
        ],
        out_specs=[
            cols(rows), whole(T, TC * N), whole(T, D), tall(EB, D), tall(EB, D), whole(T, D),
        ],
        out_shape=[
            shape(bf16, rows, E), shape(f32, T, TC * N), shape(bf16, T, D), shape(bf16, E, D),
            shape(bf16, E, D), shape(f32, T, D),
        ],
        scratch_shapes=[
            pltpu.VMEM((T * N, 128), f32), pltpu.VMEM((T, EB), bf16), pltpu.VMEM((T, EB), bf16),
            pltpu.VMEM((T, D), f32),
        ] + [pltpu.VMEM((T * 8, 128), f32)] * (EB // 128),
        compiler_params=params(),
        name="fwd_scan",
    )(dtk, u, b_cols, c_cols, g, par, entering, act, gate, gg, out_weight, cot, tokens, normed, in_weight)


def bwd_kernel(
    L, sums, blocks, dtk_ref, u_ref, g_ref, b_ref, c_ref, par_ref, wts_ref, fin_ref, h_ref, spre_ref, act_ref, proj_ref,
    gc_ref, *refs,
):
    arrays = len(sums.kinds)
    x_refs, refs = refs[:arrays], refs[arrays:]
    gap_ref, chan_ref, gproj_ref = refs[:3]
    o_refs, refs = refs[3 : 3 + arrays], refs[3 + arrays :]
    acc_ref, gb_ref, rank_ref, pre_ref = refs[:4]
    rate = lane_tiles(rates(L, par_ref))
    tiles = len(rate)
    bsum_refs, wsum_refs = refs[4 : 4 + tiles], refs[4 + tiles : 4 + 2 * tiles]
    sums.bind(x_refs, o_refs, refs[4 + 2 * tiles :])
    T, states = u_ref.shape[0], L.N
    chunks = T // TC
    width = TC * states
    i = pl.program_id(0)

    @pl.when(i == 0)
    def _():
        acc_ref[...] = jnp.zeros_like(acc_ref)
        rank_ref[...] = jnp.zeros_like(rank_ref)
        sums.barrier()

    def chunk(i, carry):
        flow, total = list(carry[:tiles]), list(carry[tiles:])
        c = chunks - 1 - i
        base = pl.multiple_of(c * TC, TC)
        row = pl.multiple_of(c * width, width)
        b_cols, c_cols = b_ref[c], c_ref[c]

        def fetch(j):
            at = pl.ds(row + j * states, states)
            rows = [row_at(ref, base + j) for ref in (dtk_ref, u_ref, g_ref)]
            return rows + [spread(b_cols, j), spread(c_cols, j), acc_ref[at, :], lane_tiles(h_ref[at, :])]

        for j, (d, u, g, b_now, c_now, acc, before) in ahead_of(reversed(range(TC)), fetch):
            part = pl.ds((base + j) * 8, 8)
            for k in range(tiles):
                adj = c_now * g[k] + flow[k]
                flow[k] = jnp.exp2(d[k] * rate[k]) * adj
                wr = flow[k] * before[k].astype(f32) * rate[k]
                total[k] = total[k] + wr * d[k]
                wsum_refs[k][part, :] = halves(wr)
                bsum_refs[k][part, :] = halves(adj * b_now)
                acc = acc + adj * u[k]
            acc_ref[pl.ds(row + j * states, states), :] = acc
        return tuple(flow) + tuple(total)

    none = jnp.zeros((states, 128), f32)
    out = tuple(lane_tiles(fin_ref[...])) + (none,) * tiles
    for q in range(BLOCK_SLOTS):
        for n in range(sums.ticks()):
            block, quarter = divmod(n, BLOCK_SLOTS)
            if quarter == q and block < blocks:
                pl.when(i == block)(functools.partial(sums.tick, n))
        out = lax.fori_loop(q * chunks // BLOCK_SLOTS, (q + 1) * chunks // BLOCK_SLOTS, chunk, out)
    total = jnp.concatenate(out[tiles:], axis=1)
    skip = par_ref[0, L.skip : L.skip + 1, :]

    def tile(k, carry):
        bias_sum, skip_sum = carry
        rows = pl.ds(pl.multiple_of(k * 16, 16), 16)
        bsum, wsum = (
            jnp.concatenate([fold_rows(refs, k * 16), fold_rows(refs, k * 16 + 8)], axis=0)
            for refs in (bsum_refs, wsum_refs)
        )
        spre, act, g = spre_ref[rows, :], act_ref[rows, :], g_ref[rows, :]
        grad = (wsum * (1.0 / LOG2E) + act * bsum) * jax.nn.sigmoid(spre)
        gap_ref[rows, :] = g * skip + softplus(spre) * bsum
        pre_ref[rows, :] = grad.astype(bf16)
        bias_sum = bias_sum + halves(grad)
        skip_sum = skip_sum + halves(g * act)
        return bias_sum, skip_sum

    none = jnp.zeros((8, EB), f32)
    bias_sum, skip_sum = lax.fori_loop(0, T // 16, tile, (none, none))
    R = L.R
    pre = pre_ref[...]
    step_low = proj_ref[...].astype(bf16)
    grad_step_w = lax.dot_general(step_low, pre, TN, preferred_element_type=f32)
    chan_ref[0] = jnp.concatenate(
        [
            grad_step_w[0:R],
            total * (1.0 / LOG2E),
            jnp.sum(bias_sum, axis=0, keepdims=True),
            jnp.sum(skip_sum, axis=0, keepdims=True),
            jnp.zeros((128 - R - states - 2, EB), f32),
        ],
        axis=0,
    ).astype(bf16)
    weights = wts_ref[0, L.step : L.step + R, :].astype(f32)
    weights = jnp.concatenate([weights, jnp.zeros((128 - R, EB), f32)], axis=0).astype(bf16)
    rank_ref[...] += lax.dot_general(pre, weights, NT, preferred_element_type=f32)

    @pl.when(i == pl.num_programs(0) - 1)
    def _():
        lane_sums(states, acc_ref, gb_ref, chunks)
        dims = (width, 128)
        state = lax.rem(lax.broadcasted_iota(jnp.int32, dims, 0), states)
        target = lax.broadcasted_iota(jnp.int32, dims, 1)
        diag = same_step(states, T)
        total = rank_ref[...]
        for ref, start in ((gb_ref, R), (gc_ref, R + states)):
            fold = (target == state + start).astype(f32).astype(bf16)
            kept = jnp.where(diag, ref[...], 0.0).astype(bf16)
            total = total + jnp.dot(kept, fold, preferred_element_type=f32)
        gproj_ref[...] = total.astype(bf16)
        for n in range(blocks * BLOCK_SLOTS, sums.ticks()):
            sums.tick(n)
        sums.drain()


def bwd_scan(L, dtk, u, g, b_cols, c_cols, par, wts, arriving, held, spre, act, proj, grad_c, arrays, sums):
    T, E = dtk.shape
    N = L.N
    blocks = E // EB
    return pl.pallas_call(
        functools.partial(bwd_kernel, L, sums, blocks),
        grid=(blocks,),
        in_specs=[
            cols(T), cols(T), cols(T), once(*b_cols.shape), once(*c_cols.shape), lead(PAR, EB),
            lead(WTS, EB), cols(N), cols(held.shape[0]), cols(T), cols(T), whole(T, 128), whole(T, TC * N),
        ] + [once(*v.shape) for v in arrays],
        out_specs=[cols(T), lead(128, EB), whole(T, 128)] + [whole(*o.shape) for o in sums.outs()],
        out_shape=[shape(f32, T, E), shape(bf16, blocks, 128, EB), shape(bf16, T, 128)] + sums.outs(),
        scratch_shapes=[
            pltpu.VMEM((T * N, 128), f32),
            pltpu.VMEM((T, TC * N), f32), pltpu.VMEM((T, 128), f32), pltpu.VMEM((T, EB), bf16),
        ] + [pltpu.VMEM((T * 8, 128), f32)] * (2 * EB // 128) + sums.scratch(),
        compiler_params=params(collective_id=3, has_side_effects=True),
        name="bwd_scan",
    )(dtk, u, g, b_cols, c_cols, par, wts, arriving, held, spre, act, proj, grad_c, *arrays)


def conv_kernel(
    L, count, gap_ref, gproj_ref, wts_ref, act_ref, cs_ref, inner_ref, marks_ref,
    gc_ref, chan_ref, after_ref, xs_ref, edge_ref, got_ref, send_sem, recv_sem,
):
    T = gap_ref.shape[0]
    i = pl.program_id(0)
    blocks = edge_ref.shape[0]
    si, ci = lax.axis_index("seq"), lax.axis_index("chan")
    before = lax.rem(ci + count - 1, count)

    @pl.when(i == 0)
    def _():
        barrier = pltpu.get_barrier_semaphore()
        for other in (before, lax.rem(ci + 1, count)):
            pl.semaphore_signal(barrier, inc=1, device_id=(si, other), device_id_type=pl.DeviceIdType.MESH)
        pl.semaphore_wait(barrier, 2)

    def edge(b):
        return pltpu.make_async_remote_copy(
            src_ref=edge_ref.at[b], dst_ref=got_ref.at[b], send_sem=send_sem.at[b], recv_sem=recv_sem.at[b],
            device_id=(si, before), device_id_type=pl.DeviceIdType.MESH,
        )

    K, wide = L.K, L.R + 2 * L.N
    weights = wts_ref[0].astype(f32)
    row = lax.broadcasted_iota(jnp.int32, weights.shape, 0)
    weights = jnp.where(row < wide, weights, 0.0).astype(bf16)
    gc_ref[...] = jnp.dot(gproj_ref[...], weights, preferred_element_type=f32)
    act_low = act_ref[...].astype(bf16)
    grad_proj = lax.dot_general(gproj_ref[...], act_low, TN, preferred_element_type=f32)
    xs_ref[...] = inner_ref[...].astype(f32)

    def tile(k, carry):
        r = pl.multiple_of(k * RT, RT)
        rows = pl.ds(r, RT)
        total = cs_ref[rows, :]
        sig = jax.nn.sigmoid(total)
        grad = (gc_ref[rows, :] + gap_ref[rows, :]) * sig * (1.0 + total * (1.0 - sig))
        gc_ref[rows, :] = grad
        block = xs_ref[pl.ds(pl.multiple_of(r + HALO - 8, 8), RT + 8), :]
        out = [carry[K] + jnp.sum(grad.reshape(RT // 8, 8, EB), axis=0)]
        for j in range(K):
            part = grad * block[8 - j : RT + 8 - j]
            if j > 0:
                part = part * marks_ref[rows, j - 1 : j]
            out.insert(0, carry[K - 1 - j] + jnp.sum(part.reshape(RT // 8, 8, EB), axis=0))
        return tuple(out)

    none = jnp.zeros((8, EB), f32)
    sums = lax.fori_loop(0, T // RT, tile, (none,) * (K + 1))
    edge_ref[i] = gc_ref[0:8, :]
    edge(i).start()
    chan_ref[0] = jnp.concatenate(
        [grad_proj[0:wide]]
        + [jnp.sum(s, axis=0, keepdims=True) for s in sums]
        + [jnp.zeros((128 - wide - K - 1, EB), f32)],
        axis=0,
    ).astype(bf16)

    @pl.when(i == blocks - 1)
    def _():
        for b in range(blocks):
            edge(b).wait()
            rows = jnp.where(ci == count - 1, 0.0, got_ref[b])
            after_ref[:, b * EB : (b + 1) * EB] = rows


def conv_back(L, count, gap, gproj, wts, act, cs, inner, marks):
    T, E = gap.shape
    blocks = E // EB
    return pl.pallas_call(
        functools.partial(conv_kernel, L, count),
        grid=(blocks,),
        in_specs=[
            cols(T), whole(T, 128), lead(WTS, EB), cols(T), cols(T), cols(T + HALO), whole(*marks.shape),
        ],
        out_specs=[cols(T), lead(128, EB), whole(8, E)],
        out_shape=[shape(f32, T, E), shape(bf16, blocks, 128, EB), shape(f32, 8, E)],
        scratch_shapes=[
            pltpu.VMEM((T + HALO, EB), f32),
            pltpu.VMEM((blocks, 8, EB), f32),
            pltpu.VMEM((blocks, 8, EB), f32),
            pltpu.SemaphoreType.DMA((blocks,)),
            pltpu.SemaphoreType.DMA((blocks,)),
        ],
        compiler_params=params(collective_id=4, has_side_effects=True),
        name="conv_back",
    )(gap, gproj, wts, act, cs, inner, marks)


def tail_kernel(
    L, gc_ref, after_ref, par_ref, marks_ref, normed_ref, wi_ref, gn_ref, tok_ref, cot_ref, gain_ref,
    gin_ref, gtok_ref, ggain_ref, ext_ref, low_ref, sum_ref,
):
    T, D = tok_ref.shape
    K = L.K
    i = pl.program_id(0)
    ext_ref[0:T, :] = gc_ref[...]
    ext_ref[T : T + 8, :] = after_ref[...]
    taps = [par_ref[0, L.conv + j : L.conv + j + 1, :] for j in range(K)]

    def tile(r):
        block = ext_ref[pl.ds(r, RT + 8), :]
        marks = marks_ref[pl.ds(r, RT + 8), :]
        total = taps[K - 1] * block[0:RT]
        for j in range(1, K):
            masked = block * marks[:, j - 1 : j]
            total = total + taps[K - 1 - j] * masked[j : RT + j]
        low_ref[pl.ds(r, RT), :] = total.astype(bf16)

    row_tiles(T, tile)
    gin_ref[...] = lax.dot_general(
        low_ref[...], normed_ref[...], TN, preferred_element_type=f32
    ).astype(bf16)
    part = lax.dot_general(low_ref[...], wi_ref[...], NT, preferred_element_type=f32)

    @pl.when(i == 0)
    def _():
        sum_ref[...] = gn_ref[...] + part

    @pl.when(i > 0)
    def _():
        sum_ref[...] += part

    @pl.when(i == pl.num_programs(0) - 1)
    def _():
        gain = gain_ref[...].reshape(1, D)

        def last(k, total):
            rows = pl.ds(pl.multiple_of(k * 16, 16), 16)
            x = tok_ref[rows, :].astype(f32)
            grad = sum_ref[rows, :]
            inv = lax.rsqrt(jnp.mean(x * x, axis=1, keepdims=True) + epsilon)
            scaled = grad * gain
            mean = jnp.mean(x * scaled, axis=1, keepdims=True)
            gtok_ref[rows, :] = (
                cot_ref[rows, :].astype(f32) + inv * scaled - x * (inv * inv * inv * mean)
            )
            return total + jnp.sum((grad * x * inv).reshape(2, 8, D), axis=0)

        total = lax.fori_loop(0, T // 16, last, jnp.zeros((8, D), f32))
        ggain_ref[...] = jnp.sum(total, axis=0, keepdims=True)


def tail(L, gc, after, par, marks, normed, in_weight, gn, tokens, cot, gain):
    T, E = gc.shape
    D = tokens.shape[1]
    blocks = E // EB
    return pl.pallas_call(
        functools.partial(tail_kernel, L),
        grid=(blocks,),
        in_specs=[
            cols(T), cols(8), lead(PAR, EB), whole(*marks.shape), whole(T, D), cols(D), whole(T, D),
            whole(T, D), whole(T, D), whole(D),
        ],
        out_specs=[tall(EB, D), whole(T, D), whole(1, D)],
        out_shape=[shape(bf16, E, D), shape(f32, T, D), shape(f32, 1, D)],
        scratch_shapes=[
            pltpu.VMEM((T + 8, EB), f32), pltpu.VMEM((T, EB), bf16), pltpu.VMEM((T, D), f32),
        ],
        compiler_params=params(),
        name="tail",
    )(gc, after, par, marks, normed, in_weight, gn, tokens, cot, gain)


class Sums:
    def __init__(self, chan_count, seq_count, kinds, shapes, phases, skew=1, pace=1, begins=None, blocked=()):
        self.cc, self.sc = chan_count, seq_count
        self.kinds = kinds
        self.phases, self.skew, self.pace = phases, skew, pace
        self.begins = begins
        self.blocked = blocked
        self.size = 8 * seq_count
        self.bits = [1 << i for i in range(chan_count.bit_length() - 1)]
        self.z_bits = [2 << i for i in range(seq_count.bit_length() - 2)]
        self.pieces = [
            (a, r, dims[2]) for a, dims in enumerate(shapes) for r in range(0, dims[1], 2 * self.size)
        ]
        self.shapes = shapes

    def half(self, p):
        return self.kinds[self.pieces[p][0]] is not None

    def stages(self, p):
        bits = self.bits if p % 2 == 0 else self.bits[::-1]
        return (
            [("core", 1)] + [("chan", b) for b in bits] + [("z", b) for b in self.z_bits]
            + [("zgather", b) for b in self.z_bits[::-1]] + ([("move", 0)] if self.half(p) else [])
            + [("cgather", 1)]
        )

    def span(self, p):
        halvings = 2 + len(self.bits)
        phase = self.phases[self.pieces[p][0]]
        first = halvings if phase == "gather" else 0
        return first, halvings if phase == "halve" else len(self.stages(p))

    def begin(self, p):
        if self.begins is not None:
            return self.begins[p]
        phase = self.phases[self.pieces[p][0]]
        before = [q for q in range(p) if self.phases[self.pieces[q][0]] == phase]
        return self.skew * (len(before) // 2)

    def ticks(self):
        return max(
            self.begin(p) + self.pace * (self.span(p)[1] - self.span(p)[0]) for p in range(len(self.pieces))
        ) + 1

    def final(self, p):
        a, first, width = self.pieces[p]
        return pl.ds(first // 4, self.size // 2)

    def outs(self):
        found = []
        for kind, dims, phase in zip(self.kinds, self.shapes, self.phases):
            if phase == "halve":
                found.append(shape(bf16, dims[1] // 4, dims[2]))
            elif len(found) in self.blocked:
                found.append(shape(bf16, 2 * dims[1], dims[2]))
            else:
                found.append(shape(bf16, *(dims[1:] if kind is None else (2,) + tuple(dims[1:]))))
        return found

    def scratch(self):
        found = []
        for p, (a, r, width) in enumerate(self.pieces):
            small = self.span(p)[0] > 0
            for k in range(len(self.bits) + 1):
                dims = (self.cc >> k, self.size, width)
                found.append(pltpu.VMEM((1, 16, 128) if small else dims, bf16))
            for k in range(len(self.z_bits)):
                found.append(pltpu.VMEM((self.size >> (k + 1), width), bf16))
            found.append(pltpu.VMEM((self.size, width), bf16))
        dims = (len(self.pieces), len(self.bits) + 2 * len(self.z_bits) + 3, self.cc)
        return found + [pltpu.SemaphoreType.DMA(dims), pltpu.SemaphoreType.DMA(dims)]

    def bind(self, x_refs, o_refs, scratch):
        self.x, self.o = x_refs, o_refs
        each = len(self.bits) + len(self.z_bits) + 2
        self.held = [scratch[p * each : (p + 1) * each] for p in range(len(self.pieces))]
        self.send_sem, self.recv_sem = scratch[-2:]
        self.si, self.ci = lax.axis_index("seq"), lax.axis_index("chan")
        self.core = lax.rem(self.si, 2)

    def side(self, bit):
        return lax.rem(self.si // bit, 2)

    def across(self, bit):
        return (self.si + bit - 2 * bit * self.side(bit), self.ci)

    def barrier(self):
        barrier = pltpu.get_barrier_semaphore()
        others = [(self.si, lax.rem(self.ci + k, self.cc)) for k in range(1, self.cc)]
        others += [self.across(bit) for bit in [1] + self.z_bits]
        for other in others:
            pl.semaphore_signal(barrier, inc=1, device_id=other, device_id_type=pl.DeviceIdType.MESH)
        pl.semaphore_wait(barrier, len(others))

    def copy(self, p, s, slot, src, dst, device):
        return pltpu.make_async_remote_copy(
            src_ref=src, dst_ref=dst, send_sem=self.send_sem.at[p, s, slot],
            recv_sem=self.recv_sem.at[p, s, slot], device_id=device, device_id_type=pl.DeviceIdType.MESH,
        )

    def kept(self, p, s, keep):
        name, bit = self.stages(p)[s]
        if name == "core":
            a, start, width = self.pieces[p]
            side = self.core if keep else 1 - self.core
            return [self.x[a].at[:, pl.ds(pl.multiple_of(start + side * self.size, 16), self.size), :]]
        ref = self.held[p][s - 1]
        if name == "z":
            side = self.side(bit) if keep else 1 - self.side(bit)
            k = self.z_bits.index(bit)
            rows = self.size >> (k + 1)
            rows = pl.ds(pl.multiple_of(side * rows, 16), rows)
            return [ref.at[0, rows, :] if k == 0 else ref.at[rows, :]]
        mine = lax.rem(self.ci // bit, 2)
        side = mine if keep else 1 - mine
        left = sorted(b for n, b in self.stages(p)[s : 1 + len(self.bits)])
        low = 1 << left.index(bit)
        return [
            ref.at[pl.ds((i // low) * 2 * low + side * low + i % low, 1)]
            for i in range((1 << len(left)) // 2)
        ]

    def landing(self, p, s):
        dst = self.held[p][s]
        return [dst.at[pl.ds(i, 1)] for i in range(dst.shape[0])] if self.stages(p)[s][0] == "chan" else [dst]

    def gathered(self, p, done):
        start, rows = 0, self.size
        for bit in self.z_bits[:done]:
            rows //= 2
            start = start + self.side(bit) * rows
        if self.half(p):
            return self.held[p][-1].at[pl.ds(pl.multiple_of(start, 16), rows), :]
        start = start + self.pieces[p][1] + self.core * self.size
        return self.o[self.pieces[p][0]].at[pl.ds(pl.multiple_of(start, 16), rows), :]

    def target(self, p, v):
        a, first, width = self.pieces[p]
        base = self.kinds[a]
        if a in self.blocked:
            row = first * self.cc + v * 2 * self.size
            owner_rows = 2 * self.shapes[a][1]
            rows = pl.ds(pl.multiple_of(row % owner_rows + self.core * self.size, 16), self.size)
            return base + row // owner_rows, self.o[a].at[rows, :]
        rows = pl.ds(pl.multiple_of(first + self.core * self.size, 16), self.size)
        return base + v // 2, self.o[a].at[v % 2, rows, :]

    def move(self, p, s, v):
        goal, place = self.target(p, v)
        return goal, place, self.copy(p, s, v, self.held[p][-1], place, (self.si, goal))

    def pass_on(self, p, s, v):
        goal, place = self.target(p, v)
        return goal, self.copy(p, s, v, place, place, self.across(1))

    def copies(self, p, s):
        name, bit = self.stages(p)[s]
        if name in ("core", "chan", "z"):
            device = (self.si, self.ci + bit - 2 * bit * lax.rem(self.ci // bit, 2))
            device = device if name == "chan" else self.across(bit)
            pairs = zip(self.kept(p, s, False), self.landing(p, s))
            return [self.copy(p, s, i, src, dst, device) for i, (src, dst) in enumerate(pairs)]
        if name == "zgather":
            place = self.gathered(p, self.z_bits.index(bit) + 1)
        else:
            a, first, width = self.pieces[p]
            rows = pl.ds(pl.multiple_of(first + self.core * self.size, 16), self.size)
            place = self.o[a].at[rows, :]
        return [self.copy(p, s, 0, place, place, self.across(bit))]

    def last_of_half(self, p, s):
        return self.half(p) and self.stages(p)[s][0] == "cgather"

    def start(self, p, s):
        if self.stages(p)[s][0] == "move":
            for v in range(self.cc):
                @pl.when(self.ci == v)
                def _(v=v):
                    goal, place, copy = self.move(p, s, v)
                    if goal == v:
                        place[...] = self.held[p][-1][...]
                    else:
                        copy.start()
        elif self.last_of_half(p, s):
            for v in range(self.cc):
                goal, copy = self.pass_on(p, s, v)
                pl.when(self.ci == goal)(copy.start)
        else:
            for copy in self.copies(p, s):
                copy.start()

    def finish(self, p, s):
        name, bit = self.stages(p)[s]
        if name == "move":
            for v in range(self.cc):
                goal, place, copy = self.move(p, s, v)
                if goal != v:
                    pl.when(self.ci == goal)(copy.wait_recv)
            return
        if self.last_of_half(p, s):
            for v in range(self.cc):
                goal, copy = self.pass_on(p, s, v)
                pl.when(self.ci == goal)(copy.wait_recv)
            return
        for copy in self.copies(p, s):
            copy.wait_recv()
        if name in ("core", "chan", "z"):
            last = s == len(self.bits) + len(self.z_bits)
            handed = self.phases[self.pieces[p][0]] == "halve" and self.span(p)[1] == s + 1
            for src, dst in zip(self.kept(p, s, True), self.landing(p, s)):
                total = (dst[...].astype(f32) + src[...].astype(f32)).astype(bf16)
                if handed:
                    dst = self.o[self.pieces[p][0]].at[self.final(p), :]
                elif last:
                    dst = self.gathered(p, len(self.z_bits))
                dst[...] = total

    def tick(self, n):
        for p in range(len(self.pieces)):
            first, end = self.span(p)
            s, rest = divmod(n - self.begin(p), self.pace)
            s += first
            if rest != 0:
                continue
            if first + 1 <= s <= end:
                self.finish(p, s - 1)
            if first > 0 and s == first:
                self.held[p][first - 1][...] = self.x[self.pieces[p][0]][self.final(p), :]
            if first <= s < end:
                self.start(p, s)

    def drain(self):
        for p in range(len(self.pieces)):
            for s in range(*self.span(p)):
                if self.stages(p)[s][0] == "move":
                    for v in range(self.cc):
                        goal, place, copy = self.move(p, s, v)
                        if goal != v:
                            pl.when(self.ci == v)(copy.wait_send)
                elif self.last_of_half(p, s):
                    for v in range(self.cc):
                        goal, copy = self.pass_on(p, s, v)
                        pl.when(self.ci == goal)(copy.wait_send)
                else:
                    for copy in self.copies(p, s):
                        copy.wait_send()

    def hand_over(self, refs):
        for kind, src, dst in zip(self.kinds, self.o, refs):
            def work(src=src, dst=dst):
                dst[...] = src[...]

            if kind is None:
                work()
            else:
                pl.when((self.ci >= kind) & (self.ci < kind + self.cc // 2))(work)


def sum_kernel(sums, *refs):
    arrays = len(sums.kinds)
    sums.bind(refs[:arrays], refs[arrays : 2 * arrays], refs[2 * arrays :])
    sums.barrier()
    for n in range(sums.ticks()):
        sums.tick(n)
    sums.drain()


def sum_owned(arrays, shapes, kinds, phases, chan_count, seq_count):
    sums = Sums(chan_count, seq_count, kinds, shapes, phases)
    vmem = pl.BlockSpec(memory_space=pltpu.VMEM)
    return pl.pallas_call(
        functools.partial(sum_kernel, sums),
        in_specs=[vmem] * len(arrays),
        out_specs=[vmem] * len(arrays),
        out_shape=sums.outs(),
        scratch_shapes=sums.scratch(),
        compiler_params=params(collective_id=0, has_side_effects=True),
        name="sum_owned",
    )(*arrays)


def tail_sum_kernel(
    L, sums, gain_row, gc_ref, after_ref, taps_ref, marks_ref, normed_ref, wi_ref, gn_ref, tok_ref, cot_ref, gain_ref,
    d_ref, e_ref, *refs,
):
    early_refs, gtok_ref, refs = refs[:2], refs[2], refs[3:]
    arrays = len(sums.kinds)
    out_refs, held_refs, refs = refs[:arrays], refs[arrays : 2 * arrays], refs[2 * arrays :]
    ext_ref, low_ref, sum_ref, xin_ref, xe_ref = refs[:5]
    sums.bind((xin_ref, d_ref, xe_ref) + early_refs, held_refs, refs[5:])
    T, D = tok_ref.shape
    K, cc = L.K, sums.cc
    i = pl.program_id(0)
    blocks = xin_ref.shape[1] // (2 * sums.size)
    width = low_ref.shape[1]

    def tick_at(place):
        for b in range(blocks):
            pl.when(i == b)(functools.partial(sums.tick, 2 * b + place))

    @pl.when(i == 0)
    def _():
        sums.barrier()
        xe_ref[...] = e_ref[...]

    tick_at(0)
    ext_ref[0:T, :] = gc_ref[...]
    ext_ref[T : T + 8, :] = after_ref[...]
    taps = [taps_ref[j : j + 1, :] for j in range(K)]

    def tile(r):
        block = ext_ref[pl.ds(r, RT + 8), :]
        marks = marks_ref[pl.ds(r, RT + 8), :]
        total = taps[K - 1] * block[0:RT]
        for j in range(1, K):
            masked = block * marks[:, j - 1 : j]
            total = total + taps[K - 1 - j] * masked[j : RT + j]
        low_ref[pl.ds(r, RT), :] = total.astype(bf16)

    row_tiles(T, tile)
    tick_at(1)
    grad = lax.dot_general(
        low_ref[...], normed_ref[...], TN, preferred_element_type=f32
    ).astype(bf16)
    rows = pl.ds(pl.multiple_of(i * 2 * sums.size, 16), 2 * sums.size)
    for v in range(cc):
        xin_ref[v, rows, :] = grad[v * 2 * sums.size : (v + 1) * 2 * sums.size]
    pl.when(i == blocks - 1)(functools.partial(sums.tick, 2 * blocks))
    part = lax.dot_general(low_ref[...], wi_ref[...], NT, preferred_element_type=f32)

    @pl.when(i == 0)
    def _():
        sum_ref[...] = gn_ref[...] + part

    @pl.when(i > 0)
    def _():
        sum_ref[...] += part

    @pl.when(i == blocks - 1)
    def _():
        gain = gain_ref[...].reshape(1, D)

        def last(k, total):
            rows = pl.ds(pl.multiple_of(k * 16, 16), 16)
            x = tok_ref[rows, :].astype(f32)
            grad = sum_ref[rows, :]
            inv = lax.rsqrt(jnp.mean(x * x, axis=1, keepdims=True) + epsilon)
            scaled = grad * gain
            mean = jnp.mean(x * scaled, axis=1, keepdims=True)
            gtok_ref[rows, :] = (
                cot_ref[rows, :].astype(f32) + inv * scaled - x * (inv * inv * inv * mean)
            )
            return total + jnp.sum((grad * x * inv).reshape(2, 8, D), axis=0)

        total = lax.fori_loop(0, T // 16, last, jnp.zeros((8, D), f32))
        total = jnp.broadcast_to(jnp.sum(total, axis=0, keepdims=True), (16, D))
        share, start = D // cc, gain_row // 16 * 16
        dims = (16, xe_ref.shape[2])
        here = lax.broadcasted_iota(jnp.int32, dims, 0) == gain_row - start
        here = here & (lax.broadcasted_iota(jnp.int32, dims, 1) < share)
        for q in range(cc):
            turned = total if q == 0 else pltpu.roll(total, D - q * share, 1)
            old = xe_ref[q, start : start + 16, :].astype(f32)
            xe_ref[q, start : start + 16, :] = jnp.where(here, turned[:, : dims[1]], old).astype(bf16)
        for n in range(2 * blocks + 1, sums.ticks()):
            sums.tick(n)
        sums.drain()
        sums.hand_over(out_refs)


def tail_sum(
    L, counts, gc, after, taps, marks, normed, in_weight, gn, tokens, cot, gain, d, e, early, early_shapes, kinds,
    gain_row,
):
    T, E = gc.shape
    D = tokens.shape[1]
    cc, sc = counts
    piece = 16 * sc
    wide = cc * piece
    blocks = E // wide
    shapes = [(cc, E // cc, D), d.shape, e.shape] + early_shapes
    pieces = [v[1] // piece for v in shapes]
    begins = [2 * (b + 1) for b in range(pieces[0])] + [0] * pieces[1] + [2 * blocks + 1] * pieces[2]
    begins += [k // 2 for k in range(pieces[3] + pieces[4])]
    sums = Sums(
        cc, sc, [0, None, None] + kinds, shapes, ["all"] * 3 + ["gather"] * 2, begins=begins, blocked=(0,)
    )
    return pl.pallas_call(
        functools.partial(tail_sum_kernel, L, sums, gain_row),
        grid=(blocks,),
        in_specs=[
            cols(T, wide), cols(8, wide), cols(8, wide), whole(*marks.shape), whole(T, D), cols(D, wide),
            whole(T, D), whole(T, D), whole(T, D), whole(D), once(*d.shape), once(*e.shape),
        ] + [once(*v.shape) for v in early],
        out_specs=[whole(T, D)] + [whole(*o.shape) for o in sums.outs()],
        out_shape=[shape(f32, T, D)] + sums.outs(),
        scratch_shapes=[pltpu.VMEM(o.shape, o.dtype) for o in sums.outs()] + [
            pltpu.VMEM((T + 8, wide), f32), pltpu.VMEM((T, wide), bf16), pltpu.VMEM((T, D), f32),
            pltpu.VMEM(shapes[0], bf16), pltpu.VMEM(e.shape, bf16),
        ] + sums.scratch(),
        compiler_params=params(collective_id=5, has_side_effects=True),
        name="tail_sum",
    )(gc, after, taps, marks, normed, in_weight, gn, tokens, cot, gain, d, e, *early)


def unpack_kernel(L, inner_ref, gate_ref, out_ref, d_ref, e_ref, gin_ref, gout_ref, *refs):
    first = lax.axis_index("chan") < lax.axis_size("chan") // 2

    @pl.when(first)
    def _():
        gin_ref[...] = inner_ref[...].astype(f32).T

    @pl.when(jnp.logical_not(first))
    def _():
        gin_ref[...] = gate_ref[...].astype(f32).T

    gout_ref[...] = out_ref[...].astype(f32)
    d, e = d_ref[...].astype(f32), e_ref[...].astype(f32)
    R, N, K = L.R, L.N, L.K
    wide = R + 2 * N
    conv_w, conv_b, proj, step_w, step_b, decay, skip, gain = refs
    width = d.shape[1]
    step_w[...] = d[0:R]
    decay[...] = d[R : R + N]
    step_b[...] = d[R + N].reshape(width)
    skip[...] = d[R + N + 1].reshape(width)
    proj[...] = e[0:wide]
    conv_w[...] = e[wide : wide + K]
    conv_b[...] = e[wide + K].reshape(width)
    gain[...] = e[wide + K + 1].reshape(width)


def unpack(L, sums):
    width = sums[3].shape[1]
    rows, D = sums[0].shape
    R, N, K = L.R, L.N, L.K
    return pl.pallas_call(
        functools.partial(unpack_kernel, L),
        out_shape=[
            shape(f32, D, rows), shape(f32, *sums[2].shape), shape(f32, K, width), shape(f32, width),
            shape(f32, R + 2 * N, width), shape(f32, R, width), shape(f32, width),
            shape(f32, N, width), shape(f32, width), shape(f32, width),
        ],
        compiler_params=params(),
        name="unpack",
    )(*sums)


def local(
    tokens, norm_gain, in_weight, conv_weight, conv_bias, proj_weight, step_weight,
    step_bias, decay_log, skip_gain, out_weight, cotangent, lengths,
):
    T, D = tokens.shape
    E = in_weight.shape[1] // 2
    L = Layout(step_weight.shape[0], decay_log.shape[0], conv_weight.shape[0])
    ci = lax.axis_index("chan")
    cc = lax.axis_size("chan")
    sc = lax.axis_size("seq")
    blocks, share = E // EB, E // cc

    parts = (conv_weight, conv_bias, proj_weight.T, step_weight, step_bias, decay_log, skip_gain)
    gathered = None
    if share != EB:
        wts, par, halo = gather_params(L, cc, parts, tokens)

        def by_block(values):
            values = jnp.moveaxis(values, 0, 1).reshape(-1, blocks, EB)
            return jnp.moveaxis(values, 1, 0)

        parts, gathered = None, (by_block(wts), by_block(par), halo)
    marks, normed, inner, gate, gg, g, cs, act, proj, b_cols, c_cols, taps, *own = front(
        L, cc, lengths, tokens, norm_gain, in_weight, out_weight, cotangent, parts, gathered
    )
    wts, par = gathered[:2] if gathered else own
    spre, dtk, u, entering, arriving = pre_scan(L, cc, proj, par, wts, act, g, marks, b_cols, c_cols)
    held, grad_c, block_out, grad_out, grad_in_gate, gn = fwd_scan(
        L, dtk, u, b_cols, c_cols, g, par, entering, act, gate, gg, out_weight, cotangent, tokens,
        normed, in_weight,
    )

    piece = 16 * sc
    fold = 2 if 2 * share <= piece else 1

    def owned(values):
        values = values.reshape(cc, -1, values.shape[-1] // fold)
        return jnp.pad(values, ((0, 0), (0, -values.shape[1] % piece), (0, 0)))

    def unfolded(values):
        if values.ndim == 2:
            return values[: share * fold].reshape(share, D)
        return values[:, : share * fold].reshape(2 * share, D)

    def by_owner(values):
        if share != EB:
            values = jnp.moveaxis(values, 0, 1).reshape(values.shape[1], cc, share)
            values = jnp.moveaxis(values, 1, 0)
        return jnp.pad(values, ((0, 0), (0, -values.shape[1] % piece), (0, 0)))

    early = [owned(grad_out), owned(grad_in_gate)]
    early_shapes = [v.shape for v in early]
    kinds = [None, cc // 2]
    sums = Sums(cc, sc, kinds, early_shapes, ["halve"] * 2, skew=1, pace=3)
    gap, chan_d, gproj, *early = bwd_scan(
        L, dtk, u, g, b_cols, c_cols, par, wts, arriving, held, spre, act, proj, grad_c, early, sums
    )
    gc, chan_e, after = conv_back(L, cc, gap, gproj, wts, act, cs, inner, marks)
    row = L.R + 2 * L.N + L.K + 1
    chan_d, chan_e = by_owner(chan_d), by_owner(chan_e)
    if share == EB and fold == 1 and E % (cc * piece) == 0:
        grad_tokens, sum_inner, sum_d, sum_e, sum_out, sum_gate = tail_sum(
            L, (cc, sc), gc, after, taps, marks, normed, in_weight, gn, tokens, cotangent, norm_gain,
            chan_d, chan_e, early, early_shapes, kinds, row,
        )
    else:
        grad_in_inner, grad_tokens, grad_gain = tail(
            L, gc, after, par, marks, normed, in_weight, gn, tokens, cotangent, norm_gain
        )
        gain_part = jnp.pad(grad_gain.reshape(cc, 1, D // cc), ((0, 0), (0, 0), (0, share - D // cc)))
        chan_e = lax.dynamic_update_slice(chan_e, gain_part.astype(bf16), (0, row, 0))
        late = [owned(grad_in_inner), chan_d, chan_e]
        sum_inner, sum_d, sum_e, sum_out, sum_gate = sum_owned(
            late + early, [v.shape for v in late] + early_shapes, [0, None, None] + kinds,
            ["all"] * 3 + ["gather"] * 2, cc, sc,
        )
        sum_inner = unfolded(sum_inner)
    sums = [sum_inner, unfolded(sum_gate), unfolded(sum_out), sum_d, sum_e]
    g_in, g_out, conv_w, conv_b, proj_w, step_w, step_b, decay, skip, g_gain = unpack(L, sums)
    return (
        block_out, grad_tokens, g_gain[: D // cc], g_in, conv_w, conv_b, proj_w.T, step_w,
        step_b, decay, skip, g_out,
    )


def solution(mesh):
    tok, row, vec = P(("seq", "chan"), None), P(None, "chan"), P("chan")
    in_specs = (
        tok, P(), P(), row, vec, P("chan", None), row, vec, row, vec, P(), tok, P("seq", None),
    )
    out_specs = (
        tok, tok, vec, row, row, vec, P("chan", None), row, vec, row, vec, P("chan", None),
    )
    return jax.shard_map(local, mesh=mesh, in_specs=in_specs, out_specs=out_specs, check_vma=False)
```
